32 devices in a mesh: dp: 8 (over y, x, core), head: 4 (over z).
Axes of the slice: x: 2, y: 2, z: 4, core: 2. Of those that a mesh axis runs over, the one named last changes fastest.
Arguments:
- hidden_in: bfloat16 [4096, 1024], P(('dp', 'head')), may hold values from -6 to 6
- segments: int32 [4096], P('dp'), may hold values from 0 to 6, as said below
- value_pick: int32 [4096, 4, 2], P('dp', 'head'), may hold values from 0 to 4, all different within a row
- output_pick: int32 [4096, 4, 2], P('dp', 'head'), may hold values from 0 to 4, all different within a row
- expert_pick: int32 [4096, 16], P(('dp', 'head')), may hold values from 0 to 95, all different within a row; in each aligned block of 128 rows (0 to 127, 128 to 255, ...) at most 32 rows name the same one
- attend_gain: bfloat16 [1024], replicated, may hold values from 0.5 to 1.5
- query_weight: bfloat16 [4, 1024, 128], P('head'), may hold values from -0.1875 to 0.1875
- key_weight: bfloat16 [4, 1024, 128], P('head'), may hold values from -0.1875 to 0.1875
- value_weight: bfloat16 [4, 1024, 640], P('head'), may hold values from -0.1875 to 0.1875
- output_weight: bfloat16 [4, 640, 1024], P('head'), may hold values from -3 to 3
- head_router: bfloat16 [4, 1024, 10], P('head'), may hold values from -0.1875 to 0.1875
- expert_gain: bfloat16 [1024], replicated, may hold values from 0.5 to 1.5
- router: bfloat16 [1024, 96], replicated, may hold values from -0.09375 to 0.09375
- expert_in: bfloat16 [96, 1024, 128], P(('dp', 'head')), may hold values from -0.1875 to 0.1875
- expert_out: bfloat16 [96, 128, 1024], P(('dp', 'head')), may hold values from -0.5 to 0.5
- cotangent: bfloat16 [4096, 1024], P(('dp', 'head')), may hold values from -6 to 6
Outputs:
- output: float32 [4096, 1024], P(('dp', 'head'))
- input_grad: float32 [4096, 1024], P(('dp', 'head'))
- grad_attend_gain: float32 [1024], replicated
- grad_query_weight: float32 [4, 1024, 128], P('head')
- grad_key_weight: float32 [4, 1024, 128], P('head')
- grad_value_weight: float32 [4, 1024, 640], P('head')
- grad_output_weight: float32 [4, 640, 1024], P('head')
- grad_head_router: float32 [4, 1024, 10], P('head')
- grad_expert_gain: float32 [1024], replicated
- grad_router: float32 [1024, 96], replicated
- grad_expert_in: float32 [96, 1024, 128], P(('dp', 'head'))
- grad_expert_out: float32 [96, 128, 1024], P(('dp', 'head'))
The draws below stay inside these ranges and needn't reach their ends.
Inputs may be any that keep to these rules, and one draw needn't show every extreme that they name: `segments`: within each group of 512 rows that share an index of dp the numbers start at 0 and rise by 0 or 1 from row to row; equal numbers in a group mark one document, and a group's longest document has 384 tokens. `value_pick`: the two numbers of a token and head differ. `output_pick`: the two numbers of a token and head differ. `expert_pick`: A token's 16 numbers differ; the 128 rows of one device name no expert more than 32 times.
All inputs are finite; a program needn't handle non-finite values.
Results may differ from the reference program's by a relative error of at most 0.019.
Values may be sent and summed in bfloat16 or wider, within the bound.
A program may use at most 128 MiB of HBM per device.

```python
import math
import jax
import jax.numpy as jnp
import numpy as np
from jax import lax

D = 1024
HEADS = 4
DH = 128
NVE = 5
TOPA = 2
EH = 128
TOPK = 16
REPEATS = 1
TOK_DEV = 128
GROUP = 512
TOKENS = 4096
LONGEST = 384
SHORT_DOCS = 4
EXP = 96
CAP = 32
N_DP = 8
DEVICES = 32


def draw_segments(key, part):
    key = jax.random.fold_in(key, 11)
    places = jnp.arange(GROUP, dtype=jnp.int32)

    def one_group(group_key):
        start_key, first_key, second_key = jax.random.split(group_key, 3)
        begin = jax.random.randint(start_key, (), 2, TOK_DEV // 2 + 1, dtype=jnp.int32)
        finish = begin + LONGEST
        first_scores = jax.random.randint(first_key, (GROUP,), 0, GROUP, dtype=jnp.int32) * GROUP + places
        second_scores = jax.random.randint(second_key, (GROUP,), 0, GROUP, dtype=jnp.int32) * GROUP + places
        first_open = (places >= 1) & (places < begin)
        second_open = places > finish
        first_cut = lax.top_k(jnp.where(first_open, first_scores, -1), 1)[1]
        second_cut = lax.top_k(jnp.where(second_open, second_scores, -1), SHORT_DOCS - 1)[1]
        flags = jnp.zeros((GROUP,), jnp.int32).at[first_cut].set(1).at[second_cut].set(1)
        flags = flags.at[begin].set(1).at[finish].set(1)
        return jnp.cumsum(flags).astype(jnp.int32)
    return jax.vmap(one_group)(jax.random.split(key, TOKENS // GROUP)).reshape(TOKENS)


def steps_of(key, extent, cuts, smallest, largest):
    gain = 1.0
    for dim, parts in cuts:
        draws = jax.random.uniform(jax.random.fold_in(jax.random.fold_in(key, 6), dim), (parts,), jnp.float32, smallest / len(cuts), largest / len(cuts))
        gain = gain * jnp.repeat(jnp.exp(draws), extent[dim] // parts).reshape((-1,) + (1,) * (len(extent) - 1 - dim))
    return gain


def different_ones(stream_key, rows, number_of, top, lift):
    order = jax.random.permutation(jax.random.fold_in(stream_key, 1), number_of)
    pull = order
    for power in range(3):
        pull = pull * pull // number_of
    pull = pull * lift // number_of
    tickets = jax.random.randint(jax.random.fold_in(stream_key, 2), (rows, number_of), 0, 4096) + pull
    sure = jax.random.permutation(jax.random.fold_in(stream_key, 3), rows)[jnp.arange(number_of) % rows]
    tickets = jnp.where(jnp.arange(rows)[:, None] == sure[None, :], 1 << 14, tickets)
    priority = tickets * number_of + jnp.arange(number_of)
    return lax.top_k(priority.astype(jnp.int32), top)[1].astype(jnp.int32)


def assign_block(rng, own, number, rows, amount, top, reach, skew):
    order = jax.random.permutation(rng, amount)
    crowded, usual = shares(amount, rows * top, reach, skew, True), shares(amount, rows * top, reach, skew, False)
    places = jnp.arange(amount)

    def named(sizes, offset_by):
        used = int((sizes > 0).sum())
        fixed = max(1, used // 4)
        passed = fixed + (places - fixed + offset_by * (used - fixed)) % max(1, amount - fixed)
        return jnp.zeros((amount,), jnp.int32).at[order[jnp.where(places < fixed, places, passed)]].set(jnp.asarray(sizes, jnp.int32))

    sizes = jnp.where(number % 4 == 0, named(crowded, number // 4), named(usual, number - number // 4 - 1))
    mixed = jax.random.permutation(jax.random.fold_in(own, 3), amount)
    donor, sink = mixed[0:amount // 2 * 2:2], mixed[1:amount // 2 * 2:2]
    slack = jnp.minimum(sizes[donor] - 1, reach - sizes[sink]) // 2
    slack = jnp.where((donor == order[0]) | (sink == order[0]) | (sizes[sink] == 0), 0, jnp.maximum(slack, 0))
    passed = jax.random.randint(jax.random.fold_in(own, 4), (amount // 2,), 0, 1 << 20) % (slack + 1)
    sizes = sizes.at[donor].add(-passed).at[sink].add(passed)
    items = jnp.searchsorted(jnp.cumsum(sizes), jnp.arange(rows * top), side="right").astype(jnp.int32)
    grid = items.reshape(top, rows).T
    grid = grid[jax.random.permutation(jax.random.fold_in(own, 1), rows)]
    offset_by = jax.random.randint(jax.random.fold_in(own, 2), (rows, 1), 0, top)
    return jnp.take_along_axis(grid, (jnp.arange(top)[None, :] + offset_by) % top, axis=1)


def shares(amount, total, reach, slope, full):
    portions = [(1 << 20) // math.isqrt(standing ** slope) + 1 for standing in range(1, amount + 1)]
    largest = reach if full else min(reach, max(-(-total // amount), total * portions[0] // sum(portions)))
    least = 1 if total - largest >= amount - 1 else 0
    given, rest = [largest] + [least] * (amount - 1), total - largest - least * (amount - 1)
    while rest > 0:
        movable = [i for i in range(1, amount) if given[i] < largest] or [i for i in range(1, amount) if given[i] < reach]
        pool, budget = sum([portions[i] for i in movable]), rest
        for i in movable:
            more = min(reach - given[i], max(1, budget * portions[i] // pool), rest)
            given[i] = given[i] + more
            rest = rest - more
    return np.array(given)


def noise(rng, dims, deviation, limit, shards=(), held_as=jnp.bfloat16):
    values = deviation * jax.random.normal(rng, dims, jnp.float32)
    if shards:
        values = values * steps_of(rng, dims, shards, -0.22, 0.18)
    return jnp.clip(values, -limit, limit).astype(held_as)


def setup_inputs(seed: int = 0) -> dict:
    splits = jax.random.split(jax.random.key(seed), 17)
    hidden_in = noise(splits[0], (TOKENS, D), 1.0, 6.0, ((0, 32),))
    segments = draw_segments(jax.random.fold_in(splits[16], 71), 0)
    value_pick = different_ones(splits[2], TOKENS * HEADS, NVE, TOPA, 0).reshape((TOKENS, HEADS, TOPA))
    output_pick = different_ones(splits[3], TOKENS * HEADS, NVE, TOPA, 0).reshape((TOKENS, HEADS, TOPA))
    expert_pick_keys = jax.random.split(jax.random.fold_in(splits[4], 1), TOKENS // TOK_DEV)
    expert_pick_turns = jax.random.permutation(jax.random.fold_in(splits[4], 3), TOKENS // TOK_DEV)
    expert_pick = jax.vmap(lambda own, number: assign_block(jax.random.fold_in(splits[4], 2), own, number, TOK_DEV, EXP, TOPK, CAP, 1))(expert_pick_keys, expert_pick_turns).reshape((TOKENS, TOPK))
    attend_gain = jnp.clip(1.0 + 0.1 * jax.random.normal(splits[5], (D,), jnp.float32), 0.5, 1.5).astype(jnp.bfloat16)
    query_weight = noise(splits[6], (HEADS, D, DH), D ** -0.5, 0.1875, ((0, 4),))
    key_weight = noise(splits[7], (HEADS, D, DH), D ** -0.5, 0.1875, ((0, 4),))
    value_weight = noise(splits[8], (HEADS, D, NVE * DH), D ** -0.5, 0.1875, ((0, 4),))
    output_weight = noise(splits[9], (HEADS, NVE * DH, D), 0.5, 3.0, ((0, 4),))
    head_router = noise(splits[10], (HEADS, D, 2 * NVE), D ** -0.5, 0.1875, ((0, 4),))
    expert_gain = jnp.clip(1.0 + 0.1 * jax.random.normal(splits[11], (D,), jnp.float32), 0.5, 1.5).astype(jnp.bfloat16)
    router = noise(splits[12], (D, EXP), (4 * D) ** -0.5, 0.09375)
    expert_in = noise(splits[13], (EXP, D, EH), D ** -0.5, 0.1875, ((0, 32),))
    expert_out = noise(splits[14], (EXP, EH, D), EH ** -0.5, 0.5, ((0, 32),))
    cotangent = noise(splits[15], (TOKENS, D), 1.0, 6.0, ((0, 32),))
    return {"hidden_in": hidden_in, "segments": segments, "value_pick": value_pick, "output_pick": output_pick, "expert_pick": expert_pick, "attend_gain": attend_gain, "query_weight": query_weight, "key_weight": key_weight, "value_weight": value_weight, "output_weight": output_weight, "head_router": head_router, "expert_gain": expert_gain, "router": router, "expert_in": expert_in, "expert_out": expert_out, "cotangent": cotangent}


@jax.custom_vjp
def low(v):
    return lax.optimization_barrier(v.astype(jnp.bfloat16)).astype(jnp.float32)

@jax.custom_vjp
def low_back(v):
    return v

def low_keep(v):
    return (low(v), None)

def low_pass(kept, grad):
    return (grad,)

def back_keep(v):
    return (v, None)

def back_low(kept, grad):
    return (low(grad),)
low.defvjp(low_keep, low_pass)
low_back.defvjp(back_keep, back_low)
epsilon = 1e-06
theta = 10000.0
negative = -1e+30
highest = lax.Precision.HIGHEST

def rms_scale(residual):
    return lax.rsqrt(lax.optimization_barrier(jnp.mean(residual * residual, axis=-1, keepdims=True)) + epsilon)

def rotate(matrix, cosine_table, sine_table):
    half_width = matrix.shape[-1] // 2
    first_half, second = (matrix[:, :half_width], matrix[:, half_width:])
    return jnp.concatenate([first_half * cosine_table - second * sine_table, second * cosine_table + first_half * sine_table], axis=-1)

def head_mixer(grouped, doc_marks, value_picks, output_picks, weights):
    attend_gain, query_weight, key_weight, value_weight, output_weight, head_router = weights
    row_count = grouped.shape[0]
    inverse = rms_scale(grouped)
    normed = low(grouped * inverse * attend_gain)
    plain_rows = low(grouped)
    position = jnp.arange(row_count, dtype=jnp.float32)[:, None]
    exponent = jnp.arange(DH // 2, dtype=jnp.float32)[None, :]
    angles = position * jnp.power(theta, -2.0 * exponent / DH)
    cosine_table, sine_table = (jnp.cos(angles), jnp.sin(angles))
    places = jnp.arange(row_count, dtype=jnp.int32)
    allowed = (places[None, :] <= places[:, None]) & (doc_marks[:, None] == doc_marks[None, :])
    numbers = jnp.arange(NVE, dtype=jnp.int32)
    value_mask = jnp.any(value_picks[:, :, :, None] == numbers, axis=2).astype(jnp.float32)
    output_mask = jnp.any(output_picks[:, :, :, None] == numbers, axis=2).astype(jnp.float32)
    summed = jnp.zeros((row_count, D), jnp.float32)
    for head_index in range(HEADS):
        queries = low(rotate(low_back(jnp.dot(normed, query_weight[head_index], precision=highest)), cosine_table, sine_table))
        key_rows = low(rotate(low_back(jnp.dot(normed, key_weight[head_index], precision=highest)), cosine_table, sine_table))
        squash = jax.nn.sigmoid(low_back(jnp.dot(normed, head_router[head_index], precision=highest)))
        value_gates = squash[:, :NVE] * value_mask[:, head_index]
        output_gates = squash[:, NVE:] * output_mask[:, head_index]
        expert_values = low_back(jnp.dot(plain_rows, value_weight[head_index], precision=highest)).reshape(row_count, NVE, DH)
        values = low(lax.optimization_barrier(jnp.sum(expert_values * value_gates[:, :, None], axis=1)))
        scores = low_back(jnp.dot(queries, key_rows.T, precision=highest) * DH ** (-0.5))
        scores = jnp.where(allowed, scores, negative)
        highest_score = lax.optimization_barrier(jnp.max(scores, axis=-1, keepdims=True))
        exponents = jnp.exp(scores - highest_score)
        probabilities = low(exponents / lax.optimization_barrier(jnp.sum(exponents, axis=-1, keepdims=True)))
        attended = low_back(jnp.dot(probabilities, values, precision=highest))
        weighted = low((output_gates[:, :, None] * attended[:, None, :]).reshape(row_count, NVE * DH))
        summed = summed + jnp.dot(weighted, output_weight[head_index], precision=highest)
    return summed

def expert_block(normed_rows, picks, router, expert_in, expert_out):
    choice_count = TOK_DEV * TOPK
    flat_picks = picks.reshape(choice_count).astype(jnp.int32)
    onehot = (flat_picks[:, None] == jnp.arange(EXP, dtype=jnp.int32)[None, :]).astype(jnp.int32)
    ranking = lax.optimization_barrier(jnp.sum((jnp.cumsum(onehot, axis=0).astype(jnp.int32) - onehot) * onehot, axis=1)).astype(jnp.int32)
    slot_of = (flat_picks * CAP + ranking).astype(jnp.int32)
    owners = jnp.full((EXP * CAP,), -1, jnp.int32).at[slot_of].set(jnp.arange(choice_count, dtype=jnp.int32))
    filled = owners >= 0
    token_of = (jnp.where(filled, owners, 0) // TOPK).astype(jnp.int32)
    logits = low_back(jnp.dot(normed_rows, router, precision=highest))
    gate_values = jax.nn.sigmoid(jnp.take_along_axis(logits, picks, axis=1))
    arrived = jnp.where(filled[:, None], low_back(normed_rows[token_of]), 0.0).reshape(EXP, CAP, D)
    hidden = low_back(jnp.einsum('ecd,edh->ech', arrived, expert_in, precision=highest))
    activations = low(jax.nn.gelu(hidden))
    produced = low(low_back(jnp.einsum('ech,ehd->ecd', activations, expert_out, precision=highest))).reshape(EXP * CAP, D)
    picked = produced[slot_of].reshape(TOK_DEV, TOPK, D)
    return lax.optimization_barrier(jnp.sum(picked * gate_values[:, :, None], axis=1))

def layer(current, segments, value_pick, output_pick, expert_pick, weights):
    head_weights = weights[:6]
    expert_gain, router, expert_in, expert_out = (weights[6], weights[7], weights[8], weights[9])
    mixer = jax.checkpoint(lambda grouped, doc_marks, vpicks, opicks: head_mixer(grouped, doc_marks, vpicks, opicks, head_weights))
    mixed_rows = lax.map(lambda pieces: mixer(pieces[0], pieces[1], pieces[2], pieces[3]), (current.reshape(N_DP, GROUP, D), segments.reshape(N_DP, GROUP), value_pick.reshape(N_DP, GROUP, HEADS, TOPA), output_pick.reshape(N_DP, GROUP, HEADS, TOPA)))
    middle = current + low_back(mixed_rows.reshape(TOKENS, D))
    normed = low(middle * rms_scale(middle) * expert_gain)
    block_apply = jax.checkpoint(lambda rows_in, picks: expert_block(rows_in, picks, router, expert_in, expert_out))
    expert_rows = lax.map(lambda pieces: block_apply(pieces[0], pieces[1]), (normed.reshape(DEVICES, TOK_DEV, D), expert_pick.reshape(DEVICES, TOK_DEV, TOPK)))
    return middle + expert_rows.reshape(TOKENS, D)

def reference(hidden_in, segments, value_pick, output_pick, expert_pick, attend_gain, query_weight, key_weight, value_weight, output_weight, head_router, expert_gain, router, expert_in, expert_out, cotangent):
    weights = (attend_gain.astype(jnp.float32), query_weight.astype(jnp.float32), key_weight.astype(jnp.float32), value_weight.astype(jnp.float32), output_weight.astype(jnp.float32), head_router.astype(jnp.float32), expert_gain.astype(jnp.float32), router.astype(jnp.float32), expert_in.astype(jnp.float32), expert_out.astype(jnp.float32))

    def forward(params, start_rows):
        current = start_rows
        for repeat in range(REPEATS):
            current = layer(current, segments, value_pick, output_pick, expert_pick, params)
        return current
    output, pullback = jax.vjp(forward, weights, hidden_in.astype(jnp.float32))
    weight_grads, input_grad = pullback(cotangent.astype(jnp.float32))
    return (output, input_grad, weight_grads[0], weight_grads[1], weight_grads[2], weight_grads[3], weight_grads[4], weight_grads[5], weight_grads[6], weight_grads[7], weight_grads[8], weight_grads[9])
```

```python
import jax
import jax.numpy as jnp
from jax import lax
from jax.sharding import PartitionSpec as P

epsilon = 1e-06
theta = 10000.0
negative = -1e30
f32 = jnp.float32
bf16 = jnp.bfloat16
everywhere = ("dp", "head")
whole_rows = 4096


def product(left, right, left_axis, right_axis):
    return lax.dot_general(
        left, right, (((left_axis,), (right_axis,)), ((), ())), preferred_element_type=f32
    )


def rms_scale(residual):
    return lax.rsqrt(jnp.mean(residual * residual, axis=-1, keepdims=True) + epsilon)


def rotary_tables(row_count, head_width):
    half_width = head_width // 2
    position = jnp.arange(row_count, dtype=f32)[:, None]
    exponent = jnp.arange(half_width, dtype=f32)[None, :]
    angles = position * jnp.power(theta, -2.0 * exponent / head_width)
    return (jnp.cos(angles), jnp.sin(angles))


def rotate(matrix, cosine, sine):
    half = matrix.shape[-1] // 2
    first, second = matrix[:, :half], matrix[:, half:]
    return jnp.concatenate([first * cosine - second * sine, second * cosine + first * sine], axis=-1)


def pick_mask(picks, expert_count):
    hits = picks[:, 0, :, None] == jnp.arange(expert_count, dtype=jnp.int32)[None, None, :]
    return jnp.any(hits, axis=1).astype(f32)


def norm_back(residual, inverse, gain, incoming):
    unit_rows = residual * inverse
    scaled = incoming * gain
    gain_grad = jnp.sum(incoming * unit_rows, axis=0)
    row_grad = inverse * (scaled - unit_rows * jnp.mean(scaled * unit_rows, axis=-1, keepdims=True))
    return (row_grad, gain_grad)


def gelu_pair(value):
    inner = jnp.tanh(0.7978845608028654 * (value + 0.044715 * value * value * value))
    slope = 0.5 * (1.0 + inner) + 0.5 * value * (1.0 - inner * inner) * 0.7978845608028654 * (
        1.0 + 3.0 * 0.044715 * value * value
    )
    return (0.5 * value * (1.0 + inner), slope)


def body(
    hidden_in,
    segments,
    value_pick,
    output_pick,
    expert_pick,
    attend_gain,
    query_weight,
    key_weight,
    value_weight,
    output_weight,
    head_router,
    expert_gain,
    router,
    expert_in,
    expert_out,
    cotangent,
):
    tokens, features = hidden_in.shape
    per_device, _, width = expert_in.shape
    head_experts = head_router.shape[2] // 2
    head_width = query_weight.shape[2]
    scale = head_width ** (-0.5)
    query_mat, key_mat, value_mat = query_weight[0], key_weight[0], value_weight[0]
    output_mat, gate_mat = output_weight[0], head_router[0]
    value_mask = pick_mask(value_pick, head_experts)
    output_mask = pick_mask(output_pick, head_experts)
    attend_scale = attend_gain.astype(f32)
    expert_scale = expert_gain.astype(f32)
    me = lax.axis_index("dp") * lax.axis_size("head") + lax.axis_index("head")

    rows = lax.all_gather(hidden_in, "head", axis=0, tiled=True)
    grouped = rows.astype(f32)
    group = grouped.shape[0]
    inverse = rms_scale(grouped)
    normed = (grouped * inverse * attend_scale).astype(bf16)
    cosine, sine = rotary_tables(group, head_width)
    queries = rotate(product(normed, query_mat, 1, 0), cosine, sine).astype(bf16)
    key_rows = rotate(product(normed, key_mat, 1, 0), cosine, sine).astype(bf16)
    squash = jax.nn.sigmoid(product(normed, gate_mat, 1, 0))
    value_gates = squash[:, :head_experts] * value_mask
    output_gates = squash[:, head_experts:] * output_mask
    expert_values = product(rows, value_mat, 1, 0).reshape(group, head_experts, head_width)
    values = jnp.sum(expert_values * value_gates[:, :, None], axis=1).astype(bf16)
    places = jnp.arange(group, dtype=jnp.int32)
    allowed = (places[None, :] <= places[:, None]) & (segments[:, None] == segments[None, :])
    scores = jnp.where(allowed, product(queries, key_rows, 1, 1) * scale, negative)
    exponents = jnp.exp(scores - jnp.max(scores, axis=-1, keepdims=True))
    probabilities = exponents / jnp.sum(exponents, axis=-1, keepdims=True)
    attended = product(probabilities.astype(bf16), values, 1, 0)
    weighted = (
        (output_gates[:, :, None] * attended[:, None, :]).reshape(group, -1).astype(bf16)
    )
    middle = hidden_in.astype(f32) + lax.psum_scatter(
        product(weighted, output_mat, 1, 0).astype(bf16), "head", scatter_dimension=0, tiled=True
    ).astype(f32)
    middle_inverse = rms_scale(middle)
    middle_normed = (middle * middle_inverse * expert_scale).astype(bf16)
    mine = me * per_device + jnp.arange(per_device, dtype=jnp.int32)
    my_router = lax.dynamic_slice_in_dim(router, me * per_device, per_device, axis=1)
    in_mat = expert_in.transpose(1, 0, 2).reshape(features, per_device * width)
    out_mat = expert_out.reshape(per_device * width, features)

    def turn(running, own):
        own_rows, own_cot, own_picks = own
        all_cot = lax.all_gather(own_cot, everywhere, axis=0, tiled=True)
        all_picks = lax.all_gather(own_picks, everywhere, axis=0, tiled=True)
        all_rows = lax.all_gather(own_rows, everywhere, axis=0, tiled=True)
        mask = jnp.any(all_picks[:, :, None] == mine[None, None, :], axis=1).astype(f32)
        gates = jax.nn.sigmoid(product(all_rows, my_router, 1, 0))
        live = gates * mask
        act, slope = gelu_pair(product(all_rows, in_mat, 1, 0).reshape(-1, per_device, width))
        lifted = product(all_cot, out_mat, 1, 1).reshape(-1, per_device, width)
        dense_grad = (jnp.sum(act * lifted, axis=-1) * live * (1.0 - gates)).astype(bf16)
        act_live = (act * live[:, :, None]).astype(bf16).reshape(-1, per_device * width)
        hidden_grad = (slope * lifted * live[:, :, None]).astype(bf16)
        hidden_grad = hidden_grad.reshape(-1, per_device * width)
        part_out = product(act_live, out_mat, 1, 0).astype(bf16)
        part_grad = (
            product(hidden_grad, in_mat, 1, 1) + product(dense_grad, my_router, 1, 1)
        ).astype(bf16)
        back = lax.psum_scatter(part_grad, everywhere, scatter_dimension=0, tiled=True)
        forth = lax.psum_scatter(part_out, everywhere, scatter_dimension=0, tiled=True)
        grads = (
            product(all_rows, hidden_grad, 0, 0),
            product(act_live, all_cot, 0, 0),
            product(dense_grad, all_rows, 0, 0),
        )
        if running is not None:
            grads = jax.tree.map(jnp.add, running, grads)
        return grads, (forth, back)

    turns = max(1, lax.axis_size("dp") * lax.axis_size("head") * tokens // whole_rows)
    owned = (middle_normed, cotangent, expert_pick)
    if turns == 1:
        grads, (summed, normed_grad) = turn(None, owned)
    else:
        owned = jax.tree.map(lambda a: a.reshape(turns, -1, a.shape[1]), owned)
        zeros = (
            jnp.zeros(in_mat.shape, f32),
            jnp.zeros(out_mat.shape, f32),
            jnp.zeros((per_device, features), f32),
        )
        grads, sums = lax.scan(turn, zeros, owned)
        summed, normed_grad = (a.reshape(tokens, features) for a in sums)
    grad_in = grads[0].reshape(features, per_device, width).transpose(1, 0, 2)
    grad_out = grads[1].reshape(per_device, width, features)
    grad_router = lax.all_gather(grads[2], everywhere, axis=0, tiled=True).T
    output = middle + summed.astype(f32)
    incoming = cotangent.astype(f32)
    row_grad, grad_gain_expert = norm_back(
        middle, middle_inverse, expert_scale, normed_grad.astype(f32)
    )
    middle_grad = incoming + row_grad
    group_grads = lax.all_gather(middle_grad.astype(bf16), "head", axis=0, tiled=True)
    weighted_grad = product(group_grads, output_mat, 1, 1).reshape(group, head_experts, head_width)
    output_grad = product(weighted, group_grads, 0, 0)
    output_gate_grad = jnp.sum(weighted_grad * attended[:, None, :], axis=-1)
    attended_grad = jnp.sum(weighted_grad * output_gates[:, :, None], axis=1).astype(bf16)
    prob_grad = product(attended_grad, values, 1, 1)
    centre = jnp.sum(probabilities * prob_grad, axis=-1, keepdims=True)
    score_grad = (probabilities * (prob_grad - centre)).astype(bf16)
    query_grad = product(score_grad, key_rows, 1, 0) * scale
    key_grad = product(score_grad, queries, 0, 0) * scale
    values_grad = product(probabilities.astype(bf16), attended_grad, 0, 0)
    expert_grad = (value_gates[:, :, None] * values_grad[:, None, :]).reshape(group, -1).astype(bf16)
    value_gate_grad = jnp.sum(expert_values * values_grad[:, None, :], axis=-1)
    query_grad = rotate(query_grad, cosine, -sine).astype(bf16)
    key_grad = rotate(key_grad, cosine, -sine).astype(bf16)
    logit_grad = (
        jnp.concatenate([value_gate_grad * value_mask, output_gate_grad * output_mask], axis=1)
        * squash
        * (1.0 - squash)
    ).astype(bf16)
    head_grads = (
        product(normed, query_grad, 0, 0),
        product(normed, key_grad, 0, 0),
        product(rows, expert_grad, 0, 0),
        output_grad,
        product(normed, logit_grad, 0, 0),
    )
    head_grads = tuple(grad.astype(bf16) for grad in head_grads)
    head_grads = tuple(grad.astype(f32)[None] for grad in lax.psum(head_grads, "dp"))
    back = (
        product(query_grad, query_mat, 1, 1)
        + product(key_grad, key_mat, 1, 1)
        + product(logit_grad, gate_mat, 1, 1)
    )
    row_back, grad_attend = norm_back(grouped, inverse, attend_scale, back)
    partial = (row_back + product(expert_grad, value_mat, 1, 1)).astype(bf16)
    input_grad = middle_grad + lax.psum_scatter(
        partial, "head", scatter_dimension=0, tiled=True
    ).astype(f32)
    grad_attend, grad_gain_expert = lax.psum((grad_attend, grad_gain_expert), everywhere)
    return (
        output,
        input_grad,
        grad_attend,
        *head_grads,
        grad_gain_expert,
        grad_router,
        grad_in,
        grad_out,
    )


def solution(mesh):
    rows = P(everywhere, None)
    heads = P("head", None, None)
    experts = P(everywhere, None, None)
    picks = P("dp", "head", None)
    in_specs = (
        rows, P("dp"), picks, picks, rows, P(), heads, heads, heads, heads, heads,
        P(), P(), experts, experts, rows,
    )
    out_specs = (
        rows, rows, P(), heads, heads, heads, heads, heads, P(), P(), experts, experts,
    )
    return jax.shard_map(body, mesh=mesh, in_specs=in_specs, out_specs=out_specs, check_vma=False)
```

```python
import functools

import jax
import jax.numpy as jnp
import numpy as np
from jax import lax
from jax.experimental import pallas as pl
from jax.experimental.pallas import tpu as pltpu
from jax.sharding import PartitionSpec as P

epsilon = 1e-06
theta = 10000.0
negative = -1e30
f32 = jnp.float32
bf16 = jnp.bfloat16
everywhere = ("dp", "head")
whole_rows = 4096
vmem_for_weights = 16 << 20


def product(left, right, left_axis, right_axis):
    return lax.dot_general(
        left, right, (((left_axis,), (right_axis,)), ((), ())), preferred_element_type=f32
    )


def rms_scale(residual):
    return lax.rsqrt(jnp.mean(residual * residual, axis=-1, keepdims=True) + epsilon)


def rotary_tables(row_count, head_width):
    half_width = head_width // 2
    position = jnp.arange(row_count, dtype=f32)[:, None]
    exponent = jnp.arange(half_width, dtype=f32)[None, :]
    angles = position * jnp.power(theta, -2.0 * exponent / head_width)
    return (jnp.cos(angles), jnp.sin(angles))


def rotate(matrix, cosine, sine):
    half = matrix.shape[-1] // 2
    first, second = matrix[:, :half], matrix[:, half:]
    return jnp.concatenate([first * cosine - second * sine, second * cosine + first * sine], axis=-1)


def pick_mask(picks, expert_count):
    hits = picks[:, 0, :, None] == jnp.arange(expert_count, dtype=jnp.int32)[None, None, :]
    return jnp.any(hits, axis=1).astype(f32)


def norm_back(residual, inverse, gain, incoming):
    unit_rows = residual * inverse
    scaled = incoming * gain
    gain_grad = jnp.sum(incoming * unit_rows, axis=0)
    row_grad = inverse * (scaled - unit_rows * jnp.mean(scaled * unit_rows, axis=-1, keepdims=True))
    return (row_grad, gain_grad)


def gelu_pair(value):
    inner = jnp.tanh(0.7978845608028654 * (value + 0.044715 * value * value * value))
    slope = 0.5 * (1.0 + inner) + 0.5 * value * (1.0 - inner * inner) * 0.7978845608028654 * (
        1.0 + 3.0 * 0.044715 * value * value
    )
    return (0.5 * value * (1.0 + inner), slope)


def body(
    hidden_in,
    segments,
    value_pick,
    output_pick,
    expert_pick,
    attend_gain,
    query_weight,
    key_weight,
    value_weight,
    output_weight,
    head_router,
    expert_gain,
    router,
    expert_in,
    expert_out,
    cotangent,
):
    tokens, features = hidden_in.shape
    per_device, _, width = expert_in.shape
    head_experts = head_router.shape[2] // 2
    head_width = query_weight.shape[2]
    scale = head_width ** (-0.5)
    query_mat, key_mat, value_mat = query_weight[0], key_weight[0], value_weight[0]
    output_mat, gate_mat = output_weight[0], head_router[0]
    value_mask = pick_mask(value_pick, head_experts)
    output_mask = pick_mask(output_pick, head_experts)
    attend_scale = attend_gain.astype(f32)
    expert_scale = expert_gain.astype(f32)
    me = lax.axis_index("dp") * lax.axis_size("head") + lax.axis_index("head")

    rows = lax.all_gather(hidden_in, "head", axis=0, tiled=True)
    grouped = rows.astype(f32)
    group = grouped.shape[0]
    inverse = rms_scale(grouped)
    normed = (grouped * inverse * attend_scale).astype(bf16)
    cosine, sine = rotary_tables(group, head_width)
    queries = rotate(product(normed, query_mat, 1, 0), cosine, sine).astype(bf16)
    key_rows = rotate(product(normed, key_mat, 1, 0), cosine, sine).astype(bf16)
    squash = jax.nn.sigmoid(product(normed, gate_mat, 1, 0))
    value_gates = squash[:, :head_experts] * value_mask
    output_gates = squash[:, head_experts:] * output_mask
    expert_values = product(rows, value_mat, 1, 0).reshape(group, head_experts, head_width)
    values = jnp.sum(expert_values * value_gates[:, :, None], axis=1).astype(bf16)
    places = jnp.arange(group, dtype=jnp.int32)
    allowed = (places[None, :] <= places[:, None]) & (segments[:, None] == segments[None, :])
    scores = jnp.where(allowed, product(queries, key_rows, 1, 1) * scale, negative)
    exponents = jnp.exp(scores - jnp.max(scores, axis=-1, keepdims=True))
    probabilities = exponents / jnp.sum(exponents, axis=-1, keepdims=True)
    attended = product(probabilities.astype(bf16), values, 1, 0)
    weighted = (
        (output_gates[:, :, None] * attended[:, None, :]).reshape(group, -1).astype(bf16)
    )
    middle = hidden_in.astype(f32) + lax.psum_scatter(
        product(weighted, output_mat, 1, 0).astype(bf16), "head", scatter_dimension=0, tiled=True
    ).astype(f32)
    middle_inverse = rms_scale(middle)
    middle_normed = (middle * middle_inverse * expert_scale).astype(bf16)
    mine = me * per_device + jnp.arange(per_device, dtype=jnp.int32)
    my_router = lax.dynamic_slice_in_dim(router, me * per_device, per_device, axis=1)
    in_mat = expert_in.transpose(1, 0, 2).reshape(features, per_device * width)
    out_mat = expert_out.reshape(per_device * width, features)

    def turn(running, own):
        own_rows, own_cot, own_picks = own
        all_cot = lax.all_gather(own_cot, everywhere, axis=0, tiled=True)
        all_picks = lax.all_gather(own_picks, everywhere, axis=0, tiled=True)
        all_rows = lax.all_gather(own_rows, everywhere, axis=0, tiled=True)
        mask = jnp.any(all_picks[:, :, None] == mine[None, None, :], axis=1).astype(f32)
        gates = jax.nn.sigmoid(product(all_rows, my_router, 1, 0))
        live = gates * mask
        act, slope = gelu_pair(product(all_rows, in_mat, 1, 0).reshape(-1, per_device, width))
        lifted = product(all_cot, out_mat, 1, 1).reshape(-1, per_device, width)
        dense_grad = (jnp.sum(act * lifted, axis=-1) * live * (1.0 - gates)).astype(bf16)
        act_live = (act * live[:, :, None]).astype(bf16).reshape(-1, per_device * width)
        hidden_grad = (slope * lifted * live[:, :, None]).astype(bf16)
        hidden_grad = hidden_grad.reshape(-1, per_device * width)
        part_out = product(act_live, out_mat, 1, 0).astype(bf16)
        part_grad = (
            product(hidden_grad, in_mat, 1, 1) + product(dense_grad, my_router, 1, 1)
        ).astype(bf16)
        back = lax.psum_scatter(part_grad, everywhere, scatter_dimension=0, tiled=True)
        forth = lax.psum_scatter(part_out, everywhere, scatter_dimension=0, tiled=True)
        grads = (
            product(all_rows, hidden_grad, 0, 0),
            product(act_live, all_cot, 0, 0),
            product(dense_grad, all_rows, 0, 0),
        )
        if running is not None:
            grads = jax.tree.map(jnp.add, running, grads)
        return grads, (forth, back)

    turns = max(1, lax.axis_size("dp") * lax.axis_size("head") * tokens // whole_rows)
    owned = (middle_normed, cotangent, expert_pick)
    if turns == 1:
        grads, (summed, normed_grad) = turn(None, owned)
    else:
        owned = jax.tree.map(lambda a: a.reshape(turns, -1, a.shape[1]), owned)
        zeros = (
            jnp.zeros(in_mat.shape, f32),
            jnp.zeros(out_mat.shape, f32),
            jnp.zeros((per_device, features), f32),
        )
        grads, sums = lax.scan(turn, zeros, owned)
        summed, normed_grad = (a.reshape(tokens, features) for a in sums)
    grad_in = grads[0].reshape(features, per_device, width).transpose(1, 0, 2)
    grad_out = grads[1].reshape(per_device, width, features)
    grad_router = lax.all_gather(grads[2], everywhere, axis=0, tiled=True).T
    output = middle + summed.astype(f32)
    incoming = cotangent.astype(f32)
    row_grad, grad_gain_expert = norm_back(
        middle, middle_inverse, expert_scale, normed_grad.astype(f32)
    )
    middle_grad = incoming + row_grad
    group_grads = lax.all_gather(middle_grad.astype(bf16), "head", axis=0, tiled=True)
    weighted_grad = product(group_grads, output_mat, 1, 1).reshape(group, head_experts, head_width)
    output_grad = product(weighted, group_grads, 0, 0)
    output_gate_grad = jnp.sum(weighted_grad * attended[:, None, :], axis=-1)
    attended_grad = jnp.sum(weighted_grad * output_gates[:, :, None], axis=1).astype(bf16)
    prob_grad = product(attended_grad, values, 1, 1)
    centre = jnp.sum(probabilities * prob_grad, axis=-1, keepdims=True)
    score_grad = (probabilities * (prob_grad - centre)).astype(bf16)
    query_grad = product(score_grad, key_rows, 1, 0) * scale
    key_grad = product(score_grad, queries, 0, 0) * scale
    values_grad = product(probabilities.astype(bf16), attended_grad, 0, 0)
    expert_grad = (value_gates[:, :, None] * values_grad[:, None, :]).reshape(group, -1).astype(bf16)
    value_gate_grad = jnp.sum(expert_values * values_grad[:, None, :], axis=-1)
    query_grad = rotate(query_grad, cosine, -sine).astype(bf16)
    key_grad = rotate(key_grad, cosine, -sine).astype(bf16)
    logit_grad = (
        jnp.concatenate([value_gate_grad * value_mask, output_gate_grad * output_mask], axis=1)
        * squash
        * (1.0 - squash)
    ).astype(bf16)
    head_grads = (
        product(normed, query_grad, 0, 0),
        product(normed, key_grad, 0, 0),
        product(rows, expert_grad, 0, 0),
        output_grad,
        product(normed, logit_grad, 0, 0),
    )
    head_grads = tuple(grad.astype(bf16) for grad in head_grads)
    head_grads = tuple(grad.astype(f32)[None] for grad in lax.psum(head_grads, "dp"))
    back = (
        product(query_grad, query_mat, 1, 1)
        + product(key_grad, key_mat, 1, 1)
        + product(logit_grad, gate_mat, 1, 1)
    )
    row_back, grad_attend = norm_back(grouped, inverse, attend_scale, back)
    partial = (row_back + product(expert_grad, value_mat, 1, 1)).astype(bf16)
    input_grad = middle_grad + lax.psum_scatter(
        partial, "head", scatter_dimension=0, tiled=True
    ).astype(f32)
    grad_attend, grad_gain_expert = lax.psum((grad_attend, grad_gain_expert), everywhere)
    return (
        output,
        input_grad,
        grad_attend,
        *head_grads,
        grad_gain_expert,
        grad_router,
        grad_in,
        grad_out,
    )


MESH = pl.DeviceIdType.MESH
VM = pl.BlockSpec(memory_space=pltpu.VMEM)
ANY = pl.BlockSpec(memory_space=pl.ANY)
NN = (((1,), (0,)), ((), ()))
NT = (((1,), (1,)), ((), ()))
TN = (((0,), (0,)), ((), ()))


def dot(left, right, dims=NN):
    return lax.dot_general(left, right, dims, preferred_element_type=f32)


def at_block(block, count):
    return pl.ds(pl.multiple_of(block * count, count), count)


def remote(src, dst, send, recv, where):
    return pltpu.make_async_remote_copy(
        src_ref=src, dst_ref=dst, send_sem=send, recv_sem=recv, device_id=where, device_id_type=MESH
    )


def greet(places):
    barrier = pltpu.get_barrier_semaphore()
    for place in places:
        pl.semaphore_signal(barrier, inc=1, device_id=place, device_id_type=MESH)
    pl.semaphore_wait(barrier, len(places))


def swap_halves(value):
    half = value.shape[-1] // 2
    return jnp.concatenate([value[:, half:], value[:, :half]], axis=-1)


def attend_kernel(
    n_dp,
    n_head,
    x_ref,
    cot_ref,
    mask_ref,
    attend_gain_ref,
    expert_gain_ref,
    cos_ref,
    sin_ref,
    gate_mask_ref,
    seg_row_ref,
    seg_col_ref,
    wq_ref,
    wk_ref,
    wg_ref,
    wv_ref,
    wo_ref,
    in_ref,
    out_ref,
    all_in_ref,
    all_out_ref,
    all_cot_ref,
    all_mask_ref,
    mid_ref,
    mr_ref,
    rows_ref,
    q_ref,
    k_ref,
    v_ref,
    prob_ref,
    vx_ref,
    squash_ref,
    att_ref,
    w_an,
    w_v,
    w_o,
    part,
    got,
    local_sem,
    z_send,
    z_recv,
    p_send,
    p_recv,
):
    d, h = lax.axis_index("dp"), lax.axis_index("head")
    chip, core = d // 2, d % 2
    chips = n_dp // 2
    tokens, features = x_ref.shape
    width = q_ref.shape[1]
    experts = vx_ref.shape[1] // width
    scale = width ** (-0.5)
    group = tokens * n_head
    steps = (2, 3, 1)
    partner = (chip * 2 + 1 - core, h)

    def along(step):
        return (d, jnp.bitwise_xor(h, step))

    def across(step):
        return (jnp.bitwise_xor(chip, step) * 2 + core, h)

    def local(src, dst, number):
        return pltpu.make_async_copy(src, dst, local_sem.at[number])

    per_device = in_ref.shape[0]
    slab = per_device * width
    out_slot = lambda place, side: all_out_ref.at[place, at_block(side, slab), :]
    in_slot = lambda place, side, e: all_in_ref.at[
        place, :, at_block(side * per_device + e, width)
    ]
    loads = [
        local(wq_ref, w_an.at[:, pl.ds(0, width)], 0),
        local(wk_ref, w_an.at[:, pl.ds(width, width)], 1),
        local(wg_ref, w_an.at[:, pl.ds(2 * width, width)], 2),
        local(wv_ref, w_v, 3),
        local(wo_ref, w_o, 4),
        local(cot_ref, all_cot_ref.at[at_block(h, tokens), :], 5),
        local(mask_ref.at[h], all_mask_ref.at[at_block(h, tokens), :], 6),
        local(out_ref, out_slot(chip, core), 7),
    ] + [local(in_ref.at[e], in_slot(chip, core, e), 8 + e) for e in range(per_device)]
    for load in loads:
        load.start()
    greet([along(s) for s in steps] + [partner] + [across(s) for s in range(1, chips)])

    def spread(kind, src, dst_of, order=steps):
        copies = {}
        for step in order:
            copies[step] = remote(
                src(step),
                dst_of(step),
                z_send.at[kind, step - 1],
                z_recv.at[kind, step - 1],
                along(step),
            )
            copies[step].start()
        return copies

    x_copies = spread(0, lambda s: x_ref, lambda s: rows_ref.at[at_block(h, tokens), :])

    def weights_to(where, slot, place, side, own):
        pieces = [
            remote(
                out_ref if own else out_slot(place, side),
                out_slot(place, side),
                p_send.at[slot, 0],
                p_recv.at[slot, 0],
                where,
            )
        ]
        for e in range(per_device):
            pieces.append(
                remote(
                    in_ref.at[e] if own else in_slot(place, side, e),
                    in_slot(place, side, e),
                    p_send.at[slot, 1 + e],
                    p_recv.at[slot, 1 + e],
                    where,
                )
            )
        return pieces

    first = [weights_to(across(s), s, chip, core, True) for s in range(1, chips)]
    first.append(weights_to(partner, 0, chip, core, True))
    for piece in range(1 + per_device):
        for pieces in first:
            pieces[piece].start()
    mask_copies = spread(
        1,
        lambda s: mask_ref.at[jnp.bitwise_xor(h, s)],
        lambda s: all_mask_ref.at[at_block(h, tokens), :],
    )

    rows_ref[at_block(h, tokens), :] = x_ref[...]
    for load in loads[:5]:
        load.wait()

    def project(block):
        at = at_block(block, tokens)
        rows = rows_ref[at, :]
        wide = rows.astype(f32)
        inverse = lax.rsqrt(jnp.mean(wide * wide, axis=-1, keepdims=True) + epsilon)
        normed = (wide * inverse * attend_gain_ref[...]).astype(bf16)
        qkg = dot(normed, w_an[...])
        cosine, sine = cos_ref[at, :], sin_ref[at, :]
        q, k = qkg[:, :width], qkg[:, width : 2 * width]
        q_ref[at, :] = (q * cosine + swap_halves(q) * sine).astype(bf16)
        k_ref[at, :] = (k * cosine + swap_halves(k) * sine).astype(bf16)
        squash = jax.nn.sigmoid(qkg[:, 2 * width :])
        squash_ref[at, :] = squash
        gates = squash * gate_mask_ref[at, :]
        vx = dot(rows, w_v[...])
        vx_ref[at, :] = vx
        value = gates[:, 0:1] * vx[:, :width]
        for e in range(1, experts):
            value += gates[:, e : e + 1] * vx[:, e * width : (e + 1) * width]
        v_ref[at, :] = value.astype(bf16)

    project(h)
    for step in (1, 2, 3):
        x_copies[step].wait_recv()
        project(jnp.bitwise_xor(h, step))
    for step in steps:
        x_copies[step].wait_send()
    cot_copies = spread(2, lambda s: cot_ref, lambda s: all_cot_ref.at[at_block(h, tokens), :])

    def attend(block):
        at = at_block(block, tokens)
        scores = dot(q_ref[at, :], k_ref[...], NT) * scale
        row = block * tokens + lax.broadcasted_iota(jnp.int32, (tokens, group), 0)
        column = lax.broadcasted_iota(jnp.int32, (tokens, group), 1)
        allowed = (column <= row) & (seg_col_ref[at, :] == seg_row_ref[...])
        scores = jnp.where(allowed, scores, negative)
        exponents = jnp.exp(scores - jnp.max(scores, axis=-1, keepdims=True))
        prob = exponents / jnp.sum(exponents, axis=-1, keepdims=True)
        prob_ref[at, :] = prob
        att = dot(prob.astype(bf16), v_ref[...])
        att_ref[at, :] = att
        gates = squash_ref[at, :] * gate_mask_ref[at, :]
        wide = jnp.concatenate(
            [(gates[:, experts + e : experts + e + 1] * att).astype(bf16) for e in range(experts)],
            axis=-1,
        )
        return dot(wide, w_o[...])

    part_copies = {}
    for step in steps:
        part[step - 1] = attend(jnp.bitwise_xor(h, step)).astype(bf16)
        part_copies[step] = remote(
            part.at[step - 1],
            got.at[step - 1],
            z_send.at[3, step - 1],
            z_recv.at[3, step - 1],
            along(step),
        )
        part_copies[step].start()
    middle = x_ref[...].astype(f32) + attend(h)
    for step in steps:
        part_copies[step].wait_recv()
    for step in steps:
        middle += got[step - 1].astype(f32)
    mid_ref[...] = middle
    inverse = lax.rsqrt(jnp.mean(middle * middle, axis=-1, keepdims=True) + epsilon)
    mr_ref[...] = (middle * inverse * expert_gain_ref[...]).astype(bf16)
    for step in steps:
        part_copies[step].wait_send()

    onward = []
    for s in range(1, chips):
        place = jnp.bitwise_xor(chip, s)
        pieces = weights_to(partner, chips - 1 + s, place, core, False)
        for piece in range(1 + per_device):
            first[s - 1][piece].wait_recv()
            pieces[piece].start()
        onward.append(pieces)
    for pieces in first[:-1]:
        for piece in pieces:
            piece.wait_send()
    for pieces in [first[-1]] + onward:
        for piece in pieces:
            piece.wait()
    for copies in (mask_copies, cot_copies):
        for step in steps:
            copies[step].wait()
    for load in loads[5:]:
        load.wait()


def attend_call(n_dp, n_head, tokens, features, width, experts, per_device, args):
    group = tokens * n_head
    chips = n_dp // 2
    slab = per_device * width
    shape = jax.ShapeDtypeStruct
    outs = [
        (shape((chips, features, 2 * slab), bf16), ANY),
        (shape((chips, 2 * slab, features), bf16), ANY),
        (shape((group, features), bf16), ANY),
        (shape((group, 128), bf16), ANY),
        (shape((tokens, features), f32), VM),
        (shape((tokens, features), bf16), VM),
        (shape((group, features), bf16), VM),
        (shape((group, width), bf16), VM),
        (shape((group, width), bf16), VM),
        (shape((group, width), bf16), VM),
        (shape((group, group), f32), VM),
        (shape((group, experts * width), f32), VM),
        (shape((group, 128), f32), VM),
        (shape((group, width), f32), VM),
    ]
    return pl.pallas_call(
        functools.partial(attend_kernel, n_dp, n_head),
        out_shape=[o[0] for o in outs],
        out_specs=[o[1] for o in outs],
        in_specs=[VM, ANY, VM] + [VM] * 7 + [ANY] * 7,
        scratch_shapes=[
            pltpu.VMEM((features, 3 * width), bf16),
            pltpu.VMEM((features, experts * width), bf16),
            pltpu.VMEM((experts * width, features), bf16),
            pltpu.VMEM((n_head - 1, tokens, features), bf16),
            pltpu.VMEM((n_head - 1, tokens, features), bf16),
            pltpu.SemaphoreType.DMA((8 + per_device,)),
            pltpu.SemaphoreType.DMA((4, n_head - 1)),
            pltpu.SemaphoreType.DMA((4, n_head - 1)),
            pltpu.SemaphoreType.DMA((2 * chips - 1, 1 + per_device)),
            pltpu.SemaphoreType.DMA((2 * chips - 1, 1 + per_device)),
        ],
        compiler_params=pltpu.CompilerParams(
            collective_id=1, has_side_effects=True, vmem_limit_bytes=40 << 20
        ),
    )(*args)


def kernel_body(
    n_dp,
    n_head,
    hidden_in,
    segments,
    value_pick,
    output_pick,
    expert_pick,
    attend_gain,
    query_weight,
    key_weight,
    value_weight,
    output_weight,
    head_router,
    expert_gain,
    router,
    expert_in,
    expert_out,
    cotangent,
):
    tokens, features = hidden_in.shape
    per_device, _, width = expert_in.shape
    experts = head_router.shape[2] // 2
    experts_total = router.shape[1]
    slab = per_device * width
    group = tokens * n_head
    chips = n_dp // 2
    d, h = lax.axis_index("dp"), lax.axis_index("head")
    lanes = 128
    owner = np.arange(n_dp * per_device)
    ids = (owner // per_device * n_head)[None, :] + np.arange(n_head)[:, None]
    ids = ids * per_device + owner % per_device
    ids = np.pad(ids, ((0, 0), (0, lanes - ids.shape[1])), constant_values=-1).astype(np.int32)
    mask4 = jnp.any(expert_pick[None, :, :, None] == ids[:, None, None, :], axis=2).astype(bf16)
    angles = np.arange(group)[:, None] * theta ** (-2.0 * np.arange(width // 2) / width)[None, :]
    cosine = np.concatenate([np.cos(angles)] * 2, axis=1).astype(np.float32)
    sine = np.concatenate([-np.sin(angles), np.sin(angles)], axis=1).astype(np.float32)
    slots = np.arange(lanes, dtype=np.int32)
    gate_mask = (
        jnp.any(value_pick[:, 0, :, None] == slots, axis=1)
        | jnp.any(output_pick[:, 0, :, None] + experts == slots, axis=1)
    ).astype(f32)
    gate_mat = jnp.pad(head_router[0], ((0, 0), (0, lanes - head_router.shape[2])))
    attend_scale = attend_gain.astype(f32)[None, :]
    expert_scale = expert_gain.astype(f32)[None, :]
    (all_in, all_out, all_cot, all_mask, middle, mr, rows, q, k, v, prob, vx, squash, att) = (
        attend_call(
            n_dp,
            n_head,
            tokens,
            features,
            width,
            experts,
            per_device,
            (
                hidden_in,
                cotangent,
                mask4,
                attend_scale,
                expert_scale,
                cosine,
                sine,
                gate_mask,
                segments[None, :],
                segments[:, None],
                query_weight[0],
                key_weight[0],
                gate_mat,
                value_weight[0],
                output_weight[0],
                expert_in,
                expert_out.reshape(slab, features),
            ),
        )
    )
    n_all = n_dp * per_device
    in_mat = all_in.transpose(1, 0, 2).reshape(features, -1)
    out_mat = all_out.reshape(-1, features)
    r_ids = jnp.maximum(jnp.asarray(ids)[h], 0)
    my_router = jnp.take(router, r_ids, axis=1)
    mr_all = lax.all_gather(mr, "head", axis=0, tiled=True)
    gates = jax.nn.sigmoid(product(mr_all, my_router, 1, 0))
    live = gates * all_mask.astype(f32)
    act, slope = gelu_pair(product(mr_all, in_mat, 1, 0).reshape(-1, n_all, width))
    lifted = product(all_cot, out_mat, 1, 1).reshape(-1, n_all, width)
    dz = (jnp.sum(act * lifted, axis=-1) * (live * (1.0 - gates))[:, :n_all]).astype(bf16)
    act_live = (act * live[:, :n_all, None]).astype(bf16).reshape(group, -1)
    hg = (slope * lifted * live[:, :n_all, None]).astype(bf16).reshape(group, -1)
    part_out = product(act_live, out_mat, 1, 0).astype(bf16)
    part_grad = (product(hg, in_mat, 1, 1) + product(dz, my_router[:, :n_all], 1, 1)).astype(bf16)
    normed_grad = lax.psum_scatter(part_grad, "head", scatter_dimension=0, tiled=True)
    summed = lax.psum_scatter(part_out, "head", scatter_dimension=0, tiled=True)
    gi = product(mr_all, hg, 0, 0).reshape(features, n_dp, per_device, width).transpose(1, 2, 0, 3)
    go = product(act_live, all_cot, 0, 0).reshape(n_dp, per_device, width, features)
    grad_in = lax.psum_scatter(gi.astype(bf16), "dp", scatter_dimension=0, tiled=False).astype(f32)
    grad_out = lax.psum_scatter(go.astype(bf16), "dp", scatter_dimension=0, tiled=False).astype(f32)
    gr = lax.psum(product(dz, mr_all, 0, 0), "dp").reshape(n_dp, per_device, features)
    gr = lax.all_gather(gr, "head", axis=1, tiled=False)
    grad_router = gr.reshape(experts_total, features).T
    output = middle + summed.astype(f32)
    incoming = cotangent.astype(f32)
    row_grad, grad_gain_expert = norm_back(
        middle, rms_scale(middle), expert_scale[0], normed_grad.astype(f32)
    )
    middle_grad = incoming + row_grad
    group_grads = lax.all_gather(middle_grad.astype(bf16), "head", axis=0, tiled=True)
    query_mat, key_mat, value_mat = query_weight[0], key_weight[0], value_weight[0]
    output_mat, gate10 = output_weight[0], head_router[0]
    grouped = rows.astype(f32)
    inverse = rms_scale(grouped)
    normed = (grouped * inverse * attend_scale).astype(bf16)
    scale = width ** (-0.5)
    og = (squash * gate_mask)[:, experts : 2 * experts]
    vg = (squash * gate_mask)[:, :experts]
    weighted = (og[:, :, None] * att[:, None, :]).reshape(group, -1).astype(bf16)
    weighted_grad = product(group_grads, output_mat, 1, 1).reshape(group, experts, width)
    output_grad = product(weighted, group_grads, 0, 0)
    ogg = jnp.sum(weighted_grad * att[:, None, :], axis=-1)
    attended_grad = jnp.sum(weighted_grad * og[:, :, None], axis=1).astype(bf16)
    prob_grad = product(attended_grad, v, 1, 1)
    centre = jnp.sum(prob * prob_grad, axis=-1, keepdims=True)
    score_grad = (prob * (prob_grad - centre)).astype(bf16)
    query_grad = product(score_grad, k, 1, 0) * scale
    key_grad = product(score_grad, q, 0, 0) * scale
    values_grad = product(prob.astype(bf16), attended_grad, 0, 0)
    expert_grad = (vg[:, :, None] * values_grad[:, None, :]).reshape(group, -1).astype(bf16)
    vgg = jnp.sum(vx.reshape(group, experts, width) * values_grad[:, None, :], axis=-1)
    c64, s64 = cosine[:, : width // 2], -sine[:, : width // 2]
    query_grad = rotate(query_grad, c64, -s64).astype(bf16)
    key_grad = rotate(key_grad, c64, -s64).astype(bf16)
    sq = squash[:, : 2 * experts]
    logit_grad = (
        jnp.concatenate([vgg, ogg], axis=1) * gate_mask[:, : 2 * experts] * sq * (1.0 - sq)
    ).astype(bf16)
    head_grads = (
        product(normed, query_grad, 0, 0),
        product(normed, key_grad, 0, 0),
        product(rows, expert_grad, 0, 0),
        output_grad,
        product(normed, logit_grad, 0, 0),
    )
    head_grads = tuple(grad.astype(bf16) for grad in head_grads)
    head_grads = tuple(grad.astype(f32)[None] for grad in lax.psum(head_grads, "dp"))
    back = (
        product(query_grad, query_mat, 1, 1)
        + product(key_grad, key_mat, 1, 1)
        + product(logit_grad, gate10, 1, 1)
    )
    row_back, grad_attend = norm_back(grouped, inverse, attend_scale[0], back)
    partial = (row_back + product(expert_grad, value_mat, 1, 1)).astype(bf16)
    input_grad = middle_grad + lax.psum_scatter(
        partial, "head", scatter_dimension=0, tiled=True
    ).astype(f32)
    grad_attend, grad_gain_expert = lax.psum((grad_attend, grad_gain_expert), everywhere)
    return (
        output,
        input_grad,
        grad_attend,
        *head_grads,
        grad_gain_expert,
        grad_router,
        grad_in,
        grad_out,
    )


def solution(mesh):
    rows = P(everywhere, None)
    heads = P("head", None, None)
    experts = P(everywhere, None, None)
    picks = P("dp", "head", None)
    in_specs = (
        rows, P("dp"), picks, picks, rows, P(), heads, heads, heads, heads, heads,
        P(), P(), experts, experts, rows,
    )
    out_specs = (
        rows, rows, P(), heads, heads, heads, heads, heads, P(), P(), experts, experts,
    )
    n_dp, n_head = mesh.shape["dp"], mesh.shape["head"]

    def program(*args):
        held = 2 * n_dp * args[13].shape[0] * args[13].shape[1] * args[13].shape[2] * 2
        if n_head == 4 and held <= vmem_for_weights:
            return kernel_body(n_dp, n_head, *args)
        return body(*args)

    return jax.shard_map(program, mesh=mesh, in_specs=in_specs, out_specs=out_specs, check_vma=False)
```

```python
import functools

import jax
import jax.numpy as jnp
import numpy as np
from jax import lax
from jax.experimental import pallas as pl
from jax.experimental.pallas import tpu as pltpu
from jax.sharding import PartitionSpec as P

epsilon = 1e-06
theta = 10000.0
negative = -1e30
f32 = jnp.float32
bf16 = jnp.bfloat16
everywhere = ("dp", "head")
whole_rows = 4096
vmem_for_weights = 16 << 20


def product(left, right, left_axis, right_axis):
    return lax.dot_general(
        left, right, (((left_axis,), (right_axis,)), ((), ())), preferred_element_type=f32
    )


def rms_scale(residual):
    return lax.rsqrt(jnp.mean(residual * residual, axis=-1, keepdims=True) + epsilon)


def rotary_tables(row_count, head_width):
    half_width = head_width // 2
    position = jnp.arange(row_count, dtype=f32)[:, None]
    exponent = jnp.arange(half_width, dtype=f32)[None, :]
    angles = position * jnp.power(theta, -2.0 * exponent / head_width)
    return (jnp.cos(angles), jnp.sin(angles))


def rotate(matrix, cosine, sine):
    half = matrix.shape[-1] // 2
    first, second = matrix[:, :half], matrix[:, half:]
    return jnp.concatenate([first * cosine - second * sine, second * cosine + first * sine], axis=-1)


def pick_mask(picks, expert_count):
    hits = picks[:, 0, :, None] == jnp.arange(expert_count, dtype=jnp.int32)[None, None, :]
    return jnp.any(hits, axis=1).astype(f32)


def norm_back(residual, inverse, gain, incoming):
    unit_rows = residual * inverse
    scaled = incoming * gain
    gain_grad = jnp.sum(incoming * unit_rows, axis=0)
    row_grad = inverse * (scaled - unit_rows * jnp.mean(scaled * unit_rows, axis=-1, keepdims=True))
    return (row_grad, gain_grad)


def gelu_pair(value):
    inner = jnp.tanh(0.7978845608028654 * (value + 0.044715 * value * value * value))
    slope = 0.5 * (1.0 + inner) + 0.5 * value * (1.0 - inner * inner) * 0.7978845608028654 * (
        1.0 + 3.0 * 0.044715 * value * value
    )
    return (0.5 * value * (1.0 + inner), slope)


def body(
    hidden_in,
    segments,
    value_pick,
    output_pick,
    expert_pick,
    attend_gain,
    query_weight,
    key_weight,
    value_weight,
    output_weight,
    head_router,
    expert_gain,
    router,
    expert_in,
    expert_out,
    cotangent,
):
    tokens, features = hidden_in.shape
    per_device, _, width = expert_in.shape
    head_experts = head_router.shape[2] // 2
    head_width = query_weight.shape[2]
    scale = head_width ** (-0.5)
    query_mat, key_mat, value_mat = query_weight[0], key_weight[0], value_weight[0]
    output_mat, gate_mat = output_weight[0], head_router[0]
    value_mask = pick_mask(value_pick, head_experts)
    output_mask = pick_mask(output_pick, head_experts)
    attend_scale = attend_gain.astype(f32)
    expert_scale = expert_gain.astype(f32)
    me = lax.axis_index("dp") * lax.axis_size("head") + lax.axis_index("head")

    rows = lax.all_gather(hidden_in, "head", axis=0, tiled=True)
    grouped = rows.astype(f32)
    group = grouped.shape[0]
    inverse = rms_scale(grouped)
    normed = (grouped * inverse * attend_scale).astype(bf16)
    cosine, sine = rotary_tables(group, head_width)
    queries = rotate(product(normed, query_mat, 1, 0), cosine, sine).astype(bf16)
    key_rows = rotate(product(normed, key_mat, 1, 0), cosine, sine).astype(bf16)
    squash = jax.nn.sigmoid(product(normed, gate_mat, 1, 0))
    value_gates = squash[:, :head_experts] * value_mask
    output_gates = squash[:, head_experts:] * output_mask
    expert_values = product(rows, value_mat, 1, 0).reshape(group, head_experts, head_width)
    values = jnp.sum(expert_values * value_gates[:, :, None], axis=1).astype(bf16)
    places = jnp.arange(group, dtype=jnp.int32)
    allowed = (places[None, :] <= places[:, None]) & (segments[:, None] == segments[None, :])
    scores = jnp.where(allowed, product(queries, key_rows, 1, 1) * scale, negative)
    exponents = jnp.exp(scores - jnp.max(scores, axis=-1, keepdims=True))
    probabilities = exponents / jnp.sum(exponents, axis=-1, keepdims=True)
    attended = product(probabilities.astype(bf16), values, 1, 0)
    weighted = (
        (output_gates[:, :, None] * attended[:, None, :]).reshape(group, -1).astype(bf16)
    )
    middle = hidden_in.astype(f32) + lax.psum_scatter(
        product(weighted, output_mat, 1, 0).astype(bf16), "head", scatter_dimension=0, tiled=True
    ).astype(f32)
    middle_inverse = rms_scale(middle)
    middle_normed = (middle * middle_inverse * expert_scale).astype(bf16)
    mine = me * per_device + jnp.arange(per_device, dtype=jnp.int32)
    my_router = lax.dynamic_slice_in_dim(router, me * per_device, per_device, axis=1)
    in_mat = expert_in.transpose(1, 0, 2).reshape(features, per_device * width)
    out_mat = expert_out.reshape(per_device * width, features)

    def turn(running, own):
        own_rows, own_cot, own_picks = own
        all_cot = lax.all_gather(own_cot, everywhere, axis=0, tiled=True)
        all_picks = lax.all_gather(own_picks, everywhere, axis=0, tiled=True)
        all_rows = lax.all_gather(own_rows, everywhere, axis=0, tiled=True)
        mask = jnp.any(all_picks[:, :, None] == mine[None, None, :], axis=1).astype(f32)
        gates = jax.nn.sigmoid(product(all_rows, my_router, 1, 0))
        live = gates * mask
        act, slope = gelu_pair(product(all_rows, in_mat, 1, 0).reshape(-1, per_device, width))
        lifted = product(all_cot, out_mat, 1, 1).reshape(-1, per_device, width)
        dense_grad = (jnp.sum(act * lifted, axis=-1) * live * (1.0 - gates)).astype(bf16)
        act_live = (act * live[:, :, None]).astype(bf16).reshape(-1, per_device * width)
        hidden_grad = (slope * lifted * live[:, :, None]).astype(bf16)
        hidden_grad = hidden_grad.reshape(-1, per_device * width)
        part_out = product(act_live, out_mat, 1, 0).astype(bf16)
        part_grad = (
            product(hidden_grad, in_mat, 1, 1) + product(dense_grad, my_router, 1, 1)
        ).astype(bf16)
        back = lax.psum_scatter(part_grad, everywhere, scatter_dimension=0, tiled=True)
        forth = lax.psum_scatter(part_out, everywhere, scatter_dimension=0, tiled=True)
        grads = (
            product(all_rows, hidden_grad, 0, 0),
            product(act_live, all_cot, 0, 0),
            product(dense_grad, all_rows, 0, 0),
        )
        if running is not None:
            grads = jax.tree.map(jnp.add, running, grads)
        return grads, (forth, back)

    turns = max(1, lax.axis_size("dp") * lax.axis_size("head") * tokens // whole_rows)
    owned = (middle_normed, cotangent, expert_pick)
    if turns == 1:
        grads, (summed, normed_grad) = turn(None, owned)
    else:
        owned = jax.tree.map(lambda a: a.reshape(turns, -1, a.shape[1]), owned)
        zeros = (
            jnp.zeros(in_mat.shape, f32),
            jnp.zeros(out_mat.shape, f32),
            jnp.zeros((per_device, features), f32),
        )
        grads, sums = lax.scan(turn, zeros, owned)
        summed, normed_grad = (a.reshape(tokens, features) for a in sums)
    grad_in = grads[0].reshape(features, per_device, width).transpose(1, 0, 2)
    grad_out = grads[1].reshape(per_device, width, features)
    grad_router = lax.all_gather(grads[2], everywhere, axis=0, tiled=True).T
    output = middle + summed.astype(f32)
    incoming = cotangent.astype(f32)
    row_grad, grad_gain_expert = norm_back(
        middle, middle_inverse, expert_scale, normed_grad.astype(f32)
    )
    middle_grad = incoming + row_grad
    group_grads = lax.all_gather(middle_grad.astype(bf16), "head", axis=0, tiled=True)
    weighted_grad = product(group_grads, output_mat, 1, 1).reshape(group, head_experts, head_width)
    output_grad = product(weighted, group_grads, 0, 0)
    output_gate_grad = jnp.sum(weighted_grad * attended[:, None, :], axis=-1)
    attended_grad = jnp.sum(weighted_grad * output_gates[:, :, None], axis=1).astype(bf16)
    prob_grad = product(attended_grad, values, 1, 1)
    centre = jnp.sum(probabilities * prob_grad, axis=-1, keepdims=True)
    score_grad = (probabilities * (prob_grad - centre)).astype(bf16)
    query_grad = product(score_grad, key_rows, 1, 0) * scale
    key_grad = product(score_grad, queries, 0, 0) * scale
    values_grad = product(probabilities.astype(bf16), attended_grad, 0, 0)
    expert_grad = (value_gates[:, :, None] * values_grad[:, None, :]).reshape(group, -1).astype(bf16)
    value_gate_grad = jnp.sum(expert_values * values_grad[:, None, :], axis=-1)
    query_grad = rotate(query_grad, cosine, -sine).astype(bf16)
    key_grad = rotate(key_grad, cosine, -sine).astype(bf16)
    logit_grad = (
        jnp.concatenate([value_gate_grad * value_mask, output_gate_grad * output_mask], axis=1)
        * squash
        * (1.0 - squash)
    ).astype(bf16)
    head_grads = (
        product(normed, query_grad, 0, 0),
        product(normed, key_grad, 0, 0),
        product(rows, expert_grad, 0, 0),
        output_grad,
        product(normed, logit_grad, 0, 0),
    )
    head_grads = tuple(grad.astype(bf16) for grad in head_grads)
    head_grads = tuple(grad.astype(f32)[None] for grad in lax.psum(head_grads, "dp"))
    back = (
        product(query_grad, query_mat, 1, 1)
        + product(key_grad, key_mat, 1, 1)
        + product(logit_grad, gate_mat, 1, 1)
    )
    row_back, grad_attend = norm_back(grouped, inverse, attend_scale, back)
    partial = (row_back + product(expert_grad, value_mat, 1, 1)).astype(bf16)
    input_grad = middle_grad + lax.psum_scatter(
        partial, "head", scatter_dimension=0, tiled=True
    ).astype(f32)
    grad_attend, grad_gain_expert = lax.psum((grad_attend, grad_gain_expert), everywhere)
    return (
        output,
        input_grad,
        grad_attend,
        *head_grads,
        grad_gain_expert,
        grad_router,
        grad_in,
        grad_out,
    )


MESH = pl.DeviceIdType.MESH
VM = pl.BlockSpec(memory_space=pltpu.VMEM)
ANY = pl.BlockSpec(memory_space=pl.ANY)
NN = (((1,), (0,)), ((), ()))
NT = (((1,), (1,)), ((), ()))
TN = (((0,), (0,)), ((), ()))


def dot(left, right, dims=NN):
    return lax.dot_general(left, right, dims, preferred_element_type=f32)


def at_block(block, count):
    return pl.ds(pl.multiple_of(block * count, count), count)


def remote(src, dst, send, recv, where):
    return pltpu.make_async_remote_copy(
        src_ref=src, dst_ref=dst, send_sem=send, recv_sem=recv, device_id=where, device_id_type=MESH
    )


def greet(places):
    barrier = pltpu.get_barrier_semaphore()
    for place in places:
        pl.semaphore_signal(barrier, inc=1, device_id=place, device_id_type=MESH)
    pl.semaphore_wait(barrier, len(places))


def swap_halves(value):
    half = value.shape[-1] // 2
    return jnp.concatenate([value[:, half:], value[:, :half]], axis=-1)


def attend_kernel(
    n_dp,
    n_head,
    x_ref,
    cot_ref,
    mask_ref,
    attend_gain_ref,
    expert_gain_ref,
    cos_ref,
    sin_ref,
    gate_mask_ref,
    seg_row_ref,
    seg_col_ref,
    wq_ref,
    wk_ref,
    wg_ref,
    wv_ref,
    wo_ref,
    in_ref,
    out_ref,
    all_in_ref,
    all_out_ref,
    all_cot_ref,
    all_mask_ref,
    mid_ref,
    mr_ref,
    rows_ref,
    q_ref,
    k_ref,
    v_ref,
    prob_ref,
    vx_ref,
    squash_ref,
    att_ref,
    w_an,
    w_v,
    w_o,
    part,
    got,
    local_sem,
    z_send,
    z_recv,
    p_send,
    p_recv,
):
    d, h = lax.axis_index("dp"), lax.axis_index("head")
    chip, core = d // 2, d % 2
    chips = n_dp // 2
    tokens, features = x_ref.shape
    width = q_ref.shape[1]
    experts = vx_ref.shape[1] // width
    scale = width ** (-0.5)
    group = tokens * n_head
    steps = (2, 3, 1)
    partner = (chip * 2 + 1 - core, h)

    def along(step):
        return (d, jnp.bitwise_xor(h, step))

    def across(step):
        return (jnp.bitwise_xor(chip, step) * 2 + core, h)

    def local(src, dst, number):
        return pltpu.make_async_copy(src, dst, local_sem.at[number])

    per_device = in_ref.shape[0]
    slab = per_device * width
    out_slot = lambda place, side: all_out_ref.at[place, at_block(side, slab), :]
    in_slot = lambda place, side, e: all_in_ref.at[
        place, :, at_block(side * per_device + e, width)
    ]
    loads = [
        local(wq_ref, w_an.at[:, pl.ds(0, width)], 0),
        local(wk_ref, w_an.at[:, pl.ds(width, width)], 1),
        local(wg_ref, w_an.at[:, pl.ds(2 * width, width)], 2),
        local(wv_ref, w_v, 3),
        local(wo_ref, w_o, 4),
        local(cot_ref, all_cot_ref.at[at_block(h, tokens), :], 5),
        local(mask_ref.at[h], all_mask_ref.at[at_block(h, tokens), :], 6),
        local(out_ref, out_slot(chip, core), 7),
    ] + [local(in_ref.at[e], in_slot(chip, core, e), 8 + e) for e in range(per_device)]
    for load in loads:
        load.start()
    greet([along(s) for s in steps] + [partner] + [across(s) for s in range(1, chips)])

    def spread(kind, src, dst_of, order=steps):
        copies = {}
        for step in order:
            copies[step] = remote(
                src(step),
                dst_of(step),
                z_send.at[kind, step - 1],
                z_recv.at[kind, step - 1],
                along(step),
            )
            copies[step].start()
        return copies

    x_copies = spread(0, lambda s: x_ref, lambda s: rows_ref.at[at_block(h, tokens), :])

    def weights_to(where, slot, place, side, own):
        pieces = [
            remote(
                out_ref if own else out_slot(place, side),
                out_slot(place, side),
                p_send.at[slot, 0],
                p_recv.at[slot, 0],
                where,
            )
        ]
        for e in range(per_device):
            pieces.append(
                remote(
                    in_ref.at[e] if own else in_slot(place, side, e),
                    in_slot(place, side, e),
                    p_send.at[slot, 1 + e],
                    p_recv.at[slot, 1 + e],
                    where,
                )
            )
        return pieces

    first = [weights_to(across(s), s, chip, core, True) for s in range(1, chips)]
    first.append(weights_to(partner, 0, chip, core, True))
    for piece in range(1 + per_device):
        for pieces in first:
            pieces[piece].start()
    mask_copies = spread(
        1,
        lambda s: mask_ref.at[jnp.bitwise_xor(h, s)],
        lambda s: all_mask_ref.at[at_block(h, tokens), :],
    )

    rows_ref[at_block(h, tokens), :] = x_ref[...]
    for load in loads[:5]:
        load.wait()

    def project(block):
        at = at_block(block, tokens)
        rows = rows_ref[at, :]
        wide = rows.astype(f32)
        inverse = lax.rsqrt(jnp.mean(wide * wide, axis=-1, keepdims=True) + epsilon)
        normed = (wide * inverse * attend_gain_ref[...]).astype(bf16)
        qkg = dot(normed, w_an[...])
        cosine, sine = cos_ref[at, :], sin_ref[at, :]
        q, k = qkg[:, :width], qkg[:, width : 2 * width]
        q_ref[at, :] = (q * cosine + swap_halves(q) * sine).astype(bf16)
        k_ref[at, :] = (k * cosine + swap_halves(k) * sine).astype(bf16)
        squash = jax.nn.sigmoid(qkg[:, 2 * width :])
        squash_ref[at, :] = squash
        gates = squash * gate_mask_ref[at, :]
        vx = dot(rows, w_v[...])
        vx_ref[at, :] = vx
        value = gates[:, 0:1] * vx[:, :width]
        for e in range(1, experts):
            value += gates[:, e : e + 1] * vx[:, e * width : (e + 1) * width]
        v_ref[at, :] = value.astype(bf16)

    project(h)
    for step in (1, 2, 3):
        x_copies[step].wait_recv()
        project(jnp.bitwise_xor(h, step))
    for step in steps:
        x_copies[step].wait_send()
    cot_copies = spread(2, lambda s: cot_ref, lambda s: all_cot_ref.at[at_block(h, tokens), :])

    def attend(block):
        at = at_block(block, tokens)
        scores = dot(q_ref[at, :], k_ref[...], NT) * scale
        row = block * tokens + lax.broadcasted_iota(jnp.int32, (tokens, group), 0)
        column = lax.broadcasted_iota(jnp.int32, (tokens, group), 1)
        allowed = (column <= row) & (seg_col_ref[at, :] == seg_row_ref[...])
        scores = jnp.where(allowed, scores, negative)
        exponents = jnp.exp(scores - jnp.max(scores, axis=-1, keepdims=True))
        prob = exponents / jnp.sum(exponents, axis=-1, keepdims=True)
        prob_ref[at, :] = prob
        att = dot(prob.astype(bf16), v_ref[...])
        att_ref[at, :] = att
        gates = squash_ref[at, :] * gate_mask_ref[at, :]
        wide = jnp.concatenate(
            [(gates[:, experts + e : experts + e + 1] * att).astype(bf16) for e in range(experts)],
            axis=-1,
        )
        return dot(wide, w_o[...])

    part_copies = {}
    for step in steps:
        part[step - 1] = attend(jnp.bitwise_xor(h, step)).astype(bf16)
        part_copies[step] = remote(
            part.at[step - 1],
            got.at[step - 1],
            z_send.at[3, step - 1],
            z_recv.at[3, step - 1],
            along(step),
        )
        part_copies[step].start()
    middle = x_ref[...].astype(f32) + attend(h)
    for step in steps:
        part_copies[step].wait_recv()
    for step in steps:
        middle += got[step - 1].astype(f32)
    mid_ref[...] = middle
    inverse = lax.rsqrt(jnp.mean(middle * middle, axis=-1, keepdims=True) + epsilon)
    mr_ref[...] = (middle * inverse * expert_gain_ref[...]).astype(bf16)
    for step in steps:
        part_copies[step].wait_send()

    onward = []
    for s in range(1, chips):
        place = jnp.bitwise_xor(chip, s)
        pieces = weights_to(partner, chips - 1 + s, place, core, False)
        for piece in range(1 + per_device):
            first[s - 1][piece].wait_recv()
            pieces[piece].start()
        onward.append(pieces)
    for pieces in first[:-1]:
        for piece in pieces:
            piece.wait_send()
    for pieces in [first[-1]] + onward:
        for piece in pieces:
            piece.wait()
    for copies in (mask_copies, cot_copies):
        for step in steps:
            copies[step].wait()
    for load in loads[5:]:
        load.wait()


def attend_call(n_dp, n_head, tokens, features, width, experts, per_device, args):
    group = tokens * n_head
    chips = n_dp // 2
    slab = per_device * width
    shape = jax.ShapeDtypeStruct
    outs = [
        (shape((chips, features, 2 * slab), bf16), ANY),
        (shape((chips, 2 * slab, features), bf16), ANY),
        (shape((group, features), bf16), ANY),
        (shape((group, 128), bf16), ANY),
        (shape((tokens, features), f32), VM),
        (shape((tokens, features), bf16), VM),
        (shape((group, features), bf16), VM),
        (shape((group, width), bf16), VM),
        (shape((group, width), bf16), VM),
        (shape((group, width), bf16), VM),
        (shape((group, group), f32), VM),
        (shape((group, experts * width), f32), VM),
        (shape((group, 128), f32), VM),
        (shape((group, width), f32), VM),
    ]
    return pl.pallas_call(
        functools.partial(attend_kernel, n_dp, n_head),
        out_shape=[o[0] for o in outs],
        out_specs=[o[1] for o in outs],
        in_specs=[VM, ANY, VM] + [VM] * 7 + [ANY] * 7,
        scratch_shapes=[
            pltpu.VMEM((features, 3 * width), bf16),
            pltpu.VMEM((features, experts * width), bf16),
            pltpu.VMEM((experts * width, features), bf16),
            pltpu.VMEM((n_head - 1, tokens, features), bf16),
            pltpu.VMEM((n_head - 1, tokens, features), bf16),
            pltpu.SemaphoreType.DMA((8 + per_device,)),
            pltpu.SemaphoreType.DMA((4, n_head - 1)),
            pltpu.SemaphoreType.DMA((4, n_head - 1)),
            pltpu.SemaphoreType.DMA((2 * chips - 1, 1 + per_device)),
            pltpu.SemaphoreType.DMA((2 * chips - 1, 1 + per_device)),
        ],
        compiler_params=pltpu.CompilerParams(
            collective_id=1, has_side_effects=True, vmem_limit_bytes=40 << 20
        ),
    )(*args)


def expert_kernel(
    n_dp,
    n_head,
    mr_ref,
    mid_ref,
    own_cot_ref,
    all_mask_ref,
    router_ref,
    gain_ref,
    all_cot_ref,
    all_in_ref,
    all_out_ref,
    da_ref,
    dmid_ref,
    po_ref,
    gr_ref,
    eg_ref,
    gi_ref,
    go_ref,
    w_in,
    w_out,
    cot,
    rows,
    rows_t,
    lifted,
    acts,
    hids,
    dzs,
    part,
    got,
    local_sem,
    store_sem,
    z_send,
    z_recv,
):
    d, h = lax.axis_index("dp"), lax.axis_index("head")
    chips = n_dp // 2
    tokens, features = mr_ref.shape
    wide = w_in.shape[2]
    slab = wide // 2
    lanes = router_ref.shape[1]
    width = 128
    group = tokens * n_head
    pair = 2 * tokens
    column = 256

    def along(step):
        return (d, jnp.bitwise_xor(h, step))

    def local(src, dst, number):
        return pltpu.make_async_copy(src, dst, local_sem.at[number])

    loads = [local(all_cot_ref, cot, 0)]
    loads += [local(all_out_ref.at[j], w_out.at[j], 1 + j) for j in range(chips)]
    loads += [local(all_in_ref.at[j], w_in.at[j], 1 + chips + j) for j in range(chips)]
    for load in loads:
        load.start()
    greet([along(s) for s in (1, 2, 3)])
    mr_copies = {}
    for step in (1, 2, 3):
        mr_copies[step] = remote(
            mr_ref,
            rows.at[at_block(h, tokens), :],
            z_send.at[0, step - 1],
            z_recv.at[0, step - 1],
            along(step),
        )
        mr_copies[step].start()
    rows[at_block(h, tokens), :] = mr_ref[...]

    loads[0].wait()
    for j in range(chips):
        loads[1 + j].wait()

    @pl.loop(0, chips)
    def _(j):
        lifted[j] = dot(cot[...], w_out[j], NT).astype(bf16)

    for j in range(chips):
        loads[1 + chips + j].wait()

    def spread_lanes(j):
        lane = lax.broadcasted_iota(jnp.int32, (lanes, wide), 1) // width
        slot = lax.broadcasted_iota(jnp.int32, (lanes, wide), 0)
        return jnp.where(slot == lane + j * (wide // width), 1.0, 0.0).astype(bf16)

    def pair_of_blocks(number):
        at = at_block(number, pair)
        own = rows[at, :]
        gates = jax.nn.sigmoid(dot(own, router_ref[...]))
        live = gates * all_mask_ref[at, :].astype(f32)
        high = live.astype(bf16)
        low = (live - high.astype(f32)).astype(bf16)
        both = jnp.concatenate([high, low], axis=-1)

        def chip_step(j, sums):
            pick = spread_lanes(j)
            hidden = dot(own, w_in[j])
            spread = dot(both, jnp.concatenate([pick, pick], axis=0))
            lift = lifted[j, at, :].astype(f32)
            square = hidden * hidden
            inner = jnp.tanh(0.7978845608028654 * hidden * (1.0 + 0.044715 * square))
            half = 0.5 * (1.0 + inner)
            act = hidden * half
            slope = half + act * (1.0 - inner) * (
                0.7978845608028654 + (0.7978845608028654 * 3.0 * 0.044715) * square
            )
            acts[j, at, :] = (act * spread).astype(bf16)
            hids[j, at, :] = (slope * (lift * spread)).astype(bf16)
            return sums + dot((act * lift).astype(bf16), pick, NT)

        sums = lax.fori_loop(0, chips, chip_step, jnp.zeros((pair, lanes), f32))
        dz = (sums * live * (1.0 - gates)).astype(bf16)
        dzs[at, :] = dz

        @pl.loop(0, features // column)
        def _(c):
            part_of = at_block(c, column)
            total = dot(dz, router_ref[part_of, :], NT)
            for j in range(chips):
                total += dot(hids[j, at, :], w_in[j, part_of, :], NT)
            part[at, part_of] = total.astype(bf16)

    def send_back(step):
        where = jnp.bitwise_xor(h, step)
        copy = remote(
            part.at[at_block(where, tokens), :],
            got.at[step - 1],
            z_send.at[1, step - 1],
            z_recv.at[1, step - 1],
            along(step),
        )
        copy.start()
        return copy

    near = h // 2
    mr_copies[1].wait_recv()
    pair_of_blocks(near)
    back = {1: send_back(1)}
    mr_copies[2].wait_recv()
    mr_copies[3].wait_recv()
    pair_of_blocks(1 - near)
    back[2], back[3] = send_back(2), send_back(3)

    @pl.loop(0, features // column)
    def _(c):
        part_of = at_block(c, column)
        total = dot(acts[0], w_out[0, :, part_of])
        for j in range(1, chips):
            total += dot(acts[j], w_out[j, :, part_of])
        po_ref[:, part_of] = total.astype(bf16)

    rows_t[...] = rows[...].T

    @pl.loop(0, chips)
    def _(j):
        for side in range(2):
            mine = pl.ds(side * slab, slab)
            w_in[j, :, mine] = dot(rows_t[...], hids[j, :, mine]).astype(bf16)
            w_out[j, mine, :] = dot(acts[j, :, mine], cot[...], TN).astype(bf16)

    stores = []
    for j in range(chips):
        for side in range(2):
            mine = pl.ds(side * slab, slab)
            number = 2 * j + side
            stores.append(
                pltpu.make_async_copy(
                    w_in.at[j, :, mine], gi_ref.at[number], store_sem.at[0, number]
                )
            )
            stores.append(
                pltpu.make_async_copy(
                    w_out.at[j, mine, :], go_ref.at[number], store_sem.at[1, number]
                )
            )
    for store in stores:
        store.start()
    gr_ref[...] = dot(dzs[...], rows[...], TN)[: gr_ref.shape[0]]

    for step in (1, 2, 3):
        back[step].wait_recv()
    incoming = part[at_block(h, tokens), :].astype(f32)
    for step in (1, 2, 3):
        incoming += got[step - 1].astype(f32)
    middle = mid_ref[...]
    inverse = lax.rsqrt(jnp.mean(middle * middle, axis=-1, keepdims=True) + epsilon)
    unit = middle * inverse
    scaled = incoming * gain_ref[...]
    eg_ref[...] = jnp.sum(incoming * unit, axis=0, keepdims=True)
    dmid = own_cot_ref[...].astype(f32) + inverse * (
        scaled - unit * jnp.mean(scaled * unit, axis=-1, keepdims=True)
    )
    dmid_ref[...] = dmid
    da_ref[...] = dmid.astype(bf16)
    for step in (1, 2, 3):
        back[step].wait_send()
        mr_copies[step].wait_send()
    for store in stores:
        store.wait()


def expert_call(n_dp, n_head, tokens, features, width, per_device, args):
    group = tokens * n_head
    chips = n_dp // 2
    slab = per_device * width
    lanes = 128
    named = -(-n_dp * per_device // 8) * 8
    shape = jax.ShapeDtypeStruct
    outs = [
        (shape((tokens, features), bf16), VM),
        (shape((tokens, features), f32), VM),
        (shape((group, features), bf16), VM),
        (shape((named, features), f32), VM),
        (shape((1, features), f32), VM),
        (shape((n_dp, features, slab), bf16), ANY),
        (shape((n_dp, slab, features), bf16), ANY),
    ]
    return pl.pallas_call(
        functools.partial(expert_kernel, n_dp, n_head),
        out_shape=[o[0] for o in outs],
        out_specs=[o[1] for o in outs],
        in_specs=[VM] * 6 + [ANY] * 3,
        scratch_shapes=[
            pltpu.VMEM((chips, features, 2 * slab), bf16),
            pltpu.VMEM((chips, 2 * slab, features), bf16),
            pltpu.VMEM((group, features), bf16),
            pltpu.VMEM((group, features), bf16),
            pltpu.VMEM((features, group), bf16),
            pltpu.VMEM((chips, group, 2 * slab), bf16),
            pltpu.VMEM((chips, group, 2 * slab), bf16),
            pltpu.VMEM((chips, group, 2 * slab), bf16),
            pltpu.VMEM((group, lanes), bf16),
            pltpu.VMEM((group, features), bf16),
            pltpu.VMEM((n_head - 1, tokens, features), bf16),
            pltpu.SemaphoreType.DMA((1 + 2 * chips,)),
            pltpu.SemaphoreType.DMA((2, n_dp)),
            pltpu.SemaphoreType.DMA((2, n_head - 1)),
            pltpu.SemaphoreType.DMA((2, n_head - 1)),
        ],
        compiler_params=pltpu.CompilerParams(
            collective_id=2, has_side_effects=True, vmem_limit_bytes=56 << 20
        ),
    )(*args)


def grads_kernel(
    n_dp,
    n_head,
    da_ref,
    dmid_ref,
    mid_ref,
    po_ref,
    gr_ref,
    eg_ref,
    rows_ref,
    q_ref,
    k_ref,
    v_ref,
    prob_ref,
    vx_ref,
    squash_ref,
    att_ref,
    gate_mask_ref,
    cos_ref,
    sin_ref,
    attend_gain_ref,
    wq_ref,
    wk_ref,
    wg_ref,
    wv_ref,
    wo_ref,
    gi_ref,
    go_ref,
    output_ref,
    grad_x_ref,
    wide_ref,
    fin_in_ref,
    fin_out_ref,
    w_an,
    w_v,
    w_o,
    das,
    normed,
    normed_t,
    rows_t,
    inverses,
    datt,
    gate_grads,
    probs,
    scores,
    qkz,
    vgrads,
    part,
    got,
    got_out,
    gain_part,
    gain_got,
    sums,
    core_got,
    chip_got,
    piece,
    blocks,
    own_in,
    own_out,
    core_in,
    core_out,
    hop_in,
    hop_out,
    last_in,
    last_out,
    local_sem,
    z_send,
    z_recv,
    c_send,
    c_recv,
    e_send,
    e_recv,
    s_send,
    s_recv,
):
    d, h = lax.axis_index("dp"), lax.axis_index("head")
    chip, core = d // 2, d % 2
    chips = n_dp // 2
    tokens, features = da_ref.shape
    width = q_ref.shape[1]
    experts = vx_ref.shape[1] // width
    scale = width ** (-0.5)
    group = tokens * n_head
    named = gr_ref.shape[0]
    side = features // 2
    slice_ = side // chips
    steps = (2, 3, 1)
    partner = (chip * 2 + 1 - core, h)
    xor = jnp.bitwise_xor

    def along(step):
        return (d, xor(h, step))

    def across(step):
        return (xor(chip, step) * 2 + core, h)

    def local(src, dst, number):
        return pltpu.make_async_copy(src, dst, local_sem.at[number])

    loads = [
        local(wo_ref, w_o, 0),
        local(wq_ref, w_an.at[:, pl.ds(0, width)], 1),
        local(wk_ref, w_an.at[:, pl.ds(width, width)], 2),
        local(wg_ref, w_an.at[:, pl.ds(2 * width, width)], 3),
        local(wv_ref, w_v, 4),
    ]
    order = (3, 1, 2, 0)
    mine = {}
    for n, s in enumerate(order):
        place = xor(chip, s)
        mine[s] = (
            local(gi_ref.at[2 * place + core], own_in.at[place], 5 + 2 * n),
            local(go_ref.at[2 * place + core], own_out.at[place], 6 + 2 * n),
        )
    for load in loads + [m for s in order for m in mine[s]]:
        load.start()
    greet([along(s) for s in steps] + [partner] + [across(s) for s in range(1, chips)])

    def spread(kind, src, dst, send=steps):
        copies = {}
        for step in send:
            copies[step] = remote(
                src(step), dst(step), z_send.at[kind, step - 1], z_recv.at[kind, step - 1], along(step)
            )
            copies[step].start()
        return copies

    da_copies = spread(0, lambda s: da_ref, lambda s: das.at[at_block(h, tokens), :])
    theirs = {}
    for n, s in enumerate(order):
        place = xor(chip, s)
        theirs[s] = (
            remote(
                gi_ref.at[2 * place + 1 - core], core_in.at[place], c_send.at[0, n], c_recv.at[0, n], partner
            ),
            remote(
                go_ref.at[2 * place + 1 - core], core_out.at[place], c_send.at[1, n], c_recv.at[1, n], partner
            ),
        )
        for copy in theirs[s]:
            copy.start()

    def section(number, first, count):
        at = pl.ds(first, count)
        col = lambda c, j: at_block(c * chips + j, slice_)
        state = {}

        def start():
            state["core"] = remote(
                sums.at[at, at_block(1 - core, side)],
                core_got.at[at, :],
                s_send.at[number, 0],
                s_recv.at[number, 0],
                partner,
            )
            state["core"].start()

        def mid():
            state["core"].wait()
            half = at_block(core, side)
            sums[at, half] = sums[at, half] + core_got[at, :]
            state["chips"] = []
            for s in range(1, chips):
                copy = remote(
                    sums.at[at, col(core, xor(chip, s))],
                    chip_got.at[s - 1, at, :],
                    s_send.at[number, s],
                    s_recv.at[number, s],
                    across(s),
                )
                copy.start()
                state["chips"].append(copy)

        def add():
            for copy in state["chips"]:
                copy.wait()
            total = sums[at, col(core, chip)].astype(f32)
            for s in range(1, chips):
                total += chip_got[s - 1, at, :].astype(f32)
            piece[at, :] = total.astype(bf16)

        def share(src=None, dst=None, at_dst=None):
            src = piece.at[at, :] if src is None else src
            dst = wide_ref if dst is None else dst
            at_dst = at if at_dst is None else at_dst
            state["end"] = (dst, at_dst)
            mine = remote(
                src,
                dst.at[at_dst, col(core, chip)],
                s_send.at[number, chips],
                s_recv.at[number, chips],
                partner,
            )
            mine.start()
            own = pltpu.make_async_copy(
                src, dst.at[at_dst, col(core, chip)], s_send.at[number, 3 * chips - 1]
            )
            own.start()
            state["share"] = []
            for s in range(1, chips):
                copy = remote(
                    src,
                    dst.at[at_dst, col(core, chip)],
                    s_send.at[number, chips + s],
                    s_recv.at[number, chips + s],
                    across(s),
                )
                copy.start()
                state["share"].append(copy)
            state["wait"] = [mine, own]

        def forward():
            dst, at_dst = state["end"]
            for s in range(1, chips):
                state["share"][s - 1].wait()
                here = dst.at[at_dst, col(core, xor(chip, s))]
                copy = remote(
                    here,
                    here,
                    s_send.at[number, 2 * chips - 1 + s],
                    s_recv.at[number, 2 * chips - 1 + s],
                    partner,
                )
                copy.start()
                state["wait"].append(copy)

        def end():
            for copy in state["wait"]:
                copy.wait()

        return start, mid, add, share, forward, end

    top = features + w_o.shape[0]
    small = -(-(named + 1) // 16) * 16
    of_o = section(0, features, w_o.shape[0])
    of_d = section(1, 0, features)
    of_g = section(2, top + 16, small)
    of_a = section(3, top, 16)

    sums[pl.ds(top + 16, small), :] = jnp.concatenate(
        [gr_ref[...], eg_ref[...], jnp.zeros((small - named - 1, features), f32)], axis=0
    ).astype(bf16)
    of_g[0]()

    for block in range(n_head):
        at = pl.ds(block * tokens, tokens)
        wide = rows_ref[at, :].astype(f32)
        inverse = lax.rsqrt(jnp.mean(wide * wide, axis=-1, keepdims=True) + epsilon)
        inverses[at, :] = jnp.broadcast_to(inverse, (tokens, width))
        normed[at, :] = (wide * inverse * attend_gain_ref[...]).astype(bf16)
    normed_t[...] = normed[...].T
    rows_t[...] = rows_ref[...].T
    das[at_block(h, tokens), :] = da_ref[...]
    for load in loads:
        load.wait()

    halves_in = (pl.ds(0, features // 2), pl.ds(features // 2, features // 2))
    slab = own_out.shape[1]
    halves_out = (pl.ds(0, slab // 2), pl.ds(slab // 2, slab // 2))
    hops = {}

    def hop(half, index, place, toward):
        copies = (
            remote(
                own_in.at[place, halves_in[half], :],
                hop_in.at[half, index],
                e_send.at[0, 2 * half + index],
                e_recv.at[0, 2 * half + index],
                across(toward),
            ),
            remote(
                own_out.at[place, halves_out[half], :],
                hop_out.at[half, index],
                e_send.at[1, 2 * half + index],
                e_recv.at[1, 2 * half + index],
                across(toward),
            ),
        )
        for copy in copies:
            copy.start()
        hops[half, index] = copies

    for s in order:
        place = xor(chip, s)
        for copy in mine[s] + theirs[s]:
            copy.wait()
        own_in[place] = own_in[place] + core_in[place]
        own_out[place] = own_out[place] + core_out[place]
        if s == 3:
            hop(0, 1, place, 1)
            hop(1, 1, place, 2)
        elif s:
            hop(s - 1, 0, place, s)

    of_g[1]()

    lane = lax.broadcasted_iota(jnp.int32, (tokens, width), 1)

    def through_output(block):
        at = at_block(block, tokens)
        wide = dot(das[at, :], w_o[...], NT)
        gates = squash_ref[at, :] * gate_mask_ref[at, :]
        att = att_ref[at, :]
        total = jnp.zeros((tokens, width), f32)
        gate = jnp.zeros((tokens, width), f32)
        for e in range(experts):
            one = wide[:, e * width : (e + 1) * width]
            total += gates[:, experts + e : experts + e + 1] * one
            gate = jnp.where(
                lane == experts + e, jnp.sum(one * att, axis=-1, keepdims=True), gate
            )
        datt[at, :] = total.astype(bf16)
        gate_grads[at, :] = gate

    through_output(h)
    for step in (1, 2, 3):
        da_copies[step].wait_recv()
        through_output(xor(h, step))
    for step in steps:
        da_copies[step].wait_send()
    out_copies = spread(1, lambda s: po_ref.at[at_block(xor(h, s), tokens), :], lambda s: got_out.at[s - 1])

    gates = squash_ref[...] * gate_mask_ref[...]
    for e in range(experts):
        one = (gates[:, experts + e : experts + e + 1] * att_ref[...]).astype(bf16)
        sums[pl.ds(features + e * width, width), :] = dot(one, das[...], TN).astype(bf16)
    of_o[0]()

    @pl.loop(0, n_head)
    def _(block):
        at = at_block(block, tokens)
        prob = prob_ref[at, :]
        dprob = dot(datt[at, :], v_ref[...], NT)
        centre = jnp.sum(prob * dprob, axis=-1, keepdims=True)
        scores[at, :] = (prob * (dprob - centre)).astype(bf16)
        probs[at, :] = prob.astype(bf16)

    dq = dot(scores[...], k_ref[...]) * scale
    dk = dot(scores[...], q_ref[...], TN) * scale
    dv = dot(probs[...], datt[...], TN)
    of_o[1]()
    cosine, sine = cos_ref[...], sin_ref[...]
    qkz[:, pl.ds(0, width)] = (dq * cosine - swap_halves(dq) * sine).astype(bf16)
    qkz[:, pl.ds(width, width)] = (dk * cosine - swap_halves(dk) * sine).astype(bf16)
    gate = gate_grads[...]
    lanes = lax.broadcasted_iota(jnp.int32, (group, width), 1)
    for e in range(experts):
        vgrads[:, pl.ds(e * width, width)] = (gates[:, e : e + 1] * dv).astype(bf16)
        one = jnp.sum(vx_ref[:, pl.ds(e * width, width)] * dv, axis=-1, keepdims=True)
        gate = jnp.where(lanes == e, one, gate)
    squash = squash_ref[...]
    qkz[:, pl.ds(2 * width, width)] = (gate * gates * (1.0 - squash)).astype(bf16)

    sums[pl.ds(0, features), pl.ds(0, 3 * width)] = dot(normed_t[...], qkz[...]).astype(bf16)
    sums[pl.ds(0, features), pl.ds(3 * width, experts * width)] = dot(
        rows_t[...], vgrads[...]
    ).astype(bf16)
    of_d[0]()

    def into_rows(block):
        at = at_block(block, tokens)
        wide = dot(qkz[at, :], w_an[...], NT)
        unit = rows_ref[at, :].astype(f32) * inverses[at, 0:1]
        scaled = wide * attend_gain_ref[...]
        gain = jnp.sum(wide * unit, axis=0, keepdims=True)
        total = inverses[at, 0:1] * (
            scaled - unit * jnp.mean(scaled * unit, axis=-1, keepdims=True)
        ) + dot(vgrads[at, :], w_v[...], NT)
        return total, gain

    x_copies = {}
    gain = jnp.zeros((1, features), f32)
    for step in steps:
        total, one = into_rows(xor(h, step))
        gain += one
        part[step - 1] = total.astype(bf16)
        x_copies[step] = remote(
            part.at[step - 1], got.at[step - 1], z_send.at[2, step - 1], z_recv.at[2, step - 1], along(step)
        )
        x_copies[step].start()
    total, one = into_rows(h)
    gain += one
    gain_part[...] = jnp.broadcast_to(gain, gain_part.shape)
    gain_copies = spread(3, lambda s: gain_part, lambda s: gain_got.at[s - 1])
    grad_x_ref[...] = dmid_ref[...] + total
    of_d[1]()
    of_g[2]()

    own_block = at_block(h, small)
    blocks[own_block, :] = piece[pl.ds(top + 16, small), :]
    g_copies = spread(4, lambda s: blocks.at[own_block, :], lambda s: blocks.at[own_block, :])
    of_o[2]()
    of_o[3]()

    lasts = {}
    for half in range(2):
        toward = 2 - half
        for index, place in ((1, xor(chip, toward)), (0, chip)):
            for copy in hops[half, index]:
                copy.wait()
            at_in, at_out = halves_in[half], halves_out[half]
            own_in[place, at_in, :] = own_in[place, at_in, :] + hop_in[half, index]
            own_out[place, at_out, :] = own_out[place, at_out, :] + hop_out[half, index]
            if index:
                lasts[half] = (
                    remote(
                        own_in.at[place, at_in, :],
                        last_in.at[half],
                        e_send.at[0, 4 + half],
                        e_recv.at[0, 4 + half],
                        across(toward),
                    ),
                    remote(
                        own_out.at[place, at_out, :],
                        last_out.at[half],
                        e_send.at[1, 4 + half],
                        e_recv.at[1, 4 + half],
                        across(toward),
                    ),
                )
                for copy in lasts[half]:
                    copy.start()

    for step in steps:
        gain_copies[step].wait()
    gain = gain_part[...]
    for step in steps:
        gain += gain_got[step - 1]
    sums[pl.ds(top, 16), :] = jnp.concatenate([gain, gain], axis=0).astype(bf16)
    of_a[0]()

    for step in steps:
        g_copies[step].wait()
    of_g[3](blocks, wide_ref, pl.ds(top + 16, n_head * small))
    of_a[1]()

    for step in steps:
        out_copies[step].wait()
    output = mid_ref[...] + po_ref[at_block(h, tokens), :].astype(f32)
    for step in steps:
        output += got_out[step - 1].astype(f32)
    output_ref[...] = output
    of_d[2]()
    of_d[3]()
    of_a[2]()
    of_a[3]()
    of_o[4]()
    of_g[4]()
    for step in steps:
        x_copies[step].wait()
        grad_x_ref[...] += got[step - 1].astype(f32)
    for half in range(2):
        for copy in lasts[half]:
            copy.wait()
        at_in, at_out = halves_in[half], halves_out[half]
        fin_in_ref[at_in, :] = own_in[chip, at_in, :] + last_in[half]
        fin_out_ref[at_out, :] = own_out[chip, at_out, :] + last_out[half]
    of_d[4]()
    of_a[4]()
    for one in (of_o, of_g, of_d, of_a):
        one[5]()


def grads_call(n_dp, n_head, tokens, features, width, experts, per_device, args):
    group = tokens * n_head
    chips = n_dp // 2
    slab = per_device * width
    named = -(-n_dp * per_device // 8) * 8
    small = -(-(named + 1) // 16) * 16
    top = features + experts * width
    held = top + 16 + small
    peers = n_head - 1
    shape = jax.ShapeDtypeStruct
    outs = [
        (shape((tokens, features), f32), VM),
        (shape((tokens, features), f32), VM),
        (shape((top + 16 + n_head * small, features), bf16), ANY),
        (shape((features, slab), bf16), VM),
        (shape((slab, features), bf16), VM),
    ]
    return pl.pallas_call(
        functools.partial(grads_kernel, n_dp, n_head),
        out_shape=[o[0] for o in outs],
        out_specs=[o[1] for o in outs],
        in_specs=[VM] * 18 + [ANY] * 7,
        scratch_shapes=[
            pltpu.VMEM((features, 3 * width), bf16),
            pltpu.VMEM((features, experts * width), bf16),
            pltpu.VMEM((experts * width, features), bf16),
            pltpu.VMEM((group, features), bf16),
            pltpu.VMEM((group, features), bf16),
            pltpu.VMEM((features, group), bf16),
            pltpu.VMEM((features, group), bf16),
            pltpu.VMEM((group, width), f32),
            pltpu.VMEM((group, width), bf16),
            pltpu.VMEM((group, width), f32),
            pltpu.VMEM((group, group), bf16),
            pltpu.VMEM((group, group), bf16),
            pltpu.VMEM((group, 3 * width), bf16),
            pltpu.VMEM((group, experts * width), bf16),
            pltpu.VMEM((peers, tokens, features), bf16),
            pltpu.VMEM((peers, tokens, features), bf16),
            pltpu.VMEM((peers, tokens, features), bf16),
            pltpu.VMEM((8, features), f32),
            pltpu.VMEM((peers, 8, features), f32),
            pltpu.VMEM((held, features), bf16),
            pltpu.VMEM((held, features // 2), bf16),
            pltpu.VMEM((chips - 1, held, features // n_dp), bf16),
            pltpu.VMEM((held, features // n_dp), bf16),
            pltpu.VMEM((n_head * small, features // n_dp), bf16),
            pltpu.VMEM((chips, features, slab), bf16),
            pltpu.VMEM((chips, slab, features), bf16),
            pltpu.VMEM((chips, features, slab), bf16),
            pltpu.VMEM((chips, slab, features), bf16),
            pltpu.VMEM((2, 2, features // 2, slab), bf16),
            pltpu.VMEM((2, 2, slab // 2, features), bf16),
            pltpu.VMEM((2, features // 2, slab), bf16),
            pltpu.VMEM((2, slab // 2, features), bf16),
            pltpu.SemaphoreType.DMA((5 + 2 * chips,)),
            pltpu.SemaphoreType.DMA((5, peers)),
            pltpu.SemaphoreType.DMA((5, peers)),
            pltpu.SemaphoreType.DMA((2, chips)),
            pltpu.SemaphoreType.DMA((2, chips)),
            pltpu.SemaphoreType.DMA((2, 6)),
            pltpu.SemaphoreType.DMA((2, 6)),
            pltpu.SemaphoreType.DMA((4, 3 * chips)),
            pltpu.SemaphoreType.DMA((4, 3 * chips)),
        ],
        compiler_params=pltpu.CompilerParams(
            collective_id=3, has_side_effects=True, vmem_limit_bytes=58 << 20
        ),
    )(*args)


def kernel_body(
    n_dp,
    n_head,
    hidden_in,
    segments,
    value_pick,
    output_pick,
    expert_pick,
    attend_gain,
    query_weight,
    key_weight,
    value_weight,
    output_weight,
    head_router,
    expert_gain,
    router,
    expert_in,
    expert_out,
    cotangent,
):
    tokens, features = hidden_in.shape
    per_device, _, width = expert_in.shape
    experts = head_router.shape[2] // 2
    experts_total = router.shape[1]
    slab = per_device * width
    group = tokens * n_head
    chips = n_dp // 2
    d, h = lax.axis_index("dp"), lax.axis_index("head")
    lanes = 128
    owner = np.arange(n_dp * per_device)
    ids = (owner // per_device * n_head)[None, :] + np.arange(n_head)[:, None]
    ids = ids * per_device + owner % per_device
    ids = np.pad(ids, ((0, 0), (0, lanes - ids.shape[1])), constant_values=-1).astype(np.int32)
    mask4 = jnp.any(expert_pick[None, :, :, None] == ids[:, None, None, :], axis=2).astype(bf16)
    angles = np.arange(group)[:, None] * theta ** (-2.0 * np.arange(width // 2) / width)[None, :]
    cosine = np.concatenate([np.cos(angles)] * 2, axis=1).astype(np.float32)
    sine = np.concatenate([-np.sin(angles), np.sin(angles)], axis=1).astype(np.float32)
    slots = np.arange(lanes, dtype=np.int32)
    gate_mask = (
        jnp.any(value_pick[:, 0, :, None] == slots, axis=1)
        | jnp.any(output_pick[:, 0, :, None] + experts == slots, axis=1)
    ).astype(f32)
    gate_mat = jnp.pad(head_router[0], ((0, 0), (0, lanes - head_router.shape[2])))
    attend_scale = attend_gain.astype(f32)[None, :]
    expert_scale = expert_gain.astype(f32)[None, :]
    (all_in, all_out, all_cot, all_mask, middle, mr, rows, q, k, v, prob, vx, squash, att) = (
        attend_call(
            n_dp,
            n_head,
            tokens,
            features,
            width,
            experts,
            per_device,
            (
                hidden_in,
                cotangent,
                mask4,
                attend_scale,
                expert_scale,
                cosine,
                sine,
                gate_mask,
                segments[None, :],
                segments[:, None],
                query_weight[0],
                key_weight[0],
                gate_mat,
                value_weight[0],
                output_weight[0],
                expert_in,
                expert_out.reshape(slab, features),
            ),
        )
    )
    my_router = jnp.take(router, jnp.maximum(jnp.asarray(ids)[h], 0), axis=1)
    my_router = jnp.where(ids[0] >= 0, my_router, jnp.zeros((), bf16))
    da, middle_grad, part_out, gr, eg, gi, go = expert_call(
        n_dp,
        n_head,
        tokens,
        features,
        width,
        per_device,
        (mr, middle, cotangent, all_mask, my_router, expert_scale, all_cot, all_in, all_out),
    )
    output, input_grad, wide, fin_in, fin_out = grads_call(
        n_dp,
        n_head,
        tokens,
        features,
        width,
        experts,
        per_device,
        (
            da,
            middle_grad,
            middle,
            part_out,
            gr,
            eg,
            rows,
            q,
            k,
            v,
            prob,
            vx,
            squash,
            att,
            gate_mask,
            cosine,
            sine,
            attend_scale,
            query_weight[0],
            key_weight[0],
            gate_mat,
            value_weight[0],
            output_weight[0],
            gi,
            go,
        ),
    )
    top = features + experts * width
    small = (wide.shape[0] - top - 16) // n_head
    named = n_dp * per_device
    planes = wide[top + 16 :].astype(f32).reshape(n_head, small, features)
    grad_router = planes[:, :named].reshape(n_head, n_dp, per_device, features)
    grad_router = grad_router.transpose(1, 0, 2, 3).reshape(experts_total, features).T
    grad_gain = jnp.sum(planes[:, -(-named // 8) * 8], axis=0)
    first = wide[:features]
    return (
        output,
        input_grad,
        wide[top].astype(f32),
        first[None, :, :width].astype(f32),
        first[None, :, width : 2 * width].astype(f32),
        first[None, :, 3 * width :].astype(f32),
        wide[None, features:top].astype(f32),
        first[None, :, 2 * width : 2 * width + 2 * experts].astype(f32),
        grad_gain,
        grad_router,
        fin_in.astype(f32).reshape(features, per_device, width).transpose(1, 0, 2),
        fin_out.astype(f32).reshape(per_device, width, features),
    )


def solution(mesh):
    rows = P(everywhere, None)
    heads = P("head", None, None)
    experts = P(everywhere, None, None)
    picks = P("dp", "head", None)
    in_specs = (
        rows, P("dp"), picks, picks, rows, P(), heads, heads, heads, heads, heads,
        P(), P(), experts, experts, rows,
    )
    out_specs = (
        rows, rows, P(), heads, heads, heads, heads, heads, P(), P(), experts, experts,
    )
    n_dp, n_head = mesh.shape["dp"], mesh.shape["head"]

    def program(*args):
        held = 2 * n_dp * args[13].shape[0] * args[13].shape[1] * args[13].shape[2] * 2
        if n_head == 4 and held <= vmem_for_weights:
            return kernel_body(n_dp, n_head, *args)
        return body(*args)

    return jax.shard_map(program, mesh=mesh, in_specs=in_specs, out_specs=out_specs, check_vma=False)
```

```python
import functools

import jax
import jax.numpy as jnp
import numpy as np
from jax import lax
from jax.experimental import pallas as pl
from jax.experimental.pallas import tpu as pltpu
from jax.sharding import PartitionSpec as P

epsilon = 1e-06
theta = 10000.0
negative = -1e30
f32 = jnp.float32
bf16 = jnp.bfloat16
everywhere = ("dp", "head")
whole_rows = 4096
vmem_for_weights = 16 << 20
vmem_bytes = 62 << 20


def product(left, right, left_axis, right_axis):
    return lax.dot_general(
        left, right, (((left_axis,), (right_axis,)), ((), ())), preferred_element_type=f32
    )


def rms_scale(residual):
    return lax.rsqrt(jnp.mean(residual * residual, axis=-1, keepdims=True) + epsilon)


def rotary_tables(row_count, head_width):
    half_width = head_width // 2
    position = jnp.arange(row_count, dtype=f32)[:, None]
    exponent = jnp.arange(half_width, dtype=f32)[None, :]
    angles = position * jnp.power(theta, -2.0 * exponent / head_width)
    return (jnp.cos(angles), jnp.sin(angles))


def rotate(matrix, cosine, sine):
    half = matrix.shape[-1] // 2
    first, second = matrix[:, :half], matrix[:, half:]
    return jnp.concatenate([first * cosine - second * sine, second * cosine + first * sine], axis=-1)


def pick_mask(picks, expert_count):
    hits = picks[:, 0, :, None] == jnp.arange(expert_count, dtype=jnp.int32)[None, None, :]
    return jnp.any(hits, axis=1).astype(f32)


def norm_back(residual, inverse, gain, incoming):
    unit_rows = residual * inverse
    scaled = incoming * gain
    gain_grad = jnp.sum(incoming * unit_rows, axis=0)
    row_grad = inverse * (scaled - unit_rows * jnp.mean(scaled * unit_rows, axis=-1, keepdims=True))
    return (row_grad, gain_grad)


def gelu_pair(value):
    inner = jnp.tanh(0.7978845608028654 * (value + 0.044715 * value * value * value))
    slope = 0.5 * (1.0 + inner) + 0.5 * value * (1.0 - inner * inner) * 0.7978845608028654 * (
        1.0 + 3.0 * 0.044715 * value * value
    )
    return (0.5 * value * (1.0 + inner), slope)


def body(
    hidden_in,
    segments,
    value_pick,
    output_pick,
    expert_pick,
    attend_gain,
    query_weight,
    key_weight,
    value_weight,
    output_weight,
    head_router,
    expert_gain,
    router,
    expert_in,
    expert_out,
    cotangent,
):
    tokens, features = hidden_in.shape
    per_device, _, width = expert_in.shape
    head_experts = head_router.shape[2] // 2
    head_width = query_weight.shape[2]
    scale = head_width ** (-0.5)
    query_mat, key_mat, value_mat = query_weight[0], key_weight[0], value_weight[0]
    output_mat, gate_mat = output_weight[0], head_router[0]
    value_mask = pick_mask(value_pick, head_experts)
    output_mask = pick_mask(output_pick, head_experts)
    attend_scale = attend_gain.astype(f32)
    expert_scale = expert_gain.astype(f32)
    me = lax.axis_index("dp") * lax.axis_size("head") + lax.axis_index("head")

    rows = lax.all_gather(hidden_in, "head", axis=0, tiled=True)
    grouped = rows.astype(f32)
    group = grouped.shape[0]
    inverse = rms_scale(grouped)
    normed = (grouped * inverse * attend_scale).astype(bf16)
    cosine, sine = rotary_tables(group, head_width)
    queries = rotate(product(normed, query_mat, 1, 0), cosine, sine).astype(bf16)
    key_rows = rotate(product(normed, key_mat, 1, 0), cosine, sine).astype(bf16)
    squash = jax.nn.sigmoid(product(normed, gate_mat, 1, 0))
    value_gates = squash[:, :head_experts] * value_mask
    output_gates = squash[:, head_experts:] * output_mask
    expert_values = product(rows, value_mat, 1, 0).reshape(group, head_experts, head_width)
    values = jnp.sum(expert_values * value_gates[:, :, None], axis=1).astype(bf16)
    places = jnp.arange(group, dtype=jnp.int32)
    allowed = (places[None, :] <= places[:, None]) & (segments[:, None] == segments[None, :])
    scores = jnp.where(allowed, product(queries, key_rows, 1, 1) * scale, negative)
    exponents = jnp.exp(scores - jnp.max(scores, axis=-1, keepdims=True))
    probabilities = exponents / jnp.sum(exponents, axis=-1, keepdims=True)
    attended = product(probabilities.astype(bf16), values, 1, 0)
    weighted = (
        (output_gates[:, :, None] * attended[:, None, :]).reshape(group, -1).astype(bf16)
    )
    middle = hidden_in.astype(f32) + lax.psum_scatter(
        product(weighted, output_mat, 1, 0).astype(bf16), "head", scatter_dimension=0, tiled=True
    ).astype(f32)
    middle_inverse = rms_scale(middle)
    middle_normed = (middle * middle_inverse * expert_scale).astype(bf16)
    mine = me * per_device + jnp.arange(per_device, dtype=jnp.int32)
    my_router = lax.dynamic_slice_in_dim(router, me * per_device, per_device, axis=1)
    in_mat = expert_in.transpose(1, 0, 2).reshape(features, per_device * width)
    out_mat = expert_out.reshape(per_device * width, features)

    def turn(running, own):
        own_rows, own_cot, own_picks = own
        all_cot = lax.all_gather(own_cot, everywhere, axis=0, tiled=True)
        all_picks = lax.all_gather(own_picks, everywhere, axis=0, tiled=True)
        all_rows = lax.all_gather(own_rows, everywhere, axis=0, tiled=True)
        mask = jnp.any(all_picks[:, :, None] == mine[None, None, :], axis=1).astype(f32)
        gates = jax.nn.sigmoid(product(all_rows, my_router, 1, 0))
        live = gates * mask
        act, slope = gelu_pair(product(all_rows, in_mat, 1, 0).reshape(-1, per_device, width))
        lifted = product(all_cot, out_mat, 1, 1).reshape(-1, per_device, width)
        dense_grad = (jnp.sum(act * lifted, axis=-1) * live * (1.0 - gates)).astype(bf16)
        act_live = (act * live[:, :, None]).astype(bf16).reshape(-1, per_device * width)
        hidden_grad = (slope * lifted * live[:, :, None]).astype(bf16)
        hidden_grad = hidden_grad.reshape(-1, per_device * width)
        part_out = product(act_live, out_mat, 1, 0).astype(bf16)
        part_grad = (
            product(hidden_grad, in_mat, 1, 1) + product(dense_grad, my_router, 1, 1)
        ).astype(bf16)
        back = lax.psum_scatter(part_grad, everywhere, scatter_dimension=0, tiled=True)
        forth = lax.psum_scatter(part_out, everywhere, scatter_dimension=0, tiled=True)
        grads = (
            product(all_rows, hidden_grad, 0, 0),
            product(act_live, all_cot, 0, 0),
            product(dense_grad, all_rows, 0, 0),
        )
        if running is not None:
            grads = jax.tree.map(jnp.add, running, grads)
        return grads, (forth, back)

    turns = max(1, lax.axis_size("dp") * lax.axis_size("head") * tokens // whole_rows)
    owned = (middle_normed, cotangent, expert_pick)
    if turns == 1:
        grads, (summed, normed_grad) = turn(None, owned)
    else:
        owned = jax.tree.map(lambda a: a.reshape(turns, -1, a.shape[1]), owned)
        zeros = (
            jnp.zeros(in_mat.shape, f32),
            jnp.zeros(out_mat.shape, f32),
            jnp.zeros((per_device, features), f32),
        )
        grads, sums = lax.scan(turn, zeros, owned)
        summed, normed_grad = (a.reshape(tokens, features) for a in sums)
    grad_in = grads[0].reshape(features, per_device, width).transpose(1, 0, 2)
    grad_out = grads[1].reshape(per_device, width, features)
    grad_router = lax.all_gather(grads[2], everywhere, axis=0, tiled=True).T
    output = middle + summed.astype(f32)
    incoming = cotangent.astype(f32)
    row_grad, grad_gain_expert = norm_back(
        middle, middle_inverse, expert_scale, normed_grad.astype(f32)
    )
    middle_grad = incoming + row_grad
    group_grads = lax.all_gather(middle_grad.astype(bf16), "head", axis=0, tiled=True)
    weighted_grad = product(group_grads, output_mat, 1, 1).reshape(group, head_experts, head_width)
    output_grad = product(weighted, group_grads, 0, 0)
    output_gate_grad = jnp.sum(weighted_grad * attended[:, None, :], axis=-1)
    attended_grad = jnp.sum(weighted_grad * output_gates[:, :, None], axis=1).astype(bf16)
    prob_grad = product(attended_grad, values, 1, 1)
    centre = jnp.sum(probabilities * prob_grad, axis=-1, keepdims=True)
    score_grad = (probabilities * (prob_grad - centre)).astype(bf16)
    query_grad = product(score_grad, key_rows, 1, 0) * scale
    key_grad = product(score_grad, queries, 0, 0) * scale
    values_grad = product(probabilities.astype(bf16), attended_grad, 0, 0)
    expert_grad = (value_gates[:, :, None] * values_grad[:, None, :]).reshape(group, -1).astype(bf16)
    value_gate_grad = jnp.sum(expert_values * values_grad[:, None, :], axis=-1)
    query_grad = rotate(query_grad, cosine, -sine).astype(bf16)
    key_grad = rotate(key_grad, cosine, -sine).astype(bf16)
    logit_grad = (
        jnp.concatenate([value_gate_grad * value_mask, output_gate_grad * output_mask], axis=1)
        * squash
        * (1.0 - squash)
    ).astype(bf16)
    head_grads = (
        product(normed, query_grad, 0, 0),
        product(normed, key_grad, 0, 0),
        product(rows, expert_grad, 0, 0),
        output_grad,
        product(normed, logit_grad, 0, 0),
    )
    head_grads = tuple(grad.astype(bf16) for grad in head_grads)
    head_grads = tuple(grad.astype(f32)[None] for grad in lax.psum(head_grads, "dp"))
    back = (
        product(query_grad, query_mat, 1, 1)
        + product(key_grad, key_mat, 1, 1)
        + product(logit_grad, gate_mat, 1, 1)
    )
    row_back, grad_attend = norm_back(grouped, inverse, attend_scale, back)
    partial = (row_back + product(expert_grad, value_mat, 1, 1)).astype(bf16)
    input_grad = middle_grad + lax.psum_scatter(
        partial, "head", scatter_dimension=0, tiled=True
    ).astype(f32)
    grad_attend, grad_gain_expert = lax.psum((grad_attend, grad_gain_expert), everywhere)
    return (
        output,
        input_grad,
        grad_attend,
        *head_grads,
        grad_gain_expert,
        grad_router,
        grad_in,
        grad_out,
    )


MESH = pl.DeviceIdType.MESH
VM = pl.BlockSpec(memory_space=pltpu.VMEM)
ANY = pl.BlockSpec(memory_space=pl.ANY)
NN = (((1,), (0,)), ((), ()))
NT = (((1,), (1,)), ((), ()))
TN = (((0,), (0,)), ((), ()))


def dot(left, right, dims=NN):
    return lax.dot_general(left, right, dims, preferred_element_type=f32)


def at_block(block, count):
    return pl.ds(pl.multiple_of(block * count, count), count)


def remote(src, dst, send, recv, where):
    return pltpu.make_async_remote_copy(
        src_ref=src, dst_ref=dst, send_sem=send, recv_sem=recv, device_id=where, device_id_type=MESH
    )


def swap_halves(value):
    half = value.shape[-1] // 2
    return jnp.concatenate([value[:, half:], value[:, :half]], axis=-1)


def ceil_to(number, step):
    return -(-number // step) * step


def layer_kernel(
    n_dp,
    n_head,
    x_ref,
    cot_ref,
    pick_ref,
    head_pick_ref,
    seg_ref,
    gain_ref,
    cos_ref,
    sin_ref,
    wq_ref,
    wk_ref,
    wg_ref,
    wv_ref,
    wo_ref,
    router_ref,
    in_ref,
    out_ref,
    output_ref,
    grad_x_ref,
    wide_ref,
    fin_in_ref,
    fin_out_ref,
    picks,
    head_picks,
    seg,
    gains,
    cosine,
    sine,
    w_an,
    w_v,
    w_o,
    my_router,
    w_in,
    w_out,
    rows,
    cot,
    mrs,
    das,
    turned,
    rows_t,
    inverses,
    my_mask,
    all_mask,
    gate_mask,
    q,
    k,
    v,
    vx,
    squash,
    att,
    middle,
    part,
    got,
    outs,
    got_out,
    lifted,
    core_out,
    acts,
    hids,
    dzs,
    datt,
    gate_grads,
    probs,
    scores,
    qkz,
    vgrads,
    gain_part,
    gain_got,
    sums,
    core_got,
    chip_got,
    piece,
    blocks,
    hop_in,
    hop_out,
    local_sem,
    z_send,
    z_recv,
    w_send,
    w_recv,
    c_send,
    c_recv,
    e_send,
    e_recv,
    s_send,
    s_recv,
    ready,
    free,
):
    xor = jnp.bitwise_xor
    d, h = lax.axis_index("dp"), lax.axis_index("head")
    chip, core = d // 2, d % 2
    chips = n_dp // 2
    tokens, features = x_ref.shape
    per_device, _, width = in_ref.shape
    slab = per_device * width
    wide = 2 * slab
    experts = wv_ref.shape[1] // width
    named = ceil_to(n_dp * per_device, 8)
    group = tokens * n_head
    pair = 2 * tokens
    column = 256
    lanes = 128
    scale = width ** (-0.5)
    peers = (2, 3, 1)
    partner = (chip * 2 + 1 - core, h)
    own_block = at_block(h, tokens)
    own_side, other_side = at_block(core, slab), at_block(1 - core, slab)
    halves_in = (pl.ds(0, features // 2), pl.ds(features // 2, features // 2))
    halves_out = lambda side: (
        at_block(2 * side, slab // 2),
        at_block(2 * side + 1, slab // 2),
    )

    def along(step):
        return (d, xor(h, step))

    def across(step):
        return (xor(chip, step) * 2 + core, h)

    loads = []

    def load(src, dst):
        copy = pltpu.make_async_copy(src, dst, local_sem.at[len(loads)])
        copy.start()
        loads.append(copy)
        return copy

    own_weights = [load(out_ref, w_out.at[chip, own_side, :])] + [
        load(in_ref.at[e], w_in.at[chip, :, at_block(core * per_device + e, width)])
        for e in range(per_device)
    ]
    for_rows = [
        load(x_ref, rows.at[own_block, :]),
        load(gain_ref, gains),
        load(wg_ref, w_an.at[:, pl.ds(2 * width, width)]),
        load(wq_ref, w_an.at[:, pl.ds(0, width)]),
        load(wk_ref, w_an.at[:, pl.ds(width, width)]),
        load(wv_ref, w_v),
        load(head_pick_ref, head_picks),
        load(cos_ref, cosine),
        load(sin_ref, sine),
    ]
    for_scores = [load(seg_ref, seg), load(wo_ref, w_o)]
    for_mask = load(pick_ref, picks)
    for_cot = load(cot_ref, cot.at[own_block, :])
    for_router = load(router_ref, turned.at[:, pl.ds(0, lanes)])

    barrier = pltpu.get_barrier_semaphore()
    friends = [along(s) for s in peers] + [partner] + [across(s) for s in range(1, chips)]
    for friend in friends:
        pl.semaphore_signal(barrier, inc=1, device_id=friend, device_id_type=MESH)
    pl.semaphore_wait(barrier, len(friends))

    def spread(kind, src, dst, steps=peers):
        copies = {}
        for step in steps:
            copies[step] = remote(
                src(step), dst(step), z_send.at[kind, step - 1], z_recv.at[kind, step - 1], along(step)
            )
            copies[step].start()
        return copies

    x_copies = spread(0, lambda s: x_ref, lambda s: rows.at[own_block, :])

    def slot(array, place, side, half=None):
        if array == 0:
            at = halves_out(side)[half] if half is not None else at_block(side, slab)
            return w_out.at[place, at, :]
        at = halves_in[half] if half is not None else pl.ds(0, features)
        return w_in.at[place, at, at_block(side, slab)]

    def weights(number, ref, where):
        copy = remote(ref, ref, w_send.at[number], w_recv.at[number], where)
        copy.start()
        return copy

    slabs, halves_on, to_core, diagonal = {}, {}, {}, {}
    for copy in own_weights:
        copy.wait()
    for array in range(2):
        for first in range(2):
            for bit in (1, 2):
                half = bit - 1 if first == 0 else 2 - bit
                number = ((bit - 1) * 2 + half) * 2 + array
                slabs[bit, half, array] = weights(
                    number, slot(array, chip, core, half), across(bit)
                )
        to_core[0, array] = weights(12 + array, slot(array, chip, core), partner)

    for_mask.wait()
    lane = lax.broadcasted_iota(jnp.int32, (tokens, lanes), 1)
    for plane in range(n_head):
        expert = (lane // per_device * n_head + plane) * per_device + lane % per_device
        expert = jnp.where(lane < n_dp * per_device, expert, -1)
        hit = picks[:, 0:1] == expert
        for c in range(1, picks.shape[1]):
            hit = hit | (picks[:, c : c + 1] == expert)
        my_mask[plane] = jnp.where(hit, 1.0, 0.0).astype(bf16)
    mask_copies = spread(1, lambda s: my_mask.at[xor(h, s)], lambda s: all_mask.at[own_block, :])
    all_mask[own_block, :] = my_mask[h]

    for copy in for_rows:
        copy.wait()
    attend_gain = gains[0:1, :]
    expert_gain = gains[1:2, :]
    lane = lax.broadcasted_iota(jnp.int32, (group, width), 1)
    hit = lane == head_picks[:, 0:1]
    for c in range(1, head_picks.shape[1]):
        hit = hit | (lane == head_picks[:, c : c + 1])
    gate_mask[...] = jnp.where(hit, 1.0, 0.0)

    def project(block):
        at = at_block(block, tokens)
        own = rows[at, :]
        full = own.astype(f32)
        inverse = lax.rsqrt(jnp.mean(full * full, axis=-1, keepdims=True) + epsilon)
        inverses[at, :] = jnp.broadcast_to(inverse, (tokens, width))
        unit = (full * inverse * attend_gain).astype(bf16)
        qkg = dot(unit, w_an[...])
        c, s = cosine[at, :], sine[at, :]
        one, two = qkg[:, :width], qkg[:, width : 2 * width]
        q[at, :] = (one * c + swap_halves(one) * s).astype(bf16)
        k[at, :] = (two * c + swap_halves(two) * s).astype(bf16)
        squashed = jax.nn.sigmoid(qkg[:, 2 * width :])
        squash[at, :] = squashed
        gates = squashed * gate_mask[at, :]
        values = dot(own, w_v[...])
        vx[at, :] = values.astype(bf16)
        value = gates[:, 0:1] * values[:, :width]
        for e in range(1, experts):
            value += gates[:, e : e + 1] * values[:, e * width : (e + 1) * width]
        v[at, :] = value.astype(bf16)

    project(h)
    for step in (1, 2, 3):
        x_copies[step].wait_recv()
        project(xor(h, step))
    cot_copies = spread(2, lambda s: cot_ref, lambda s: cot.at[own_block, :])
    for half in range(2):
        for array in range(2):
            slabs[1 + half, half, array].wait_recv()
            halves_on[half, array] = weights(
                8 + 2 * half + array,
                slot(array, xor(chip, 1 + half), core, half),
                across(2 - half),
            )

    for copy in for_scores:
        copy.wait()
    seg_col = gate_grads
    seg_col[...] = jnp.broadcast_to(seg[...].astype(f32), (lanes, group)).T

    def attend(block):
        at = at_block(block, tokens)
        score = dot(q[at, :], k[...], NT) * scale
        row = block * tokens + lax.broadcasted_iota(jnp.int32, (tokens, group), 0)
        place = lax.broadcasted_iota(jnp.int32, (tokens, group), 1)
        allowed = (place <= row) & (seg_col[at, 0:1] == seg[...].astype(f32))
        score = jnp.where(allowed, score, negative)
        exponents = jnp.exp(score - jnp.max(score, axis=-1, keepdims=True))
        chance = exponents / jnp.sum(exponents, axis=-1, keepdims=True)
        probs[at, :] = chance.astype(bf16)
        attended = dot(chance.astype(bf16), v[...])
        att[at, :] = attended
        gates = squash[at, :] * gate_mask[at, :]
        weighted = jnp.concatenate(
            [
                (gates[:, experts + e : experts + e + 1] * attended).astype(bf16)
                for e in range(experts)
            ],
            axis=-1,
        )
        return dot(weighted, w_o[...])

    def send_part(kind, step):
        copy = remote(
            part.at[at_block(xor(h, step), tokens), :],
            got.at[step - 1],
            z_send.at[kind, step - 1],
            z_recv.at[kind, step - 1],
            along(step),
        )
        copy.start()
        return copy

    back = {}
    for step in peers:
        part[at_block(xor(h, step), tokens), :] = attend(xor(h, step)).astype(bf16)
        back[step] = send_part(3, step)
    mid = rows[own_block, :].astype(f32) + attend(h)

    for bit in (1, 2):
        slabs[bit, 2 - bit, 0].wait_recv()
        to_core[bit, 0] = weights(14 + (bit - 1) * 2, slot(0, xor(chip, bit), core), partner)
        slabs[bit, 2 - bit, 1].wait_recv()
        to_core[bit, 1] = weights(15 + (bit - 1) * 2, slot(1, xor(chip, bit), core), partner)
    for_router.wait()
    slot_of = lax.broadcasted_iota(jnp.int32, (lanes, lanes), 1)
    name = lax.broadcasted_iota(jnp.int32, (lanes, lanes), 0)
    expert = (slot_of // per_device * n_head + h) * per_device + slot_of % per_device
    expert = jnp.where(slot_of < n_dp * per_device, expert, -1)
    my_router[...] = dot(turned[:, pl.ds(0, lanes)], jnp.where(name == expert, 1.0, 0.0).astype(bf16)).astype(bf16)

    for step in peers:
        back[step].wait()
        mid += got[step - 1].astype(f32)
    middle[...] = mid
    inverse = lax.rsqrt(jnp.mean(mid * mid, axis=-1, keepdims=True) + epsilon)
    mrs[own_block, :] = (mid * inverse * expert_gain).astype(bf16)
    mr_copies = spread(4, lambda s: mrs.at[own_block, :], lambda s: mrs.at[own_block, :], (1, 2, 3))

    for array in range(2):
        for half in range(2):
            halves_on[half, array].wait_recv()
            diagonal[half, array] = weights(
                18 + 2 * half + array, slot(array, xor(chip, 3), core, half), partner
            )
    for_cot.wait()
    for step in peers:
        cot_copies[step].wait()
        x_copies[step].wait_send()
        mask_copies[step].wait()

    def weights_here(array):
        for bit in range(3):
            to_core[bit, array].wait()
        for half in range(2):
            diagonal[half, array].wait()
            halves_on[half, array].wait_send()
            for bit in (1, 2):
                slabs[bit, half, array].wait_send()

    weights_here(0)

    @pl.loop(0, chips)
    def _(j):
        lift = dot(cot[...], w_out[j], NT)
        lifted[j, 0] = lift[:, :slab].astype(bf16)
        lifted[j, 1] = lift[:, slab:].astype(bf16)

    weights_here(1)

    def spread_lanes(j):
        lane = lax.broadcasted_iota(jnp.int32, (lanes, wide), 1) // width
        slot = lax.broadcasted_iota(jnp.int32, (lanes, wide), 0)
        return jnp.where(slot == lane + j * (wide // width), 1.0, 0.0).astype(bf16)

    def pair_of_blocks(number):
        at = at_block(number, pair)
        own = mrs[at, :]
        gates = jax.nn.sigmoid(dot(own, my_router[...]))
        live = gates * all_mask[at, :].astype(f32)
        high = live.astype(bf16)
        low = (live - high.astype(f32)).astype(bf16)
        both = jnp.concatenate([high, low], axis=-1)

        def chip_step(j, total):
            pick = spread_lanes(j)
            hidden = dot(own, w_in[j])
            gate = dot(both, jnp.concatenate([pick, pick], axis=0))
            lift = jnp.concatenate([lifted[j, 0, at, :], lifted[j, 1, at, :]], axis=-1).astype(f32)
            square = hidden * hidden
            inner = jnp.tanh(0.7978845608028654 * hidden * (1.0 + 0.044715 * square))
            half = 0.5 * (1.0 + inner)
            act = hidden * half
            slope = half + act * (1.0 - inner) * (
                0.7978845608028654 + (0.7978845608028654 * 3.0 * 0.044715) * square
            )
            acts[j, at, :] = (act * gate).astype(bf16)
            hids[j, at, :] = (slope * (lift * gate)).astype(bf16)
            return total + dot((act * lift).astype(bf16), pick, NT)

        total = lax.fori_loop(0, chips, chip_step, jnp.zeros((pair, lanes), f32))
        dz = (total * live * (1.0 - gates)).astype(bf16)
        dzs[at, :] = dz

        @pl.loop(0, features // column)
        def _(c):
            part_of = at_block(c, column)
            total = dot(dz, my_router[part_of, :], NT)
            for j in range(chips):
                total += dot(hids[j, at, :], w_in[j, part_of, :], NT)
            part[at, part_of] = total.astype(bf16)

    near = h // 2
    mr_copies[1].wait_recv()
    pair_of_blocks(near)
    back = {1: send_part(5, 1)}
    mr_copies[2].wait_recv()
    mr_copies[3].wait_recv()
    pair_of_blocks(1 - near)
    back[2], back[3] = send_part(5, 2), send_part(5, 3)
    pl.semaphore_signal(ready, inc=1, device_id=partner, device_id_type=MESH)

    @pl.loop(0, features // column)
    def _(c):
        part_of = at_block(c, column)
        total = dot(acts[0], w_out[0, :, part_of])
        for j in range(1, chips):
            total += dot(acts[j], w_out[j, :, part_of])
        outs[:, part_of] = total.astype(bf16)

    turned[...] = mrs[...].T

    def expert_grads(place, at):
        for half in halves_in:
            w_in[place, half, at] = dot(turned[half, :], hids[place, :, at]).astype(bf16)
            w_out[place, at, half] = dot(acts[place, :, at], cot[:, half], TN).astype(bf16)

    def to_other_core(n):
        place = xor(chip, chips - 1 - n)
        copies = [
            remote(
                w_in.at[place, halves_in[half], other_side],
                lifted.at[place, half],
                c_send.at[half, n],
                c_recv.at[half, n],
                partner,
            )
            for half in range(2)
        ]
        copies.append(
            remote(
                w_out.at[place, other_side, :],
                core_out.at[place],
                c_send.at[2, n],
                c_recv.at[2, n],
                partner,
            )
        )
        return copies

    pl.semaphore_wait(ready, 1)

    @pl.loop(0, chips)
    def _(n):
        expert_grads(xor(chip, chips - 1 - n), other_side)
        for copy in to_other_core(n):
            copy.start()

    @pl.loop(0, chips)
    def _(n):
        expert_grads(xor(chip, chips - 1 - n), own_side)

    hops = {}

    def hop(half, index, place, toward):
        copies = (
            remote(
                slot(1, place, core, half),
                hop_in.at[half, index],
                e_send.at[0, 2 * half + index],
                e_recv.at[0, 2 * half + index],
                across(toward),
            ),
            remote(
                slot(0, place, core, half),
                hop_out.at[half, index],
                e_send.at[1, 2 * half + index],
                e_recv.at[1, 2 * half + index],
                across(toward),
            ),
        )
        for copy in copies:
            copy.start()
        hops[half, index] = copies

    for n in range(chips):
        s = chips - 1 - n
        place = xor(chip, s)
        for copy in to_other_core(n):
            copy.wait()
        for half in range(2):
            here = (place, halves_in[half], own_side)
            w_in[here] = w_in[here] + lifted[place, half]
        w_out[place, own_side, :] = w_out[place, own_side, :] + core_out[place]
        if s == 3:
            hop(0, 1, place, 1)
            hop(1, 1, place, 2)
        elif s:
            hop(s - 1, 0, place, s)

    side = features // 2
    strip = side // chips

    def section(number, first, count):
        at = pl.ds(first, count)
        col = lambda c, j: at_block(c * chips + j, strip)
        state = {}

        def sem(n):
            return s_send.at[number, n], s_recv.at[number, n]

        def start():
            state["core"] = remote(
                sums.at[at, at_block(1 - core, side)], core_got.at[at, :], *sem(0), partner
            )
            state["core"].start()

        def mid():
            state["core"].wait()
            half = at_block(core, side)
            sums[at, half] = sums[at, half] + core_got[at, :]
            state["chips"] = []
            for s in range(1, chips):
                copy = remote(
                    sums.at[at, col(core, xor(chip, s))], chip_got.at[s - 1, at, :], *sem(s), across(s)
                )
                copy.start()
                state["chips"].append(copy)

        def add():
            for copy in state["chips"]:
                copy.wait()
            total = sums[at, col(core, chip)].astype(f32)
            for s in range(1, chips):
                total += chip_got[s - 1, at, :].astype(f32)
            piece[at, :] = total.astype(bf16)

        def share(src=None, rows_to=at):
            src = piece.at[at, :] if src is None else src
            state["rows"] = rows_to
            here = wide_ref.at[rows_to, col(core, chip)]
            state["share"] = []
            for s in range(1, chips):
                copy = remote(src, here, *sem(chips + s), across(s))
                copy.start()
                state["share"].append(copy)
            over = remote(src, here, *sem(chips), partner)
            own = pltpu.make_async_copy(src, here, s_send.at[number, 3 * chips - 1])
            over.start()
            own.start()
            state["wait"] = [over, own]

        def forward():
            for s in range(1, chips):
                state["share"][s - 1].wait()
                here = wide_ref.at[state["rows"], col(core, xor(chip, s))]
                copy = remote(here, here, *sem(2 * chips - 1 + s), partner)
                copy.start()
                state["wait"].append(copy)

        def end():
            for copy in state["wait"]:
                copy.wait()

        return start, mid, add, share, forward, end

    top = features + w_o.shape[0]
    small = ceil_to(named + 1, 16)
    of_o = section(0, features, w_o.shape[0])
    of_d = section(1, 0, features)
    of_g = section(2, top + 16, small)
    of_a = section(3, top, 16)
    router_part = dot(dzs[...], mrs[...], TN)[:named]

    incoming = part[own_block, :].astype(f32)
    for step in (1, 2, 3):
        back[step].wait()
        incoming += got[step - 1].astype(f32)
    mid = middle[...]
    inverse = lax.rsqrt(jnp.mean(mid * mid, axis=-1, keepdims=True) + epsilon)
    unit = mid * inverse
    scaled = incoming * expert_gain
    dmid = cot[own_block, :].astype(f32) + inverse * (
        scaled - unit * jnp.mean(scaled * unit, axis=-1, keepdims=True)
    )
    grad_x_ref[...] = dmid
    das[own_block, :] = dmid.astype(bf16)
    da_copies = spread(6, lambda s: das.at[own_block, :], lambda s: das.at[own_block, :])
    sums[pl.ds(top + 16, small), :] = jnp.concatenate(
        [
            router_part,
            jnp.sum(incoming * unit, axis=0, keepdims=True),
            jnp.zeros((small - named - 1, features), f32),
        ],
        axis=0,
    ).astype(bf16)
    of_g[0]()
    for block in range(n_head):
        at = pl.ds(block * tokens, tokens)
        unit = rows[at, :].astype(f32) * inverses[at, 0:1] * attend_gain
        turned[:, at] = unit.astype(bf16).T
    rows_t[...] = rows[...].T
    of_g[1]()

    lane = lax.broadcasted_iota(jnp.int32, (tokens, width), 1)

    def through_output(block):
        at = at_block(block, tokens)
        all_five = dot(das[at, :], w_o[...], NT)
        gates = squash[at, :] * gate_mask[at, :]
        attended = att[at, :]
        total = jnp.zeros((tokens, width), f32)
        gate = jnp.zeros((tokens, width), f32)
        for e in range(experts):
            one = all_five[:, e * width : (e + 1) * width]
            total += gates[:, experts + e : experts + e + 1] * one
            gate = jnp.where(
                lane == experts + e, jnp.sum(one * attended, axis=-1, keepdims=True), gate
            )
        datt[at, :] = total.astype(bf16)
        gate_grads[at, :] = gate

    through_output(h)
    for step in (1, 2, 3):
        da_copies[step].wait_recv()
        through_output(xor(h, step))
    out_copies = spread(
        7, lambda s: outs.at[at_block(xor(h, s), tokens), :], lambda s: got_out.at[s - 1]
    )

    gates = squash[...] * gate_mask[...]
    for e in range(experts):
        one = (gates[:, experts + e : experts + e + 1] * att[...]).astype(bf16)
        sums[pl.ds(features + e * width, width), :] = dot(one, das[...], TN).astype(bf16)
    of_o[0]()

    @pl.loop(0, n_head)
    def _(block):
        at = at_block(block, tokens)
        chance = probs[at, :].astype(f32)
        dprob = dot(datt[at, :], v[...], NT)
        centre = jnp.sum(chance * dprob, axis=-1, keepdims=True)
        scores[at, :] = (chance * (dprob - centre)).astype(bf16)

    dq = dot(scores[...], k[...]) * scale
    dk = dot(scores[...], q[...], TN) * scale
    dv = dot(probs[...], datt[...], TN)
    of_o[1]()
    qkz[:, pl.ds(0, width)] = (dq * cosine[...] - swap_halves(dq) * sine[...]).astype(bf16)
    qkz[:, pl.ds(width, width)] = (dk * cosine[...] - swap_halves(dk) * sine[...]).astype(bf16)
    gate = gate_grads[...]
    lane = lax.broadcasted_iota(jnp.int32, (group, width), 1)
    for e in range(experts):
        vgrads[:, pl.ds(e * width, width)] = (gates[:, e : e + 1] * dv).astype(bf16)
        one = jnp.sum(vx[:, pl.ds(e * width, width)].astype(f32) * dv, axis=-1, keepdims=True)
        gate = jnp.where(lane == e, one, gate)
    qkz[:, pl.ds(2 * width, width)] = (gate * gates * (1.0 - squash[...])).astype(bf16)

    @pl.loop(0, features // column)
    def _(c):
        at = at_block(c, column)
        sums[at, pl.ds(0, 3 * width)] = dot(turned[at, :], qkz[...]).astype(bf16)
        sums[at, pl.ds(3 * width, experts * width)] = dot(rows_t[at, :], vgrads[...]).astype(bf16)

    of_d[0]()

    def into_rows(block):
        at = at_block(block, tokens)
        inverse = inverses[at, 0:1]
        unit = rows[at, :].astype(f32) * inverse
        through = dot(qkz[at, :], w_an[...], NT)
        scaled = through * attend_gain
        total = inverse * (
            scaled - unit * jnp.mean(scaled * unit, axis=-1, keepdims=True)
        ) + dot(vgrads[at, :], w_v[...], NT)
        return total, jnp.sum(through * unit, axis=0, keepdims=True)

    gain = jnp.zeros((1, features), f32)
    for step in peers:
        total, one = into_rows(xor(h, step))
        gain += one
        part[at_block(xor(h, step), tokens), :] = total.astype(bf16)
        back[step] = send_part(8, step)
    total, one = into_rows(h)
    gain_part[...] = jnp.broadcast_to(gain + one, gain_part.shape)
    gain_copies = spread(9, lambda s: gain_part, lambda s: gain_got.at[s - 1])
    grad_x_ref[...] += total
    of_d[1]()
    of_g[2]()

    small_block = at_block(h, small)
    blocks[small_block, :] = piece[pl.ds(top + 16, small), :]
    g_copies = spread(10, lambda s: blocks.at[small_block, :], lambda s: blocks.at[small_block, :])
    of_o[2]()
    of_o[3]()

    lasts = {}
    for half in range(2):
        toward = 2 - half
        for index, place in ((1, xor(chip, toward)), (0, chip)):
            for copy in hops[half, index]:
                copy.wait()
            at_in = (place, halves_in[half], own_side)
            at_out = (place, halves_out(core)[half], slice(None))
            w_in[at_in] = w_in[at_in] + hop_in[half, index]
            w_out[at_out] = w_out[at_out] + hop_out[half, index]
            if index:
                pl.semaphore_signal(
                    free.at[half], inc=1, device_id=across(toward), device_id_type=MESH
                )
                pl.semaphore_wait(free.at[half], 1)
                lasts[half] = (
                    remote(
                        w_in.at[at_in],
                        hop_in.at[half, 1],
                        e_send.at[0, 4 + half],
                        e_recv.at[0, 4 + half],
                        across(toward),
                    ),
                    remote(
                        w_out.at[at_out],
                        hop_out.at[half, 1],
                        e_send.at[1, 4 + half],
                        e_recv.at[1, 4 + half],
                        across(toward),
                    ),
                )
                for copy in lasts[half]:
                    copy.start()

    gain = gain_part[...]
    for step in peers:
        gain_copies[step].wait()
        gain += gain_got[step - 1]
    sums[pl.ds(top, 16), :] = jnp.concatenate([gain, gain], axis=0).astype(bf16)
    of_a[0]()
    for step in peers:
        g_copies[step].wait()
    of_g[3](blocks, pl.ds(top + 16, n_head * small))
    of_a[1]()

    output = middle[...] + outs[own_block, :].astype(f32)
    for step in peers:
        out_copies[step].wait()
        output += got_out[step - 1].astype(f32)
    output_ref[...] = output
    of_d[2]()
    of_d[3]()
    of_a[2]()
    of_a[3]()
    of_o[4]()
    of_g[4]()
    for step in peers:
        back[step].wait()
        grad_x_ref[...] += got[step - 1].astype(f32)
    for half in range(2):
        for copy in lasts[half]:
            copy.wait()
        at_in = (chip, halves_in[half], own_side)
        at_out = (chip, halves_out(core)[half], slice(None))
        w_in[at_in] = w_in[at_in] + hop_in[half, 1]
        w_out[at_out] = w_out[at_out] + hop_out[half, 1]
    stores = (
        pltpu.make_async_copy(w_in.at[chip, :, own_side], fin_in_ref, local_sem.at[0]),
        pltpu.make_async_copy(w_out.at[chip, own_side, :], fin_out_ref, local_sem.at[1]),
    )
    for store in stores:
        store.start()
    of_d[4]()
    of_a[4]()
    for one in (of_o, of_g, of_d, of_a):
        one[5]()
    for store in stores:
        store.wait()
    for step in peers:
        mr_copies[step].wait_send()
        da_copies[step].wait_send()


def layer_call(n_dp, n_head, args):
    x, picks, router, value_mat, expert_in = args[0], args[2], args[13], args[11], args[14]
    tokens, features = x.shape
    per_device, _, width = expert_in.shape
    held_experts = value_mat.shape[1]
    group = tokens * n_head
    chips = n_dp // 2
    slab = per_device * width
    lanes = 128
    peers = n_head - 1
    named = ceil_to(n_dp * per_device, 8)
    small = ceil_to(named + 1, 16)
    top = features + held_experts
    held = top + 16 + small
    strip = features // n_dp
    shape = jax.ShapeDtypeStruct
    vm, dma = pltpu.VMEM, pltpu.SemaphoreType.DMA
    outs = [
        (shape((tokens, features), f32), VM),
        (shape((tokens, features), f32), VM),
        (shape((top + 16 + n_head * small, features), bf16), ANY),
        (shape((features, slab), bf16), ANY),
        (shape((slab, features), bf16), ANY),
    ]
    scratch = dict(
        picks=vm(picks.shape, jnp.int32),
        head_picks=vm(args[3].shape, jnp.int32),
        seg=vm((1, group), jnp.int32),
        gains=vm(args[5].shape, f32),
        cosine=vm((group, width), f32),
        sine=vm((group, width), f32),
        w_an=vm((features, 3 * width), bf16),
        w_v=vm((features, held_experts), bf16),
        w_o=vm((held_experts, features), bf16),
        my_router=vm((features, lanes), bf16),
        w_in=vm((chips, features, 2 * slab), bf16),
        w_out=vm((chips, 2 * slab, features), bf16),
        rows=vm((group, features), bf16),
        cot=vm((group, features), bf16),
        mrs=vm((group, features), bf16),
        das=vm((group, features), bf16),
        turned=vm((features, group), bf16),
        rows_t=vm((features, group), bf16),
        inverses=vm((group, width), f32),
        my_mask=vm((n_head, tokens, lanes), bf16),
        all_mask=vm((group, lanes), bf16),
        gate_mask=vm((group, width), f32),
        q=vm((group, width), bf16),
        k=vm((group, width), bf16),
        v=vm((group, width), bf16),
        vx=vm((group, held_experts), bf16),
        squash=vm((group, width), f32),
        att=vm((group, width), f32),
        middle=vm((tokens, features), f32),
        part=vm((group, features), bf16),
        got=vm((peers, tokens, features), bf16),
        outs=vm((group, features), bf16),
        got_out=vm((peers, tokens, features), bf16),
        lifted=vm((chips, 2, group, slab), bf16),
        core_out=vm((chips, slab, features), bf16),
        acts=vm((chips, group, 2 * slab), bf16),
        hids=vm((chips, group, 2 * slab), bf16),
        dzs=vm((group, lanes), bf16),
        datt=vm((group, width), bf16),
        gate_grads=vm((group, width), f32),
        probs=vm((group, group), bf16),
        scores=vm((group, group), bf16),
        qkz=vm((group, 3 * width), bf16),
        vgrads=vm((group, held_experts), bf16),
        gain_part=vm((8, features), f32),
        gain_got=vm((peers, 8, features), f32),
        sums=vm((held, features), bf16),
        core_got=vm((held, features // 2), bf16),
        chip_got=vm((chips - 1, held, strip), bf16),
        piece=vm((held, strip), bf16),
        blocks=vm((n_head * small, strip), bf16),
        hop_in=vm((2, 2, features // 2, slab), bf16),
        hop_out=vm((2, 2, slab // 2, features), bf16),
        local_sem=dma((15 + 1 + per_device,)),
        z_send=dma((11, peers)),
        z_recv=dma((11, peers)),
        w_send=dma((22,)),
        w_recv=dma((22,)),
        c_send=dma((3, chips)),
        c_recv=dma((3, chips)),
        e_send=dma((2, 6)),
        e_recv=dma((2, 6)),
        s_send=dma((4, 3 * chips)),
        s_recv=dma((4, 3 * chips)),
        ready=pltpu.SemaphoreType.REGULAR,
        free=pltpu.SemaphoreType.REGULAR((2,)),
    )
    return pl.pallas_call(
        functools.partial(layer_kernel, n_dp, n_head),
        out_shape=[o[0] for o in outs],
        out_specs=[o[1] for o in outs],
        in_specs=[ANY] * 16,
        scratch_shapes=list(scratch.values()),
        compiler_params=pltpu.CompilerParams(
            collective_id=1, has_side_effects=True, vmem_limit_bytes=vmem_bytes
        ),
    )(*args)


def finish_kernel(
    n_dp,
    n_head,
    output_ref,
    grad_x_ref,
    wide_ref,
    in_ref,
    out_ref,
    final_ref,
    input_ref,
    attend_ref,
    query_ref,
    key_ref,
    value_ref,
    mix_ref,
    gate_ref,
    expert_ref,
    router_ref,
    grad_in_ref,
    grad_out_ref,
    wide,
    flat_in,
    flat_out,
    value,
    mix,
    grad_in,
    grad_out,
    sem,
):
    features, slab = in_ref.shape
    per_device, _, width = grad_in_ref.shape
    experts_total = router_ref.shape[1]
    gates = gate_ref.shape[1]
    top = features + mix_ref.shape[0]
    small = (wide_ref.shape[0] - top - 16) // n_head
    named = n_dp * per_device

    def copy(src, dst, number):
        one = pltpu.make_async_copy(src, dst, sem.at[number])
        one.start()
        return one

    rest = pl.ds(top, wide_ref.shape[0] - top)
    loads = [
        copy(wide_ref.at[pl.ds(0, features), :], wide.at[pl.ds(0, features), :], 0),
        copy(wide_ref.at[pl.ds(features, top - features), :], wide.at[pl.ds(features, top - features), :], 1),
        copy(in_ref, flat_in, 2),
        copy(out_ref, flat_out, 3),
        copy(wide_ref.at[rest, :], wide.at[rest, :], 4),
    ]
    stores = [copy(output_ref, final_ref, 5), copy(grad_x_ref, input_ref, 6)]
    loads[0].wait()
    first = pl.ds(0, features)
    value[...] = wide[first, pl.ds(3 * width, value.shape[1])].astype(f32)
    stores.append(copy(value, value_ref, 7))
    query_ref[...] = wide[first, pl.ds(0, width)].astype(f32)
    key_ref[...] = wide[first, pl.ds(width, width)].astype(f32)
    gate_ref[...] = wide[first, pl.ds(2 * width, width)][:, :gates].astype(f32)
    loads[1].wait()
    mix[...] = wide[pl.ds(features, top - features), :].astype(f32)
    stores.append(copy(mix, mix_ref, 8))
    loads[2].wait()
    for e in range(per_device):
        grad_in[e] = flat_in[:, pl.ds(e * width, width)].astype(f32)
    stores.append(copy(grad_in, grad_in_ref, 9))
    loads[3].wait()
    for e in range(per_device):
        grad_out[e] = flat_out[pl.ds(e * width, width), :].astype(f32)
    stores.append(copy(grad_out, grad_out_ref, 10))
    loads[4].wait()
    attend_ref[...] = wide[pl.ds(top, 16), :][0:1].astype(f32)
    planes = wide[pl.ds(top + 16, n_head * small), :]
    place = lax.broadcasted_iota(jnp.int32, (n_head * small, experts_total), 0)
    name = lax.broadcasted_iota(jnp.int32, (n_head * small, experts_total), 1)
    slot, plane = place % small, place // small
    expert = (slot // per_device * n_head + plane) * per_device + slot % per_device
    chosen = (slot < named) & (expert == name)
    router_ref[...] = dot(planes, jnp.where(chosen, 1.0, 0.0).astype(bf16), TN)
    gain = jnp.zeros((1, features), f32)
    for z in range(n_head):
        row = z * small + ceil_to(named, 8)
        gain += planes[row : row + 1].astype(f32)
    expert_ref[...] = gain
    for store in stores:
        store.wait()


def finish_call(n_dp, n_head, shapes, args):
    shape = jax.ShapeDtypeStruct
    wide, flat_in, flat_out = args[2], args[3], args[4]
    value, mix, grad_in, grad_out = shapes[5], shapes[6], shapes[10], shapes[11]
    specs = [VM] * 12
    for number in (0, 1, 5, 6, 10, 11):
        specs[number] = ANY
    return pl.pallas_call(
        functools.partial(finish_kernel, n_dp, n_head),
        out_shape=[shape(s, f32) for s in shapes],
        out_specs=specs,
        in_specs=[ANY] * 5,
        scratch_shapes=[
            pltpu.VMEM(wide.shape, bf16),
            pltpu.VMEM(flat_in.shape, bf16),
            pltpu.VMEM(flat_out.shape, bf16),
            pltpu.VMEM(value, f32),
            pltpu.VMEM(mix, f32),
            pltpu.VMEM(grad_in, f32),
            pltpu.VMEM(grad_out, f32),
            pltpu.SemaphoreType.DMA((11,)),
        ],
        compiler_params=pltpu.CompilerParams(vmem_limit_bytes=48 << 20),
    )(*args)


def kernel_body(
    n_dp,
    n_head,
    hidden_in,
    segments,
    value_pick,
    output_pick,
    expert_pick,
    attend_gain,
    query_weight,
    key_weight,
    value_weight,
    output_weight,
    head_router,
    expert_gain,
    router,
    expert_in,
    expert_out,
    cotangent,
):
    tokens, features = hidden_in.shape
    per_device, _, width = expert_in.shape
    experts = head_router.shape[2] // 2
    group = tokens * n_head
    angles = np.arange(group)[:, None] * theta ** (-2.0 * np.arange(width // 2) / width)[None, :]
    cosine = np.concatenate([np.cos(angles)] * 2, axis=1).astype(np.float32)
    sine = np.concatenate([-np.sin(angles), np.sin(angles)], axis=1).astype(np.float32)
    head_picks = jnp.concatenate([value_pick[:, 0], output_pick[:, 0] + experts], axis=1)
    gains = jnp.stack([attend_gain, expert_gain]).astype(f32)
    results = layer_call(
        n_dp,
        n_head,
        (
            hidden_in,
            cotangent,
            expert_pick,
            head_picks,
            segments[None, :],
            gains,
            cosine,
            sine,
            query_weight[0],
            key_weight[0],
            jnp.pad(head_router[0], ((0, 0), (0, width - 2 * experts))),
            value_weight[0],
            output_weight[0],
            jnp.pad(router, ((0, 0), (0, width - router.shape[1]))),
            expert_in,
            expert_out.reshape(per_device * width, features),
        ),
    )
    shapes = (
        (tokens, features),
        (tokens, features),
        (1, features),
        query_weight.shape[1:],
        key_weight.shape[1:],
        value_weight.shape[1:],
        output_weight.shape[1:],
        head_router.shape[1:],
        (1, features),
        router.shape,
        expert_in.shape,
        expert_out.shape,
    )
    done = list(finish_call(n_dp, n_head, shapes, results))
    for number in (3, 4, 5, 6, 7):
        done[number] = done[number][None]
    done[2], done[8] = done[2][0], done[8][0]
    return tuple(done)


def solution(mesh):
    rows = P(everywhere, None)
    heads = P("head", None, None)
    experts = P(everywhere, None, None)
    picks = P("dp", "head", None)
    in_specs = (
        rows, P("dp"), picks, picks, rows, P(), heads, heads, heads, heads, heads,
        P(), P(), experts, experts, rows,
    )
    out_specs = (
        rows, rows, P(), heads, heads, heads, heads, heads, P(), P(), experts, experts,
    )
    n_dp, n_head = mesh.shape["dp"], mesh.shape["head"]

    def program(*args):
        held = 2 * n_dp * args[13].shape[0] * args[13].shape[1] * args[13].shape[2] * 2
        if n_head == 4 and held <= vmem_for_weights:
            return kernel_body(n_dp, n_head, *args)
        return body(*args)

    return jax.shard_map(program, mesh=mesh, in_specs=in_specs, out_specs=out_specs, check_vma=False)
```

```python
import functools

import jax
import jax.numpy as jnp
import numpy as np
from jax import lax
from jax.experimental import pallas as pl
from jax.experimental.pallas import tpu as pltpu
from jax.sharding import PartitionSpec as P

epsilon = 1e-06
theta = 10000.0
negative = -1e30
f32 = jnp.float32
bf16 = jnp.bfloat16
everywhere = ("dp", "head")
whole_rows = 4096
vmem_for_weights = 16 << 20
vmem_bytes = 62 << 20


def product(left, right, left_axis, right_axis):
    return lax.dot_general(
        left, right, (((left_axis,), (right_axis,)), ((), ())), preferred_element_type=f32
    )


def rms_scale(residual):
    return lax.rsqrt(jnp.mean(residual * residual, axis=-1, keepdims=True) + epsilon)


def rotary_tables(row_count, head_width):
    half_width = head_width // 2
    position = jnp.arange(row_count, dtype=f32)[:, None]
    exponent = jnp.arange(half_width, dtype=f32)[None, :]
    angles = position * jnp.power(theta, -2.0 * exponent / head_width)
    return (jnp.cos(angles), jnp.sin(angles))


def rotate(matrix, cosine, sine):
    half = matrix.shape[-1] // 2
    first, second = matrix[:, :half], matrix[:, half:]
    return jnp.concatenate([first * cosine - second * sine, second * cosine + first * sine], axis=-1)


def pick_mask(picks, expert_count):
    hits = picks[:, 0, :, None] == jnp.arange(expert_count, dtype=jnp.int32)[None, None, :]
    return jnp.any(hits, axis=1).astype(f32)


def norm_back(residual, inverse, gain, incoming):
    unit_rows = residual * inverse
    scaled = incoming * gain
    gain_grad = jnp.sum(incoming * unit_rows, axis=0)
    row_grad = inverse * (scaled - unit_rows * jnp.mean(scaled * unit_rows, axis=-1, keepdims=True))
    return (row_grad, gain_grad)


def gelu_pair(value):
    inner = jnp.tanh(0.7978845608028654 * (value + 0.044715 * value * value * value))
    slope = 0.5 * (1.0 + inner) + 0.5 * value * (1.0 - inner * inner) * 0.7978845608028654 * (
        1.0 + 3.0 * 0.044715 * value * value
    )
    return (0.5 * value * (1.0 + inner), slope)


def body(
    hidden_in,
    segments,
    value_pick,
    output_pick,
    expert_pick,
    attend_gain,
    query_weight,
    key_weight,
    value_weight,
    output_weight,
    head_router,
    expert_gain,
    router,
    expert_in,
    expert_out,
    cotangent,
):
    tokens, features = hidden_in.shape
    per_device, _, width = expert_in.shape
    head_experts = head_router.shape[2] // 2
    head_width = query_weight.shape[2]
    scale = head_width ** (-0.5)
    query_mat, key_mat, value_mat = query_weight[0], key_weight[0], value_weight[0]
    output_mat, gate_mat = output_weight[0], head_router[0]
    value_mask = pick_mask(value_pick, head_experts)
    output_mask = pick_mask(output_pick, head_experts)
    attend_scale = attend_gain.astype(f32)
    expert_scale = expert_gain.astype(f32)
    me = lax.axis_index("dp") * lax.axis_size("head") + lax.axis_index("head")

    rows = lax.all_gather(hidden_in, "head", axis=0, tiled=True)
    grouped = rows.astype(f32)
    group = grouped.shape[0]
    inverse = rms_scale(grouped)
    normed = (grouped * inverse * attend_scale).astype(bf16)
    cosine, sine = rotary_tables(group, head_width)
    queries = rotate(product(normed, query_mat, 1, 0), cosine, sine).astype(bf16)
    key_rows = rotate(product(normed, key_mat, 1, 0), cosine, sine).astype(bf16)
    squash = jax.nn.sigmoid(product(normed, gate_mat, 1, 0))
    value_gates = squash[:, :head_experts] * value_mask
    output_gates = squash[:, head_experts:] * output_mask
    expert_values = product(rows, value_mat, 1, 0).reshape(group, head_experts, head_width)
    values = jnp.sum(expert_values * value_gates[:, :, None], axis=1).astype(bf16)
    places = jnp.arange(group, dtype=jnp.int32)
    allowed = (places[None, :] <= places[:, None]) & (segments[:, None] == segments[None, :])
    scores = jnp.where(allowed, product(queries, key_rows, 1, 1) * scale, negative)
    exponents = jnp.exp(scores - jnp.max(scores, axis=-1, keepdims=True))
    probabilities = exponents / jnp.sum(exponents, axis=-1, keepdims=True)
    attended = product(probabilities.astype(bf16), values, 1, 0)
    weighted = (
        (output_gates[:, :, None] * attended[:, None, :]).reshape(group, -1).astype(bf16)
    )
    middle = hidden_in.astype(f32) + lax.psum_scatter(
        product(weighted, output_mat, 1, 0).astype(bf16), "head", scatter_dimension=0, tiled=True
    ).astype(f32)
    middle_inverse = rms_scale(middle)
    middle_normed = (middle * middle_inverse * expert_scale).astype(bf16)
    mine = me * per_device + jnp.arange(per_device, dtype=jnp.int32)
    my_router = lax.dynamic_slice_in_dim(router, me * per_device, per_device, axis=1)
    in_mat = expert_in.transpose(1, 0, 2).reshape(features, per_device * width)
    out_mat = expert_out.reshape(per_device * width, features)

    def turn(running, own):
        own_rows, own_cot, own_picks = own
        all_cot = lax.all_gather(own_cot, everywhere, axis=0, tiled=True)
        all_picks = lax.all_gather(own_picks, everywhere, axis=0, tiled=True)
        all_rows = lax.all_gather(own_rows, everywhere, axis=0, tiled=True)
        mask = jnp.any(all_picks[:, :, None] == mine[None, None, :], axis=1).astype(f32)
        gates = jax.nn.sigmoid(product(all_rows, my_router, 1, 0))
        live = gates * mask
        act, slope = gelu_pair(product(all_rows, in_mat, 1, 0).reshape(-1, per_device, width))
        lifted = product(all_cot, out_mat, 1, 1).reshape(-1, per_device, width)
        dense_grad = (jnp.sum(act * lifted, axis=-1) * live * (1.0 - gates)).astype(bf16)
        act_live = (act * live[:, :, None]).astype(bf16).reshape(-1, per_device * width)
        hidden_grad = (slope * lifted * live[:, :, None]).astype(bf16)
        hidden_grad = hidden_grad.reshape(-1, per_device * width)
        part_out = product(act_live, out_mat, 1, 0).astype(bf16)
        part_grad = (
            product(hidden_grad, in_mat, 1, 1) + product(dense_grad, my_router, 1, 1)
        ).astype(bf16)
        back = lax.psum_scatter(part_grad, everywhere, scatter_dimension=0, tiled=True)
        forth = lax.psum_scatter(part_out, everywhere, scatter_dimension=0, tiled=True)
        grads = (
            product(all_rows, hidden_grad, 0, 0),
            product(act_live, all_cot, 0, 0),
            product(dense_grad, all_rows, 0, 0),
        )
        if running is not None:
            grads = jax.tree.map(jnp.add, running, grads)
        return grads, (forth, back)

    turns = max(1, lax.axis_size("dp") * lax.axis_size("head") * tokens // whole_rows)
    owned = (middle_normed, cotangent, expert_pick)
    if turns == 1:
        grads, (summed, normed_grad) = turn(None, owned)
    else:
        owned = jax.tree.map(lambda a: a.reshape(turns, -1, a.shape[1]), owned)
        zeros = (
            jnp.zeros(in_mat.shape, f32),
            jnp.zeros(out_mat.shape, f32),
            jnp.zeros((per_device, features), f32),
        )
        grads, sums = lax.scan(turn, zeros, owned)
        summed, normed_grad = (a.reshape(tokens, features) for a in sums)
    grad_in = grads[0].reshape(features, per_device, width).transpose(1, 0, 2)
    grad_out = grads[1].reshape(per_device, width, features)
    grad_router = lax.all_gather(grads[2], everywhere, axis=0, tiled=True).T
    output = middle + summed.astype(f32)
    incoming = cotangent.astype(f32)
    row_grad, grad_gain_expert = norm_back(
        middle, middle_inverse, expert_scale, normed_grad.astype(f32)
    )
    middle_grad = incoming + row_grad
    group_grads = lax.all_gather(middle_grad.astype(bf16), "head", axis=0, tiled=True)
    weighted_grad = product(group_grads, output_mat, 1, 1).reshape(group, head_experts, head_width)
    output_grad = product(weighted, group_grads, 0, 0)
    output_gate_grad = jnp.sum(weighted_grad * attended[:, None, :], axis=-1)
    attended_grad = jnp.sum(weighted_grad * output_gates[:, :, None], axis=1).astype(bf16)
    prob_grad = product(attended_grad, values, 1, 1)
    centre = jnp.sum(probabilities * prob_grad, axis=-1, keepdims=True)
    score_grad = (probabilities * (prob_grad - centre)).astype(bf16)
    query_grad = product(score_grad, key_rows, 1, 0) * scale
    key_grad = product(score_grad, queries, 0, 0) * scale
    values_grad = product(probabilities.astype(bf16), attended_grad, 0, 0)
    expert_grad = (value_gates[:, :, None] * values_grad[:, None, :]).reshape(group, -1).astype(bf16)
    value_gate_grad = jnp.sum(expert_values * values_grad[:, None, :], axis=-1)
    query_grad = rotate(query_grad, cosine, -sine).astype(bf16)
    key_grad = rotate(key_grad, cosine, -sine).astype(bf16)
    logit_grad = (
        jnp.concatenate([value_gate_grad * value_mask, output_gate_grad * output_mask], axis=1)
        * squash
        * (1.0 - squash)
    ).astype(bf16)
    head_grads = (
        product(normed, query_grad, 0, 0),
        product(normed, key_grad, 0, 0),
        product(rows, expert_grad, 0, 0),
        output_grad,
        product(normed, logit_grad, 0, 0),
    )
    head_grads = tuple(grad.astype(bf16) for grad in head_grads)
    head_grads = tuple(grad.astype(f32)[None] for grad in lax.psum(head_grads, "dp"))
    back = (
        product(query_grad, query_mat, 1, 1)
        + product(key_grad, key_mat, 1, 1)
        + product(logit_grad, gate_mat, 1, 1)
    )
    row_back, grad_attend = norm_back(grouped, inverse, attend_scale, back)
    partial = (row_back + product(expert_grad, value_mat, 1, 1)).astype(bf16)
    input_grad = middle_grad + lax.psum_scatter(
        partial, "head", scatter_dimension=0, tiled=True
    ).astype(f32)
    grad_attend, grad_gain_expert = lax.psum((grad_attend, grad_gain_expert), everywhere)
    return (
        output,
        input_grad,
        grad_attend,
        *head_grads,
        grad_gain_expert,
        grad_router,
        grad_in,
        grad_out,
    )


MESH = pl.DeviceIdType.MESH
VM = pl.BlockSpec(memory_space=pltpu.VMEM)
ANY = pl.BlockSpec(memory_space=pl.ANY)
NN = (((1,), (0,)), ((), ()))
NT = (((1,), (1,)), ((), ()))
TN = (((0,), (0,)), ((), ()))


def dot(left, right, dims=NN):
    return lax.dot_general(left, right, dims, preferred_element_type=f32)


def at_block(block, count):
    return pl.ds(pl.multiple_of(block * count, count), count)


def remote(src, dst, send, recv, where):
    return pltpu.make_async_remote_copy(
        src_ref=src, dst_ref=dst, send_sem=send, recv_sem=recv, device_id=where, device_id_type=MESH
    )


def swap_halves(value):
    half = value.shape[-1] // 2
    return jnp.concatenate([value[:, half:], value[:, :half]], axis=-1)


def ceil_to(number, step):
    return -(-number // step) * step


def layer_kernel(
    n_dp,
    n_head,
    x_ref,
    cot_ref,
    pick_ref,
    head_pick_ref,
    seg_ref,
    gain_ref,
    angle_ref,
    wq_ref,
    wk_ref,
    wg_ref,
    wv_ref,
    wo_ref,
    router_ref,
    in_ref,
    out_ref,
    output_ref,
    grad_x_ref,
    wide_ref,
    fin_in_ref,
    fin_out_ref,
    picks,
    head_picks,
    seg,
    gains,
    angles,
    w_an,
    w_v,
    w_o,
    my_router,
    w_in,
    w_out,
    rows,
    cot,
    mrs,
    das,
    turned,
    my_mask,
    all_mask,
    gates,
    q,
    k,
    v,
    vx,
    att,
    part,
    got,
    outs,
    got_out,
    lifted,
    core_out,
    acts,
    hids,
    dzs,
    datt,
    gate_grads,
    probs,
    scores,
    qkz,
    vgrads,
    gain_part,
    gain_got,
    sums,
    core_got,
    chip_got,
    piece,
    blocks,
    hop_in,
    hop_out,
    local_sem,
    z_send,
    z_recv,
    w_send,
    w_recv,
    c_send,
    c_recv,
    e_send,
    e_recv,
    s_send,
    s_recv,
    ready,
    free,
):
    middle = output_ref
    xor = jnp.bitwise_xor
    d, h = lax.axis_index("dp"), lax.axis_index("head")
    chip, core = d // 2, d % 2
    chips = n_dp // 2
    tokens, features = x_ref.shape
    per_device, _, width = in_ref.shape
    slab = per_device * width
    wide = 2 * slab
    experts = wv_ref.shape[1] // width
    named = ceil_to(n_dp * per_device, 8)
    group = tokens * n_head
    pair = 2 * tokens
    column = 256
    lanes = 128
    scale = width ** (-0.5)
    peers = (2, 3, 1)
    partner = (chip * 2 + 1 - core, h)
    own_block = at_block(h, tokens)
    own_side, other_side = at_block(core, slab), at_block(1 - core, slab)
    halves_in = (pl.ds(0, features // 2), pl.ds(features // 2, features // 2))
    halves_out = lambda side: (
        at_block(2 * side, slab // 2),
        at_block(2 * side + 1, slab // 2),
    )

    def along(step):
        return (d, xor(h, step))

    def across(step):
        return (xor(chip, step) * 2 + core, h)

    loads = []

    def load(src, dst):
        copy = pltpu.make_async_copy(src, dst, local_sem.at[len(loads)])
        copy.start()
        loads.append(copy)
        return copy

    own_weights = [load(out_ref, w_out.at[chip, own_side, :])] + [
        load(in_ref.at[e], w_in.at[chip, :, at_block(core * per_device + e, width)])
        for e in range(per_device)
    ]
    for_rows = [
        load(x_ref, rows.at[own_block, :]),
        load(gain_ref, gains),
        load(wg_ref, w_an.at[:, pl.ds(2 * width, width)]),
        load(wq_ref, w_an.at[:, pl.ds(0, width)]),
        load(wk_ref, w_an.at[:, pl.ds(width, width)]),
        load(wv_ref, w_v),
        load(head_pick_ref, head_picks),
        load(angle_ref, angles),
    ]
    for_scores = [load(seg_ref, seg), load(wo_ref, w_o)]
    for_mask = load(pick_ref, picks)
    for_cot = load(cot_ref, cot.at[own_block, :])
    for_router = load(router_ref, turned.at[:, pl.ds(0, lanes)])

    barrier = pltpu.get_barrier_semaphore()
    friends = [along(s) for s in peers] + [partner] + [across(s) for s in range(1, chips)]
    for friend in friends:
        pl.semaphore_signal(barrier, inc=1, device_id=friend, device_id_type=MESH)
    pl.semaphore_wait(barrier, len(friends))

    right, left = (d, jnp.minimum(h + 1, n_head - 1)), (d, jnp.maximum(h - 1, 0))
    last = n_head - 1

    def pick(*by_place):
        value = jnp.int32(by_place[-1])
        for place in range(n_head - 2, -1, -1):
            value = jnp.where(h == place, by_place[place], value)
        return value

    arrival = (xor(h, 1), pick(2, 2, 1, 1), pick(3, 3, 0, 0))
    leaving = (pick(3, 3, 0, 0), pick(2, 0, 3, 1), pick(1, 2, 1, 2))

    def gather(kind, buffer):
        def go(side, step):
            block = jnp.clip(h - step if side == 0 else h + step, 0, last)
            here = buffer.at[at_block(block, tokens), :]
            number = side * last + step
            return remote(
                here, here, z_send.at[kind, number], z_recv.at[kind, number], (right, left)[side]
            )

        def start():
            @pl.when(h < last)
            def _():
                go(0, 0).start()

            @pl.when(h > 0)
            def _():
                go(1, 0).start()

        def stage(step):
            @pl.when(h >= step)
            def _():
                go(0, step - 1).wait_recv()

            if step < last:

                @pl.when((h >= step) & (h < last))
                def _():
                    go(0, step).start()

            @pl.when(h + step <= last)
            def _():
                go(1, step - 1).wait_recv()

            if step < last:

                @pl.when((h + step <= last) & (h > 0))
                def _():
                    go(1, step).start()

        def end():
            for step in range(last):

                @pl.when((h >= step) & (h < last))
                def _():
                    go(0, step).wait_send()

                @pl.when((h + step <= last) & (h > 0))
                def _():
                    go(1, step).wait_send()

        return start, stage, end

    def chain_sum(kind, parts, slots):
        def go(number):
            block = leaving[number]
            rightward = block > h
            slot = jnp.where(rightward, block - 1, last + block)
            where = (d, jnp.clip(jnp.where(rightward, h + 1, h - 1), 0, last))
            at = at_block(block, tokens)
            copy = remote(
                parts.at[at, :], slots.at[slot], z_send.at[kind, number], z_recv.at[kind, slot], where
            )
            middle_one = (rightward & (h > 0)) | (jnp.logical_not(rightward) & (h < last))
            return copy, middle_one, at, slot

        def now(number):
            copy, middle_one, _, _ = go(number)

            @pl.when(jnp.logical_not(middle_one))
            def _():
                copy.start()

        def later(number):
            copy, middle_one, at, slot = go(number)

            @pl.when(middle_one)
            def _():
                copy.wait_recv()
                parts[at, :] = parts[at, :] + slots[slot]
                copy.start()

        def end(total):
            for slot, there in ((jnp.maximum(h - 1, 0), h > 0), (last + jnp.minimum(h, last - 1), h < last)):

                @pl.when(there)
                def _():
                    remote(
                        parts.at[own_block, :], slots.at[slot], z_send.at[kind, 0], z_recv.at[kind, slot], right
                    ).wait_recv()
                    total[...] += slots[slot].astype(f32)

            for number in range(last):
                go(number)[0].wait_send()

        return now, later, end

    def spread(kind, src, dst, steps=peers):
        copies = {}
        for step in steps:
            copies[step] = remote(
                src(step), dst(step), z_send.at[kind, step - 1], z_recv.at[kind, step - 1], along(step)
            )
            copies[step].start()
        return copies

    x_start, x_stage, x_end = gather(0, rows)
    for_rows[0].wait()
    x_start()

    def slot(array, place, side, half=None):
        if array == 0:
            at = halves_out(side)[half] if half is not None else at_block(side, slab)
            return w_out.at[place, at, :]
        at = halves_in[half] if half is not None else pl.ds(0, features)
        return w_in.at[place, at, at_block(side, slab)]

    def weights(number, ref, where):
        copy = remote(ref, ref, w_send.at[number], w_recv.at[number], where)
        copy.start()
        return copy

    slabs, halves_on, to_core, diagonal = {}, {}, {}, {}
    for copy in own_weights:
        copy.wait()
    for array in range(2):
        for first in range(2):
            for bit in (1, 2):
                half = bit - 1 if first == 0 else 2 - bit
                number = ((bit - 1) * 2 + half) * 2 + array
                slabs[bit, half, array] = weights(
                    number, slot(array, chip, core, half), across(bit)
                )
        to_core[0, array] = weights(12 + array, slot(array, chip, core), partner)

    for_mask.wait()
    lane = lax.broadcasted_iota(jnp.int32, (tokens, lanes), 1)
    for plane in range(n_head):
        expert = (lane // per_device * n_head + plane) * per_device + lane % per_device
        expert = jnp.where(lane < n_dp * per_device, expert, -1)
        hit = picks[:, 0:1] == expert
        for c in range(1, picks.shape[1]):
            hit = hit | (picks[:, c : c + 1] == expert)
        my_mask[plane] = jnp.where(hit, 1.0, 0.0).astype(bf16)
    mask_copies = spread(1, lambda s: my_mask.at[xor(h, s)], lambda s: all_mask.at[own_block, :])
    all_mask[own_block, :] = my_mask[h]

    for copy in for_rows[1:]:
        copy.wait()
    attend_gain = gains[0:1, :]
    expert_gain = gains[1:2, :]
    half_lanes = lax.broadcasted_iota(jnp.int32, (1, width), 1) < width // 2

    def turns(at):
        both = angles[at, :]
        turned_over = swap_halves(both)
        return (
            jnp.where(half_lanes, both, turned_over),
            jnp.where(half_lanes, -turned_over, both),
        )

    def project(block):
        at = at_block(block, tokens)
        own = rows[at, :]
        full = own.astype(f32)
        inverse = lax.rsqrt(jnp.mean(full * full, axis=-1, keepdims=True) + epsilon)
        unit = (full * inverse * attend_gain).astype(bf16)
        qkg = dot(unit, w_an[...])
        c, s = turns(at)
        one, two = qkg[:, :width], qkg[:, width : 2 * width]
        q[at, :] = (one * c + swap_halves(one) * s).astype(bf16)
        k[at, :] = (two * c + swap_halves(two) * s).astype(bf16)
        lane = lax.broadcasted_iota(jnp.int32, (tokens, width), 1)
        chosen = head_picks[at, :]
        hit = lane == chosen[:, 0:1]
        for c in range(1, chosen.shape[1]):
            hit = hit | (lane == chosen[:, c : c + 1])
        gate = jnp.where(hit, jax.nn.sigmoid(qkg[:, 2 * width :]), 0.0)
        gates[at, :] = jnp.where(lane == width - 1, inverse, gate)
        values = dot(own, w_v[...])
        vx[at, :] = values.astype(bf16)
        value = gate[:, 0:1] * values[:, :width]
        for e in range(1, experts):
            value += gate[:, e : e + 1] * values[:, e * width : (e + 1) * width]
        v[at, :] = value.astype(bf16)

    project(h)
    for step in (1, 2, 3):
        x_stage(step)
        project(arrival[step - 1])
    cot_start, cot_stage, cot_end = gather(2, cot)
    for_cot.wait()
    cot_start()
    for copy in for_scores:
        copy.wait()
    seg_col = gate_grads
    seg_col[...] = jnp.broadcast_to(seg[...].astype(f32), (lanes, group)).T

    def attend(block):
        at = at_block(block, tokens)
        score = dot(q[at, :], k[...], NT) * scale
        row = block * tokens + lax.broadcasted_iota(jnp.int32, (tokens, group), 0)
        place = lax.broadcasted_iota(jnp.int32, (tokens, group), 1)
        allowed = (place <= row) & (seg_col[at, 0:1] == seg[...].astype(f32))
        score = jnp.where(allowed, score, negative)
        exponents = jnp.exp(score - jnp.max(score, axis=-1, keepdims=True))
        chance = exponents / jnp.sum(exponents, axis=-1, keepdims=True)
        probs[at, :] = chance.astype(bf16)
        attended = dot(chance.astype(bf16), v[...])
        att[at, :] = attended
        gate = gates[at, :]
        weighted = jnp.concatenate(
            [
                (gate[:, experts + e : experts + e + 1] * attended).astype(bf16)
                for e in range(experts)
            ],
            axis=-1,
        )
        return dot(weighted, w_o[...])

    to_mid = chain_sum(3, part, got)
    for number in range(last):
        block = leaving[number]
        part[at_block(block, tokens), :] = attend(block).astype(bf16)
        to_mid[0](number)
    middle[...] = rows[own_block, :].astype(f32) + attend(h)
    to_mid[1](0)
    cot_stage(1)
    for half in range(2):
        for array in range(2):
            slabs[1 + half, half, array].wait_recv()
            halves_on[half, array] = weights(
                8 + 2 * half + array,
                slot(array, xor(chip, 1 + half), core, half),
                across(2 - half),
            )

    to_mid[1](1)
    cot_stage(2)
    to_mid[1](2)
    for bit in (1, 2):
        slabs[bit, 2 - bit, 0].wait_recv()
        to_core[bit, 0] = weights(14 + (bit - 1) * 2, slot(0, xor(chip, bit), core), partner)
        slabs[bit, 2 - bit, 1].wait_recv()
        to_core[bit, 1] = weights(15 + (bit - 1) * 2, slot(1, xor(chip, bit), core), partner)
    for_router.wait()
    slot_of = lax.broadcasted_iota(jnp.int32, (lanes, lanes), 1)
    name = lax.broadcasted_iota(jnp.int32, (lanes, lanes), 0)
    expert = (slot_of // per_device * n_head + h) * per_device + slot_of % per_device
    expert = jnp.where(slot_of < n_dp * per_device, expert, -1)
    my_router[...] = dot(turned[:, pl.ds(0, lanes)], jnp.where(name == expert, 1.0, 0.0).astype(bf16)).astype(bf16)

    to_mid[2](middle)
    mid = middle[...]
    inverse = lax.rsqrt(jnp.mean(mid * mid, axis=-1, keepdims=True) + epsilon)
    mrs[own_block, :] = (mid * inverse * expert_gain).astype(bf16)
    mr_start, mr_stage, mr_end = gather(4, mrs)
    mr_start()
    cot_stage(3)

    for array in range(2):
        for half in range(2):
            halves_on[half, array].wait_recv()
            diagonal[half, array] = weights(
                18 + 2 * half + array, slot(array, xor(chip, 3), core, half), partner
            )
    for step in peers:
        mask_copies[step].wait()
    cot_end()
    x_end()

    def weights_here(array):
        for bit in range(3):
            to_core[bit, array].wait()
        for half in range(2):
            diagonal[half, array].wait()
            halves_on[half, array].wait_send()
            for bit in (1, 2):
                slabs[bit, half, array].wait_send()

    weights_here(0)

    @pl.loop(0, chips)
    def _(j):
        lift = dot(cot[...], w_out[j], NT)
        lifted[j, 0] = lift[:, :slab].astype(bf16)
        lifted[j, 1] = lift[:, slab:].astype(bf16)

    weights_here(1)

    def spread_lanes(j):
        lane = lax.broadcasted_iota(jnp.int32, (lanes, wide), 1) // width
        slot = lax.broadcasted_iota(jnp.int32, (lanes, wide), 0)
        return jnp.where(slot == lane + j * (wide // width), 1.0, 0.0).astype(bf16)

    def pair_of_blocks(number, between):
        at = at_block(number, pair)
        own = mrs[at, :]
        gates = jax.nn.sigmoid(dot(own, my_router[...]))
        live = gates * all_mask[at, :].astype(f32)
        high = live.astype(bf16)
        low = (live - high.astype(f32)).astype(bf16)
        both = jnp.concatenate([high, low], axis=-1)

        def chip_step(j, total):
            pick = spread_lanes(j)
            hidden = dot(own, w_in[j])
            gate = dot(both, jnp.concatenate([pick, pick], axis=0))
            lift = jnp.concatenate([lifted[j, 0, at, :], lifted[j, 1, at, :]], axis=-1).astype(f32)
            square = hidden * hidden
            inner = jnp.tanh(0.7978845608028654 * hidden * (1.0 + 0.044715 * square))
            half = 0.5 * (1.0 + inner)
            act = hidden * half
            slope = half + act * (1.0 - inner) * (
                0.7978845608028654 + (0.7978845608028654 * 3.0 * 0.044715) * square
            )
            acts[j, at, :] = (act * gate).astype(bf16)
            hids[j, at, :] = (slope * (lift * gate)).astype(bf16)
            return total + dot((act * lift).astype(bf16), pick, NT)

        total = lax.fori_loop(0, chips, chip_step, jnp.zeros((pair, lanes), f32))
        dz = (total * live * (1.0 - gates)).astype(bf16)
        dzs[at, :] = dz
        between()

        @pl.loop(0, features // column)
        def _(c):
            part_of = at_block(c, column)
            total = dot(dz, my_router[part_of, :], NT)
            for j in range(chips):
                total += dot(hids[j, at, :], w_in[j, part_of, :], NT)
            part[at, part_of] = total.astype(bf16)

    def outputs(number):
        at = at_block(number, pair)

        @pl.loop(0, features // column)
        def _(c):
            part_of = at_block(c, column)
            total = dot(acts[0, at, :], w_out[0, :, part_of])
            for j in range(1, chips):
                total += dot(acts[j, at, :], w_out[j, :, part_of])
            outs[at, part_of] = total.astype(bf16)

    near = h // 2
    to_dmr = chain_sum(5, part, got)
    mr_stage(1)
    pair_of_blocks(near, lambda: mr_stage(2))
    to_dmr[0](2)
    outputs(near)
    mr_stage(3)
    pair_of_blocks(1 - near, lambda: None)
    to_dmr[0](0)
    to_dmr[0](1)
    outputs(1 - near)
    pl.semaphore_signal(ready, inc=1, device_id=partner, device_id_type=MESH)

    turned[...] = mrs[...].T

    def expert_grads(place, at):
        for half in halves_in:
            w_in[place, half, at] = dot(turned[half, :], hids[place, :, at]).astype(bf16)
            w_out[place, at, half] = dot(acts[place, :, at], cot[:, half], TN).astype(bf16)

    def to_other_core(n):
        place = xor(chip, chips - 1 - n)
        copies = [
            remote(
                w_in.at[place, halves_in[half], other_side],
                lifted.at[place, half],
                c_send.at[half, n],
                c_recv.at[half, n],
                partner,
            )
            for half in range(2)
        ]
        copies.append(
            remote(
                w_out.at[place, other_side, :],
                core_out.at[place],
                c_send.at[2, n],
                c_recv.at[2, n],
                partner,
            )
        )
        return copies

    pl.semaphore_wait(ready, 1)

    @pl.loop(0, chips)
    def _(n):
        expert_grads(xor(chip, chips - 1 - n), other_side)
        for copy in to_other_core(n):
            copy.start()

    @pl.loop(0, chips)
    def _(n):
        expert_grads(xor(chip, chips - 1 - n), own_side)

    to_dmr[1](0)
    hops = {}

    def hop(half, index, place, toward):
        copies = (
            remote(
                slot(1, place, core, half),
                hop_in.at[half, index],
                e_send.at[0, 2 * half + index],
                e_recv.at[0, 2 * half + index],
                across(toward),
            ),
            remote(
                slot(0, place, core, half),
                hop_out.at[half, index],
                e_send.at[1, 2 * half + index],
                e_recv.at[1, 2 * half + index],
                across(toward),
            ),
        )
        for copy in copies:
            copy.start()
        hops[half, index] = copies

    for n in range(chips):
        s = chips - 1 - n
        place = xor(chip, s)
        for copy in to_other_core(n):
            copy.wait()
        for half in range(2):
            here = (place, halves_in[half], own_side)
            w_in[here] = w_in[here] + lifted[place, half]
        w_out[place, own_side, :] = w_out[place, own_side, :] + core_out[place]
        if s == 3:
            hop(0, 1, place, 1)
            hop(1, 1, place, 2)
        elif s:
            hop(s - 1, 0, place, s)

    to_dmr[1](1)
    to_dmr[1](2)
    side = features // 2
    strip = side // chips

    def section(number, first, count):
        at = pl.ds(first, count)
        col = lambda c, j: at_block(c * chips + j, strip)
        state = {}

        def sem(n):
            return s_send.at[number, n], s_recv.at[number, n]

        def start():
            state["core"] = remote(
                sums.at[at, at_block(1 - core, side)], core_got.at[at, :], *sem(0), partner
            )
            state["core"].start()

        def mid():
            state["core"].wait()
            half = at_block(core, side)
            sums[at, half] = sums[at, half] + core_got[at, :]
            state["chips"] = []
            for s in range(1, chips):
                copy = remote(
                    sums.at[at, col(core, xor(chip, s))], chip_got.at[s - 1, at, :], *sem(s), across(s)
                )
                copy.start()
                state["chips"].append(copy)

        def add():
            for copy in state["chips"]:
                copy.wait()
            total = sums[at, col(core, chip)].astype(f32)
            for s in range(1, chips):
                total += chip_got[s - 1, at, :].astype(f32)
            piece[at, :] = total.astype(bf16)

        def share(src=None, rows_to=at):
            src = piece.at[at, :] if src is None else src
            state["rows"] = rows_to
            here = wide_ref.at[rows_to, col(core, chip)]
            state["share"] = []
            for s in range(1, chips):
                copy = remote(src, here, *sem(chips + s), across(s))
                copy.start()
                state["share"].append(copy)
            over = remote(src, here, *sem(chips), partner)
            own = pltpu.make_async_copy(src, here, s_send.at[number, 3 * chips - 1])
            over.start()
            own.start()
            state["wait"] = [over, own]

        def forward():
            for s in range(1, chips):
                state["share"][s - 1].wait()
                here = wide_ref.at[state["rows"], col(core, xor(chip, s))]
                copy = remote(here, here, *sem(2 * chips - 1 + s), partner)
                copy.start()
                state["wait"].append(copy)

        def end():
            for copy in state["wait"]:
                copy.wait()

        return start, mid, add, share, forward, end

    top = features + w_o.shape[0]
    small = ceil_to(named + 1, 16)
    of_o = section(0, features, w_o.shape[0])
    of_d = section(1, 0, features)
    of_g = section(2, top + 16, small)
    of_a = section(3, top, 16)
    router_part = dot(dzs[...], mrs[...], TN)[:named]

    grad_x_ref[...] = part[own_block, :].astype(f32)
    to_dmr[2](grad_x_ref)
    incoming = grad_x_ref[...]
    mid = middle[...]
    inverse = lax.rsqrt(jnp.mean(mid * mid, axis=-1, keepdims=True) + epsilon)
    unit = mid * inverse
    scaled = incoming * expert_gain
    dmid = cot[own_block, :].astype(f32) + inverse * (
        scaled - unit * jnp.mean(scaled * unit, axis=-1, keepdims=True)
    )
    grad_x_ref[...] = dmid
    das[own_block, :] = dmid.astype(bf16)
    da_start, da_stage, da_end = gather(6, das)
    da_start()
    sums[pl.ds(top + 16, small), :] = jnp.concatenate(
        [
            router_part,
            jnp.sum(incoming * unit, axis=0, keepdims=True),
            jnp.zeros((small - named - 1, features), f32),
        ],
        axis=0,
    ).astype(bf16)
    of_g[0]()
    turned[...] = rows[...].T
    of_g[1]()
    lane = lax.broadcasted_iota(jnp.int32, (tokens, width), 1)

    def through_output(block):
        at = at_block(block, tokens)
        all_five = dot(das[at, :], w_o[...], NT)
        attended = att[at, :]
        total = jnp.zeros((tokens, width), f32)
        gate = jnp.zeros((tokens, width), f32)
        for e in range(experts):
            one = all_five[:, e * width : (e + 1) * width]
            total += gates[at, experts + e : experts + e + 1] * one
            gate = jnp.where(
                lane == experts + e, jnp.sum(one * attended, axis=-1, keepdims=True), gate
            )
        datt[at, :] = total.astype(bf16)
        gate_grads[at, :] = gate

    through_output(h)
    for step in (1, 2, 3):
        da_stage(step)
        through_output(arrival[step - 1])
    to_out = chain_sum(7, outs, got_out)
    to_out[0](0)

    for e in range(experts):
        one = (gates[:, experts + e : experts + e + 1] * att[...]).astype(bf16)
        sums[pl.ds(features + e * width, width), :] = dot(one, das[...], TN).astype(bf16)
    of_o[0]()

    @pl.loop(0, n_head)
    def _(block):
        at = at_block(block, tokens)
        chance = probs[at, :].astype(f32)
        dprob = dot(datt[at, :], v[...], NT)
        centre = jnp.sum(chance * dprob, axis=-1, keepdims=True)
        scores[at, :] = (chance * (dprob - centre)).astype(bf16)

    dq = dot(scores[...], k[...]) * scale
    dk = dot(scores[...], q[...], TN) * scale
    dv = dot(probs[...], datt[...], TN)
    of_o[1]()
    c, s = turns(slice(None))
    qkz[:, pl.ds(0, width)] = (dq * c - swap_halves(dq) * s).astype(bf16)
    qkz[:, pl.ds(width, width)] = (dk * c - swap_halves(dk) * s).astype(bf16)
    gate = gate_grads[...]
    lane = lax.broadcasted_iota(jnp.int32, (group, width), 1)
    for e in range(experts):
        vgrads[:, pl.ds(e * width, width)] = (gates[:, e : e + 1] * dv).astype(bf16)
        one = jnp.sum(vx[:, pl.ds(e * width, width)].astype(f32) * dv, axis=-1, keepdims=True)
        gate = jnp.where(lane == e, one, gate)
    qkz[:, pl.ds(2 * width, width)] = (gate * gates[...] * (1.0 - gates[...])).astype(bf16)

    scaled_qkz = (qkz[...].astype(f32) * gates[:, width - 1 : width]).astype(bf16)

    @pl.loop(0, features // column)
    def _(c):
        at = at_block(c, column)
        sums[at, pl.ds(0, 3 * width)] = dot(turned[at, :], scaled_qkz).astype(bf16)
        sums[at, pl.ds(3 * width, experts * width)] = dot(turned[at, :], vgrads[...]).astype(bf16)

    of_d[0]()

    def into_rows(block):
        at = at_block(block, tokens)
        inverse = gates[at, width - 1 : width]
        unit = rows[at, :].astype(f32) * inverse
        through = dot(qkz[at, :], w_an[...], NT)
        scaled = through * attend_gain
        total = inverse * (
            scaled - unit * jnp.mean(scaled * unit, axis=-1, keepdims=True)
        ) + dot(vgrads[at, :], w_v[...], NT)
        return total, jnp.sum(through * unit, axis=0, keepdims=True)

    to_x = chain_sum(8, part, got)
    gain = jnp.zeros((1, features), f32)
    for number in range(last):
        total, one = into_rows(leaving[number])
        gain += one
        part[at_block(leaving[number], tokens), :] = total.astype(bf16)
        to_x[0](number)
    total, one = into_rows(h)
    gain_part[...] = jnp.broadcast_to(gain + one, gain_part.shape)
    gain_copies = spread(9, lambda s: gain_part, lambda s: gain_got.at[s - 1])
    grad_x_ref[...] += total
    of_d[1]()
    lasts = {}
    for half in range(2):
        toward = 2 - half
        for index, place in ((1, xor(chip, toward)), (0, chip)):
            for copy in hops[half, index]:
                copy.wait()
            at_in = (place, halves_in[half], own_side)
            at_out = (place, halves_out(core)[half], slice(None))
            w_in[at_in] = w_in[at_in] + hop_in[half, index]
            w_out[at_out] = w_out[at_out] + hop_out[half, index]
            if index:
                pl.semaphore_signal(
                    free.at[half], inc=1, device_id=across(toward), device_id_type=MESH
                )
                pl.semaphore_wait(free.at[half], 1)
                lasts[half] = (
                    remote(
                        w_in.at[at_in],
                        hop_in.at[half, 1],
                        e_send.at[0, 4 + half],
                        e_recv.at[0, 4 + half],
                        across(toward),
                    ),
                    remote(
                        w_out.at[at_out],
                        hop_out.at[half, 1],
                        e_send.at[1, 4 + half],
                        e_recv.at[1, 4 + half],
                        across(toward),
                    ),
                )
                for copy in lasts[half]:
                    copy.start()

    to_x[1](0)
    of_o[2]()
    of_o[3]()
    of_g[2]()
    small_block = at_block(h, small)
    blocks[small_block, :] = piece[pl.ds(top + 16, small), :]
    g_copies = spread(10, lambda s: blocks.at[small_block, :], lambda s: blocks.at[small_block, :])
    to_x[1](1)
    to_x[1](2)
    to_out[0](1)
    to_out[0](2)
    of_d[2]()
    of_d[3]()
    to_x[2](grad_x_ref)
    to_out[1](0)
    gain = gain_part[...]
    for step in peers:
        gain_copies[step].wait()
        gain += gain_got[step - 1]
    sums[pl.ds(top, 16), :] = jnp.concatenate([gain, gain], axis=0).astype(bf16)
    of_a[0]()
    for step in peers:
        g_copies[step].wait()
    of_g[3](blocks, pl.ds(top + 16, n_head * small))
    of_o[4]()
    to_out[1](1)
    of_a[1]()
    to_out[1](2)
    of_a[2]()
    of_a[3]()
    of_d[4]()
    of_g[4]()
    output_ref[...] = middle[...] + outs[own_block, :].astype(f32)
    to_out[2](output_ref)
    for half in range(2):
        for copy in lasts[half]:
            copy.wait()
        at_in = (chip, halves_in[half], own_side)
        at_out = (chip, halves_out(core)[half], slice(None))
        w_in[at_in] = w_in[at_in] + hop_in[half, 1]
        w_out[at_out] = w_out[at_out] + hop_out[half, 1]
    stores = (
        pltpu.make_async_copy(w_in.at[chip, :, own_side], fin_in_ref, local_sem.at[0]),
        pltpu.make_async_copy(w_out.at[chip, own_side, :], fin_out_ref, local_sem.at[1]),
    )
    for store in stores:
        store.start()
    of_a[4]()
    for one in (of_o, of_g, of_d, of_a):
        one[5]()
    for store in stores:
        store.wait()
    mr_end()
    da_end()


def layer_call(n_dp, n_head, args):
    x, picks, _, value_mat, expert_in = args[0], args[2], args[12], args[10], args[13]
    tokens, features = x.shape
    per_device, _, width = expert_in.shape
    held_experts = value_mat.shape[1]
    group = tokens * n_head
    chips = n_dp // 2
    slab = per_device * width
    lanes = 128
    peers = n_head - 1
    named = ceil_to(n_dp * per_device, 8)
    small = ceil_to(named + 1, 16)
    top = features + held_experts
    held = top + 16 + small
    strip = features // n_dp
    shape = jax.ShapeDtypeStruct
    vm, dma = pltpu.VMEM, pltpu.SemaphoreType.DMA
    outs = [
        (shape((tokens, features), f32), VM),
        (shape((tokens, features), f32), VM),
        (shape((top + 16 + n_head * small, features), bf16), ANY),
        (shape((features, slab), bf16), ANY),
        (shape((slab, features), bf16), ANY),
    ]
    scratch = dict(
        picks=vm(picks.shape, jnp.int32),
        head_picks=vm(args[3].shape, jnp.int32),
        seg=vm((1, group), jnp.int32),
        gains=vm(args[5].shape, f32),
        angles=vm((group, width), f32),
        w_an=vm((features, 3 * width), bf16),
        w_v=vm((features, held_experts), bf16),
        w_o=vm((held_experts, features), bf16),
        my_router=vm((features, lanes), bf16),
        w_in=vm((chips, features, 2 * slab), bf16),
        w_out=vm((chips, 2 * slab, features), bf16),
        rows=vm((group, features), bf16),
        cot=vm((group, features), bf16),
        mrs=vm((group, features), bf16),
        das=vm((group, features), bf16),
        turned=vm((features, group), bf16),
        my_mask=vm((n_head, tokens, lanes), bf16),
        all_mask=vm((group, lanes), bf16),
        gates=vm((group, width), f32),
        q=vm((group, width), bf16),
        k=vm((group, width), bf16),
        v=vm((group, width), bf16),
        vx=vm((group, held_experts), bf16),
        att=vm((group, width), f32),
        part=vm((group, features), bf16),
        got=vm((2 * peers, tokens, features), bf16),
        outs=vm((group, features), bf16),
        got_out=vm((2 * peers, tokens, features), bf16),
        lifted=vm((chips, 2, group, slab), bf16),
        core_out=vm((chips, slab, features), bf16),
        acts=vm((chips, group, 2 * slab), bf16),
        hids=vm((chips, group, 2 * slab), bf16),
        dzs=vm((group, lanes), bf16),
        datt=vm((group, width), bf16),
        gate_grads=vm((group, width), f32),
        probs=vm((group, group), bf16),
        scores=vm((group, group), bf16),
        qkz=vm((group, 3 * width), bf16),
        vgrads=vm((group, held_experts), bf16),
        gain_part=vm((8, features), f32),
        gain_got=vm((peers, 8, features), f32),
        sums=vm((held, features), bf16),
        core_got=vm((held, features // 2), bf16),
        chip_got=vm((chips - 1, held, strip), bf16),
        piece=vm((held, strip), bf16),
        blocks=vm((n_head * small, strip), bf16),
        hop_in=vm((2, 2, features // 2, slab), bf16),
        hop_out=vm((2, 2, slab // 2, features), bf16),
        local_sem=dma((15 + 1 + per_device,)),
        z_send=dma((11, 2 * peers)),
        z_recv=dma((11, 2 * peers)),
        w_send=dma((22,)),
        w_recv=dma((22,)),
        c_send=dma((3, chips)),
        c_recv=dma((3, chips)),
        e_send=dma((2, 6)),
        e_recv=dma((2, 6)),
        s_send=dma((4, 3 * chips)),
        s_recv=dma((4, 3 * chips)),
        ready=pltpu.SemaphoreType.REGULAR,
        free=pltpu.SemaphoreType.REGULAR((2,)),
    )
    return pl.pallas_call(
        functools.partial(layer_kernel, n_dp, n_head),
        out_shape=[o[0] for o in outs],
        out_specs=[o[1] for o in outs],
        in_specs=[ANY] * 15,
        scratch_shapes=list(scratch.values()),
        compiler_params=pltpu.CompilerParams(
            collective_id=1, has_side_effects=True, vmem_limit_bytes=vmem_bytes
        ),
    )(*args)


def finish_kernel(
    n_dp,
    n_head,
    output_ref,
    grad_x_ref,
    wide_ref,
    in_ref,
    out_ref,
    gain_ref,
    final_ref,
    input_ref,
    attend_ref,
    query_ref,
    key_ref,
    value_ref,
    mix_ref,
    gate_ref,
    expert_ref,
    router_ref,
    grad_in_ref,
    grad_out_ref,
    wide,
    flat_in,
    flat_out,
    value,
    mix,
    grad_in,
    grad_out,
    output,
    grad_x,
    sem,
):
    features, slab = in_ref.shape
    per_device, _, width = grad_in_ref.shape
    experts_total = router_ref.shape[1]
    gates = gate_ref.shape[1]
    top = features + mix_ref.shape[0]
    small = (wide_ref.shape[0] - top - 16) // n_head
    named = n_dp * per_device

    def copy(src, dst, number):
        one = pltpu.make_async_copy(src, dst, sem.at[number])
        one.start()
        return one

    rest = pl.ds(top, wide_ref.shape[0] - top)
    loads = [
        copy(wide_ref.at[pl.ds(0, features), :], wide.at[pl.ds(0, features), :], 0),
        copy(wide_ref.at[pl.ds(features, top - features), :], wide.at[pl.ds(features, top - features), :], 1),
        copy(in_ref, flat_in, 2),
        copy(out_ref, flat_out, 3),
        copy(wide_ref.at[rest, :], wide.at[rest, :], 4),
    ]
    loads += [copy(output_ref, output, 11), copy(grad_x_ref, grad_x, 12)]
    stores = []
    for number, (held, result) in enumerate(((output, final_ref), (grad_x, input_ref))):
        loads[5 + number].wait()
        stores.append(copy(held, result, 5 + number))
    loads[0].wait()
    first = pl.ds(0, features)
    value[...] = wide[first, pl.ds(3 * width, value.shape[1])].astype(f32)
    stores.append(copy(value, value_ref, 7))
    gain = jnp.broadcast_to(gain_ref[0:1, :], (width, features)).T
    query_ref[...] = wide[first, pl.ds(0, width)].astype(f32) * gain
    key_ref[...] = wide[first, pl.ds(width, width)].astype(f32) * gain
    gate_ref[...] = (wide[first, pl.ds(2 * width, width)].astype(f32) * gain)[:, :gates]
    loads[1].wait()
    mix[...] = wide[pl.ds(features, top - features), :].astype(f32)
    stores.append(copy(mix, mix_ref, 8))
    loads[2].wait()
    for e in range(per_device):
        grad_in[e] = flat_in[:, pl.ds(e * width, width)].astype(f32)
    stores.append(copy(grad_in, grad_in_ref, 9))
    loads[3].wait()
    for e in range(per_device):
        grad_out[e] = flat_out[pl.ds(e * width, width), :].astype(f32)
    stores.append(copy(grad_out, grad_out_ref, 10))
    loads[4].wait()
    attend_ref[...] = wide[pl.ds(top, 16), :][0:1].astype(f32)
    planes = wide[pl.ds(top + 16, n_head * small), :]
    place = lax.broadcasted_iota(jnp.int32, (n_head * small, experts_total), 0)
    name = lax.broadcasted_iota(jnp.int32, (n_head * small, experts_total), 1)
    slot, plane = place % small, place // small
    expert = (slot // per_device * n_head + plane) * per_device + slot % per_device
    chosen = (slot < named) & (expert == name)
    router_ref[...] = dot(planes, jnp.where(chosen, 1.0, 0.0).astype(bf16), TN)
    gain = jnp.zeros((1, features), f32)
    for z in range(n_head):
        row = z * small + ceil_to(named, 8)
        gain += planes[row : row + 1].astype(f32)
    expert_ref[...] = gain
    for store in stores:
        store.wait()


def finish_call(n_dp, n_head, shapes, args):
    shape = jax.ShapeDtypeStruct
    wide, flat_in, flat_out = args[2], args[3], args[4]
    value, mix, grad_in, grad_out = shapes[5], shapes[6], shapes[10], shapes[11]
    specs = [VM] * 12
    for number in (0, 1, 5, 6, 10, 11):
        specs[number] = ANY
    return pl.pallas_call(
        functools.partial(finish_kernel, n_dp, n_head),
        out_shape=[shape(s, f32) for s in shapes],
        out_specs=specs,
        in_specs=[ANY] * 5 + [VM],
        scratch_shapes=[
            pltpu.VMEM(wide.shape, bf16),
            pltpu.VMEM(flat_in.shape, bf16),
            pltpu.VMEM(flat_out.shape, bf16),
            pltpu.VMEM(value, f32),
            pltpu.VMEM(mix, f32),
            pltpu.VMEM(grad_in, f32),
            pltpu.VMEM(grad_out, f32),
            pltpu.VMEM(shapes[0], f32),
            pltpu.VMEM(shapes[1], f32),
            pltpu.SemaphoreType.DMA((13,)),
        ],
        compiler_params=pltpu.CompilerParams(vmem_limit_bytes=60 << 20),
    )(*args)


def kernel_body(
    n_dp,
    n_head,
    hidden_in,
    segments,
    value_pick,
    output_pick,
    expert_pick,
    attend_gain,
    query_weight,
    key_weight,
    value_weight,
    output_weight,
    head_router,
    expert_gain,
    router,
    expert_in,
    expert_out,
    cotangent,
):
    tokens, features = hidden_in.shape
    per_device, _, width = expert_in.shape
    experts = head_router.shape[2] // 2
    group = tokens * n_head
    angles = np.arange(group)[:, None] * theta ** (-2.0 * np.arange(width // 2) / width)[None, :]
    angles = np.concatenate([np.cos(angles), np.sin(angles)], axis=1).astype(np.float32)
    head_picks = jnp.concatenate([value_pick[:, 0], output_pick[:, 0] + experts], axis=1)
    gains = jnp.stack([attend_gain, expert_gain]).astype(f32)
    results = layer_call(
        n_dp,
        n_head,
        (
            hidden_in,
            cotangent,
            expert_pick,
            head_picks,
            segments[None, :],
            gains,
            angles,
            query_weight[0],
            key_weight[0],
            jnp.pad(head_router[0], ((0, 0), (0, width - 2 * experts))),
            value_weight[0],
            output_weight[0],
            jnp.pad(router, ((0, 0), (0, width - router.shape[1]))),
            expert_in,
            expert_out.reshape(per_device * width, features),
        ),
    )
    shapes = (
        (tokens, features),
        (tokens, features),
        (1, features),
        query_weight.shape[1:],
        key_weight.shape[1:],
        value_weight.shape[1:],
        output_weight.shape[1:],
        head_router.shape[1:],
        (1, features),
        router.shape,
        expert_in.shape,
        expert_out.shape,
    )
    done = list(finish_call(n_dp, n_head, shapes, (*results, gains)))
    for number in (3, 4, 5, 6, 7):
        done[number] = done[number][None]
    done[2], done[8] = done[2][0], done[8][0]
    return tuple(done)


def solution(mesh):
    rows = P(everywhere, None)
    heads = P("head", None, None)
    experts = P(everywhere, None, None)
    picks = P("dp", "head", None)
    in_specs = (
        rows, P("dp"), picks, picks, rows, P(), heads, heads, heads, heads, heads,
        P(), P(), experts, experts, rows,
    )
    out_specs = (
        rows, rows, P(), heads, heads, heads, heads, heads, P(), P(), experts, experts,
    )
    n_dp, n_head = mesh.shape["dp"], mesh.shape["head"]

    def program(*args):
        held = 2 * n_dp * args[13].shape[0] * args[13].shape[1] * args[13].shape[2] * 2
        if n_head == 4 and held <= vmem_for_weights:
            return kernel_body(n_dp, n_head, *args)
        return body(*args)

    return jax.shard_map(program, mesh=mesh, in_specs=in_specs, out_specs=out_specs, check_vma=False)
```

```python
import functools

import jax
import jax.numpy as jnp
import numpy as np
from jax import lax
from jax.experimental import pallas as pl
from jax.experimental.pallas import tpu as pltpu
from jax.sharding import PartitionSpec as P

epsilon = 1e-06
theta = 10000.0
negative = -1e30
f32 = jnp.float32
bf16 = jnp.bfloat16
everywhere = ("dp", "head")
whole_rows = 4096
vmem_for_weights = 16 << 20
vmem_bytes = 62 << 20


def product(left, right, left_axis, right_axis):
    return lax.dot_general(
        left, right, (((left_axis,), (right_axis,)), ((), ())), preferred_element_type=f32
    )


def rms_scale(residual):
    return lax.rsqrt(jnp.mean(residual * residual, axis=-1, keepdims=True) + epsilon)


def rotary_tables(row_count, head_width):
    half_width = head_width // 2
    position = jnp.arange(row_count, dtype=f32)[:, None]
    exponent = jnp.arange(half_width, dtype=f32)[None, :]
    angles = position * jnp.power(theta, -2.0 * exponent / head_width)
    return (jnp.cos(angles), jnp.sin(angles))


def rotate(matrix, cosine, sine):
    half = matrix.shape[-1] // 2
    first, second = matrix[:, :half], matrix[:, half:]
    return jnp.concatenate([first * cosine - second * sine, second * cosine + first * sine], axis=-1)


def pick_mask(picks, expert_count):
    hits = picks[:, 0, :, None] == jnp.arange(expert_count, dtype=jnp.int32)[None, None, :]
    return jnp.any(hits, axis=1).astype(f32)


def norm_back(residual, inverse, gain, incoming):
    unit_rows = residual * inverse
    scaled = incoming * gain
    gain_grad = jnp.sum(incoming * unit_rows, axis=0)
    row_grad = inverse * (scaled - unit_rows * jnp.mean(scaled * unit_rows, axis=-1, keepdims=True))
    return (row_grad, gain_grad)


def gelu_pair(value):
    inner = jnp.tanh(0.7978845608028654 * (value + 0.044715 * value * value * value))
    slope = 0.5 * (1.0 + inner) + 0.5 * value * (1.0 - inner * inner) * 0.7978845608028654 * (
        1.0 + 3.0 * 0.044715 * value * value
    )
    return (0.5 * value * (1.0 + inner), slope)


def body(
    hidden_in,
    segments,
    value_pick,
    output_pick,
    expert_pick,
    attend_gain,
    query_weight,
    key_weight,
    value_weight,
    output_weight,
    head_router,
    expert_gain,
    router,
    expert_in,
    expert_out,
    cotangent,
):
    tokens, features = hidden_in.shape
    per_device, _, width = expert_in.shape
    head_experts = head_router.shape[2] // 2
    head_width = query_weight.shape[2]
    scale = head_width ** (-0.5)
    query_mat, key_mat, value_mat = query_weight[0], key_weight[0], value_weight[0]
    output_mat, gate_mat = output_weight[0], head_router[0]
    value_mask = pick_mask(value_pick, head_experts)
    output_mask = pick_mask(output_pick, head_experts)
    attend_scale = attend_gain.astype(f32)
    expert_scale = expert_gain.astype(f32)
    me = lax.axis_index("dp") * lax.axis_size("head") + lax.axis_index("head")

    rows = lax.all_gather(hidden_in, "head", axis=0, tiled=True)
    grouped = rows.astype(f32)
    group = grouped.shape[0]
    inverse = rms_scale(grouped)
    normed = (grouped * inverse * attend_scale).astype(bf16)
    cosine, sine = rotary_tables(group, head_width)
    queries = rotate(product(normed, query_mat, 1, 0), cosine, sine).astype(bf16)
    key_rows = rotate(product(normed, key_mat, 1, 0), cosine, sine).astype(bf16)
    squash = jax.nn.sigmoid(product(normed, gate_mat, 1, 0))
    value_gates = squash[:, :head_experts] * value_mask
    output_gates = squash[:, head_experts:] * output_mask
    expert_values = product(rows, value_mat, 1, 0).reshape(group, head_experts, head_width)
    values = jnp.sum(expert_values * value_gates[:, :, None], axis=1).astype(bf16)
    places = jnp.arange(group, dtype=jnp.int32)
    allowed = (places[None, :] <= places[:, None]) & (segments[:, None] == segments[None, :])
    scores = jnp.where(allowed, product(queries, key_rows, 1, 1) * scale, negative)
    exponents = jnp.exp(scores - jnp.max(scores, axis=-1, keepdims=True))
    probabilities = exponents / jnp.sum(exponents, axis=-1, keepdims=True)
    attended = product(probabilities.astype(bf16), values, 1, 0)
    weighted = (
        (output_gates[:, :, None] * attended[:, None, :]).reshape(group, -1).astype(bf16)
    )
    middle = hidden_in.astype(f32) + lax.psum_scatter(
        product(weighted, output_mat, 1, 0).astype(bf16), "head", scatter_dimension=0, tiled=True
    ).astype(f32)
    middle_inverse = rms_scale(middle)
    middle_normed = (middle * middle_inverse * expert_scale).astype(bf16)
    mine = me * per_device + jnp.arange(per_device, dtype=jnp.int32)
    my_router = lax.dynamic_slice_in_dim(router, me * per_device, per_device, axis=1)
    in_mat = expert_in.transpose(1, 0, 2).reshape(features, per_device * width)
    out_mat = expert_out.reshape(per_device * width, features)

    def turn(running, own):
        own_rows, own_cot, own_picks = own
        all_cot = lax.all_gather(own_cot, everywhere, axis=0, tiled=True)
        all_picks = lax.all_gather(own_picks, everywhere, axis=0, tiled=True)
        all_rows = lax.all_gather(own_rows, everywhere, axis=0, tiled=True)
        mask = jnp.any(all_picks[:, :, None] == mine[None, None, :], axis=1).astype(f32)
        gates = jax.nn.sigmoid(product(all_rows, my_router, 1, 0))
        live = gates * mask
        act, slope = gelu_pair(product(all_rows, in_mat, 1, 0).reshape(-1, per_device, width))
        lifted = product(all_cot, out_mat, 1, 1).reshape(-1, per_device, width)
        dense_grad = (jnp.sum(act * lifted, axis=-1) * live * (1.0 - gates)).astype(bf16)
        act_live = (act * live[:, :, None]).astype(bf16).reshape(-1, per_device * width)
        hidden_grad = (slope * lifted * live[:, :, None]).astype(bf16)
        hidden_grad = hidden_grad.reshape(-1, per_device * width)
        part_out = product(act_live, out_mat, 1, 0).astype(bf16)
        part_grad = (
            product(hidden_grad, in_mat, 1, 1) + product(dense_grad, my_router, 1, 1)
        ).astype(bf16)
        back = lax.psum_scatter(part_grad, everywhere, scatter_dimension=0, tiled=True)
        forth = lax.psum_scatter(part_out, everywhere, scatter_dimension=0, tiled=True)
        grads = (
            product(all_rows, hidden_grad, 0, 0),
            product(act_live, all_cot, 0, 0),
            product(dense_grad, all_rows, 0, 0),
        )
        if running is not None:
            grads = jax.tree.map(jnp.add, running, grads)
        return grads, (forth, back)

    turns = max(1, lax.axis_size("dp") * lax.axis_size("head") * tokens // whole_rows)
    owned = (middle_normed, cotangent, expert_pick)
    if turns == 1:
        grads, (summed, normed_grad) = turn(None, owned)
    else:
        owned = jax.tree.map(lambda a: a.reshape(turns, -1, a.shape[1]), owned)
        zeros = (
            jnp.zeros(in_mat.shape, f32),
            jnp.zeros(out_mat.shape, f32),
            jnp.zeros((per_device, features), f32),
        )
        grads, sums = lax.scan(turn, zeros, owned)
        summed, normed_grad = (a.reshape(tokens, features) for a in sums)
    grad_in = grads[0].reshape(features, per_device, width).transpose(1, 0, 2)
    grad_out = grads[1].reshape(per_device, width, features)
    grad_router = lax.all_gather(grads[2], everywhere, axis=0, tiled=True).T
    output = middle + summed.astype(f32)
    incoming = cotangent.astype(f32)
    row_grad, grad_gain_expert = norm_back(
        middle, middle_inverse, expert_scale, normed_grad.astype(f32)
    )
    middle_grad = incoming + row_grad
    group_grads = lax.all_gather(middle_grad.astype(bf16), "head", axis=0, tiled=True)
    weighted_grad = product(group_grads, output_mat, 1, 1).reshape(group, head_experts, head_width)
    output_grad = product(weighted, group_grads, 0, 0)
    output_gate_grad = jnp.sum(weighted_grad * attended[:, None, :], axis=-1)
    attended_grad = jnp.sum(weighted_grad * output_gates[:, :, None], axis=1).astype(bf16)
    prob_grad = product(attended_grad, values, 1, 1)
    centre = jnp.sum(probabilities * prob_grad, axis=-1, keepdims=True)
    score_grad = (probabilities * (prob_grad - centre)).astype(bf16)
    query_grad = product(score_grad, key_rows, 1, 0) * scale
    key_grad = product(score_grad, queries, 0, 0) * scale
    values_grad = product(probabilities.astype(bf16), attended_grad, 0, 0)
    expert_grad = (value_gates[:, :, None] * values_grad[:, None, :]).reshape(group, -1).astype(bf16)
    value_gate_grad = jnp.sum(expert_values * values_grad[:, None, :], axis=-1)
    query_grad = rotate(query_grad, cosine, -sine).astype(bf16)
    key_grad = rotate(key_grad, cosine, -sine).astype(bf16)
    logit_grad = (
        jnp.concatenate([value_gate_grad * value_mask, output_gate_grad * output_mask], axis=1)
        * squash
        * (1.0 - squash)
    ).astype(bf16)
    head_grads = (
        product(normed, query_grad, 0, 0),
        product(normed, key_grad, 0, 0),
        product(rows, expert_grad, 0, 0),
        output_grad,
        product(normed, logit_grad, 0, 0),
    )
    head_grads = tuple(grad.astype(bf16) for grad in head_grads)
    head_grads = tuple(grad.astype(f32)[None] for grad in lax.psum(head_grads, "dp"))
    back = (
        product(query_grad, query_mat, 1, 1)
        + product(key_grad, key_mat, 1, 1)
        + product(logit_grad, gate_mat, 1, 1)
    )
    row_back, grad_attend = norm_back(grouped, inverse, attend_scale, back)
    partial = (row_back + product(expert_grad, value_mat, 1, 1)).astype(bf16)
    input_grad = middle_grad + lax.psum_scatter(
        partial, "head", scatter_dimension=0, tiled=True
    ).astype(f32)
    grad_attend, grad_gain_expert = lax.psum((grad_attend, grad_gain_expert), everywhere)
    return (
        output,
        input_grad,
        grad_attend,
        *head_grads,
        grad_gain_expert,
        grad_router,
        grad_in,
        grad_out,
    )


MESH = pl.DeviceIdType.MESH
VM = pl.BlockSpec(memory_space=pltpu.VMEM)
ANY = pl.BlockSpec(memory_space=pl.ANY)
NN = (((1,), (0,)), ((), ()))
NT = (((1,), (1,)), ((), ()))
TN = (((0,), (0,)), ((), ()))


def dot(left, right, dims=NN):
    return lax.dot_general(left, right, dims, preferred_element_type=f32)


def at_block(block, count):
    return pl.ds(pl.multiple_of(block * count, count), count)


def remote(src, dst, send, recv, where):
    return pltpu.make_async_remote_copy(
        src_ref=src, dst_ref=dst, send_sem=send, recv_sem=recv, device_id=where, device_id_type=MESH
    )


def swap_halves(value):
    half = value.shape[-1] // 2
    return jnp.concatenate([value[:, half:], value[:, :half]], axis=-1)


def ceil_to(number, step):
    return -(-number // step) * step


def layer_kernel(
    n_dp,
    n_head,
    x_ref,
    cot_ref,
    pick_ref,
    value_pick_ref,
    output_pick_ref,
    seg_ref,
    gain_ref,
    angle_ref,
    wq_ref,
    wk_ref,
    wg_ref,
    wv_ref,
    wo_ref,
    router_ref,
    in_ref,
    out_ref,
    output_ref,
    grad_x_ref,
    wide_ref,
    fin_in_ref,
    fin_out_ref,
    picks,
    two_picks,
    head_picks,
    w_g,
    w_r,
    seg,
    gains,
    angles,
    w_an,
    w_v,
    w_o,
    my_router,
    w_in,
    w_out,
    rows,
    cot,
    mrs,
    das,
    turned,
    my_mask,
    all_mask,
    gates,
    q,
    k,
    v,
    vx,
    att,
    part,
    got,
    outs,
    got_out,
    lifted,
    core_out,
    acts,
    hids,
    dzs,
    datt,
    gate_grads,
    probs,
    scores,
    qkz,
    vgrads,
    gain_part,
    gain_got,
    sums,
    core_got,
    chip_got,
    piece,
    blocks,
    hop_in,
    hop_out,
    local_sem,
    z_send,
    z_recv,
    w_send,
    w_recv,
    c_send,
    c_recv,
    e_send,
    e_recv,
    s_send,
    s_recv,
    ready,
    free,
):
    middle = output_ref
    xor = jnp.bitwise_xor
    d, h = lax.axis_index("dp"), lax.axis_index("head")
    chip, core = d // 2, d % 2
    chips = n_dp // 2
    tokens, features = x_ref.shape
    per_device, _, width = in_ref.shape
    slab = per_device * width
    wide = 2 * slab
    experts = wv_ref.shape[1] // width
    named = ceil_to(n_dp * per_device, 8)
    group = tokens * n_head
    pair = 2 * tokens
    column = 256
    lanes = 128
    scale = width ** (-0.5)
    peers = (2, 3, 1)
    partner = (chip * 2 + 1 - core, h)
    own_block = at_block(h, tokens)
    own_side, other_side = at_block(core, slab), at_block(1 - core, slab)
    halves_in = (pl.ds(0, features // 2), pl.ds(features // 2, features // 2))
    halves_out = lambda side: (
        at_block(2 * side, slab // 2),
        at_block(2 * side + 1, slab // 2),
    )

    def along(step):
        return (d, xor(h, step))

    def across(step):
        return (xor(chip, step) * 2 + core, h)

    loads = []

    def load(src, dst):
        copy = pltpu.make_async_copy(src, dst, local_sem.at[len(loads)])
        copy.start()
        loads.append(copy)
        return copy

    own_weights = [load(out_ref, w_out.at[chip, own_side, :])] + [
        load(in_ref.at[e], w_in.at[chip, :, at_block(core * per_device + e, width)])
        for e in range(per_device)
    ]
    for_rows = [
        load(x_ref, rows.at[own_block, :]),
        load(gain_ref, gains),
        load(wg_ref, w_g),
        load(wq_ref, w_an.at[:, pl.ds(0, width)]),
        load(wk_ref, w_an.at[:, pl.ds(width, width)]),
        load(wv_ref, w_v),
        load(value_pick_ref, two_picks.at[0]),
        load(output_pick_ref, two_picks.at[1]),
        load(angle_ref, angles),
    ]
    for_scores = [load(seg_ref, seg), load(wo_ref, w_o)]
    for_mask = load(pick_ref, picks)
    for_cot = load(cot_ref, cot.at[own_block, :])
    for_router = load(router_ref, w_r)

    barrier = pltpu.get_barrier_semaphore()
    friends = [along(s) for s in peers] + [partner] + [across(s) for s in range(1, chips)]
    for friend in friends:
        pl.semaphore_signal(barrier, inc=1, device_id=friend, device_id_type=MESH)
    pl.semaphore_wait(barrier, len(friends))

    right, left = (d, jnp.minimum(h + 1, n_head - 1)), (d, jnp.maximum(h - 1, 0))
    last = n_head - 1

    def pick(*by_place):
        value = jnp.int32(by_place[-1])
        for place in range(n_head - 2, -1, -1):
            value = jnp.where(h == place, by_place[place], value)
        return value

    arrival = (xor(h, 1), pick(2, 2, 1, 1), pick(3, 3, 0, 0))
    leaving = (pick(3, 3, 0, 0), pick(2, 0, 3, 1), pick(1, 2, 1, 2))

    def gather(kind, buffer):
        def go(side, step):
            block = jnp.clip(h - step if side == 0 else h + step, 0, last)
            here = buffer.at[at_block(block, tokens), :]
            number = side * last + step
            return remote(
                here, here, z_send.at[kind, number], z_recv.at[kind, number], (right, left)[side]
            )

        def start():
            @pl.when(h < last)
            def _():
                go(0, 0).start()

            @pl.when(h > 0)
            def _():
                go(1, 0).start()

        def stage(step):
            @pl.when(h >= step)
            def _():
                go(0, step - 1).wait_recv()

            if step < last:

                @pl.when((h >= step) & (h < last))
                def _():
                    go(0, step).start()

            @pl.when(h + step <= last)
            def _():
                go(1, step - 1).wait_recv()

            if step < last:

                @pl.when((h + step <= last) & (h > 0))
                def _():
                    go(1, step).start()

        def follow(step):
            @pl.when((h < last) & (jnp.maximum(h, 1) == step))
            def _():
                go(0, 0).start()

            @pl.when((h > 0) & (jnp.maximum(last - h, 1) == step))
            def _():
                go(1, 0).start()

        def end():
            for step in range(last):

                @pl.when((h >= step) & (h < last))
                def _():
                    go(0, step).wait_send()

                @pl.when((h + step <= last) & (h > 0))
                def _():
                    go(1, step).wait_send()

        return start, stage, end, follow

    def chain_sum(kind, parts, slots):
        def go(number):
            block = leaving[number]
            rightward = block > h
            slot = jnp.where(rightward, block - 1, last + block)
            where = (d, jnp.clip(jnp.where(rightward, h + 1, h - 1), 0, last))
            at = at_block(block, tokens)
            copy = remote(
                parts.at[at, :], slots.at[slot], z_send.at[kind, number], z_recv.at[kind, slot], where
            )
            middle_one = (rightward & (h > 0)) | (jnp.logical_not(rightward) & (h < last))
            return copy, middle_one, at, slot

        def now(number):
            copy, middle_one, _, _ = go(number)

            @pl.when(jnp.logical_not(middle_one))
            def _():
                copy.start()

        def later(number):
            copy, middle_one, at, slot = go(number)

            @pl.when(middle_one)
            def _():
                copy.wait_recv()
                parts[at, :] = parts[at, :] + slots[slot]
                copy.start()

        def end(total):
            for slot, there in ((jnp.maximum(h - 1, 0), h > 0), (last + jnp.minimum(h, last - 1), h < last)):

                @pl.when(there)
                def _():
                    remote(
                        parts.at[own_block, :], slots.at[slot], z_send.at[kind, 0], z_recv.at[kind, slot], right
                    ).wait_recv()
                    total[...] += slots[slot].astype(f32)

            for number in range(last):
                go(number)[0].wait_send()

        return now, later, end

    def spread(kind, src, dst, steps=peers):
        copies = {}
        for step in steps:
            copies[step] = remote(
                src(step), dst(step), z_send.at[kind, step - 1], z_recv.at[kind, step - 1], along(step)
            )
            copies[step].start()
        return copies

    x_start, x_stage, x_end, _ = gather(0, rows)
    for_rows[0].wait()
    x_start()

    def slot(array, place, side, half=None):
        if array == 0:
            at = halves_out(side)[half] if half is not None else at_block(side, slab)
            return w_out.at[place, at, :]
        at = halves_in[half] if half is not None else pl.ds(0, features)
        return w_in.at[place, at, at_block(side, slab)]

    def weights(number, ref, where):
        copy = remote(ref, ref, w_send.at[number], w_recv.at[number], where)
        copy.start()
        return copy

    slabs, halves_on, to_core, diagonal = {}, {}, {}, {}
    for copy in own_weights:
        copy.wait()
    for array in range(2):
        for first in range(2):
            for bit in (1, 2):
                half = bit - 1 if first == 0 else 2 - bit
                number = ((bit - 1) * 2 + half) * 2 + array
                slabs[bit, half, array] = weights(
                    number, slot(array, chip, core, half), across(bit)
                )
        to_core[0, array] = weights(12 + array, slot(array, chip, core), partner)

    for_mask.wait()
    own_picks = jnp.concatenate(
        [picks[...].astype(f32), jnp.zeros((lanes - picks.shape[0], tokens), f32)], axis=0
    ).T.astype(jnp.int32)
    lane = lax.broadcasted_iota(jnp.int32, (tokens, lanes), 1)
    for plane in range(n_head):
        expert = (lane // per_device * n_head + plane) * per_device + lane % per_device
        expert = jnp.where(lane < n_dp * per_device, expert, -1)
        hit = own_picks[:, 0:1] == expert
        for c in range(1, picks.shape[0]):
            hit = hit | (own_picks[:, c : c + 1] == expert)
        my_mask[plane] = jnp.where(hit, 1.0, 0.0).astype(bf16)
    mask_copies = spread(1, lambda s: my_mask.at[xor(h, s)], lambda s: all_mask.at[own_block, :])
    all_mask[own_block, :] = my_mask[h]

    for copy in for_rows[1:]:
        copy.wait()
    attend_gain = gains[0:1, :]
    expert_gain = gains[1:2, :]
    one_hot = lambda count: jnp.where(
        lax.broadcasted_iota(jnp.int32, (count, width), 0)
        == lax.broadcasted_iota(jnp.int32, (count, width), 1),
        1.0,
        0.0,
    ).astype(bf16)
    w_an[:, pl.ds(2 * width, width)] = dot(w_g[...], one_hot(w_g.shape[0]), TN).astype(bf16)
    uses = two_picks.shape[1]
    head_picks[...] = jnp.concatenate(
        [
            two_picks[0].astype(f32),
            two_picks[1].astype(f32) + experts,
            jnp.zeros((lanes - 2 * uses, group), f32),
        ],
        axis=0,
    ).T.astype(jnp.int32)
    half_lanes = lax.broadcasted_iota(jnp.int32, (1, width), 1) < width // 2

    def turns(at):
        both = angles[at, :]
        turned_over = swap_halves(both)
        return (
            jnp.where(half_lanes, both, turned_over),
            jnp.where(half_lanes, -turned_over, both),
        )

    def project(block):
        at = at_block(block, tokens)
        own = rows[at, :]
        full = own.astype(f32)
        inverse = lax.rsqrt(jnp.mean(full * full, axis=-1, keepdims=True) + epsilon)
        unit = (full * inverse * attend_gain).astype(bf16)
        qkg = dot(unit, w_an[...])
        c, s = turns(at)
        one, two = qkg[:, :width], qkg[:, width : 2 * width]
        q[at, :] = (one * c + swap_halves(one) * s).astype(bf16)
        k[at, :] = (two * c + swap_halves(two) * s).astype(bf16)
        lane = lax.broadcasted_iota(jnp.int32, (tokens, width), 1)
        chosen = head_picks[at, :]
        hit = lane == chosen[:, 0:1]
        for c in range(1, 2 * uses):
            hit = hit | (lane == chosen[:, c : c + 1])
        gate = jnp.where(hit, jax.nn.sigmoid(qkg[:, 2 * width :]), 0.0)
        gates[at, :] = jnp.where(lane == width - 1, inverse, gate)
        values = dot(own, w_v[...])
        vx[at, :] = values.astype(bf16)
        value = gate[:, 0:1] * values[:, :width]
        for e in range(1, experts):
            value += gate[:, e : e + 1] * values[:, e * width : (e + 1) * width]
        v[at, :] = value.astype(bf16)

    project(h)
    _, cot_stage, cot_end, cot_follow = gather(2, cot)
    for_cot.wait()
    for step in (1, 2, 3):
        x_stage(step)
        cot_follow(step)
        project(arrival[step - 1])
    for copy in for_scores:
        copy.wait()
    seg_col = gate_grads
    seg_col[...] = jnp.broadcast_to(seg[...].astype(f32), (lanes, group)).T

    def attend(block):
        at = at_block(block, tokens)
        score = dot(q[at, :], k[...], NT) * scale
        row = block * tokens + lax.broadcasted_iota(jnp.int32, (tokens, group), 0)
        place = lax.broadcasted_iota(jnp.int32, (tokens, group), 1)
        allowed = (place <= row) & (seg_col[at, 0:1] == seg[...].astype(f32))
        score = jnp.where(allowed, score, negative)
        exponents = jnp.exp(score - jnp.max(score, axis=-1, keepdims=True))
        chance = exponents / jnp.sum(exponents, axis=-1, keepdims=True)
        probs[at, :] = chance.astype(bf16)
        attended = dot(chance.astype(bf16), v[...])
        att[at, :] = attended
        gate = gates[at, :]
        weighted = jnp.concatenate(
            [
                (gate[:, experts + e : experts + e + 1] * attended).astype(bf16)
                for e in range(experts)
            ],
            axis=-1,
        )
        return dot(weighted, w_o[...])

    to_mid = chain_sum(3, part, got)
    for number in range(last):
        block = leaving[number]
        part[at_block(block, tokens), :] = attend(block).astype(bf16)
        to_mid[0](number)
    middle[...] = rows[own_block, :].astype(f32) + attend(h)
    cot_stage(1)
    to_mid[1](0)
    for half in range(2):
        for array in range(2):
            slabs[1 + half, half, array].wait_recv()
            halves_on[half, array] = weights(
                8 + 2 * half + array,
                slot(array, xor(chip, 1 + half), core, half),
                across(2 - half),
            )

    to_mid[1](1)
    cot_stage(2)
    to_mid[1](2)
    cot_stage(3)
    for bit in (1, 2):
        slabs[bit, 2 - bit, 0].wait_recv()
        to_core[bit, 0] = weights(14 + (bit - 1) * 2, slot(0, xor(chip, bit), core), partner)
        slabs[bit, 2 - bit, 1].wait_recv()
        to_core[bit, 1] = weights(15 + (bit - 1) * 2, slot(1, xor(chip, bit), core), partner)
    for_router.wait()
    slot_of = lax.broadcasted_iota(jnp.int32, (w_r.shape[0], lanes), 1)
    name = lax.broadcasted_iota(jnp.int32, (w_r.shape[0], lanes), 0)
    expert = (slot_of // per_device * n_head + h) * per_device + slot_of % per_device
    expert = jnp.where(slot_of < n_dp * per_device, expert, -1)
    my_router[...] = dot(
        w_r[...], jnp.where(name == expert, 1.0, 0.0).astype(bf16), TN
    ).astype(bf16)

    to_mid[2](middle)
    mid = middle[...]
    inverse = lax.rsqrt(jnp.mean(mid * mid, axis=-1, keepdims=True) + epsilon)
    mrs[own_block, :] = (mid * inverse * expert_gain).astype(bf16)
    mr_start, mr_stage, mr_end, _ = gather(4, mrs)
    mr_start()

    for array in range(2):
        for half in range(2):
            halves_on[half, array].wait_recv()
            diagonal[half, array] = weights(
                18 + 2 * half + array, slot(array, xor(chip, 3), core, half), partner
            )
    for step in peers:
        mask_copies[step].wait()
    cot_end()
    x_end()

    def weights_here(array):
        for bit in range(3):
            to_core[bit, array].wait()
        for half in range(2):
            diagonal[half, array].wait()
            halves_on[half, array].wait_send()
            for bit in (1, 2):
                slabs[bit, half, array].wait_send()

    weights_here(0)

    def lift_chip(j):
        lift = dot(cot[...], w_out[j], NT)
        lifted[j, 0] = lift[:, :slab].astype(bf16)
        lifted[j, 1] = lift[:, slab:].astype(bf16)

    pl.loop(0, chips // 2)(lift_chip)
    mr_stage(1)
    pl.loop(chips // 2, chips)(lift_chip)

    weights_here(1)

    def spread_lanes(j):
        lane = lax.broadcasted_iota(jnp.int32, (lanes, wide), 1) // width
        slot = lax.broadcasted_iota(jnp.int32, (lanes, wide), 0)
        return jnp.where(slot == lane + j * (wide // width), 1.0, 0.0).astype(bf16)

    def pair_of_blocks(number, between):
        at = at_block(number, pair)
        own = mrs[at, :]
        gates = jax.nn.sigmoid(dot(own, my_router[...]))
        live = gates * all_mask[at, :].astype(f32)
        high = live.astype(bf16)
        low = (live - high.astype(f32)).astype(bf16)
        both = jnp.concatenate([high, low], axis=-1)

        def chip_step(j, total):
            pick = spread_lanes(j)
            hidden = dot(own, w_in[j])
            gate = dot(both, jnp.concatenate([pick, pick], axis=0))
            lift = jnp.concatenate([lifted[j, 0, at, :], lifted[j, 1, at, :]], axis=-1).astype(f32)
            square = hidden * hidden
            inner = jnp.tanh(0.7978845608028654 * hidden * (1.0 + 0.044715 * square))
            half = 0.5 * (1.0 + inner)
            act = hidden * half
            slope = half + act * (1.0 - inner) * (
                0.7978845608028654 + (0.7978845608028654 * 3.0 * 0.044715) * square
            )
            acts[j, at, :] = (act * gate).astype(bf16)
            hids[j, at, :] = (slope * (lift * gate)).astype(bf16)
            return total + dot((act * lift).astype(bf16), pick, NT)

        total = lax.fori_loop(0, chips, chip_step, jnp.zeros((pair, lanes), f32))
        dz = (total * live * (1.0 - gates)).astype(bf16)
        dzs[at, :] = dz
        between()

        @pl.loop(0, features // column)
        def _(c):
            part_of = at_block(c, column)
            total = dot(dz, my_router[part_of, :], NT)
            for j in range(chips):
                total += dot(hids[j, at, :], w_in[j, part_of, :], NT)
            part[at, part_of] = total.astype(bf16)

    def outputs(number):
        at = at_block(number, pair)

        @pl.loop(0, features // column)
        def _(c):
            part_of = at_block(c, column)
            total = dot(acts[0, at, :], w_out[0, :, part_of])
            for j in range(1, chips):
                total += dot(acts[j, at, :], w_out[j, :, part_of])
            outs[at, part_of] = total.astype(bf16)

    near = h // 2
    to_dmr = chain_sum(5, part, got)
    pair_of_blocks(near, lambda: mr_stage(2))
    to_dmr[0](2)
    outputs(near)
    mr_stage(3)
    pair_of_blocks(1 - near, lambda: None)
    to_dmr[0](0)
    to_dmr[0](1)
    outputs(1 - near)
    pl.semaphore_signal(ready, inc=1, device_id=partner, device_id_type=MESH)

    turned[...] = mrs[...].T

    def expert_grads(place, at):
        for half in halves_in:
            w_in[place, half, at] = dot(turned[half, :], hids[place, :, at]).astype(bf16)
            w_out[place, at, half] = dot(acts[place, :, at], cot[:, half], TN).astype(bf16)

    def to_other_core(n):
        place = xor(chip, chips - 1 - n)
        copies = [
            remote(
                w_in.at[place, halves_in[half], other_side],
                lifted.at[place, half],
                c_send.at[half, n],
                c_recv.at[half, n],
                partner,
            )
            for half in range(2)
        ]
        copies.append(
            remote(
                w_out.at[place, other_side, :],
                core_out.at[place],
                c_send.at[2, n],
                c_recv.at[2, n],
                partner,
            )
        )
        return copies

    pl.semaphore_wait(ready, 1)

    hops = {}

    def hop(half, index, place, toward):
        copies = (
            remote(
                slot(1, place, core, half),
                hop_in.at[half, index],
                e_send.at[0, 2 * half + index],
                e_recv.at[0, 2 * half + index],
                across(toward),
            ),
            remote(
                slot(0, place, core, half),
                hop_out.at[half, index],
                e_send.at[1, 2 * half + index],
                e_recv.at[1, 2 * half + index],
                across(toward),
            ),
        )
        for copy in copies:
            copy.start()
        hops[half, index] = copies

    def both_cores(n):
        step = chips - 1 - n
        place = xor(chip, step)
        for copy in to_other_core(n):
            copy.wait()
        for half in range(2):
            here = (place, halves_in[half], own_side)
            w_in[here] = w_in[here] + lifted[place, half]
        w_out[place, own_side, :] = w_out[place, own_side, :] + core_out[place]
        if step == 3:
            hop(0, 1, place, 1)
            hop(1, 1, place, 2)
        elif step:
            hop(step - 1, 0, place, step)

    for n in range(chips):
        place = xor(chip, chips - 1 - n)
        expert_grads(place, other_side)
        for copy in to_other_core(n):
            copy.start()
        if n:
            both_cores(n - 1)
        expert_grads(place, own_side)
    to_dmr[1](0)
    both_cores(chips - 1)
    to_dmr[1](1)
    to_dmr[1](2)
    side = features // 2
    strip = side // chips

    def section(number, first, count):
        at = pl.ds(first, count)
        col = lambda c, j: at_block(c * chips + j, strip)
        state = {}

        def sem(n):
            return s_send.at[number, n], s_recv.at[number, n]

        def start():
            state["core"] = remote(
                sums.at[at, at_block(1 - core, side)], core_got.at[at, :], *sem(0), partner
            )
            state["core"].start()

        def mid():
            state["core"].wait()
            half = at_block(core, side)
            sums[at, half] = sums[at, half] + core_got[at, :]
            state["chips"] = []
            for s in range(1, chips):
                copy = remote(
                    sums.at[at, col(core, xor(chip, s))], chip_got.at[s - 1, at, :], *sem(s), across(s)
                )
                copy.start()
                state["chips"].append(copy)

        def add():
            for copy in state["chips"]:
                copy.wait()
            total = sums[at, col(core, chip)].astype(f32)
            for s in range(1, chips):
                total += chip_got[s - 1, at, :].astype(f32)
            piece[at, :] = total.astype(bf16)

        def share(src=None, rows_to=at):
            src = piece.at[at, :] if src is None else src
            state["rows"] = rows_to
            here = wide_ref.at[rows_to, col(core, chip)]
            state["share"] = []
            for s in range(1, chips):
                copy = remote(src, here, *sem(chips + s), across(s))
                copy.start()
                state["share"].append(copy)
            over = remote(src, here, *sem(chips), partner)
            own = pltpu.make_async_copy(src, here, s_send.at[number, 3 * chips - 1])
            over.start()
            own.start()
            state["wait"] = [over, own]

        def forward():
            for s in range(1, chips):
                state["share"][s - 1].wait()
                here = wide_ref.at[state["rows"], col(core, xor(chip, s))]
                copy = remote(here, here, *sem(2 * chips - 1 + s), partner)
                copy.start()
                state["wait"].append(copy)

        def end():
            for copy in state["wait"]:
                copy.wait()

        return start, mid, add, share, forward, end

    top = features + w_o.shape[0]
    small = ceil_to(named + 1, 16)
    of_o = section(0, features, w_o.shape[0])
    of_d = section(1, 0, features)
    of_g = section(2, top + 16, small)
    of_a = section(3, top, 16)
    router_part = dot(dzs[...], mrs[...], TN)[:named]

    grad_x_ref[...] = part[own_block, :].astype(f32)
    to_dmr[2](grad_x_ref)
    incoming = grad_x_ref[...]
    mid = middle[...]
    inverse = lax.rsqrt(jnp.mean(mid * mid, axis=-1, keepdims=True) + epsilon)
    unit = mid * inverse
    scaled = incoming * expert_gain
    dmid = cot[own_block, :].astype(f32) + inverse * (
        scaled - unit * jnp.mean(scaled * unit, axis=-1, keepdims=True)
    )
    grad_x_ref[...] = dmid
    das[own_block, :] = dmid.astype(bf16)
    da_start, da_stage, da_end, _ = gather(6, das)
    da_start()
    sums[pl.ds(top + 16, small), :] = jnp.concatenate(
        [
            router_part,
            jnp.sum(incoming * unit, axis=0, keepdims=True),
            jnp.zeros((small - named - 1, features), f32),
        ],
        axis=0,
    ).astype(bf16)
    of_g[0]()
    turned[...] = rows[...].T
    of_g[1]()
    lane = lax.broadcasted_iota(jnp.int32, (tokens, width), 1)

    def through_output(block):
        at = at_block(block, tokens)
        all_five = dot(das[at, :], w_o[...], NT)
        attended = att[at, :]
        total = jnp.zeros((tokens, width), f32)
        gate = jnp.zeros((tokens, width), f32)
        for e in range(experts):
            one = all_five[:, e * width : (e + 1) * width]
            total += gates[at, experts + e : experts + e + 1] * one
            gate = jnp.where(
                lane == experts + e, jnp.sum(one * attended, axis=-1, keepdims=True), gate
            )
        datt[at, :] = total.astype(bf16)
        gate_grads[at, :] = gate

    through_output(h)
    to_out = chain_sum(7, outs, got_out)
    for step in (1, 2, 3):
        da_stage(step)
        if step == 1:
            for number in range(last):
                to_out[0](number)
        through_output(arrival[step - 1])

    for e in range(experts):
        one = (gates[:, experts + e : experts + e + 1] * att[...]).astype(bf16)
        sums[pl.ds(features + e * width, width), :] = dot(one, das[...], TN).astype(bf16)
    of_o[0]()
    to_out[1](0)

    @pl.loop(0, n_head)
    def _(block):
        at = at_block(block, tokens)
        chance = probs[at, :].astype(f32)
        dprob = dot(datt[at, :], v[...], NT)
        centre = jnp.sum(chance * dprob, axis=-1, keepdims=True)
        scores[at, :] = (chance * (dprob - centre)).astype(bf16)

    dq = dot(scores[...], k[...]) * scale
    dk = dot(scores[...], q[...], TN) * scale
    dv = dot(probs[...], datt[...], TN)
    of_o[1]()
    to_out[1](1)
    c, s = turns(slice(None))
    qkz[:, pl.ds(0, width)] = (dq * c - swap_halves(dq) * s).astype(bf16)
    qkz[:, pl.ds(width, width)] = (dk * c - swap_halves(dk) * s).astype(bf16)
    gate = gate_grads[...]
    lane = lax.broadcasted_iota(jnp.int32, (group, width), 1)
    for e in range(experts):
        vgrads[:, pl.ds(e * width, width)] = (gates[:, e : e + 1] * dv).astype(bf16)
        one = jnp.sum(vx[:, pl.ds(e * width, width)].astype(f32) * dv, axis=-1, keepdims=True)
        gate = jnp.where(lane == e, one, gate)
    qkz[:, pl.ds(2 * width, width)] = (gate * gates[...] * (1.0 - gates[...])).astype(bf16)

    scaled_qkz = (qkz[...].astype(f32) * gates[:, width - 1 : width]).astype(bf16)

    @pl.loop(0, features // column)
    def _(c):
        at = at_block(c, column)
        sums[at, pl.ds(0, 3 * width)] = dot(turned[at, :], scaled_qkz).astype(bf16)
        sums[at, pl.ds(3 * width, experts * width)] = dot(turned[at, :], vgrads[...]).astype(bf16)

    of_d[0]()

    to_out[1](2)
    def into_rows(block):
        at = at_block(block, tokens)
        inverse = gates[at, width - 1 : width]
        unit = rows[at, :].astype(f32) * inverse
        through = dot(qkz[at, :], w_an[...], NT)
        scaled = through * attend_gain
        total = inverse * (
            scaled - unit * jnp.mean(scaled * unit, axis=-1, keepdims=True)
        ) + dot(vgrads[at, :], w_v[...], NT)
        return total, jnp.sum(through * unit, axis=0, keepdims=True)

    to_x = chain_sum(8, part, got)
    gain = jnp.zeros((1, features), f32)
    for number in range(last):
        total, one = into_rows(leaving[number])
        gain += one
        part[at_block(leaving[number], tokens), :] = total.astype(bf16)
        to_x[0](number)
    total, one = into_rows(h)
    gain_part[...] = jnp.broadcast_to(gain + one, gain_part.shape)
    gain_copies = spread(9, lambda s: gain_part, lambda s: gain_got.at[s - 1])
    grad_x_ref[...] += total
    of_d[1]()
    lasts = {}
    for half in range(2):
        toward = 2 - half
        for index, place in ((1, xor(chip, toward)), (0, chip)):
            for copy in hops[half, index]:
                copy.wait()
            at_in = (place, halves_in[half], own_side)
            at_out = (place, halves_out(core)[half], slice(None))
            w_in[at_in] = w_in[at_in] + hop_in[half, index]
            w_out[at_out] = w_out[at_out] + hop_out[half, index]
            if index:
                pl.semaphore_signal(
                    free.at[half], inc=1, device_id=across(toward), device_id_type=MESH
                )
                pl.semaphore_wait(free.at[half], 1)
                lasts[half] = (
                    remote(
                        w_in.at[at_in],
                        hop_in.at[half, 1],
                        e_send.at[0, 4 + half],
                        e_recv.at[0, 4 + half],
                        across(toward),
                    ),
                    remote(
                        w_out.at[at_out],
                        hop_out.at[half, 1],
                        e_send.at[1, 4 + half],
                        e_recv.at[1, 4 + half],
                        across(toward),
                    ),
                )
                for copy in lasts[half]:
                    copy.start()

    to_x[1](0)
    of_o[2]()
    of_o[3]()
    of_g[2]()
    small_block = at_block(h, small)
    blocks[small_block, :] = piece[pl.ds(top + 16, small), :]
    g_copies = spread(10, lambda s: blocks.at[small_block, :], lambda s: blocks.at[small_block, :])
    to_x[1](1)
    to_x[1](2)
    of_d[2]()
    of_d[3]()
    to_x[2](grad_x_ref)
    gain = gain_part[...]
    for step in peers:
        gain_copies[step].wait()
        gain += gain_got[step - 1]
    sums[pl.ds(top, 16), :] = jnp.concatenate([gain, gain], axis=0).astype(bf16)
    of_a[0]()
    for step in peers:
        g_copies[step].wait()
    of_g[3](blocks, pl.ds(top + 16, n_head * small))
    of_o[4]()
    of_a[1]()
    of_a[2]()
    of_a[3]()
    of_d[4]()
    of_g[4]()
    output_ref[...] = middle[...] + outs[own_block, :].astype(f32)
    to_out[2](output_ref)
    for half in range(2):
        for copy in lasts[half]:
            copy.wait()
        at_in = (chip, halves_in[half], own_side)
        at_out = (chip, halves_out(core)[half], slice(None))
        w_in[at_in] = w_in[at_in] + hop_in[half, 1]
        w_out[at_out] = w_out[at_out] + hop_out[half, 1]
    stores = (
        pltpu.make_async_copy(w_in.at[chip, :, own_side], fin_in_ref, local_sem.at[0]),
        pltpu.make_async_copy(w_out.at[chip, own_side, :], fin_out_ref, local_sem.at[1]),
    )
    for store in stores:
        store.start()
    of_a[4]()
    for one in (of_o, of_g, of_d, of_a):
        one[5]()
    for store in stores:
        store.wait()
    mr_end()
    da_end()


def layer_call(n_dp, n_head, args):
    x, picks, router, value_mat, expert_in = args[0], args[2], args[13], args[11], args[14]
    tokens, features = x.shape
    per_device, _, width = expert_in.shape
    held_experts = value_mat.shape[1]
    group = tokens * n_head
    chips = n_dp // 2
    slab = per_device * width
    lanes = 128
    peers = n_head - 1
    named = ceil_to(n_dp * per_device, 8)
    small = ceil_to(named + 1, 16)
    top = features + held_experts
    held = top + 16 + small
    strip = features // n_dp
    shape = jax.ShapeDtypeStruct
    vm, dma = pltpu.VMEM, pltpu.SemaphoreType.DMA
    outs = [
        (shape((tokens, features), f32), VM),
        (shape((tokens, features), f32), VM),
        (shape((top + 16 + n_head * small, features), bf16), ANY),
        (shape((features, slab), bf16), ANY),
        (shape((slab, features), bf16), ANY),
    ]
    scratch = dict(
        picks=vm(picks.shape, jnp.int32),
        two_picks=vm((2, *args[3].shape), jnp.int32),
        head_picks=vm((group, lanes), jnp.int32),
        w_g=vm(args[10].shape, bf16),
        w_r=vm(router.shape, bf16),
        seg=vm((1, group), jnp.int32),
        gains=vm(args[6].shape, f32),
        angles=vm((group, width), f32),
        w_an=vm((features, 3 * width), bf16),
        w_v=vm((features, held_experts), bf16),
        w_o=vm((held_experts, features), bf16),
        my_router=vm((features, lanes), bf16),
        w_in=vm((chips, features, 2 * slab), bf16),
        w_out=vm((chips, 2 * slab, features), bf16),
        rows=vm((group, features), bf16),
        cot=vm((group, features), bf16),
        mrs=vm((group, features), bf16),
        das=vm((group, features), bf16),
        turned=vm((features, group), bf16),
        my_mask=vm((n_head, tokens, lanes), bf16),
        all_mask=vm((group, lanes), bf16),
        gates=vm((group, width), f32),
        q=vm((group, width), bf16),
        k=vm((group, width), bf16),
        v=vm((group, width), bf16),
        vx=vm((group, held_experts), bf16),
        att=vm((group, width), f32),
        part=vm((group, features), bf16),
        got=vm((2 * peers, tokens, features), bf16),
        outs=vm((group, features), bf16),
        got_out=vm((2 * peers, tokens, features), bf16),
        lifted=vm((chips, 2, group, slab), bf16),
        core_out=vm((chips, slab, features), bf16),
        acts=vm((chips, group, 2 * slab), bf16),
        hids=vm((chips, group, 2 * slab), bf16),
        dzs=vm((group, lanes), bf16),
        datt=vm((group, width), bf16),
        gate_grads=vm((group, width), f32),
        probs=vm((group, group), bf16),
        scores=vm((group, group), bf16),
        qkz=vm((group, 3 * width), bf16),
        vgrads=vm((group, held_experts), bf16),
        gain_part=vm((8, features), f32),
        gain_got=vm((peers, 8, features), f32),
        sums=vm((held, features), bf16),
        core_got=vm((held, features // 2), bf16),
        chip_got=vm((chips - 1, held, strip), bf16),
        piece=vm((held, strip), bf16),
        blocks=vm((n_head * small, strip), bf16),
        hop_in=vm((2, 2, features // 2, slab), bf16),
        hop_out=vm((2, 2, slab // 2, features), bf16),
        local_sem=dma((16 + 1 + per_device,)),
        z_send=dma((11, 2 * peers)),
        z_recv=dma((11, 2 * peers)),
        w_send=dma((22,)),
        w_recv=dma((22,)),
        c_send=dma((3, chips)),
        c_recv=dma((3, chips)),
        e_send=dma((2, 6)),
        e_recv=dma((2, 6)),
        s_send=dma((4, 3 * chips)),
        s_recv=dma((4, 3 * chips)),
        ready=pltpu.SemaphoreType.REGULAR,
        free=pltpu.SemaphoreType.REGULAR((2,)),
    )
    return pl.pallas_call(
        functools.partial(layer_kernel, n_dp, n_head),
        out_shape=[o[0] for o in outs],
        out_specs=[o[1] for o in outs],
        in_specs=[ANY] * 16,
        scratch_shapes=list(scratch.values()),
        compiler_params=pltpu.CompilerParams(
            collective_id=1, has_side_effects=True, vmem_limit_bytes=vmem_bytes
        ),
    )(*args)


def finish_kernel(
    n_dp,
    n_head,
    output_ref,
    grad_x_ref,
    wide_ref,
    in_ref,
    out_ref,
    gain_ref,
    final_ref,
    input_ref,
    attend_ref,
    query_ref,
    key_ref,
    value_ref,
    mix_ref,
    gate_ref,
    expert_ref,
    router_ref,
    grad_in_ref,
    grad_out_ref,
    wide,
    flat_in,
    flat_out,
    value,
    mix,
    grad_in,
    grad_out,
    output,
    grad_x,
    sem,
):
    features, slab = in_ref.shape
    per_device, _, width = grad_in_ref.shape
    experts_total, gates = router_ref.shape[0], gate_ref.shape[0]
    top = features + mix_ref.shape[0]
    small = (wide_ref.shape[0] - top - 16) // n_head
    named = n_dp * per_device

    def copy(src, dst, number):
        one = pltpu.make_async_copy(src, dst, sem.at[number])
        one.start()
        return one

    rest = pl.ds(top, wide_ref.shape[0] - top)
    loads = [
        copy(wide_ref.at[pl.ds(0, features), :], wide.at[pl.ds(0, features), :], 0),
        copy(wide_ref.at[pl.ds(features, top - features), :], wide.at[pl.ds(features, top - features), :], 1),
        copy(in_ref, flat_in, 2),
        copy(out_ref, flat_out, 3),
        copy(wide_ref.at[rest, :], wide.at[rest, :], 4),
    ]
    loads += [copy(output_ref, output, 11), copy(grad_x_ref, grad_x, 12)]
    stores = []
    for number, (held, result) in enumerate(((output, final_ref), (grad_x, input_ref))):
        loads[5 + number].wait()
        stores.append(copy(held, result, 5 + number))
    loads[0].wait()
    first = pl.ds(0, features)
    value[...] = wide[first, pl.ds(3 * width, value.shape[1])].astype(f32)
    stores.append(copy(value, value_ref, 7))
    gain = jnp.broadcast_to(gain_ref[0:1, :], (width, features)).T
    query_ref[...] = wide[first, pl.ds(0, width)].astype(f32) * gain
    key_ref[...] = wide[first, pl.ds(width, width)].astype(f32) * gain
    gate_ref[...] = (wide[first, pl.ds(2 * width, width)].astype(f32) * gain).T[:gates]
    loads[1].wait()
    mix[...] = wide[pl.ds(features, top - features), :].astype(f32)
    stores.append(copy(mix, mix_ref, 8))
    loads[2].wait()
    for e in range(per_device):
        grad_in[e] = flat_in[:, pl.ds(e * width, width)].astype(f32)
    stores.append(copy(grad_in, grad_in_ref, 9))
    loads[3].wait()
    for e in range(per_device):
        grad_out[e] = flat_out[pl.ds(e * width, width), :].astype(f32)
    stores.append(copy(grad_out, grad_out_ref, 10))
    loads[4].wait()
    attend_ref[...] = wide[pl.ds(top, 16), :][0:1].astype(f32)
    planes = wide[pl.ds(top + 16, n_head * small), :]
    place = lax.broadcasted_iota(jnp.int32, (n_head * small, experts_total), 0)
    name = lax.broadcasted_iota(jnp.int32, (n_head * small, experts_total), 1)
    slot, plane = place % small, place // small
    expert = (slot // per_device * n_head + plane) * per_device + slot % per_device
    chosen = (slot < named) & (expert == name)
    router_ref[...] = dot(jnp.where(chosen, 1.0, 0.0).astype(bf16), planes, TN)
    gain = jnp.zeros((1, features), f32)
    for z in range(n_head):
        row = z * small + ceil_to(named, 8)
        gain += planes[row : row + 1].astype(f32)
    expert_ref[...] = gain
    for store in stores:
        store.wait()


def finish_call(n_dp, n_head, shapes, args):
    shape = jax.ShapeDtypeStruct
    wide, flat_in, flat_out = args[2], args[3], args[4]
    value, mix, grad_in, grad_out = shapes[5], shapes[6], shapes[10], shapes[11]
    specs = [VM] * 12
    for number in (0, 1, 5, 6, 10, 11):
        specs[number] = ANY
    return pl.pallas_call(
        functools.partial(finish_kernel, n_dp, n_head),
        out_shape=[shape(s, f32) for s in shapes],
        out_specs=specs,
        in_specs=[ANY] * 5 + [VM],
        scratch_shapes=[
            pltpu.VMEM(wide.shape, bf16),
            pltpu.VMEM(flat_in.shape, bf16),
            pltpu.VMEM(flat_out.shape, bf16),
            pltpu.VMEM(value, f32),
            pltpu.VMEM(mix, f32),
            pltpu.VMEM(grad_in, f32),
            pltpu.VMEM(grad_out, f32),
            pltpu.VMEM(shapes[0], f32),
            pltpu.VMEM(shapes[1], f32),
            pltpu.SemaphoreType.DMA((13,)),
        ],
        compiler_params=pltpu.CompilerParams(vmem_limit_bytes=60 << 20),
    )(*args)


def kernel_body(
    n_dp,
    n_head,
    hidden_in,
    segments,
    value_pick,
    output_pick,
    expert_pick,
    attend_gain,
    query_weight,
    key_weight,
    value_weight,
    output_weight,
    head_router,
    expert_gain,
    router,
    expert_in,
    expert_out,
    cotangent,
):
    tokens, features = hidden_in.shape
    per_device, _, width = expert_in.shape
    experts = head_router.shape[2] // 2
    group = tokens * n_head
    angles = np.arange(group)[:, None] * theta ** (-2.0 * np.arange(width // 2) / width)[None, :]
    angles = np.concatenate([np.cos(angles), np.sin(angles)], axis=1).astype(np.float32)
    both = np.eye(2, dtype=np.float32)
    gains = attend_gain.astype(f32) * both[:, :1] + expert_gain.astype(f32) * both[:, 1:]
    results = layer_call(
        n_dp,
        n_head,
        (
            hidden_in,
            cotangent,
            expert_pick.T,
            value_pick.transpose(1, 2, 0)[0],
            output_pick.transpose(1, 2, 0)[0],
            segments[None, :],
            gains,
            angles,
            query_weight[0],
            key_weight[0],
            head_router.transpose(0, 2, 1)[0],
            value_weight[0],
            output_weight[0],
            router.T,
            expert_in,
            expert_out.reshape(per_device * width, features),
        ),
    )
    shapes = (
        (tokens, features),
        (tokens, features),
        (1, features),
        query_weight.shape[1:],
        key_weight.shape[1:],
        value_weight.shape[1:],
        output_weight.shape[1:],
        (2 * experts, features),
        (1, features),
        (router.shape[1], features),
        expert_in.shape,
        expert_out.shape,
    )
    done = list(finish_call(n_dp, n_head, shapes, (*results, gains)))
    for number in (3, 4, 5, 6, 7):
        done[number] = done[number][None]
    done[7] = done[7].transpose(0, 2, 1)
    done[9] = done[9].T
    done[2], done[8] = done[2][0], done[8][0]
    return tuple(done)


def solution(mesh):
    rows = P(everywhere, None)
    heads = P("head", None, None)
    experts = P(everywhere, None, None)
    picks = P("dp", "head", None)
    in_specs = (
        rows, P("dp"), picks, picks, rows, P(), heads, heads, heads, heads, heads,
        P(), P(), experts, experts, rows,
    )
    out_specs = (
        rows, rows, P(), heads, heads, heads, heads, heads, P(), P(), experts, experts,
    )
    n_dp, n_head = mesh.shape["dp"], mesh.shape["head"]

    def program(*args):
        held = 2 * n_dp * args[13].shape[0] * args[13].shape[1] * args[13].shape[2] * 2
        if n_head == 4 and held <= vmem_for_weights:
            return kernel_body(n_dp, n_head, *args)
        return body(*args)

    return jax.shard_map(program, mesh=mesh, in_specs=in_specs, out_specs=out_specs, check_vma=False)
```

```python
import functools

import jax
import jax.numpy as jnp
import numpy as np
from jax import lax
from jax.experimental import pallas as pl
from jax.experimental.pallas import tpu as pltpu
from jax.sharding import PartitionSpec as P

epsilon = 1e-06
theta = 10000.0
negative = -1e30
f32 = jnp.float32
bf16 = jnp.bfloat16
everywhere = ("dp", "head")
whole_rows = 4096
vmem_for_weights = 16 << 20
vmem_bytes = 62 << 20


def product(left, right, left_axis, right_axis):
    return lax.dot_general(
        left, right, (((left_axis,), (right_axis,)), ((), ())), preferred_element_type=f32
    )


def rms_scale(residual):
    return lax.rsqrt(jnp.mean(residual * residual, axis=-1, keepdims=True) + epsilon)


def rotary_tables(row_count, head_width):
    half_width = head_width // 2
    position = jnp.arange(row_count, dtype=f32)[:, None]
    exponent = jnp.arange(half_width, dtype=f32)[None, :]
    angles = position * jnp.power(theta, -2.0 * exponent / head_width)
    return (jnp.cos(angles), jnp.sin(angles))


def rotate(matrix, cosine, sine):
    half = matrix.shape[-1] // 2
    first, second = matrix[:, :half], matrix[:, half:]
    return jnp.concatenate([first * cosine - second * sine, second * cosine + first * sine], axis=-1)


def pick_mask(picks, expert_count):
    hits = picks[:, 0, :, None] == jnp.arange(expert_count, dtype=jnp.int32)[None, None, :]
    return jnp.any(hits, axis=1).astype(f32)


def norm_back(residual, inverse, gain, incoming):
    unit_rows = residual * inverse
    scaled = incoming * gain
    gain_grad = jnp.sum(incoming * unit_rows, axis=0)
    row_grad = inverse * (scaled - unit_rows * jnp.mean(scaled * unit_rows, axis=-1, keepdims=True))
    return (row_grad, gain_grad)


def gelu_pair(value):
    inner = jnp.tanh(0.7978845608028654 * (value + 0.044715 * value * value * value))
    slope = 0.5 * (1.0 + inner) + 0.5 * value * (1.0 - inner * inner) * 0.7978845608028654 * (
        1.0 + 3.0 * 0.044715 * value * value
    )
    return (0.5 * value * (1.0 + inner), slope)


def body(
    hidden_in,
    segments,
    value_pick,
    output_pick,
    expert_pick,
    attend_gain,
    query_weight,
    key_weight,
    value_weight,
    output_weight,
    head_router,
    expert_gain,
    router,
    expert_in,
    expert_out,
    cotangent,
):
    tokens, features = hidden_in.shape
    per_device, _, width = expert_in.shape
    head_experts = head_router.shape[2] // 2
    head_width = query_weight.shape[2]
    scale = head_width ** (-0.5)
    query_mat, key_mat, value_mat = query_weight[0], key_weight[0], value_weight[0]
    output_mat, gate_mat = output_weight[0], head_router[0]
    value_mask = pick_mask(value_pick, head_experts)
    output_mask = pick_mask(output_pick, head_experts)
    attend_scale = attend_gain.astype(f32)
    expert_scale = expert_gain.astype(f32)
    me = lax.axis_index("dp") * lax.axis_size("head") + lax.axis_index("head")

    rows = lax.all_gather(hidden_in, "head", axis=0, tiled=True)
    grouped = rows.astype(f32)
    group = grouped.shape[0]
    inverse = rms_scale(grouped)
    normed = (grouped * inverse * attend_scale).astype(bf16)
    cosine, sine = rotary_tables(group, head_width)
    queries = rotate(product(normed, query_mat, 1, 0), cosine, sine).astype(bf16)
    key_rows = rotate(product(normed, key_mat, 1, 0), cosine, sine).astype(bf16)
    squash = jax.nn.sigmoid(product(normed, gate_mat, 1, 0))
    value_gates = squash[:, :head_experts] * value_mask
    output_gates = squash[:, head_experts:] * output_mask
    expert_values = product(rows, value_mat, 1, 0).reshape(group, head_experts, head_width)
    values = jnp.sum(expert_values * value_gates[:, :, None], axis=1).astype(bf16)
    places = jnp.arange(group, dtype=jnp.int32)
    allowed = (places[None, :] <= places[:, None]) & (segments[:, None] == segments[None, :])
    scores = jnp.where(allowed, product(queries, key_rows, 1, 1) * scale, negative)
    exponents = jnp.exp(scores - jnp.max(scores, axis=-1, keepdims=True))
    probabilities = exponents / jnp.sum(exponents, axis=-1, keepdims=True)
    attended = product(probabilities.astype(bf16), values, 1, 0)
    weighted = (
        (output_gates[:, :, None] * attended[:, None, :]).reshape(group, -1).astype(bf16)
    )
    middle = hidden_in.astype(f32) + lax.psum_scatter(
        product(weighted, output_mat, 1, 0).astype(bf16), "head", scatter_dimension=0, tiled=True
    ).astype(f32)
    middle_inverse = rms_scale(middle)
    middle_normed = (middle * middle_inverse * expert_scale).astype(bf16)
    mine = me * per_device + jnp.arange(per_device, dtype=jnp.int32)
    my_router = lax.dynamic_slice_in_dim(router, me * per_device, per_device, axis=1)
    in_mat = expert_in.transpose(1, 0, 2).reshape(features, per_device * width)
    out_mat = expert_out.reshape(per_device * width, features)

    def turn(running, own):
        own_rows, own_cot, own_picks = own
        all_cot = lax.all_gather(own_cot, everywhere, axis=0, tiled=True)
        all_picks = lax.all_gather(own_picks, everywhere, axis=0, tiled=True)
        all_rows = lax.all_gather(own_rows, everywhere, axis=0, tiled=True)
        mask = jnp.any(all_picks[:, :, None] == mine[None, None, :], axis=1).astype(f32)
        gates = jax.nn.sigmoid(product(all_rows, my_router, 1, 0))
        live = gates * mask
        act, slope = gelu_pair(product(all_rows, in_mat, 1, 0).reshape(-1, per_device, width))
        lifted = product(all_cot, out_mat, 1, 1).reshape(-1, per_device, width)
        dense_grad = (jnp.sum(act * lifted, axis=-1) * live * (1.0 - gates)).astype(bf16)
        act_live = (act * live[:, :, None]).astype(bf16).reshape(-1, per_device * width)
        hidden_grad = (slope * lifted * live[:, :, None]).astype(bf16)
        hidden_grad = hidden_grad.reshape(-1, per_device * width)
        part_out = product(act_live, out_mat, 1, 0).astype(bf16)
        part_grad = (
            product(hidden_grad, in_mat, 1, 1) + product(dense_grad, my_router, 1, 1)
        ).astype(bf16)
        back = lax.psum_scatter(part_grad, everywhere, scatter_dimension=0, tiled=True)
        forth = lax.psum_scatter(part_out, everywhere, scatter_dimension=0, tiled=True)
        grads = (
            product(all_rows, hidden_grad, 0, 0),
            product(act_live, all_cot, 0, 0),
            product(dense_grad, all_rows, 0, 0),
        )
        if running is not None:
            grads = jax.tree.map(jnp.add, running, grads)
        return grads, (forth, back)

    turns = max(1, lax.axis_size("dp") * lax.axis_size("head") * tokens // whole_rows)
    owned = (middle_normed, cotangent, expert_pick)
    if turns == 1:
        grads, (summed, normed_grad) = turn(None, owned)
    else:
        owned = jax.tree.map(lambda a: a.reshape(turns, -1, a.shape[1]), owned)
        zeros = (
            jnp.zeros(in_mat.shape, f32),
            jnp.zeros(out_mat.shape, f32),
            jnp.zeros((per_device, features), f32),
        )
        grads, sums = lax.scan(turn, zeros, owned)
        summed, normed_grad = (a.reshape(tokens, features) for a in sums)
    grad_in = grads[0].reshape(features, per_device, width).transpose(1, 0, 2)
    grad_out = grads[1].reshape(per_device, width, features)
    grad_router = lax.all_gather(grads[2], everywhere, axis=0, tiled=True).T
    output = middle + summed.astype(f32)
    incoming = cotangent.astype(f32)
    row_grad, grad_gain_expert = norm_back(
        middle, middle_inverse, expert_scale, normed_grad.astype(f32)
    )
    middle_grad = incoming + row_grad
    group_grads = lax.all_gather(middle_grad.astype(bf16), "head", axis=0, tiled=True)
    weighted_grad = product(group_grads, output_mat, 1, 1).reshape(group, head_experts, head_width)
    output_grad = product(weighted, group_grads, 0, 0)
    output_gate_grad = jnp.sum(weighted_grad * attended[:, None, :], axis=-1)
    attended_grad = jnp.sum(weighted_grad * output_gates[:, :, None], axis=1).astype(bf16)
    prob_grad = product(attended_grad, values, 1, 1)
    centre = jnp.sum(probabilities * prob_grad, axis=-1, keepdims=True)
    score_grad = (probabilities * (prob_grad - centre)).astype(bf16)
    query_grad = product(score_grad, key_rows, 1, 0) * scale
    key_grad = product(score_grad, queries, 0, 0) * scale
    values_grad = product(probabilities.astype(bf16), attended_grad, 0, 0)
    expert_grad = (value_gates[:, :, None] * values_grad[:, None, :]).reshape(group, -1).astype(bf16)
    value_gate_grad = jnp.sum(expert_values * values_grad[:, None, :], axis=-1)
    query_grad = rotate(query_grad, cosine, -sine).astype(bf16)
    key_grad = rotate(key_grad, cosine, -sine).astype(bf16)
    logit_grad = (
        jnp.concatenate([value_gate_grad * value_mask, output_gate_grad * output_mask], axis=1)
        * squash
        * (1.0 - squash)
    ).astype(bf16)
    head_grads = (
        product(normed, query_grad, 0, 0),
        product(normed, key_grad, 0, 0),
        product(rows, expert_grad, 0, 0),
        output_grad,
        product(normed, logit_grad, 0, 0),
    )
    head_grads = tuple(grad.astype(bf16) for grad in head_grads)
    head_grads = tuple(grad.astype(f32)[None] for grad in lax.psum(head_grads, "dp"))
    back = (
        product(query_grad, query_mat, 1, 1)
        + product(key_grad, key_mat, 1, 1)
        + product(logit_grad, gate_mat, 1, 1)
    )
    row_back, grad_attend = norm_back(grouped, inverse, attend_scale, back)
    partial = (row_back + product(expert_grad, value_mat, 1, 1)).astype(bf16)
    input_grad = middle_grad + lax.psum_scatter(
        partial, "head", scatter_dimension=0, tiled=True
    ).astype(f32)
    grad_attend, grad_gain_expert = lax.psum((grad_attend, grad_gain_expert), everywhere)
    return (
        output,
        input_grad,
        grad_attend,
        *head_grads,
        grad_gain_expert,
        grad_router,
        grad_in,
        grad_out,
    )


MESH = pl.DeviceIdType.MESH
VM = pl.BlockSpec(memory_space=pltpu.VMEM)
ANY = pl.BlockSpec(memory_space=pl.ANY)
NN = (((1,), (0,)), ((), ()))
NT = (((1,), (1,)), ((), ()))
TN = (((0,), (0,)), ((), ()))


def dot(left, right, dims=NN):
    return lax.dot_general(left, right, dims, preferred_element_type=f32)


def at_block(block, count):
    return pl.ds(pl.multiple_of(block * count, count), count)


def remote(src, dst, send, recv, where):
    return pltpu.make_async_remote_copy(
        src_ref=src, dst_ref=dst, send_sem=send, recv_sem=recv, device_id=where, device_id_type=MESH
    )


def swap_halves(value):
    half = value.shape[-1] // 2
    return jnp.concatenate([value[:, half:], value[:, :half]], axis=-1)


def ceil_to(number, step):
    return -(-number // step) * step


def layer_kernel(
    n_dp,
    n_head,
    x_ref,
    cot_ref,
    pick_ref,
    value_pick_ref,
    output_pick_ref,
    seg_ref,
    gain_ref,
    angle_ref,
    wq_ref,
    wk_ref,
    wg_ref,
    wv_ref,
    wo_ref,
    router_ref,
    in_ref,
    out_ref,
    output_ref,
    grad_x_ref,
    wide_ref,
    fin_in_ref,
    fin_out_ref,
    picks,
    two_picks,
    head_picks,
    w_g,
    w_r,
    seg,
    gains,
    angles,
    w_an,
    w_v,
    w_o,
    my_router,
    w_in,
    w_out,
    rows,
    cot,
    mrs,
    das,
    turned,
    my_mask,
    all_mask,
    gates,
    q,
    k,
    v,
    vx,
    att,
    part,
    got,
    outs,
    got_out,
    lifted,
    core_out,
    acts,
    hids,
    dzs,
    datt,
    gate_grads,
    probs,
    scores,
    qkz,
    vgrads,
    gain_part,
    gain_got,
    sums,
    core_got,
    chip_got,
    piece,
    blocks,
    hop_in,
    hop_out,
    local_sem,
    z_send,
    z_recv,
    w_send,
    w_recv,
    c_send,
    c_recv,
    e_send,
    e_recv,
    s_send,
    s_recv,
    ready,
    free,
):
    middle = output_ref
    xor = jnp.bitwise_xor
    d, h = lax.axis_index("dp"), lax.axis_index("head")
    chip, core = d // 2, d % 2
    chips = n_dp // 2
    tokens, features = x_ref.shape
    per_device, _, width = in_ref.shape
    slab = per_device * width
    wide = 2 * slab
    experts = wv_ref.shape[1] // width
    named = ceil_to(n_dp * per_device, 8)
    group = tokens * n_head
    pair = 2 * tokens
    column = 256
    lanes = 128
    scale = width ** (-0.5)
    peers = (2, 3, 1)
    partner = (chip * 2 + 1 - core, h)
    own_block = at_block(h, tokens)
    own_side, other_side = at_block(core, slab), at_block(1 - core, slab)
    halves_in = (pl.ds(0, features // 2), pl.ds(features // 2, features // 2))
    halves_out = lambda side: (
        at_block(2 * side, slab // 2),
        at_block(2 * side + 1, slab // 2),
    )

    def along(step):
        return (d, xor(h, step))

    def across(step):
        return (xor(chip, step) * 2 + core, h)

    loads = []

    def load(src, dst):
        copy = pltpu.make_async_copy(src, dst, local_sem.at[len(loads)])
        copy.start()
        loads.append(copy)
        return copy

    own_weights = [load(out_ref, w_out.at[chip, own_side, :])] + [
        load(in_ref.at[e], w_in.at[chip, :, at_block(core * per_device + e, width)])
        for e in range(per_device)
    ]
    for_rows = [
        load(x_ref, rows.at[own_block, :]),
        load(gain_ref, gains),
        load(wg_ref, w_g),
        load(wq_ref, w_an.at[:, pl.ds(0, width)]),
        load(wk_ref, w_an.at[:, pl.ds(width, width)]),
        load(wv_ref, w_v),
        load(value_pick_ref, two_picks.at[0]),
        load(output_pick_ref, two_picks.at[1]),
        load(angle_ref, angles),
    ]
    for_scores = [load(seg_ref, seg), load(wo_ref, w_o)]
    for_mask = load(pick_ref, picks)
    for_cot = load(cot_ref, cot.at[own_block, :])
    for_router = load(router_ref, w_r)

    barrier = pltpu.get_barrier_semaphore()
    friends = [along(s) for s in peers] + [partner] + [across(s) for s in range(1, chips)]
    for friend in friends:
        pl.semaphore_signal(barrier, inc=1, device_id=friend, device_id_type=MESH)
    pl.semaphore_wait(barrier, len(friends))

    right, left = (d, jnp.minimum(h + 1, n_head - 1)), (d, jnp.maximum(h - 1, 0))
    last = n_head - 1

    def pick(*by_place):
        value = jnp.int32(by_place[-1])
        for place in range(n_head - 2, -1, -1):
            value = jnp.where(h == place, by_place[place], value)
        return value

    arrival = (xor(h, 1), pick(2, 2, 1, 1), pick(3, 3, 0, 0))
    leaving = (pick(3, 3, 0, 0), pick(2, 0, 3, 1), pick(1, 2, 1, 2))

    def gather(kind, buffer):
        def go(side, step):
            block = jnp.clip(h - step if side == 0 else h + step, 0, last)
            copies = []
            for half in range(2):
                here = buffer.at[at_block(2 * block + half, tokens // 2), :]
                number = (side * last + step) * 2 + half
                copies.append(
                    remote(
                        here, here, z_send.at[kind, number], z_recv.at[kind, number], (right, left)[side]
                    )
                )
            return copies

        def begin(side):
            for copy in go(side, 0):
                copy.start()

        def start():
            pl.when(h < last)(lambda: begin(0))
            pl.when(h > 0)(lambda: begin(1))

        def pass_on(side, step, there, onward):
            for half in range(2):

                @pl.when(there)
                def _():
                    go(side, step - 1)[half].wait_recv()

                if step < last:

                    @pl.when(there & onward)
                    def _():
                        go(side, step)[half].start()

        def stage(step):
            pass_on(0, step, h >= step, h < last)
            pass_on(1, step, h + step <= last, h > 0)

        def follow(step):
            pl.when((h < last) & (jnp.maximum(h, 1) == step))(lambda: begin(0))
            pl.when((h > 0) & (jnp.maximum(last - h, 1) == step))(lambda: begin(1))

        def end():
            for step in range(last):
                for side, sent in (
                    (0, (h >= step) & (h < last)),
                    (1, (h + step <= last) & (h > 0)),
                ):

                    @pl.when(sent)
                    def _():
                        for copy in go(side, step):
                            copy.wait_send()

        return start, stage, end, follow

    def chain_sum(kind, parts, slots):
        def go(number):
            block = leaving[number]
            rightward = block > h
            slot = jnp.where(rightward, block - 1, last + block)
            where = (d, jnp.clip(jnp.where(rightward, h + 1, h - 1), 0, last))
            middle_one = (rightward & (h > 0)) | (jnp.logical_not(rightward) & (h < last))
            pieces = []
            for half in range(2):
                at = at_block(2 * block + half, tokens // 2)
                rows_of = pl.ds(half * (tokens // 2), tokens // 2)
                copy = remote(
                    parts.at[at, :],
                    slots.at[slot, rows_of, :],
                    z_send.at[kind, 2 * number + half],
                    z_recv.at[kind, 2 * slot + half],
                    where,
                )
                pieces.append((copy, at, slot, rows_of))
            return pieces, middle_one

        def now(number):
            pieces, middle_one = go(number)

            @pl.when(jnp.logical_not(middle_one))
            def _():
                for copy, _, _, _ in pieces:
                    copy.start()

        def later(number):
            pieces, middle_one = go(number)

            @pl.when(middle_one)
            def _():
                for copy, at, slot, rows_of in pieces:
                    copy.wait_recv()
                    parts[at, :] = parts[at, :] + slots[slot, rows_of, :]
                    copy.start()

        def end(total):
            ends = ((jnp.maximum(h - 1, 0), h > 0), (last + jnp.minimum(h, last - 1), h < last))
            for slot, there in ends:

                @pl.when(there)
                def _():
                    for half in range(2):
                        rows_of = pl.ds(half * (tokens // 2), tokens // 2)
                        remote(
                            parts.at[at_block(2 * h, tokens // 2), :],
                            slots.at[slot, rows_of, :],
                            z_send.at[kind, 0],
                            z_recv.at[kind, 2 * slot + half],
                            right,
                        ).wait_recv()
                    total[...] += slots[slot].astype(f32)

            for number in range(last):
                for copy, _, _, _ in go(number)[0]:
                    copy.wait_send()

        return now, later, end

    def spread(kind, src, dst, steps=peers):
        copies = {}
        for step in steps:
            copies[step] = remote(
                src(step), dst(step), z_send.at[kind, step - 1], z_recv.at[kind, step - 1], along(step)
            )
            copies[step].start()
        return copies

    x_start, x_stage, x_end, _ = gather(0, rows)
    for_rows[0].wait()
    x_start()

    def slot(array, place, side, half=None):
        if array == 0:
            at = halves_out(side)[half] if half is not None else at_block(side, slab)
            return w_out.at[place, at, :]
        at = halves_in[half] if half is not None else pl.ds(0, features)
        return w_in.at[place, at, at_block(side, slab)]

    def weights(number, ref, where):
        copy = remote(ref, ref, w_send.at[number], w_recv.at[number], where)
        copy.start()
        return copy

    slabs, halves_on, to_core, diagonal = {}, {}, {}, {}
    for copy in own_weights:
        copy.wait()
    for array in range(2):
        for first in range(2):
            for bit in (1, 2):
                half = bit - 1 if first == 0 else 2 - bit
                number = ((bit - 1) * 2 + half) * 2 + array
                slabs[bit, half, array] = weights(
                    number, slot(array, chip, core, half), across(bit)
                )
        to_core[0, array] = weights(12 + array, slot(array, chip, core), partner)

    for_mask.wait()
    own_picks = jnp.concatenate(
        [picks[...].astype(f32), jnp.zeros((lanes - picks.shape[0], tokens), f32)], axis=0
    ).T.astype(jnp.int32)
    lane = lax.broadcasted_iota(jnp.int32, (tokens, lanes), 1)
    for plane in range(n_head):
        expert = (lane // per_device * n_head + plane) * per_device + lane % per_device
        expert = jnp.where(lane < n_dp * per_device, expert, -1)
        hit = own_picks[:, 0:1] == expert
        for c in range(1, picks.shape[0]):
            hit = hit | (own_picks[:, c : c + 1] == expert)
        my_mask[plane] = jnp.where(hit, 1.0, 0.0).astype(bf16)
    mask_copies = spread(1, lambda s: my_mask.at[xor(h, s)], lambda s: all_mask.at[own_block, :])
    all_mask[own_block, :] = my_mask[h]

    for copy in for_rows[1:]:
        copy.wait()
    attend_gain = gains[0:1, :]
    expert_gain = gains[1:2, :]
    one_hot = lambda count: jnp.where(
        lax.broadcasted_iota(jnp.int32, (count, width), 0)
        == lax.broadcasted_iota(jnp.int32, (count, width), 1),
        1.0,
        0.0,
    ).astype(bf16)
    w_an[:, pl.ds(2 * width, width)] = dot(w_g[...], one_hot(w_g.shape[0]), TN).astype(bf16)
    uses = two_picks.shape[1]
    head_picks[...] = jnp.concatenate(
        [
            two_picks[0].astype(f32),
            two_picks[1].astype(f32) + experts,
            jnp.zeros((lanes - 2 * uses, group), f32),
        ],
        axis=0,
    ).T.astype(jnp.int32)
    half_lanes = lax.broadcasted_iota(jnp.int32, (1, width), 1) < width // 2

    def turns(at):
        both = angles[at, :]
        turned_over = swap_halves(both)
        return (
            jnp.where(half_lanes, both, turned_over),
            jnp.where(half_lanes, -turned_over, both),
        )

    def project(block):
        at = at_block(block, tokens)
        own = rows[at, :]
        full = own.astype(f32)
        inverse = lax.rsqrt(jnp.mean(full * full, axis=-1, keepdims=True) + epsilon)
        unit = (full * inverse * attend_gain).astype(bf16)
        qkg = dot(unit, w_an[...])
        c, s = turns(at)
        one, two = qkg[:, :width], qkg[:, width : 2 * width]
        q[at, :] = (one * c + swap_halves(one) * s).astype(bf16)
        k[at, :] = (two * c + swap_halves(two) * s).astype(bf16)
        lane = lax.broadcasted_iota(jnp.int32, (tokens, width), 1)
        chosen = head_picks[at, :]
        hit = lane == chosen[:, 0:1]
        for c in range(1, 2 * uses):
            hit = hit | (lane == chosen[:, c : c + 1])
        gate = jnp.where(hit, jax.nn.sigmoid(qkg[:, 2 * width :]), 0.0)
        gates[at, :] = jnp.where(lane == width - 1, inverse, gate)
        values = dot(own, w_v[...])
        vx[at, :] = values.astype(bf16)
        value = gate[:, 0:1] * values[:, :width]
        for e in range(1, experts):
            value += gate[:, e : e + 1] * values[:, e * width : (e + 1) * width]
        v[at, :] = value.astype(bf16)

    project(h)
    _, cot_stage, cot_end, cot_follow = gather(2, cot)
    for_cot.wait()
    for step in (1, 2, 3):
        x_stage(step)
        cot_follow(step)
        project(arrival[step - 1])
    for copy in for_scores:
        copy.wait()
    seg_col = gate_grads
    seg_col[...] = jnp.broadcast_to(seg[...].astype(f32), (lanes, group)).T

    def attend(block):
        at = at_block(block, tokens)
        score = dot(q[at, :], k[...], NT) * scale
        row = block * tokens + lax.broadcasted_iota(jnp.int32, (tokens, group), 0)
        place = lax.broadcasted_iota(jnp.int32, (tokens, group), 1)
        allowed = (place <= row) & (seg_col[at, 0:1] == seg[...].astype(f32))
        score = jnp.where(allowed, score, negative)
        exponents = jnp.exp(score - jnp.max(score, axis=-1, keepdims=True))
        chance = exponents / jnp.sum(exponents, axis=-1, keepdims=True)
        probs[at, :] = chance.astype(bf16)
        attended = dot(chance.astype(bf16), v[...])
        att[at, :] = attended
        gate = gates[at, :]
        weighted = jnp.concatenate(
            [
                (gate[:, experts + e : experts + e + 1] * attended).astype(bf16)
                for e in range(experts)
            ],
            axis=-1,
        )
        return dot(weighted, w_o[...])

    to_mid = chain_sum(3, part, got)
    for number in range(last):
        block = leaving[number]
        part[at_block(block, tokens), :] = attend(block).astype(bf16)
        to_mid[0](number)
    middle[...] = rows[own_block, :].astype(f32) + attend(h)
    cot_stage(1)
    to_mid[1](0)
    for array in range(2):
        for half in range(2):
            slabs[1 + half, half, array].wait_recv()
            halves_on[half, array] = weights(
                8 + 2 * half + array,
                slot(array, xor(chip, 1 + half), core, half),
                across(2 - half),
            )

    to_mid[1](1)
    cot_stage(2)
    to_mid[1](2)
    cot_stage(3)
    for bit in (1, 2):
        slabs[bit, 2 - bit, 0].wait_recv()
        to_core[bit, 0] = weights(14 + (bit - 1) * 2, slot(0, xor(chip, bit), core), partner)
        slabs[bit, 2 - bit, 1].wait_recv()
        to_core[bit, 1] = weights(15 + (bit - 1) * 2, slot(1, xor(chip, bit), core), partner)
    for_router.wait()
    slot_of = lax.broadcasted_iota(jnp.int32, (w_r.shape[0], lanes), 1)
    name = lax.broadcasted_iota(jnp.int32, (w_r.shape[0], lanes), 0)
    expert = (slot_of // per_device * n_head + h) * per_device + slot_of % per_device
    expert = jnp.where(slot_of < n_dp * per_device, expert, -1)
    my_router[...] = dot(
        w_r[...], jnp.where(name == expert, 1.0, 0.0).astype(bf16), TN
    ).astype(bf16)

    to_mid[2](middle)
    mid = middle[...]
    inverse = lax.rsqrt(jnp.mean(mid * mid, axis=-1, keepdims=True) + epsilon)
    mrs[own_block, :] = (mid * inverse * expert_gain).astype(bf16)
    mr_start, mr_stage, mr_end, _ = gather(4, mrs)
    mr_start()

    def last_halves(array):
        for half in range(2):
            halves_on[half, array].wait_recv()
            diagonal[half, array] = weights(
                18 + 2 * half + array, slot(array, xor(chip, 3), core, half), partner
            )

    last_halves(0)
    for step in peers:
        mask_copies[step].wait()
    cot_end()
    x_end()

    def weights_here(array):
        for bit in range(3):
            to_core[bit, array].wait_recv()
        for half in range(2):
            diagonal[half, array].wait_recv()

    def weights_sent():
        for array in range(2):
            for bit in range(3):
                to_core[bit, array].wait_send()
            for half in range(2):
                diagonal[half, array].wait_send()
                halves_on[half, array].wait_send()
                for bit in (1, 2):
                    slabs[bit, half, array].wait_send()

    weights_here(0)

    def lift_chip(j):
        lift = dot(cot[...], w_out[j], NT)
        lifted[j, 0] = lift[:, :slab].astype(bf16)
        lifted[j, 1] = lift[:, slab:].astype(bf16)

    pl.loop(0, chips // 2)(lift_chip)
    mr_stage(1)
    last_halves(1)
    pl.loop(chips // 2, chips)(lift_chip)

    weights_here(1)

    def spread_lanes(j):
        lane = lax.broadcasted_iota(jnp.int32, (lanes, wide), 1) // width
        slot = lax.broadcasted_iota(jnp.int32, (lanes, wide), 0)
        return jnp.where(slot == lane + j * (wide // width), 1.0, 0.0).astype(bf16)

    def pair_of_blocks(number, between):
        at = at_block(number, pair)
        own = mrs[at, :]
        gates = jax.nn.sigmoid(dot(own, my_router[...]))
        live = gates * all_mask[at, :].astype(f32)
        narrow = live.astype(bf16)

        def chip_step(j, total):
            pick = spread_lanes(j)
            hidden = dot(own, w_in[j])
            gate = dot(narrow, pick).astype(bf16)
            lift = jnp.concatenate([lifted[j, 0, at, :], lifted[j, 1, at, :]], axis=-1)
            square = hidden * hidden
            inner = jnp.tanh(0.7978845608028654 * hidden * (1.0 + 0.044715 * square))
            half = 0.5 * (1.0 + inner)
            act = hidden * half
            slope = half + act * (1.0 - inner) * (
                0.7978845608028654 + (0.7978845608028654 * 3.0 * 0.044715) * square
            )
            act = act.astype(bf16)
            acts[j, at, :] = act * gate
            hids[j, at, :] = slope.astype(bf16) * (lift * gate)
            return total + dot(act * lift, pick, NT)

        total = lax.fori_loop(0, chips, chip_step, jnp.zeros((pair, lanes), f32))
        dz = (total * live * (1.0 - gates)).astype(bf16)
        dzs[at, :] = dz
        between()

        @pl.loop(0, features // column)
        def _(c):
            part_of = at_block(c, column)
            total = dot(dz, my_router[part_of, :], NT)
            for j in range(chips):
                total += dot(hids[j, at, :], w_in[j, part_of, :], NT)
            part[at, part_of] = total.astype(bf16)

    def outputs():
        @pl.loop(0, features // column)
        def _(c):
            part_of = at_block(c, column)
            total = dot(acts[0], w_out[0, :, part_of])
            for j in range(1, chips):
                total += dot(acts[j], w_out[j, :, part_of])
            outs[:, part_of] = total.astype(bf16)

    near = h // 2
    to_dmr = chain_sum(5, part, got)
    pair_of_blocks(near, lambda: mr_stage(2))
    to_dmr[0](2)
    mr_stage(3)
    pair_of_blocks(1 - near, lambda: None)
    to_dmr[0](0)
    to_dmr[0](1)
    outputs()
    pl.semaphore_signal(ready, inc=1, device_id=partner, device_id_type=MESH)

    weights_sent()
    turned[...] = mrs[...].T

    def expert_grads(place, at):
        for half in halves_in:
            w_in[place, half, at] = dot(turned[half, :], hids[place, :, at]).astype(bf16)
            w_out[place, at, half] = dot(acts[place, :, at], cot[:, half], TN).astype(bf16)

    def to_other_core(n):
        place = xor(chip, chips - 1 - n)
        copies = [
            remote(
                w_in.at[place, halves_in[half], other_side],
                lifted.at[place, half],
                c_send.at[half, n],
                c_recv.at[half, n],
                partner,
            )
            for half in range(2)
        ]
        copies.append(
            remote(
                w_out.at[place, other_side, :],
                core_out.at[place],
                c_send.at[2, n],
                c_recv.at[2, n],
                partner,
            )
        )
        return copies

    pl.semaphore_wait(ready, 1)

    hops = {}

    def hop(half, index, place, toward):
        copies = (
            remote(
                slot(1, place, core, half),
                hop_in.at[half, index],
                e_send.at[0, 2 * half + index],
                e_recv.at[0, 2 * half + index],
                across(toward),
            ),
            remote(
                slot(0, place, core, half),
                hop_out.at[half, index],
                e_send.at[1, 2 * half + index],
                e_recv.at[1, 2 * half + index],
                across(toward),
            ),
        )
        for copy in copies:
            copy.start()
        hops[half, index] = copies

    def both_cores(n):
        step = chips - 1 - n
        place = xor(chip, step)
        for copy in to_other_core(n):
            copy.wait()
        for half in range(2):
            here = (place, halves_in[half], own_side)
            w_in[here] = w_in[here] + lifted[place, half]
        w_out[place, own_side, :] = w_out[place, own_side, :] + core_out[place]
        if step == 3:
            hop(0, 1, place, 1)
            hop(1, 1, place, 2)
        elif step:
            hop(step - 1, 0, place, step)

    for n in range(chips):
        place = xor(chip, chips - 1 - n)
        expert_grads(place, other_side)
        for copy in to_other_core(n):
            copy.start()
        if n:
            both_cores(n - 1)
        expert_grads(place, own_side)
    to_dmr[1](0)
    both_cores(chips - 1)
    to_dmr[1](1)
    to_dmr[1](2)
    side = features // 2
    strip = side // chips
    col = lambda c, j: at_block(c * chips + j, strip)

    def section(number, first, count):
        at = pl.ds(first, count)
        state = {}

        def sem(n):
            return s_send.at[number, n], s_recv.at[number, n]

        def start():
            state["core"] = remote(
                sums.at[at, at_block(1 - core, side)], core_got.at[at, :], *sem(0), partner
            )
            state["core"].start()

        def mid():
            state["core"].wait()
            half = at_block(core, side)
            sums[at, half] = sums[at, half] + core_got[at, :]
            state["chips"] = []
            for s in range(1, chips):
                copy = remote(
                    sums.at[at, col(core, xor(chip, s))], chip_got.at[s - 1, at, :], *sem(s), across(s)
                )
                copy.start()
                state["chips"].append(copy)

        def add():
            for copy in state["chips"]:
                copy.wait()
            total = sums[at, col(core, chip)].astype(f32)
            for s in range(1, chips):
                total += chip_got[s - 1, at, :].astype(f32)
            piece[at, :] = total.astype(bf16)

        return start, mid, add

    def to_plane(number, src, rows_to):
        state = {}

        def sem(n):
            return s_send.at[number, chips + n], s_recv.at[number, chips + n]

        def start():
            here = wide_ref.at[rows_to, col(core, chip)]
            state["share"] = [remote(src, here, *sem(s), across(s)) for s in range(1, chips)]
            over = remote(src, here, *sem(0), partner)
            own = pltpu.make_async_copy(src, here, s_send.at[number, 3 * chips - 1])
            state["wait"] = [over, own]
            for copy in state["share"] + state["wait"]:
                copy.start()

        def forward():
            for s in range(1, chips):
                state["share"][s - 1].wait()
                here = wide_ref.at[rows_to, col(core, xor(chip, s))]
                copy = remote(here, here, *sem(chips - 1 + s), partner)
                copy.start()
                state["wait"].append(copy)

        def end():
            for copy in state["wait"]:
                copy.wait()

        return start, forward, end

    mixed = w_o.shape[0]
    small = ceil_to(named + 1, 16)
    at_a = pl.ds(features, 16)
    at_o = pl.ds(features + 16, mixed)
    at_g = pl.ds(features + 16 + mixed, small)
    of_d = [section(n, n * features // 2, features // 2) for n in range(2)]
    of_o = section(2, features + 16, mixed)
    of_g = section(3, features + 16 + mixed, small)
    of_a = section(4, features, 16)
    out_d = [to_plane(n, piece.at[halves_in[n], :], halves_in[n]) for n in range(2)]
    out_o = to_plane(2, piece.at[at_o, :], at_o)
    out_g = to_plane(3, blocks, pl.ds(features + 16 + mixed, n_head * small))
    out_a = to_plane(4, piece.at[at_a, :], at_a)
    router_part = dot(dzs[...], mrs[...], TN)[:named]

    grad_x_ref[...] = part[own_block, :].astype(f32)
    to_dmr[2](grad_x_ref)
    incoming = grad_x_ref[...]
    mid = middle[...]
    inverse = lax.rsqrt(jnp.mean(mid * mid, axis=-1, keepdims=True) + epsilon)
    unit = mid * inverse
    scaled = incoming * expert_gain
    dmid = cot[own_block, :].astype(f32) + inverse * (
        scaled - unit * jnp.mean(scaled * unit, axis=-1, keepdims=True)
    )
    grad_x_ref[...] = dmid
    das[own_block, :] = dmid.astype(bf16)
    da_start, da_stage, da_end, _ = gather(6, das)
    da_start()
    sums[at_g, :] = jnp.concatenate(
        [
            router_part,
            jnp.sum(incoming * unit, axis=0, keepdims=True),
            jnp.zeros((small - named - 1, features), f32),
        ],
        axis=0,
    ).astype(bf16)
    of_g[0]()
    turned[...] = rows[...].T
    of_g[1]()
    lasts = {}

    def first_hop(half, index, place):
        for copy in hops[half, index]:
            copy.wait()
        at_in = (place, halves_in[half], own_side)
        at_out = (place, halves_out(core)[half], slice(None))
        w_in[at_in] = w_in[at_in] + hop_in[half, index]
        w_out[at_out] = w_out[at_out] + hop_out[half, index]

    for half in range(2):
        toward = 2 - half
        place = xor(chip, toward)
        first_hop(half, 1, place)
        pl.semaphore_signal(free.at[half], inc=1, device_id=across(toward), device_id_type=MESH)
        pl.semaphore_wait(free.at[half], 1)
        lasts[half] = (
            remote(
                slot(1, place, core, half),
                hop_in.at[half, 1],
                e_send.at[0, 4 + half],
                e_recv.at[0, 4 + half],
                across(toward),
            ),
            remote(
                slot(0, place, core, half),
                hop_out.at[half, 1],
                e_send.at[1, 4 + half],
                e_recv.at[1, 4 + half],
                across(toward),
            ),
        )
        for copy in lasts[half]:
            copy.start()
    lane = lax.broadcasted_iota(jnp.int32, (tokens, width), 1)

    def through_output(block):
        at = at_block(block, tokens)
        all_five = dot(das[at, :], w_o[...], NT)
        attended = att[at, :]
        total = jnp.zeros((tokens, width), f32)
        gate = jnp.zeros((tokens, width), f32)
        for e in range(experts):
            one = all_five[:, e * width : (e + 1) * width]
            total += gates[at, experts + e : experts + e + 1] * one
            gate = jnp.where(
                lane == experts + e, jnp.sum(one * attended, axis=-1, keepdims=True), gate
            )
        datt[at, :] = total.astype(bf16)
        gate_grads[at, :] = gate

    through_output(h)
    to_out = chain_sum(7, outs, got_out)
    for step in (1, 2, 3):
        da_stage(step)
        if step == 1:
            for number in range(last):
                to_out[0](number)
        through_output(arrival[step - 1])

    for e in range(experts):
        one = (gates[:, experts + e : experts + e + 1] * att[...]).astype(bf16)
        sums[pl.ds(features + 16 + e * width, width), :] = dot(one, das[...], TN).astype(bf16)
    of_o[0]()

    @pl.loop(0, n_head)
    def _(block):
        at = at_block(block, tokens)
        chance = probs[at, :].astype(f32)
        dprob = dot(datt[at, :], v[...], NT)
        centre = jnp.sum(chance * dprob, axis=-1, keepdims=True)
        scores[at, :] = (chance * (dprob - centre)).astype(bf16)

    dq = dot(scores[...], k[...]) * scale
    dk = dot(scores[...], q[...], TN) * scale
    dv = dot(probs[...], datt[...], TN)
    of_o[1]()
    c, s = turns(slice(None))
    qkz[:, pl.ds(0, width)] = (dq * c - swap_halves(dq) * s).astype(bf16)
    qkz[:, pl.ds(width, width)] = (dk * c - swap_halves(dk) * s).astype(bf16)
    gate = gate_grads[...]
    lane = lax.broadcasted_iota(jnp.int32, (group, width), 1)
    for e in range(experts):
        vgrads[:, pl.ds(e * width, width)] = (gates[:, e : e + 1] * dv).astype(bf16)
        one = jnp.sum(vx[:, pl.ds(e * width, width)].astype(f32) * dv, axis=-1, keepdims=True)
        gate = jnp.where(lane == e, one, gate)
    qkz[:, pl.ds(2 * width, width)] = (gate * gates[...] * (1.0 - gates[...])).astype(bf16)

    scaled_qkz = (qkz[...].astype(f32) * gates[:, width - 1 : width]).astype(bf16)

    def matrix_rows(c):
        at = at_block(c, column)
        sums[at, pl.ds(0, 3 * width)] = dot(turned[at, :], scaled_qkz).astype(bf16)
        sums[at, pl.ds(3 * width, experts * width)] = dot(turned[at, :], vgrads[...]).astype(bf16)

    steps_each = features // column // 2
    for n in range(2):
        pl.loop(n * steps_each, (n + 1) * steps_each)(matrix_rows)
        of_d[n][0]()
    def into_rows(block):
        at = at_block(block, tokens)
        inverse = gates[at, width - 1 : width]
        unit = rows[at, :].astype(f32) * inverse
        through = dot(qkz[at, :], w_an[...], NT)
        scaled = through * attend_gain
        total = inverse * (
            scaled - unit * jnp.mean(scaled * unit, axis=-1, keepdims=True)
        ) + dot(vgrads[at, :], w_v[...], NT)
        return total, jnp.sum(through * unit, axis=0, keepdims=True)

    to_x = chain_sum(8, part, got)
    gain = jnp.zeros((1, features), f32)
    for number in range(last):
        total, one = into_rows(leaving[number])
        gain += one
        part[at_block(leaving[number], tokens), :] = total.astype(bf16)
        to_x[0](number)
        if number < 2:
            of_d[number][1]()
    total, one = into_rows(h)
    sums[at_a, :] = jnp.broadcast_to(gain + one, (16, features)).astype(bf16)
    of_a[0]()
    grad_x_ref[...] += total
    to_out[1](0)
    to_out[1](1)
    of_a[1]()
    of_g[2]()
    small_block = at_block(h, small)
    blocks[small_block, :] = piece[at_g, :]
    g_copies = spread(9, lambda s: blocks.at[small_block, :], lambda s: blocks.at[small_block, :])
    to_x[1](0)
    to_out[1](2)
    of_o[2]()
    out_o[0]()
    to_x[1](1)
    to_x[1](2)
    of_d[0][2]()
    out_d[0][0]()
    of_a[2]()
    gain_part[...] = piece[at_a, :]
    gain_copies = spread(10, lambda s: gain_part, lambda s: gain_got.at[s - 1])
    of_d[1][2]()
    out_d[1][0]()
    for step in peers:
        g_copies[step].wait()
    out_g[0]()
    gain = gain_part[...].astype(f32)
    for step in peers:
        gain_copies[step].wait()
        gain += gain_got[step - 1].astype(f32)
    piece[at_a, :] = gain.astype(bf16)
    out_a[0]()
    to_x[2](grad_x_ref)
    output_ref[...] = middle[...] + outs[own_block, :].astype(f32)
    to_out[2](output_ref)
    for half in range(2):
        first_hop(half, 0, chip)
        for copy in lasts[half]:
            copy.wait()
        at_in = (chip, halves_in[half], own_side)
        at_out = (chip, halves_out(core)[half], slice(None))
        w_in[at_in] = w_in[at_in] + hop_in[half, 1]
        w_out[at_out] = w_out[at_out] + hop_out[half, 1]
    stores = (
        pltpu.make_async_copy(w_in.at[chip, :, own_side], fin_in_ref, local_sem.at[0]),
        pltpu.make_async_copy(w_out.at[chip, own_side, :], fin_out_ref, local_sem.at[1]),
    )
    for store in stores:
        store.start()
    for one in (out_o, out_d[0], out_g, out_a, out_d[1]):
        one[1]()
    for one in (out_o, out_d[0], out_g, out_a, out_d[1]):
        one[2]()
    for store in stores:
        store.wait()
    mr_end()
    da_end()


def layer_call(n_dp, n_head, args):
    x, picks, router, value_mat, expert_in = args[0], args[2], args[13], args[11], args[14]
    tokens, features = x.shape
    per_device, _, width = expert_in.shape
    held_experts = value_mat.shape[1]
    group = tokens * n_head
    chips = n_dp // 2
    slab = per_device * width
    lanes = 128
    peers = n_head - 1
    named = ceil_to(n_dp * per_device, 8)
    small = ceil_to(named + 1, 16)
    top = features + held_experts
    held = top + 16 + small
    strip = features // n_dp
    shape = jax.ShapeDtypeStruct
    vm, dma = pltpu.VMEM, pltpu.SemaphoreType.DMA
    outs = [
        (shape((tokens, features), f32), VM),
        (shape((tokens, features), f32), VM),
        (shape((top + 16 + n_head * small, features), bf16), ANY),
        (shape((features, slab), bf16), ANY),
        (shape((slab, features), bf16), ANY),
    ]
    scratch = dict(
        picks=vm(picks.shape, jnp.int32),
        two_picks=vm((2, *args[3].shape), jnp.int32),
        head_picks=vm((group, lanes), jnp.int32),
        w_g=vm(args[10].shape, bf16),
        w_r=vm(router.shape, bf16),
        seg=vm((1, group), jnp.int32),
        gains=vm(args[6].shape, f32),
        angles=vm((group, width), f32),
        w_an=vm((features, 3 * width), bf16),
        w_v=vm((features, held_experts), bf16),
        w_o=vm((held_experts, features), bf16),
        my_router=vm((features, lanes), bf16),
        w_in=vm((chips, features, 2 * slab), bf16),
        w_out=vm((chips, 2 * slab, features), bf16),
        rows=vm((group, features), bf16),
        cot=vm((group, features), bf16),
        mrs=vm((group, features), bf16),
        das=vm((group, features), bf16),
        turned=vm((features, group), bf16),
        my_mask=vm((n_head, tokens, lanes), bf16),
        all_mask=vm((group, lanes), bf16),
        gates=vm((group, width), f32),
        q=vm((group, width), bf16),
        k=vm((group, width), bf16),
        v=vm((group, width), bf16),
        vx=vm((group, held_experts), bf16),
        att=vm((group, width), f32),
        part=vm((group, features), bf16),
        got=vm((2 * peers, tokens, features), bf16),
        outs=vm((group, features), bf16),
        got_out=vm((2 * peers, tokens, features), bf16),
        lifted=vm((chips, 2, group, slab), bf16),
        core_out=vm((chips, slab, features), bf16),
        acts=vm((chips, group, 2 * slab), bf16),
        hids=vm((chips, group, 2 * slab), bf16),
        dzs=vm((group, lanes), bf16),
        datt=vm((group, width), bf16),
        gate_grads=vm((group, width), f32),
        probs=vm((group, group), bf16),
        scores=vm((group, group), bf16),
        qkz=vm((group, 3 * width), bf16),
        vgrads=vm((group, held_experts), bf16),
        gain_part=vm((16, strip), bf16),
        gain_got=vm((peers, 16, strip), bf16),
        sums=vm((held, features), bf16),
        core_got=vm((held, features // 2), bf16),
        chip_got=vm((chips - 1, held, strip), bf16),
        piece=vm((held, strip), bf16),
        blocks=vm((n_head * small, strip), bf16),
        hop_in=vm((2, 2, features // 2, slab), bf16),
        hop_out=vm((2, 2, slab // 2, features), bf16),
        local_sem=dma((16 + 1 + per_device,)),
        z_send=dma((11, 4 * peers)),
        z_recv=dma((11, 4 * peers)),
        w_send=dma((22,)),
        w_recv=dma((22,)),
        c_send=dma((3, chips)),
        c_recv=dma((3, chips)),
        e_send=dma((2, 6)),
        e_recv=dma((2, 6)),
        s_send=dma((5, 3 * chips)),
        s_recv=dma((5, 3 * chips)),
        ready=pltpu.SemaphoreType.REGULAR,
        free=pltpu.SemaphoreType.REGULAR((2,)),
    )
    return pl.pallas_call(
        functools.partial(layer_kernel, n_dp, n_head),
        out_shape=[o[0] for o in outs],
        out_specs=[o[1] for o in outs],
        in_specs=[ANY] * 16,
        scratch_shapes=list(scratch.values()),
        compiler_params=pltpu.CompilerParams(
            collective_id=1, has_side_effects=True, vmem_limit_bytes=vmem_bytes
        ),
    )(*args)


def finish_kernel(
    n_dp,
    n_head,
    output_ref,
    grad_x_ref,
    wide_ref,
    in_ref,
    out_ref,
    gain_ref,
    final_ref,
    input_ref,
    attend_ref,
    query_ref,
    key_ref,
    value_ref,
    mix_ref,
    gate_ref,
    expert_ref,
    router_ref,
    grad_in_ref,
    grad_out_ref,
    wide,
    flat_in,
    flat_out,
    value,
    mix,
    grad_in,
    grad_out,
    output,
    grad_x,
    sem,
):
    features, slab = in_ref.shape
    per_device, _, width = grad_in_ref.shape
    experts_total, gates = router_ref.shape[0], gate_ref.shape[0]
    mixed = mix_ref.shape[0]
    top = features + 16 + mixed
    small = (wide_ref.shape[0] - top) // n_head
    named = n_dp * per_device

    def copy(src, dst, number):
        one = pltpu.make_async_copy(src, dst, sem.at[number])
        one.start()
        return one

    rest = pl.ds(top, wide_ref.shape[0] - top)
    loads = [
        copy(wide_ref.at[pl.ds(0, features), :], wide.at[pl.ds(0, features), :], 0),
        copy(wide_ref.at[pl.ds(features, top - features), :], wide.at[pl.ds(features, top - features), :], 1),
        copy(in_ref, flat_in, 2),
        copy(out_ref, flat_out, 3),
        copy(wide_ref.at[rest, :], wide.at[rest, :], 4),
    ]
    loads += [copy(output_ref, output, 11), copy(grad_x_ref, grad_x, 12)]
    stores = []
    for number, (held, result) in enumerate(((output, final_ref), (grad_x, input_ref))):
        loads[5 + number].wait()
        stores.append(copy(held, result, 5 + number))
    loads[0].wait()
    first = pl.ds(0, features)
    value[...] = wide[first, pl.ds(3 * width, value.shape[1])].astype(f32)
    stores.append(copy(value, value_ref, 7))
    gain = jnp.broadcast_to(gain_ref[0:1, :], (width, features)).T
    query_ref[...] = wide[first, pl.ds(0, width)].astype(f32) * gain
    key_ref[...] = wide[first, pl.ds(width, width)].astype(f32) * gain
    gate_ref[...] = (wide[first, pl.ds(2 * width, width)].astype(f32) * gain).T[:gates]
    loads[1].wait()
    mix[...] = wide[pl.ds(features + 16, mixed), :].astype(f32)
    stores.append(copy(mix, mix_ref, 8))
    loads[2].wait()
    for e in range(per_device):
        grad_in[e] = flat_in[:, pl.ds(e * width, width)].astype(f32)
    stores.append(copy(grad_in, grad_in_ref, 9))
    loads[3].wait()
    for e in range(per_device):
        grad_out[e] = flat_out[pl.ds(e * width, width), :].astype(f32)
    stores.append(copy(grad_out, grad_out_ref, 10))
    loads[4].wait()
    attend_ref[...] = wide[pl.ds(features, 16), :][0:1].astype(f32)
    planes = wide[pl.ds(top, n_head * small), :]
    place = lax.broadcasted_iota(jnp.int32, (n_head * small, experts_total), 0)
    name = lax.broadcasted_iota(jnp.int32, (n_head * small, experts_total), 1)
    slot, plane = place % small, place // small
    expert = (slot // per_device * n_head + plane) * per_device + slot % per_device
    chosen = (slot < named) & (expert == name)
    router_ref[...] = dot(jnp.where(chosen, 1.0, 0.0).astype(bf16), planes, TN)
    gain = jnp.zeros((1, features), f32)
    for z in range(n_head):
        row = z * small + ceil_to(named, 8)
        gain += planes[row : row + 1].astype(f32)
    expert_ref[...] = gain
    for store in stores:
        store.wait()


def finish_call(n_dp, n_head, shapes, args):
    shape = jax.ShapeDtypeStruct
    wide, flat_in, flat_out = args[2], args[3], args[4]
    value, mix, grad_in, grad_out = shapes[5], shapes[6], shapes[10], shapes[11]
    specs = [VM] * 12
    for number in (0, 1, 5, 6, 10, 11):
        specs[number] = ANY
    return pl.pallas_call(
        functools.partial(finish_kernel, n_dp, n_head),
        out_shape=[shape(s, f32) for s in shapes],
        out_specs=specs,
        in_specs=[ANY] * 5 + [VM],
        scratch_shapes=[
            pltpu.VMEM(wide.shape, bf16),
            pltpu.VMEM(flat_in.shape, bf16),
            pltpu.VMEM(flat_out.shape, bf16),
            pltpu.VMEM(value, f32),
            pltpu.VMEM(mix, f32),
            pltpu.VMEM(grad_in, f32),
            pltpu.VMEM(grad_out, f32),
            pltpu.VMEM(shapes[0], f32),
            pltpu.VMEM(shapes[1], f32),
            pltpu.SemaphoreType.DMA((13,)),
        ],
        compiler_params=pltpu.CompilerParams(vmem_limit_bytes=60 << 20),
    )(*args)


def kernel_body(
    n_dp,
    n_head,
    hidden_in,
    segments,
    value_pick,
    output_pick,
    expert_pick,
    attend_gain,
    query_weight,
    key_weight,
    value_weight,
    output_weight,
    head_router,
    expert_gain,
    router,
    expert_in,
    expert_out,
    cotangent,
):
    tokens, features = hidden_in.shape
    per_device, _, width = expert_in.shape
    experts = head_router.shape[2] // 2
    group = tokens * n_head
    angles = np.arange(group)[:, None] * theta ** (-2.0 * np.arange(width // 2) / width)[None, :]
    angles = np.concatenate([np.cos(angles), np.sin(angles)], axis=1).astype(np.float32)
    both = np.eye(2, dtype=np.float32)
    gains = attend_gain.astype(f32) * both[:, :1] + expert_gain.astype(f32) * both[:, 1:]
    results = layer_call(
        n_dp,
        n_head,
        (
            hidden_in,
            cotangent,
            expert_pick.T,
            value_pick.transpose(1, 2, 0)[0],
            output_pick.transpose(1, 2, 0)[0],
            segments[None, :],
            gains,
            angles,
            query_weight[0],
            key_weight[0],
            head_router.transpose(0, 2, 1)[0],
            value_weight[0],
            output_weight[0],
            router.T,
            expert_in,
            expert_out.reshape(per_device * width, features),
        ),
    )
    shapes = (
        (tokens, features),
        (tokens, features),
        (1, features),
        query_weight.shape[1:],
        key_weight.shape[1:],
        value_weight.shape[1:],
        output_weight.shape[1:],
        (2 * experts, features),
        (1, features),
        (router.shape[1], features),
        expert_in.shape,
        expert_out.shape,
    )
    done = list(finish_call(n_dp, n_head, shapes, (*results, gains)))
    for number in (3, 4, 5, 6, 7):
        done[number] = done[number][None]
    done[7] = done[7].transpose(0, 2, 1)
    done[9] = done[9].T
    done[2], done[8] = done[2][0], done[8][0]
    return tuple(done)


def solution(mesh):
    rows = P(everywhere, None)
    heads = P("head", None, None)
    experts = P(everywhere, None, None)
    picks = P("dp", "head", None)
    in_specs = (
        rows, P("dp"), picks, picks, rows, P(), heads, heads, heads, heads, heads,
        P(), P(), experts, experts, rows,
    )
    out_specs = (
        rows, rows, P(), heads, heads, heads, heads, heads, P(), P(), experts, experts,
    )
    n_dp, n_head = mesh.shape["dp"], mesh.shape["head"]

    def program(*args):
        held = 2 * n_dp * args[13].shape[0] * args[13].shape[1] * args[13].shape[2] * 2
        if n_head == 4 and held <= vmem_for_weights:
            return kernel_body(n_dp, n_head, *args)
        return body(*args)

    return jax.shard_map(program, mesh=mesh, in_specs=in_specs, out_specs=out_specs, check_vma=False)
```

```python
import functools

import jax
import jax.numpy as jnp
import numpy as np
from jax import lax
from jax.experimental import pallas as pl
from jax.experimental.pallas import tpu as pltpu
from jax.sharding import PartitionSpec as P

epsilon = 1e-06
theta = 10000.0
negative = -1e30
f32 = jnp.float32
bf16 = jnp.bfloat16
everywhere = ("dp", "head")
whole_rows = 4096
vmem_for_weights = 16 << 20
vmem_bytes = 62 << 20


def product(left, right, left_axis, right_axis):
    return lax.dot_general(
        left, right, (((left_axis,), (right_axis,)), ((), ())), preferred_element_type=f32
    )


def rms_scale(residual):
    return lax.rsqrt(jnp.mean(residual * residual, axis=-1, keepdims=True) + epsilon)


def rotary_tables(row_count, head_width):
    half_width = head_width // 2
    position = jnp.arange(row_count, dtype=f32)[:, None]
    exponent = jnp.arange(half_width, dtype=f32)[None, :]
    angles = position * jnp.power(theta, -2.0 * exponent / head_width)
    return (jnp.cos(angles), jnp.sin(angles))


def rotate(matrix, cosine, sine):
    half = matrix.shape[-1] // 2
    first, second = matrix[:, :half], matrix[:, half:]
    return jnp.concatenate([first * cosine - second * sine, second * cosine + first * sine], axis=-1)


def pick_mask(picks, expert_count):
    hits = picks[:, 0, :, None] == jnp.arange(expert_count, dtype=jnp.int32)[None, None, :]
    return jnp.any(hits, axis=1).astype(f32)


def norm_back(residual, inverse, gain, incoming):
    unit_rows = residual * inverse
    scaled = incoming * gain
    gain_grad = jnp.sum(incoming * unit_rows, axis=0)
    row_grad = inverse * (scaled - unit_rows * jnp.mean(scaled * unit_rows, axis=-1, keepdims=True))
    return (row_grad, gain_grad)


def gelu_pair(value):
    inner = jnp.tanh(0.7978845608028654 * (value + 0.044715 * value * value * value))
    slope = 0.5 * (1.0 + inner) + 0.5 * value * (1.0 - inner * inner) * 0.7978845608028654 * (
        1.0 + 3.0 * 0.044715 * value * value
    )
    return (0.5 * value * (1.0 + inner), slope)


def body(
    hidden_in,
    segments,
    value_pick,
    output_pick,
    expert_pick,
    attend_gain,
    query_weight,
    key_weight,
    value_weight,
    output_weight,
    head_router,
    expert_gain,
    router,
    expert_in,
    expert_out,
    cotangent,
):
    tokens, features = hidden_in.shape
    per_device, _, width = expert_in.shape
    head_experts = head_router.shape[2] // 2
    head_width = query_weight.shape[2]
    scale = head_width ** (-0.5)
    query_mat, key_mat, value_mat = query_weight[0], key_weight[0], value_weight[0]
    output_mat, gate_mat = output_weight[0], head_router[0]
    value_mask = pick_mask(value_pick, head_experts)
    output_mask = pick_mask(output_pick, head_experts)
    attend_scale = attend_gain.astype(f32)
    expert_scale = expert_gain.astype(f32)
    me = lax.axis_index("dp") * lax.axis_size("head") + lax.axis_index("head")

    rows = lax.all_gather(hidden_in, "head", axis=0, tiled=True)
    grouped = rows.astype(f32)
    group = grouped.shape[0]
    inverse = rms_scale(grouped)
    normed = (grouped * inverse * attend_scale).astype(bf16)
    cosine, sine = rotary_tables(group, head_width)
    queries = rotate(product(normed, query_mat, 1, 0), cosine, sine).astype(bf16)
    key_rows = rotate(product(normed, key_mat, 1, 0), cosine, sine).astype(bf16)
    squash = jax.nn.sigmoid(product(normed, gate_mat, 1, 0))
    value_gates = squash[:, :head_experts] * value_mask
    output_gates = squash[:, head_experts:] * output_mask
    expert_values = product(rows, value_mat, 1, 0).reshape(group, head_experts, head_width)
    values = jnp.sum(expert_values * value_gates[:, :, None], axis=1).astype(bf16)
    places = jnp.arange(group, dtype=jnp.int32)
    allowed = (places[None, :] <= places[:, None]) & (segments[:, None] == segments[None, :])
    scores = jnp.where(allowed, product(queries, key_rows, 1, 1) * scale, negative)
    exponents = jnp.exp(scores - jnp.max(scores, axis=-1, keepdims=True))
    probabilities = exponents / jnp.sum(exponents, axis=-1, keepdims=True)
    attended = product(probabilities.astype(bf16), values, 1, 0)
    weighted = (
        (output_gates[:, :, None] * attended[:, None, :]).reshape(group, -1).astype(bf16)
    )
    middle = hidden_in.astype(f32) + lax.psum_scatter(
        product(weighted, output_mat, 1, 0).astype(bf16), "head", scatter_dimension=0, tiled=True
    ).astype(f32)
    middle_inverse = rms_scale(middle)
    middle_normed = (middle * middle_inverse * expert_scale).astype(bf16)
    mine = me * per_device + jnp.arange(per_device, dtype=jnp.int32)
    my_router = lax.dynamic_slice_in_dim(router, me * per_device, per_device, axis=1)
    in_mat = expert_in.transpose(1, 0, 2).reshape(features, per_device * width)
    out_mat = expert_out.reshape(per_device * width, features)

    def turn(running, own):
        own_rows, own_cot, own_picks = own
        all_cot = lax.all_gather(own_cot, everywhere, axis=0, tiled=True)
        all_picks = lax.all_gather(own_picks, everywhere, axis=0, tiled=True)
        all_rows = lax.all_gather(own_rows, everywhere, axis=0, tiled=True)
        mask = jnp.any(all_picks[:, :, None] == mine[None, None, :], axis=1).astype(f32)
        gates = jax.nn.sigmoid(product(all_rows, my_router, 1, 0))
        live = gates * mask
        act, slope = gelu_pair(product(all_rows, in_mat, 1, 0).reshape(-1, per_device, width))
        lifted = product(all_cot, out_mat, 1, 1).reshape(-1, per_device, width)
        dense_grad = (jnp.sum(act * lifted, axis=-1) * live * (1.0 - gates)).astype(bf16)
        act_live = (act * live[:, :, None]).astype(bf16).reshape(-1, per_device * width)
        hidden_grad = (slope * lifted * live[:, :, None]).astype(bf16)
        hidden_grad = hidden_grad.reshape(-1, per_device * width)
        part_out = product(act_live, out_mat, 1, 0).astype(bf16)
        part_grad = (
            product(hidden_grad, in_mat, 1, 1) + product(dense_grad, my_router, 1, 1)
        ).astype(bf16)
        back = lax.psum_scatter(part_grad, everywhere, scatter_dimension=0, tiled=True)
        forth = lax.psum_scatter(part_out, everywhere, scatter_dimension=0, tiled=True)
        grads = (
            product(all_rows, hidden_grad, 0, 0),
            product(act_live, all_cot, 0, 0),
            product(dense_grad, all_rows, 0, 0),
        )
        if running is not None:
            grads = jax.tree.map(jnp.add, running, grads)
        return grads, (forth, back)

    turns = max(1, lax.axis_size("dp") * lax.axis_size("head") * tokens // whole_rows)
    owned = (middle_normed, cotangent, expert_pick)
    if turns == 1:
        grads, (summed, normed_grad) = turn(None, owned)
    else:
        owned = jax.tree.map(lambda a: a.reshape(turns, -1, a.shape[1]), owned)
        zeros = (
            jnp.zeros(in_mat.shape, f32),
            jnp.zeros(out_mat.shape, f32),
            jnp.zeros((per_device, features), f32),
        )
        grads, sums = lax.scan(turn, zeros, owned)
        summed, normed_grad = (a.reshape(tokens, features) for a in sums)
    grad_in = grads[0].reshape(features, per_device, width).transpose(1, 0, 2)
    grad_out = grads[1].reshape(per_device, width, features)
    grad_router = lax.all_gather(grads[2], everywhere, axis=0, tiled=True).T
    output = middle + summed.astype(f32)
    incoming = cotangent.astype(f32)
    row_grad, grad_gain_expert = norm_back(
        middle, middle_inverse, expert_scale, normed_grad.astype(f32)
    )
    middle_grad = incoming + row_grad
    group_grads = lax.all_gather(middle_grad.astype(bf16), "head", axis=0, tiled=True)
    weighted_grad = product(group_grads, output_mat, 1, 1).reshape(group, head_experts, head_width)
    output_grad = product(weighted, group_grads, 0, 0)
    output_gate_grad = jnp.sum(weighted_grad * attended[:, None, :], axis=-1)
    attended_grad = jnp.sum(weighted_grad * output_gates[:, :, None], axis=1).astype(bf16)
    prob_grad = product(attended_grad, values, 1, 1)
    centre = jnp.sum(probabilities * prob_grad, axis=-1, keepdims=True)
    score_grad = (probabilities * (prob_grad - centre)).astype(bf16)
    query_grad = product(score_grad, key_rows, 1, 0) * scale
    key_grad = product(score_grad, queries, 0, 0) * scale
    values_grad = product(probabilities.astype(bf16), attended_grad, 0, 0)
    expert_grad = (value_gates[:, :, None] * values_grad[:, None, :]).reshape(group, -1).astype(bf16)
    value_gate_grad = jnp.sum(expert_values * values_grad[:, None, :], axis=-1)
    query_grad = rotate(query_grad, cosine, -sine).astype(bf16)
    key_grad = rotate(key_grad, cosine, -sine).astype(bf16)
    logit_grad = (
        jnp.concatenate([value_gate_grad * value_mask, output_gate_grad * output_mask], axis=1)
        * squash
        * (1.0 - squash)
    ).astype(bf16)
    head_grads = (
        product(normed, query_grad, 0, 0),
        product(normed, key_grad, 0, 0),
        product(rows, expert_grad, 0, 0),
        output_grad,
        product(normed, logit_grad, 0, 0),
    )
    head_grads = tuple(grad.astype(bf16) for grad in head_grads)
    head_grads = tuple(grad.astype(f32)[None] for grad in lax.psum(head_grads, "dp"))
    back = (
        product(query_grad, query_mat, 1, 1)
        + product(key_grad, key_mat, 1, 1)
        + product(logit_grad, gate_mat, 1, 1)
    )
    row_back, grad_attend = norm_back(grouped, inverse, attend_scale, back)
    partial = (row_back + product(expert_grad, value_mat, 1, 1)).astype(bf16)
    input_grad = middle_grad + lax.psum_scatter(
        partial, "head", scatter_dimension=0, tiled=True
    ).astype(f32)
    grad_attend, grad_gain_expert = lax.psum((grad_attend, grad_gain_expert), everywhere)
    return (
        output,
        input_grad,
        grad_attend,
        *head_grads,
        grad_gain_expert,
        grad_router,
        grad_in,
        grad_out,
    )


MESH = pl.DeviceIdType.MESH
VM = pl.BlockSpec(memory_space=pltpu.VMEM)
ANY = pl.BlockSpec(memory_space=pl.ANY)
NN = (((1,), (0,)), ((), ()))
NT = (((1,), (1,)), ((), ()))
TN = (((0,), (0,)), ((), ()))


def dot(left, right, dims=NN):
    return lax.dot_general(left, right, dims, preferred_element_type=f32)


def at_block(block, count):
    return pl.ds(pl.multiple_of(block * count, count), count)


def remote(src, dst, send, recv, where):
    return pltpu.make_async_remote_copy(
        src_ref=src, dst_ref=dst, send_sem=send, recv_sem=recv, device_id=where, device_id_type=MESH
    )


def swap_halves(value):
    half = value.shape[-1] // 2
    return jnp.concatenate([value[:, half:], value[:, :half]], axis=-1)


def ceil_to(number, step):
    return -(-number // step) * step


def layer_kernel(
    n_dp,
    n_head,
    x_ref,
    cot_ref,
    pick_ref,
    value_pick_ref,
    output_pick_ref,
    seg_ref,
    gain_ref,
    angle_ref,
    wq_ref,
    wk_ref,
    wg_ref,
    wv_ref,
    wo_ref,
    router_ref,
    in_ref,
    out_ref,
    output_ref,
    grad_x_ref,
    wide_ref,
    fin_in_ref,
    fin_out_ref,
    picks,
    two_picks,
    head_picks,
    w_g,
    w_r,
    seg,
    gains,
    angles,
    w_an,
    w_v,
    w_o,
    my_router,
    w_in,
    w_out,
    rows,
    cot,
    mrs,
    das,
    turned,
    my_mask,
    all_mask,
    gates,
    q,
    k,
    v,
    vx,
    att,
    part,
    got,
    outs,
    got_out,
    lifted,
    core_out,
    acts,
    hids,
    dzs,
    datt,
    gate_grads,
    probs,
    scores,
    qkz,
    vgrads,
    gain_part,
    gain_got,
    sums,
    core_got,
    chip_got,
    piece,
    blocks,
    hop_in,
    hop_out,
    local_sem,
    z_send,
    z_recv,
    w_send,
    w_recv,
    c_send,
    c_recv,
    e_send,
    e_recv,
    s_send,
    s_recv,
    t_send,
    t_recv,
    ready,
    free,
):
    middle = output_ref
    xor = jnp.bitwise_xor
    d, h = lax.axis_index("dp"), lax.axis_index("head")
    chip, core = d // 2, d % 2
    chips = n_dp // 2
    tokens, features = x_ref.shape
    per_device, _, width = in_ref.shape
    slab = per_device * width
    wide = 2 * slab
    experts = wv_ref.shape[1] // width
    named = ceil_to(n_dp * per_device, 8)
    group = tokens * n_head
    pair = 2 * tokens
    column = 256
    lanes = 128
    scale = width ** (-0.5)
    peers = (2, 3, 1)
    partner = (chip * 2 + 1 - core, h)
    own_block = at_block(h, tokens)
    own_side, other_side = at_block(core, slab), at_block(1 - core, slab)
    halves_in = (pl.ds(0, features // 2), pl.ds(features // 2, features // 2))
    halves_out = lambda side: (
        at_block(2 * side, slab // 2),
        at_block(2 * side + 1, slab // 2),
    )

    def along(step):
        return (d, xor(h, step))

    def across(step):
        return (xor(chip, step) * 2 + core, h)

    loads = []

    def load(src, dst):
        copy = pltpu.make_async_copy(src, dst, local_sem.at[len(loads)])
        copy.start()
        loads.append(copy)
        return copy

    own_weights = [load(out_ref, w_out.at[chip, own_side, :])] + [
        load(in_ref.at[e], w_in.at[chip, :, at_block(core * per_device + e, width)])
        for e in range(per_device)
    ]
    for_rows = [
        load(x_ref, rows.at[own_block, :]),
        load(gain_ref, gains),
        load(wg_ref, w_g),
        load(wq_ref, w_an.at[:, pl.ds(0, width)]),
        load(wk_ref, w_an.at[:, pl.ds(width, width)]),
        load(wv_ref, w_v),
        load(value_pick_ref, two_picks.at[0]),
        load(output_pick_ref, two_picks.at[1]),
        load(angle_ref, angles),
    ]
    for_scores = [load(seg_ref, seg), load(wo_ref, w_o)]
    for_mask = load(pick_ref, picks)
    for_cot = load(cot_ref, cot.at[own_block, :])
    for_router = load(router_ref, w_r)

    barrier = pltpu.get_barrier_semaphore()
    friends = [along(s) for s in peers] + [partner] + [across(s) for s in range(1, chips)]
    for friend in friends:
        pl.semaphore_signal(barrier, inc=1, device_id=friend, device_id_type=MESH)
    pl.semaphore_wait(barrier, len(friends))

    right, left = (d, jnp.minimum(h + 1, n_head - 1)), (d, jnp.maximum(h - 1, 0))
    last = n_head - 1

    def pick(*by_place):
        value = jnp.int32(by_place[-1])
        for place in range(n_head - 2, -1, -1):
            value = jnp.where(h == place, by_place[place], value)
        return value

    arrival = (xor(h, 1), pick(2, 2, 1, 1), pick(3, 3, 0, 0))
    leaving = (pick(3, 3, 0, 0), pick(2, 0, 3, 1), pick(1, 2, 1, 2))

    def gather(kind, buffer):
        def go(side, step):
            block = jnp.clip(h - step if side == 0 else h + step, 0, last)
            copies = []
            for half in range(2):
                here = buffer.at[at_block(2 * block + half, tokens // 2), :]
                number = (side * last + step) * 2 + half
                copies.append(
                    remote(
                        here, here, z_send.at[kind, number], z_recv.at[kind, number], (right, left)[side]
                    )
                )
            return copies

        def begin(side):
            for copy in go(side, 0):
                copy.start()

        def start():
            pl.when(h < last)(lambda: begin(0))
            pl.when(h > 0)(lambda: begin(1))

        def arrive(side, step, there, onward):
            for half in range(2):

                @pl.when(there)
                def _():
                    go(side, step - 1)[half].wait_recv()
                    if onward:
                        go(side, step)[half].start()

        def stage(step, which="all"):
            ways = ((0, h >= step, h < last), (1, h + step <= last, h > 0))
            for side, there, onward in ways:
                if step < last and which != "rest":
                    arrive(side, step, there & onward, True)
            for side, there, onward in ways:
                if which != "duty":
                    ends_here = there if step == last else there & jnp.logical_not(onward)
                    arrive(side, step, ends_here, False)

        def follow(step):
            pl.when((h < last) & (jnp.maximum(h, 1) == step))(lambda: begin(0))
            pl.when((h > 0) & (jnp.maximum(last - h, 1) == step))(lambda: begin(1))

        def end():
            for step in range(last):
                for side, sent in (
                    (0, (h >= step) & (h < last)),
                    (1, (h + step <= last) & (h > 0)),
                ):

                    @pl.when(sent)
                    def _():
                        for copy in go(side, step):
                            copy.wait_send()

        return start, stage, end, follow

    def chain_sum(kind, parts, slots):
        def go(number):
            block = leaving[number]
            rightward = block > h
            slot = jnp.where(rightward, block - 1, last + block)
            where = (d, jnp.clip(jnp.where(rightward, h + 1, h - 1), 0, last))
            middle_one = (rightward & (h > 0)) | (jnp.logical_not(rightward) & (h < last))
            pieces = []
            for half in range(2):
                at = at_block(2 * block + half, tokens // 2)
                rows_of = pl.ds(half * (tokens // 2), tokens // 2)
                copy = remote(
                    parts.at[at, :],
                    slots.at[slot, rows_of, :],
                    z_send.at[kind, 2 * number + half],
                    z_recv.at[kind, 2 * slot + half],
                    where,
                )
                pieces.append((copy, at, slot, rows_of))
            return pieces, middle_one

        def now(number):
            pieces, middle_one = go(number)

            @pl.when(jnp.logical_not(middle_one))
            def _():
                for copy, _, _, _ in pieces:
                    copy.start()

        def later(number):
            pieces, middle_one = go(number)

            @pl.when(middle_one)
            def _():
                for copy, at, slot, rows_of in pieces:
                    copy.wait_recv()
                    parts[at, :] = parts[at, :] + slots[slot, rows_of, :]
                    copy.start()

        def end(total):
            ends = ((jnp.maximum(h - 1, 0), h > 0), (last + jnp.minimum(h, last - 1), h < last))
            for slot, there in ends:

                @pl.when(there)
                def _():
                    for half in range(2):
                        rows_of = pl.ds(half * (tokens // 2), tokens // 2)
                        remote(
                            parts.at[at_block(2 * h, tokens // 2), :],
                            slots.at[slot, rows_of, :],
                            z_send.at[kind, 0],
                            z_recv.at[kind, 2 * slot + half],
                            right,
                        ).wait_recv()
                    total[...] += slots[slot].astype(f32)

            for number in range(last):
                for copy, _, _, _ in go(number)[0]:
                    copy.wait_send()

        return now, later, end

    def spread(kind, src, dst, steps=peers):
        copies = {}
        for step in steps:
            copies[step] = remote(
                src(step), dst(step), z_send.at[kind, step - 1], z_recv.at[kind, step - 1], along(step)
            )
            copies[step].start()
        return copies

    x_start, x_stage, x_end, _ = gather(0, rows)
    for_rows[0].wait()
    x_start()

    def slot(array, place, side, half=None):
        if array == 0:
            at = halves_out(side)[half] if half is not None else at_block(side, slab)
            return w_out.at[place, at, :]
        at = halves_in[half] if half is not None else pl.ds(0, features)
        return w_in.at[place, at, at_block(side, slab)]

    def weights(number, ref, where):
        copy = remote(ref, ref, w_send.at[number], w_recv.at[number], where)
        copy.start()
        return copy

    slabs, halves_on, to_core, diagonal = {}, {}, {}, {}
    for copy in own_weights:
        copy.wait()
    for array in range(2):
        for first in range(2):
            for bit in (1, 2):
                half = bit - 1 if first == 0 else 2 - bit
                number = ((bit - 1) * 2 + half) * 2 + array
                slabs[bit, half, array] = weights(
                    number, slot(array, chip, core, half), across(bit)
                )
        to_core[0, array] = weights(12 + array, slot(array, chip, core), partner)

    for_mask.wait()
    own_picks = jnp.concatenate(
        [picks[...].astype(f32), jnp.zeros((lanes - picks.shape[0], tokens), f32)], axis=0
    ).T.astype(jnp.int32)
    lane = lax.broadcasted_iota(jnp.int32, (tokens, lanes), 1)
    for plane in range(n_head):
        expert = (lane // per_device * n_head + plane) * per_device + lane % per_device
        expert = jnp.where(lane < n_dp * per_device, expert, -1)
        hit = own_picks[:, 0:1] == expert
        for c in range(1, picks.shape[0]):
            hit = hit | (own_picks[:, c : c + 1] == expert)
        my_mask[plane] = jnp.where(hit, 1.0, 0.0).astype(bf16)
    mask_copies = spread(1, lambda s: my_mask.at[xor(h, s)], lambda s: all_mask.at[own_block, :])
    all_mask[own_block, :] = my_mask[h]

    for copy in for_rows[1:]:
        copy.wait()
    attend_gain = gains[0:1, :]
    expert_gain = gains[1:2, :]
    one_hot = lambda count: jnp.where(
        lax.broadcasted_iota(jnp.int32, (count, width), 0)
        == lax.broadcasted_iota(jnp.int32, (count, width), 1),
        1.0,
        0.0,
    ).astype(bf16)
    w_an[:, pl.ds(2 * width, width)] = dot(w_g[...], one_hot(w_g.shape[0]), TN).astype(bf16)
    uses = two_picks.shape[1]
    head_picks[...] = jnp.concatenate(
        [
            two_picks[0].astype(f32),
            two_picks[1].astype(f32) + experts,
            jnp.zeros((lanes - 2 * uses, group), f32),
        ],
        axis=0,
    ).T.astype(jnp.int32)
    half_lanes = lax.broadcasted_iota(jnp.int32, (1, width), 1) < width // 2

    def turns(at):
        both = angles[at, :]
        turned_over = swap_halves(both)
        return (
            jnp.where(half_lanes, both, turned_over),
            jnp.where(half_lanes, -turned_over, both),
        )

    def project(block):
        at = at_block(block, tokens)
        own = rows[at, :]
        full = own.astype(f32)
        inverse = lax.rsqrt(jnp.mean(full * full, axis=-1, keepdims=True) + epsilon)
        unit = (full * inverse * attend_gain).astype(bf16)
        qkg = dot(unit, w_an[...])
        c, s = turns(at)
        one, two = qkg[:, :width], qkg[:, width : 2 * width]
        q[at, :] = (one * c + swap_halves(one) * s).astype(bf16)
        k[at, :] = (two * c + swap_halves(two) * s).astype(bf16)
        lane = lax.broadcasted_iota(jnp.int32, (tokens, width), 1)
        chosen = head_picks[at, :]
        hit = lane == chosen[:, 0:1]
        for c in range(1, 2 * uses):
            hit = hit | (lane == chosen[:, c : c + 1])
        gate = jnp.where(hit, jax.nn.sigmoid(qkg[:, 2 * width :]), 0.0)
        gates[at, :] = jnp.where(lane == width - 1, inverse, gate)
        values = dot(own, w_v[...])
        vx[at, :] = values.astype(bf16)
        value = gate[:, 0:1] * values[:, :width]
        for e in range(1, experts):
            value += gate[:, e : e + 1] * values[:, e * width : (e + 1) * width]
        v[at, :] = value.astype(bf16)

    project(h)
    _, cot_stage, cot_end, cot_follow = gather(2, cot)
    for_cot.wait()
    for step in (1, 2, 3):
        x_stage(step)
        cot_follow(step)
        project(arrival[step - 1])
    for copy in for_scores:
        copy.wait()
    seg_col = gate_grads
    seg_col[...] = jnp.broadcast_to(seg[...].astype(f32), (lanes, group)).T

    def attend(block):
        at = at_block(block, tokens)
        score = dot(q[at, :], k[...], NT) * scale
        row = block * tokens + lax.broadcasted_iota(jnp.int32, (tokens, group), 0)
        place = lax.broadcasted_iota(jnp.int32, (tokens, group), 1)
        allowed = (place <= row) & (seg_col[at, 0:1] == seg[...].astype(f32))
        score = jnp.where(allowed, score, negative)
        exponents = jnp.exp(score - jnp.max(score, axis=-1, keepdims=True))
        chance = exponents / jnp.sum(exponents, axis=-1, keepdims=True)
        probs[at, :] = chance.astype(bf16)
        attended = dot(chance.astype(bf16), v[...])
        att[at, :] = attended
        gate = gates[at, :]
        weighted = jnp.concatenate(
            [
                (gate[:, experts + e : experts + e + 1] * attended).astype(bf16)
                for e in range(experts)
            ],
            axis=-1,
        )
        return dot(weighted, w_o[...])

    to_mid = chain_sum(3, part, got)
    for number in range(last):
        block = leaving[number]
        part[at_block(block, tokens), :] = attend(block).astype(bf16)
        to_mid[0](number)
    middle[...] = rows[own_block, :].astype(f32) + attend(h)
    cot_stage(1, "duty")
    to_mid[1](0)
    for array in range(2):
        for half in range(2):
            slabs[1 + half, half, array].wait_recv()
            halves_on[half, array] = weights(
                8 + 2 * half + array,
                slot(array, xor(chip, 1 + half), core, half),
                across(2 - half),
            )

    to_mid[1](1)
    cot_stage(2, "duty")
    to_mid[1](2)
    for bit in (1, 2):
        slabs[bit, 2 - bit, 0].wait_recv()
        to_core[bit, 0] = weights(14 + (bit - 1) * 2, slot(0, xor(chip, bit), core), partner)
        slabs[bit, 2 - bit, 1].wait_recv()
        to_core[bit, 1] = weights(15 + (bit - 1) * 2, slot(1, xor(chip, bit), core), partner)
    for_router.wait()
    slot_of = lax.broadcasted_iota(jnp.int32, (w_r.shape[0], lanes), 1)
    name = lax.broadcasted_iota(jnp.int32, (w_r.shape[0], lanes), 0)
    expert = (slot_of // per_device * n_head + h) * per_device + slot_of % per_device
    expert = jnp.where(slot_of < n_dp * per_device, expert, -1)
    my_router[...] = dot(
        w_r[...], jnp.where(name == expert, 1.0, 0.0).astype(bf16), TN
    ).astype(bf16)

    to_mid[2](middle)
    mid = middle[...]
    inverse = lax.rsqrt(jnp.mean(mid * mid, axis=-1, keepdims=True) + epsilon)
    mrs[own_block, :] = (mid * inverse * expert_gain).astype(bf16)
    mr_start, mr_stage, mr_end, _ = gather(4, mrs)
    mr_start()

    def last_halves(array):
        for half in range(2):
            halves_on[half, array].wait_recv()
            diagonal[half, array] = weights(
                18 + 2 * half + array, slot(array, xor(chip, 3), core, half), partner
            )

    for step in (1, 2, 3):
        cot_stage(step, "rest")
    last_halves(0)
    for step in peers:
        mask_copies[step].wait()
    cot_end()
    x_end()

    def weights_here(array):
        for bit in range(3):
            to_core[bit, array].wait_recv()
        for half in range(2):
            diagonal[half, array].wait_recv()

    def weights_sent():
        for array in range(2):
            for bit in range(3):
                to_core[bit, array].wait_send()
            for half in range(2):
                diagonal[half, array].wait_send()
                halves_on[half, array].wait_send()
                for bit in (1, 2):
                    slabs[bit, half, array].wait_send()

    weights_here(0)

    def lift_chip(j):
        lift = dot(cot[...], w_out[j], NT)
        lifted[j, 0] = lift[:, :slab].astype(bf16)
        lifted[j, 1] = lift[:, slab:].astype(bf16)

    pl.loop(0, chips // 2)(lift_chip)
    last_halves(1)
    mr_stage(1)
    pl.loop(chips // 2, chips)(lift_chip)

    weights_here(1)

    def spread_lanes(j):
        lane = lax.broadcasted_iota(jnp.int32, (lanes, wide), 1) // width
        slot = lax.broadcasted_iota(jnp.int32, (lanes, wide), 0)
        return jnp.where(slot == lane + j * (wide // width), 1.0, 0.0).astype(bf16)

    def pair_of_blocks(number, between):
        at = at_block(number, pair)
        own = mrs[at, :]
        gates = jax.nn.sigmoid(dot(own, my_router[...]))
        live = gates * all_mask[at, :].astype(f32)
        narrow = live.astype(bf16)

        def chip_step(j, total):
            pick = spread_lanes(j)
            hidden = dot(own, w_in[j])
            gate = dot(narrow, pick).astype(bf16)
            lift = jnp.concatenate([lifted[j, 0, at, :], lifted[j, 1, at, :]], axis=-1)
            square = hidden * hidden
            inner = jnp.tanh(0.7978845608028654 * hidden * (1.0 + 0.044715 * square))
            half = 0.5 * (1.0 + inner)
            act = hidden * half
            slope = half + act * (1.0 - inner) * (
                0.7978845608028654 + (0.7978845608028654 * 3.0 * 0.044715) * square
            )
            act = act.astype(bf16)
            acts[j, at, :] = act * gate
            hids[j, at, :] = slope.astype(bf16) * (lift * gate)
            return total + dot(act * lift, pick, NT)

        total = lax.fori_loop(0, chips, chip_step, jnp.zeros((pair, lanes), f32))
        dz = (total * live * (1.0 - gates)).astype(bf16)
        dzs[at, :] = dz
        between()

        @pl.loop(0, features // column)
        def _(c):
            part_of = at_block(c, column)
            total = dot(dz, my_router[part_of, :], NT)
            for j in range(chips):
                total += dot(hids[j, at, :], w_in[j, part_of, :], NT)
            part[at, part_of] = total.astype(bf16)

    def outputs():
        @pl.loop(0, features // column)
        def _(c):
            part_of = at_block(c, column)
            total = dot(acts[0], w_out[0, :, part_of])
            for j in range(1, chips):
                total += dot(acts[j], w_out[j, :, part_of])
            outs[:, part_of] = total.astype(bf16)

    near = h // 2
    to_dmr = chain_sum(5, part, got)
    pair_of_blocks(near, lambda: mr_stage(2, "duty"))
    to_dmr[0](2)
    mr_stage(2, "rest")
    mr_stage(3)
    pair_of_blocks(1 - near, lambda: None)
    to_dmr[0](0)
    to_dmr[0](1)
    outputs()
    pl.semaphore_signal(ready, inc=1, device_id=partner, device_id_type=MESH)

    weights_sent()
    turned[...] = mrs[...].T

    def expert_grads(place, at):
        for half in halves_in:
            w_in[place, half, at] = dot(turned[half, :], hids[place, :, at]).astype(bf16)
            w_out[place, at, half] = dot(acts[place, :, at], cot[:, half], TN).astype(bf16)

    def to_other_core(n):
        place = xor(chip, chips - 1 - n)
        copies = [
            remote(
                w_in.at[place, halves_in[half], other_side],
                lifted.at[place, half],
                c_send.at[half, n],
                c_recv.at[half, n],
                partner,
            )
            for half in range(2)
        ]
        copies.append(
            remote(
                w_out.at[place, other_side, :],
                core_out.at[place],
                c_send.at[2, n],
                c_recv.at[2, n],
                partner,
            )
        )
        return copies

    pl.semaphore_wait(ready, 1)

    hops = {}

    def hop(half, index, place, toward):
        copies = (
            remote(
                slot(1, place, core, half),
                hop_in.at[half, index],
                e_send.at[0, 2 * half + index],
                e_recv.at[0, 2 * half + index],
                across(toward),
            ),
            remote(
                slot(0, place, core, half),
                hop_out.at[half, index],
                e_send.at[1, 2 * half + index],
                e_recv.at[1, 2 * half + index],
                across(toward),
            ),
        )
        for copy in copies:
            copy.start()
        hops[half, index] = copies

    def both_cores(n):
        step = chips - 1 - n
        place = xor(chip, step)
        for copy in to_other_core(n):
            copy.wait()
        for half in range(2):
            here = (place, halves_in[half], own_side)
            w_in[here] = w_in[here] + lifted[place, half]
        w_out[place, own_side, :] = w_out[place, own_side, :] + core_out[place]
        if step == 3:
            hop(0, 1, place, 1)
            hop(1, 1, place, 2)
        elif step:
            hop(step - 1, 0, place, step)

    for n in range(chips):
        place = xor(chip, chips - 1 - n)
        expert_grads(place, other_side)
        for copy in to_other_core(n):
            copy.start()
        if n:
            both_cores(n - 1)
        expert_grads(place, own_side)
    to_dmr[1](0)
    both_cores(chips - 1)
    to_dmr[1](1)
    to_dmr[1](2)
    side = features // 2
    strip = side // chips
    col = lambda c, j: at_block(c * chips + j, strip)

    def section(number, first, count):
        at = pl.ds(first, count)
        state = {}

        def sem(n):
            return s_send.at[number, n], s_recv.at[number, n]

        def start():
            state["core"] = remote(
                sums.at[at, at_block(1 - core, side)], core_got.at[at, :], *sem(0), partner
            )
            state["core"].start()

        def mid():
            state["core"].wait()
            half = at_block(core, side)
            sums[at, half] = sums[at, half] + core_got[at, :]
            state["chips"] = []
            for s in range(1, chips):
                copy = remote(
                    sums.at[at, col(core, xor(chip, s))], chip_got.at[s - 1, at, :], *sem(s), across(s)
                )
                copy.start()
                state["chips"].append(copy)

        def add():
            for copy in state["chips"]:
                copy.wait()
            total = sums[at, col(core, chip)].astype(f32)
            for s in range(1, chips):
                total += chip_got[s - 1, at, :].astype(f32)
            piece[at, :] = total.astype(bf16)

        return start, mid, add

    def two_hop_section(number, first, count):
        at = pl.ds(first, count)
        half_at = [pl.ds(first + n * (count // 2), count // 2) for n in range(2)]
        begin, state = section(number, first, count)[0], {}

        def hop(half, index, place, toward, n):
            copy = remote(
                sums.at[half_at[half], col(core, place)],
                chip_got.at[index, half_at[half], :],
                t_send.at[number, n],
                t_recv.at[number, n],
                across(toward),
            )
            copy.start()
            return copy

        def mid():
            over = remote(
                sums.at[at, at_block(1 - core, side)],
                core_got.at[at, :],
                s_send.at[number, 0],
                s_recv.at[number, 0],
                partner,
            )
            over.wait()
            half = at_block(core, side)
            sums[at, half] = sums[at, half] + core_got[at, :]
            for half in range(2):
                toward = 1 + half
                state[half, 1] = hop(half, 1, xor(chip, 3), toward, 2 * half + 1)
                state[half, 0] = hop(half, 0, xor(chip, toward), toward, 2 * half)

        def second():
            for half in range(2):
                here = (half_at[half], col(core, xor(chip, 2 - half)))
                state[half, 1].wait()
                sums[here] = sums[here] + chip_got[1, half_at[half], :]
                state[half, 2] = hop(half, 2, xor(chip, 2 - half), 2 - half, 4 + half)

        def add():
            for half in range(2):
                state[half, 0].wait()
                state[half, 2].wait()
            total = sums[at, col(core, chip)].astype(f32)
            for index in (0, 2):
                total += chip_got[index, at, :].astype(f32)
            piece[at, :] = total.astype(bf16)

        return begin, mid, second, add

    def two_hop_to_plane(number, first, count):
        at = pl.ds(first, count)
        half_at = [pl.ds(first + n * (count // 2), count // 2) for n in range(2)]
        state = {}

        def send(src, rows_of, place, where, n):
            copy = remote(
                src,
                wide_ref.at[rows_of, col(core, place)],
                t_send.at[number, n],
                t_recv.at[number, n],
                where,
            )
            copy.start()
            return copy

        def start():
            for urgent in range(2):
                for bit in (1, 2):
                    half = bit - 1 if urgent == 0 else 2 - bit
                    state[bit, half] = send(
                        piece.at[half_at[half], :],
                        half_at[half],
                        chip,
                        across(bit),
                        6 + 2 * (bit - 1) + half,
                    )
            over = send(piece.at[at, :], at, chip, partner, 12)
            own = pltpu.make_async_copy(
                piece.at[at, :], wide_ref.at[at, col(core, chip)], t_send.at[number, 15]
            )
            own.start()
            state["wait"] = [over, own]

        def relay():
            for half in range(2):
                bit = 1 + half
                state[bit, half].wait_recv()
                place = xor(chip, bit)
                here = wide_ref.at[half_at[half], col(core, place)]
                state[3, half] = send(here, half_at[half], place, across(2 - half), 10 + half)

        def forward():
            for bit in (1, 2):
                state[bit, 2 - bit].wait_recv()
                place = xor(chip, bit)
                here = wide_ref.at[at, col(core, place)]
                state["wait"].append(send(here, at, place, partner, 12 + bit))

        def end():
            for half in range(2):
                state[3, half].wait_recv()
            place = xor(chip, 3)
            here = wide_ref.at[at, col(core, place)]
            state["wait"].append(send(here, at, place, partner, 16))

        def done():
            for copy in state["wait"]:
                copy.wait()
            for half in range(2):
                state[3, half].wait_send()
                for bit in (1, 2):
                    state[bit, half].wait_send()

        return start, relay, forward, end, done

    def to_plane(number, src, rows_to):
        state = {}

        def sem(n):
            return s_send.at[number, chips + n], s_recv.at[number, chips + n]

        def start():
            here = wide_ref.at[rows_to, col(core, chip)]
            state["share"] = [remote(src, here, *sem(s), across(s)) for s in range(1, chips)]
            over = remote(src, here, *sem(0), partner)
            own = pltpu.make_async_copy(src, here, s_send.at[number, 3 * chips - 1])
            state["wait"] = [over, own]
            for copy in state["share"] + state["wait"]:
                copy.start()

        def forward():
            for s in range(1, chips):
                state["share"][s - 1].wait()
                here = wide_ref.at[rows_to, col(core, xor(chip, s))]
                copy = remote(here, here, *sem(chips - 1 + s), partner)
                copy.start()
                state["wait"].append(copy)

        def end():
            for copy in state["wait"]:
                copy.wait()

        return start, forward, end

    mixed = w_o.shape[0]
    small = ceil_to(named + 1, 16)
    at_a = pl.ds(features, 16)
    at_o = pl.ds(features + 16, mixed)
    at_g = pl.ds(features + 16 + mixed, small)
    of_d = [two_hop_section(n, n * features // 2, features // 2) for n in range(2)]
    of_o = two_hop_section(2, features + 16, mixed)
    of_g = section(3, features + 16 + mixed, small)
    of_a = section(4, features, 16)
    out_d = [two_hop_to_plane(n, n * features // 2, features // 2) for n in range(2)]
    out_o = two_hop_to_plane(2, features + 16, mixed)
    out_g = to_plane(3, blocks, pl.ds(features + 16 + mixed, n_head * small))
    out_a = to_plane(4, piece.at[at_a, :], at_a)
    router_part = dot(dzs[...], mrs[...], TN)[:named]

    grad_x_ref[...] = part[own_block, :].astype(f32)
    to_dmr[2](grad_x_ref)
    incoming = grad_x_ref[...]
    mid = middle[...]
    inverse = lax.rsqrt(jnp.mean(mid * mid, axis=-1, keepdims=True) + epsilon)
    unit = mid * inverse
    scaled = incoming * expert_gain
    dmid = cot[own_block, :].astype(f32) + inverse * (
        scaled - unit * jnp.mean(scaled * unit, axis=-1, keepdims=True)
    )
    grad_x_ref[...] = dmid
    das[own_block, :] = dmid.astype(bf16)
    da_start, da_stage, da_end, _ = gather(6, das)
    da_start()
    sums[at_g, :] = jnp.concatenate(
        [
            router_part,
            jnp.sum(incoming * unit, axis=0, keepdims=True),
            jnp.zeros((small - named - 1, features), f32),
        ],
        axis=0,
    ).astype(bf16)
    of_g[0]()
    turned[...] = rows[...].T
    of_g[1]()
    lasts = {}

    def first_hop(half, index, place):
        for copy in hops[half, index]:
            copy.wait()
        at_in = (place, halves_in[half], own_side)
        at_out = (place, halves_out(core)[half], slice(None))
        w_in[at_in] = w_in[at_in] + hop_in[half, index]
        w_out[at_out] = w_out[at_out] + hop_out[half, index]

    for half in range(2):
        toward = 2 - half
        place = xor(chip, toward)
        first_hop(half, 1, place)
        pl.semaphore_signal(free.at[half], inc=1, device_id=across(toward), device_id_type=MESH)
        pl.semaphore_wait(free.at[half], 1)
        lasts[half] = (
            remote(
                slot(1, place, core, half),
                hop_in.at[half, 1],
                e_send.at[0, 4 + half],
                e_recv.at[0, 4 + half],
                across(toward),
            ),
            remote(
                slot(0, place, core, half),
                hop_out.at[half, 1],
                e_send.at[1, 4 + half],
                e_recv.at[1, 4 + half],
                across(toward),
            ),
        )
        for copy in lasts[half]:
            copy.start()
    lane = lax.broadcasted_iota(jnp.int32, (tokens, width), 1)

    def through_output(block):
        at = at_block(block, tokens)
        all_five = dot(das[at, :], w_o[...], NT)
        attended = att[at, :]
        total = jnp.zeros((tokens, width), f32)
        gate = jnp.zeros((tokens, width), f32)
        for e in range(experts):
            one = all_five[:, e * width : (e + 1) * width]
            total += gates[at, experts + e : experts + e + 1] * one
            gate = jnp.where(
                lane == experts + e, jnp.sum(one * attended, axis=-1, keepdims=True), gate
            )
        datt[at, :] = total.astype(bf16)
        gate_grads[at, :] = gate

    through_output(h)
    to_out = chain_sum(7, outs, got_out)
    for step in (1, 2, 3):
        da_stage(step)
        if step == 1:
            for number in range(last):
                to_out[0](number)
        through_output(arrival[step - 1])

    for e in range(experts):
        one = (gates[:, experts + e : experts + e + 1] * att[...]).astype(bf16)
        sums[pl.ds(features + 16 + e * width, width), :] = dot(one, das[...], TN).astype(bf16)
    of_o[0]()

    @pl.loop(0, n_head)
    def _(block):
        at = at_block(block, tokens)
        chance = probs[at, :].astype(f32)
        dprob = dot(datt[at, :], v[...], NT)
        centre = jnp.sum(chance * dprob, axis=-1, keepdims=True)
        scores[at, :] = (chance * (dprob - centre)).astype(bf16)

    dq = dot(scores[...], k[...]) * scale
    dk = dot(scores[...], q[...], TN) * scale
    dv = dot(probs[...], datt[...], TN)
    of_o[1]()
    c, s = turns(slice(None))
    qkz[:, pl.ds(0, width)] = (dq * c - swap_halves(dq) * s).astype(bf16)
    qkz[:, pl.ds(width, width)] = (dk * c - swap_halves(dk) * s).astype(bf16)
    gate = gate_grads[...]
    lane = lax.broadcasted_iota(jnp.int32, (group, width), 1)
    for e in range(experts):
        vgrads[:, pl.ds(e * width, width)] = (gates[:, e : e + 1] * dv).astype(bf16)
        one = jnp.sum(vx[:, pl.ds(e * width, width)].astype(f32) * dv, axis=-1, keepdims=True)
        gate = jnp.where(lane == e, one, gate)
    qkz[:, pl.ds(2 * width, width)] = (gate * gates[...] * (1.0 - gates[...])).astype(bf16)

    scaled_qkz = (qkz[...].astype(f32) * gates[:, width - 1 : width]).astype(bf16)

    def matrix_rows(c):
        at = at_block(c, column)
        sums[at, pl.ds(0, 3 * width)] = dot(turned[at, :], scaled_qkz).astype(bf16)
        sums[at, pl.ds(3 * width, experts * width)] = dot(turned[at, :], vgrads[...]).astype(bf16)

    steps_each = features // column // 2
    for n in range(2):
        pl.loop(n * steps_each, (n + 1) * steps_each)(matrix_rows)
        of_d[n][0]()
    def into_rows(block):
        at = at_block(block, tokens)
        inverse = gates[at, width - 1 : width]
        unit = rows[at, :].astype(f32) * inverse
        through = dot(qkz[at, :], w_an[...], NT)
        scaled = through * attend_gain
        total = inverse * (
            scaled - unit * jnp.mean(scaled * unit, axis=-1, keepdims=True)
        ) + dot(vgrads[at, :], w_v[...], NT)
        return total, jnp.sum(through * unit, axis=0, keepdims=True)

    to_x = chain_sum(8, part, got)
    gain = jnp.zeros((1, features), f32)
    for number in range(last):
        total, one = into_rows(leaving[number])
        gain += one
        part[at_block(leaving[number], tokens), :] = total.astype(bf16)
        to_x[0](number)
        if number < 2:
            of_d[number][1]()
    total, one = into_rows(h)
    sums[at_a, :] = jnp.broadcast_to(gain + one, (16, features)).astype(bf16)
    of_a[0]()
    grad_x_ref[...] += total
    to_out[1](0)
    to_out[1](1)
    of_a[1]()
    of_o[2]()
    of_g[2]()
    small_block = at_block(h, small)
    blocks[small_block, :] = piece[at_g, :]
    g_copies = spread(9, lambda s: blocks.at[small_block, :], lambda s: blocks.at[small_block, :])
    to_x[1](0)
    to_out[1](2)
    of_o[3]()
    out_o[0]()
    of_d[0][2]()
    to_x[1](1)
    to_x[1](2)
    of_d[1][2]()
    out_o[1]()
    of_d[0][3]()
    out_d[0][0]()
    of_a[2]()
    gain_part[...] = piece[at_a, :]
    gain_copies = spread(10, lambda s: gain_part, lambda s: gain_got.at[s - 1])
    out_o[2]()
    of_d[1][3]()
    out_d[1][0]()
    for step in peers:
        g_copies[step].wait()
    out_g[0]()
    gain = gain_part[...].astype(f32)
    for step in peers:
        gain_copies[step].wait()
        gain += gain_got[step - 1].astype(f32)
    piece[at_a, :] = gain.astype(bf16)
    out_a[0]()
    out_d[0][1]()
    to_x[2](grad_x_ref)
    output_ref[...] = middle[...] + outs[own_block, :].astype(f32)
    to_out[2](output_ref)
    for half in range(2):
        first_hop(half, 0, chip)
        for copy in lasts[half]:
            copy.wait()
        at_in = (chip, halves_in[half], own_side)
        at_out = (chip, halves_out(core)[half], slice(None))
        w_in[at_in] = w_in[at_in] + hop_in[half, 1]
        w_out[at_out] = w_out[at_out] + hop_out[half, 1]
    stores = (
        pltpu.make_async_copy(w_in.at[chip, :, own_side], fin_in_ref, local_sem.at[0]),
        pltpu.make_async_copy(w_out.at[chip, own_side, :], fin_out_ref, local_sem.at[1]),
    )
    for store in stores:
        store.start()
    out_d[1][1]()
    out_o[3]()
    out_d[0][2]()
    out_g[1]()
    out_a[1]()
    out_d[1][2]()
    out_d[0][3]()
    out_d[1][3]()
    for one in (out_o, out_d[0], out_g, out_a, out_d[1]):
        one[-1]()
    for store in stores:
        store.wait()
    mr_end()
    da_end()


def layer_call(n_dp, n_head, args):
    x, picks, router, value_mat, expert_in = args[0], args[2], args[13], args[11], args[14]
    tokens, features = x.shape
    per_device, _, width = expert_in.shape
    held_experts = value_mat.shape[1]
    group = tokens * n_head
    chips = n_dp // 2
    slab = per_device * width
    lanes = 128
    peers = n_head - 1
    named = ceil_to(n_dp * per_device, 8)
    small = ceil_to(named + 1, 16)
    top = features + held_experts
    held = top + 16 + small
    strip = features // n_dp
    shape = jax.ShapeDtypeStruct
    vm, dma = pltpu.VMEM, pltpu.SemaphoreType.DMA
    outs = [
        (shape((tokens, features), f32), VM),
        (shape((tokens, features), f32), VM),
        (shape((top + 16 + n_head * small, features), bf16), ANY),
        (shape((features, slab), bf16), ANY),
        (shape((slab, features), bf16), ANY),
    ]
    scratch = dict(
        picks=vm(picks.shape, jnp.int32),
        two_picks=vm((2, *args[3].shape), jnp.int32),
        head_picks=vm((group, lanes), jnp.int32),
        w_g=vm(args[10].shape, bf16),
        w_r=vm(router.shape, bf16),
        seg=vm((1, group), jnp.int32),
        gains=vm(args[6].shape, f32),
        angles=vm((group, width), f32),
        w_an=vm((features, 3 * width), bf16),
        w_v=vm((features, held_experts), bf16),
        w_o=vm((held_experts, features), bf16),
        my_router=vm((features, lanes), bf16),
        w_in=vm((chips, features, 2 * slab), bf16),
        w_out=vm((chips, 2 * slab, features), bf16),
        rows=vm((group, features), bf16),
        cot=vm((group, features), bf16),
        mrs=vm((group, features), bf16),
        das=vm((group, features), bf16),
        turned=vm((features, group), bf16),
        my_mask=vm((n_head, tokens, lanes), bf16),
        all_mask=vm((group, lanes), bf16),
        gates=vm((group, width), f32),
        q=vm((group, width), bf16),
        k=vm((group, width), bf16),
        v=vm((group, width), bf16),
        vx=vm((group, held_experts), bf16),
        att=vm((group, width), f32),
        part=vm((group, features), bf16),
        got=vm((2 * peers, tokens, features), bf16),
        outs=vm((group, features), bf16),
        got_out=vm((2 * peers, tokens, features), bf16),
        lifted=vm((chips, 2, group, slab), bf16),
        core_out=vm((chips, slab, features), bf16),
        acts=vm((chips, group, 2 * slab), bf16),
        hids=vm((chips, group, 2 * slab), bf16),
        dzs=vm((group, lanes), bf16),
        datt=vm((group, width), bf16),
        gate_grads=vm((group, width), f32),
        probs=vm((group, group), bf16),
        scores=vm((group, group), bf16),
        qkz=vm((group, 3 * width), bf16),
        vgrads=vm((group, held_experts), bf16),
        gain_part=vm((16, strip), bf16),
        gain_got=vm((peers, 16, strip), bf16),
        sums=vm((held, features), bf16),
        core_got=vm((held, features // 2), bf16),
        chip_got=vm((chips - 1, held, strip), bf16),
        piece=vm((held, strip), bf16),
        blocks=vm((n_head * small, strip), bf16),
        hop_in=vm((2, 2, features // 2, slab), bf16),
        hop_out=vm((2, 2, slab // 2, features), bf16),
        local_sem=dma((16 + 1 + per_device,)),
        z_send=dma((11, 4 * peers)),
        z_recv=dma((11, 4 * peers)),
        w_send=dma((22,)),
        w_recv=dma((22,)),
        c_send=dma((3, chips)),
        c_recv=dma((3, chips)),
        e_send=dma((2, 6)),
        e_recv=dma((2, 6)),
        s_send=dma((5, 3 * chips)),
        s_recv=dma((5, 3 * chips)),
        t_send=dma((3, 17)),
        t_recv=dma((3, 17)),
        ready=pltpu.SemaphoreType.REGULAR,
        free=pltpu.SemaphoreType.REGULAR((2,)),
    )
    return pl.pallas_call(
        functools.partial(layer_kernel, n_dp, n_head),
        out_shape=[o[0] for o in outs],
        out_specs=[o[1] for o in outs],
        in_specs=[ANY] * 16,
        scratch_shapes=list(scratch.values()),
        compiler_params=pltpu.CompilerParams(
            collective_id=1, has_side_effects=True, vmem_limit_bytes=vmem_bytes
        ),
    )(*args)


def finish_kernel(
    n_dp,
    n_head,
    output_ref,
    grad_x_ref,
    wide_ref,
    in_ref,
    out_ref,
    gain_ref,
    final_ref,
    input_ref,
    attend_ref,
    query_ref,
    key_ref,
    value_ref,
    mix_ref,
    gate_ref,
    expert_ref,
    router_ref,
    grad_in_ref,
    grad_out_ref,
    wide,
    flat_in,
    flat_out,
    value,
    mix,
    grad_in,
    grad_out,
    output,
    grad_x,
    sem,
):
    features, slab = in_ref.shape
    per_device, _, width = grad_in_ref.shape
    experts_total, gates = router_ref.shape[0], gate_ref.shape[0]
    mixed = mix_ref.shape[0]
    top = features + 16 + mixed
    small = (wide_ref.shape[0] - top) // n_head
    named = n_dp * per_device

    def copy(src, dst, number):
        one = pltpu.make_async_copy(src, dst, sem.at[number])
        one.start()
        return one

    rest = pl.ds(top, wide_ref.shape[0] - top)
    loads = [
        copy(wide_ref.at[pl.ds(0, features), :], wide.at[pl.ds(0, features), :], 0),
        copy(wide_ref.at[pl.ds(features, top - features), :], wide.at[pl.ds(features, top - features), :], 1),
        copy(in_ref, flat_in, 2),
        copy(out_ref, flat_out, 3),
        copy(wide_ref.at[rest, :], wide.at[rest, :], 4),
    ]
    loads += [copy(output_ref, output, 11), copy(grad_x_ref, grad_x, 12)]
    stores = []
    for number, (held, result) in enumerate(((output, final_ref), (grad_x, input_ref))):
        loads[5 + number].wait()
        stores.append(copy(held, result, 5 + number))
    loads[0].wait()
    first = pl.ds(0, features)
    value[...] = wide[first, pl.ds(3 * width, value.shape[1])].astype(f32)
    stores.append(copy(value, value_ref, 7))
    gain = jnp.broadcast_to(gain_ref[0:1, :], (width, features)).T
    query_ref[...] = wide[first, pl.ds(0, width)].astype(f32) * gain
    key_ref[...] = wide[first, pl.ds(width, width)].astype(f32) * gain
    gate_ref[...] = (wide[first, pl.ds(2 * width, width)].astype(f32) * gain).T[:gates]
    loads[1].wait()
    mix[...] = wide[pl.ds(features + 16, mixed), :].astype(f32)
    stores.append(copy(mix, mix_ref, 8))
    loads[2].wait()
    for e in range(per_device):
        grad_in[e] = flat_in[:, pl.ds(e * width, width)].astype(f32)
    stores.append(copy(grad_in, grad_in_ref, 9))
    loads[3].wait()
    for e in range(per_device):
        grad_out[e] = flat_out[pl.ds(e * width, width), :].astype(f32)
    stores.append(copy(grad_out, grad_out_ref, 10))
    loads[4].wait()
    attend_ref[...] = wide[pl.ds(features, 16), :][0:1].astype(f32)
    planes = wide[pl.ds(top, n_head * small), :]
    place = lax.broadcasted_iota(jnp.int32, (n_head * small, experts_total), 0)
    name = lax.broadcasted_iota(jnp.int32, (n_head * small, experts_total), 1)
    slot, plane = place % small, place // small
    expert = (slot // per_device * n_head + plane) * per_device + slot % per_device
    chosen = (slot < named) & (expert == name)
    router_ref[...] = dot(jnp.where(chosen, 1.0, 0.0).astype(bf16), planes, TN)
    gain = jnp.zeros((1, features), f32)
    for z in range(n_head):
        row = z * small + ceil_to(named, 8)
        gain += planes[row : row + 1].astype(f32)
    expert_ref[...] = gain
    for store in stores:
        store.wait()


def finish_call(n_dp, n_head, shapes, args):
    shape = jax.ShapeDtypeStruct
    wide, flat_in, flat_out = args[2], args[3], args[4]
    value, mix, grad_in, grad_out = shapes[5], shapes[6], shapes[10], shapes[11]
    specs = [VM] * 12
    for number in (0, 1, 5, 6, 10, 11):
        specs[number] = ANY
    return pl.pallas_call(
        functools.partial(finish_kernel, n_dp, n_head),
        out_shape=[shape(s, f32) for s in shapes],
        out_specs=specs,
        in_specs=[ANY] * 5 + [VM],
        scratch_shapes=[
            pltpu.VMEM(wide.shape, bf16),
            pltpu.VMEM(flat_in.shape, bf16),
            pltpu.VMEM(flat_out.shape, bf16),
            pltpu.VMEM(value, f32),
            pltpu.VMEM(mix, f32),
            pltpu.VMEM(grad_in, f32),
            pltpu.VMEM(grad_out, f32),
            pltpu.VMEM(shapes[0], f32),
            pltpu.VMEM(shapes[1], f32),
            pltpu.SemaphoreType.DMA((13,)),
        ],
        compiler_params=pltpu.CompilerParams(vmem_limit_bytes=60 << 20),
    )(*args)


def kernel_body(
    n_dp,
    n_head,
    hidden_in,
    segments,
    value_pick,
    output_pick,
    expert_pick,
    attend_gain,
    query_weight,
    key_weight,
    value_weight,
    output_weight,
    head_router,
    expert_gain,
    router,
    expert_in,
    expert_out,
    cotangent,
):
    tokens, features = hidden_in.shape
    per_device, _, width = expert_in.shape
    experts = head_router.shape[2] // 2
    group = tokens * n_head
    angles = np.arange(group)[:, None] * theta ** (-2.0 * np.arange(width // 2) / width)[None, :]
    angles = np.concatenate([np.cos(angles), np.sin(angles)], axis=1).astype(np.float32)
    both = np.eye(2, dtype=np.float32)
    gains = attend_gain.astype(f32) * both[:, :1] + expert_gain.astype(f32) * both[:, 1:]
    results = layer_call(
        n_dp,
        n_head,
        (
            hidden_in,
            cotangent,
            expert_pick.T,
            value_pick.transpose(1, 2, 0)[0],
            output_pick.transpose(1, 2, 0)[0],
            segments[None, :],
            gains,
            angles,
            query_weight[0],
            key_weight[0],
            head_router.transpose(0, 2, 1)[0],
            value_weight[0],
            output_weight[0],
            router.T,
            expert_in,
            expert_out.reshape(per_device * width, features),
        ),
    )
    shapes = (
        (tokens, features),
        (tokens, features),
        (1, features),
        query_weight.shape[1:],
        key_weight.shape[1:],
        value_weight.shape[1:],
        output_weight.shape[1:],
        (2 * experts, features),
        (1, features),
        (router.shape[1], features),
        expert_in.shape,
        expert_out.shape,
    )
    done = list(finish_call(n_dp, n_head, shapes, (*results, gains)))
    for number in (3, 4, 5, 6, 7):
        done[number] = done[number][None]
    done[7] = done[7].transpose(0, 2, 1)
    done[9] = done[9].T
    done[2], done[8] = done[2][0], done[8][0]
    return tuple(done)


def solution(mesh):
    rows = P(everywhere, None)
    heads = P("head", None, None)
    experts = P(everywhere, None, None)
    picks = P("dp", "head", None)
    in_specs = (
        rows, P("dp"), picks, picks, rows, P(), heads, heads, heads, heads, heads,
        P(), P(), experts, experts, rows,
    )
    out_specs = (
        rows, rows, P(), heads, heads, heads, heads, heads, P(), P(), experts, experts,
    )
    n_dp, n_head = mesh.shape["dp"], mesh.shape["head"]

    def program(*args):
        held = 2 * n_dp * args[13].shape[0] * args[13].shape[1] * args[13].shape[2] * 2
        if n_head == 4 and held <= vmem_for_weights:
            return kernel_body(n_dp, n_head, *args)
        return body(*args)

    return jax.shard_map(program, mesh=mesh, in_specs=in_specs, out_specs=out_specs, check_vma=False)
```

```python
import functools

import jax
import jax.numpy as jnp
import numpy as np
from jax import lax
from jax.experimental import pallas as pl
from jax.experimental.pallas import tpu as pltpu
from jax.sharding import PartitionSpec as P

epsilon = 1e-06
theta = 10000.0
negative = -1e30
f32 = jnp.float32
bf16 = jnp.bfloat16
everywhere = ("dp", "head")
whole_rows = 4096
vmem_for_weights = 16 << 20
vmem_bytes = 62 << 20


def product(left, right, left_axis, right_axis):
    return lax.dot_general(
        left, right, (((left_axis,), (right_axis,)), ((), ())), preferred_element_type=f32
    )


def rms_scale(residual):
    return lax.rsqrt(jnp.mean(residual * residual, axis=-1, keepdims=True) + epsilon)


def rotary_tables(row_count, head_width):
    half_width = head_width // 2
    position = jnp.arange(row_count, dtype=f32)[:, None]
    exponent = jnp.arange(half_width, dtype=f32)[None, :]
    angles = position * jnp.power(theta, -2.0 * exponent / head_width)
    return (jnp.cos(angles), jnp.sin(angles))


def rotate(matrix, cosine, sine):
    half = matrix.shape[-1] // 2
    first, second = matrix[:, :half], matrix[:, half:]
    return jnp.concatenate([first * cosine - second * sine, second * cosine + first * sine], axis=-1)


def pick_mask(picks, expert_count):
    hits = picks[:, 0, :, None] == jnp.arange(expert_count, dtype=jnp.int32)[None, None, :]
    return jnp.any(hits, axis=1).astype(f32)


def norm_back(residual, inverse, gain, incoming):
    unit_rows = residual * inverse
    scaled = incoming * gain
    gain_grad = jnp.sum(incoming * unit_rows, axis=0)
    row_grad = inverse * (scaled - unit_rows * jnp.mean(scaled * unit_rows, axis=-1, keepdims=True))
    return (row_grad, gain_grad)


def gelu_pair(value):
    inner = jnp.tanh(0.7978845608028654 * (value + 0.044715 * value * value * value))
    slope = 0.5 * (1.0 + inner) + 0.5 * value * (1.0 - inner * inner) * 0.7978845608028654 * (
        1.0 + 3.0 * 0.044715 * value * value
    )
    return (0.5 * value * (1.0 + inner), slope)


def body(
    hidden_in,
    segments,
    value_pick,
    output_pick,
    expert_pick,
    attend_gain,
    query_weight,
    key_weight,
    value_weight,
    output_weight,
    head_router,
    expert_gain,
    router,
    expert_in,
    expert_out,
    cotangent,
):
    tokens, features = hidden_in.shape
    per_device, _, width = expert_in.shape
    head_experts = head_router.shape[2] // 2
    head_width = query_weight.shape[2]
    scale = head_width ** (-0.5)
    query_mat, key_mat, value_mat = query_weight[0], key_weight[0], value_weight[0]
    output_mat, gate_mat = output_weight[0], head_router[0]
    value_mask = pick_mask(value_pick, head_experts)
    output_mask = pick_mask(output_pick, head_experts)
    attend_scale = attend_gain.astype(f32)
    expert_scale = expert_gain.astype(f32)
    me = lax.axis_index("dp") * lax.axis_size("head") + lax.axis_index("head")

    rows = lax.all_gather(hidden_in, "head", axis=0, tiled=True)
    grouped = rows.astype(f32)
    group = grouped.shape[0]
    inverse = rms_scale(grouped)
    normed = (grouped * inverse * attend_scale).astype(bf16)
    cosine, sine = rotary_tables(group, head_width)
    queries = rotate(product(normed, query_mat, 1, 0), cosine, sine).astype(bf16)
    key_rows = rotate(product(normed, key_mat, 1, 0), cosine, sine).astype(bf16)
    squash = jax.nn.sigmoid(product(normed, gate_mat, 1, 0))
    value_gates = squash[:, :head_experts] * value_mask
    output_gates = squash[:, head_experts:] * output_mask
    expert_values = product(rows, value_mat, 1, 0).reshape(group, head_experts, head_width)
    values = jnp.sum(expert_values * value_gates[:, :, None], axis=1).astype(bf16)
    places = jnp.arange(group, dtype=jnp.int32)
    allowed = (places[None, :] <= places[:, None]) & (segments[:, None] == segments[None, :])
    scores = jnp.where(allowed, product(queries, key_rows, 1, 1) * scale, negative)
    exponents = jnp.exp(scores - jnp.max(scores, axis=-1, keepdims=True))
    probabilities = exponents / jnp.sum(exponents, axis=-1, keepdims=True)
    attended = product(probabilities.astype(bf16), values, 1, 0)
    weighted = (
        (output_gates[:, :, None] * attended[:, None, :]).reshape(group, -1).astype(bf16)
    )
    middle = hidden_in.astype(f32) + lax.psum_scatter(
        product(weighted, output_mat, 1, 0).astype(bf16), "head", scatter_dimension=0, tiled=True
    ).astype(f32)
    middle_inverse = rms_scale(middle)
    middle_normed = (middle * middle_inverse * expert_scale).astype(bf16)
    mine = me * per_device + jnp.arange(per_device, dtype=jnp.int32)
    my_router = lax.dynamic_slice_in_dim(router, me * per_device, per_device, axis=1)
    in_mat = expert_in.transpose(1, 0, 2).reshape(features, per_device * width)
    out_mat = expert_out.reshape(per_device * width, features)

    def turn(running, own):
        own_rows, own_cot, own_picks = own
        all_cot = lax.all_gather(own_cot, everywhere, axis=0, tiled=True)
        all_picks = lax.all_gather(own_picks, everywhere, axis=0, tiled=True)
        all_rows = lax.all_gather(own_rows, everywhere, axis=0, tiled=True)
        mask = jnp.any(all_picks[:, :, None] == mine[None, None, :], axis=1).astype(f32)
        gates = jax.nn.sigmoid(product(all_rows, my_router, 1, 0))
        live = gates * mask
        act, slope = gelu_pair(product(all_rows, in_mat, 1, 0).reshape(-1, per_device, width))
        lifted = product(all_cot, out_mat, 1, 1).reshape(-1, per_device, width)
        dense_grad = (jnp.sum(act * lifted, axis=-1) * live * (1.0 - gates)).astype(bf16)
        act_live = (act * live[:, :, None]).astype(bf16).reshape(-1, per_device * width)
        hidden_grad = (slope * lifted * live[:, :, None]).astype(bf16)
        hidden_grad = hidden_grad.reshape(-1, per_device * width)
        part_out = product(act_live, out_mat, 1, 0).astype(bf16)
        part_grad = (
            product(hidden_grad, in_mat, 1, 1) + product(dense_grad, my_router, 1, 1)
        ).astype(bf16)
        back = lax.psum_scatter(part_grad, everywhere, scatter_dimension=0, tiled=True)
        forth = lax.psum_scatter(part_out, everywhere, scatter_dimension=0, tiled=True)
        grads = (
            product(all_rows, hidden_grad, 0, 0),
            product(act_live, all_cot, 0, 0),
            product(dense_grad, all_rows, 0, 0),
        )
        if running is not None:
            grads = jax.tree.map(jnp.add, running, grads)
        return grads, (forth, back)

    turns = max(1, lax.axis_size("dp") * lax.axis_size("head") * tokens // whole_rows)
    owned = (middle_normed, cotangent, expert_pick)
    if turns == 1:
        grads, (summed, normed_grad) = turn(None, owned)
    else:
        owned = jax.tree.map(lambda a: a.reshape(turns, -1, a.shape[1]), owned)
        zeros = (
            jnp.zeros(in_mat.shape, f32),
            jnp.zeros(out_mat.shape, f32),
            jnp.zeros((per_device, features), f32),
        )
        grads, sums = lax.scan(turn, zeros, owned)
        summed, normed_grad = (a.reshape(tokens, features) for a in sums)
    grad_in = grads[0].reshape(features, per_device, width).transpose(1, 0, 2)
    grad_out = grads[1].reshape(per_device, width, features)
    grad_router = lax.all_gather(grads[2], everywhere, axis=0, tiled=True).T
    output = middle + summed.astype(f32)
    incoming = cotangent.astype(f32)
    row_grad, grad_gain_expert = norm_back(
        middle, middle_inverse, expert_scale, normed_grad.astype(f32)
    )
    middle_grad = incoming + row_grad
    group_grads = lax.all_gather(middle_grad.astype(bf16), "head", axis=0, tiled=True)
    weighted_grad = product(group_grads, output_mat, 1, 1).reshape(group, head_experts, head_width)
    output_grad = product(weighted, group_grads, 0, 0)
    output_gate_grad = jnp.sum(weighted_grad * attended[:, None, :], axis=-1)
    attended_grad = jnp.sum(weighted_grad * output_gates[:, :, None], axis=1).astype(bf16)
    prob_grad = product(attended_grad, values, 1, 1)
    centre = jnp.sum(probabilities * prob_grad, axis=-1, keepdims=True)
    score_grad = (probabilities * (prob_grad - centre)).astype(bf16)
    query_grad = product(score_grad, key_rows, 1, 0) * scale
    key_grad = product(score_grad, queries, 0, 0) * scale
    values_grad = product(probabilities.astype(bf16), attended_grad, 0, 0)
    expert_grad = (value_gates[:, :, None] * values_grad[:, None, :]).reshape(group, -1).astype(bf16)
    value_gate_grad = jnp.sum(expert_values * values_grad[:, None, :], axis=-1)
    query_grad = rotate(query_grad, cosine, -sine).astype(bf16)
    key_grad = rotate(key_grad, cosine, -sine).astype(bf16)
    logit_grad = (
        jnp.concatenate([value_gate_grad * value_mask, output_gate_grad * output_mask], axis=1)
        * squash
        * (1.0 - squash)
    ).astype(bf16)
    head_grads = (
        product(normed, query_grad, 0, 0),
        product(normed, key_grad, 0, 0),
        product(rows, expert_grad, 0, 0),
        output_grad,
        product(normed, logit_grad, 0, 0),
    )
    head_grads = tuple(grad.astype(bf16) for grad in head_grads)
    head_grads = tuple(grad.astype(f32)[None] for grad in lax.psum(head_grads, "dp"))
    back = (
        product(query_grad, query_mat, 1, 1)
        + product(key_grad, key_mat, 1, 1)
        + product(logit_grad, gate_mat, 1, 1)
    )
    row_back, grad_attend = norm_back(grouped, inverse, attend_scale, back)
    partial = (row_back + product(expert_grad, value_mat, 1, 1)).astype(bf16)
    input_grad = middle_grad + lax.psum_scatter(
        partial, "head", scatter_dimension=0, tiled=True
    ).astype(f32)
    grad_attend, grad_gain_expert = lax.psum((grad_attend, grad_gain_expert), everywhere)
    return (
        output,
        input_grad,
        grad_attend,
        *head_grads,
        grad_gain_expert,
        grad_router,
        grad_in,
        grad_out,
    )


MESH = pl.DeviceIdType.MESH
VM = pl.BlockSpec(memory_space=pltpu.VMEM)
ANY = pl.BlockSpec(memory_space=pl.ANY)
NN = (((1,), (0,)), ((), ()))
NT = (((1,), (1,)), ((), ()))
TN = (((0,), (0,)), ((), ()))


def dot(left, right, dims=NN):
    return lax.dot_general(left, right, dims, preferred_element_type=f32)


def at_block(block, count):
    return pl.ds(pl.multiple_of(block * count, count), count)


def remote(src, dst, send, recv, where):
    return pltpu.make_async_remote_copy(
        src_ref=src, dst_ref=dst, send_sem=send, recv_sem=recv, device_id=where, device_id_type=MESH
    )


def swap_halves(value):
    half = value.shape[-1] // 2
    return jnp.concatenate([value[:, half:], value[:, :half]], axis=-1)


def ceil_to(number, step):
    return -(-number // step) * step


def layer_kernel(
    n_dp,
    n_head,
    x_ref,
    cot_ref,
    pick_ref,
    value_pick_ref,
    output_pick_ref,
    seg_ref,
    gain_ref,
    angle_ref,
    wq_ref,
    wk_ref,
    wg_ref,
    wv_ref,
    wo_ref,
    router_ref,
    in_ref,
    out_ref,
    output_ref,
    grad_x_ref,
    wide_ref,
    fin_in_ref,
    fin_out_ref,
    picks,
    two_picks,
    head_picks,
    w_g,
    w_r,
    seg,
    gains,
    angles,
    w_an,
    w_v,
    w_o,
    my_router,
    w_in,
    w_out,
    rows,
    cot,
    mrs,
    das,
    turned,
    my_mask,
    all_mask,
    gates,
    q,
    k,
    v,
    vx,
    att,
    part,
    got,
    outs,
    got_out,
    lifted,
    core_out,
    acts,
    hids,
    dzs,
    datt,
    gate_grads,
    probs,
    scores,
    qkz,
    vgrads,
    gain_part,
    gain_got,
    sums,
    core_got,
    chip_got,
    piece,
    blocks,
    hop_in,
    hop_out,
    local_sem,
    z_send,
    z_recv,
    w_send,
    w_recv,
    c_send,
    c_recv,
    e_send,
    e_recv,
    s_send,
    s_recv,
    t_send,
    t_recv,
    ready,
    free,
):
    middle = output_ref
    xor = jnp.bitwise_xor
    d, h = lax.axis_index("dp"), lax.axis_index("head")
    chip, core = d // 2, d % 2
    chips = n_dp // 2
    tokens, features = x_ref.shape
    per_device, _, width = in_ref.shape
    slab = per_device * width
    wide = 2 * slab
    experts = wv_ref.shape[1] // width
    named = ceil_to(n_dp * per_device, 8)
    group = tokens * n_head
    pair = 2 * tokens
    column = 256
    lanes = 128
    scale = width ** (-0.5)
    peers = (2, 3, 1)
    partner = (chip * 2 + 1 - core, h)
    own_block = at_block(h, tokens)
    own_side, other_side = at_block(core, slab), at_block(1 - core, slab)
    halves_in = (pl.ds(0, features // 2), pl.ds(features // 2, features // 2))
    halves_out = lambda side: (
        at_block(2 * side, slab // 2),
        at_block(2 * side + 1, slab // 2),
    )

    def along(step):
        return (d, xor(h, step))

    def across(step):
        return (xor(chip, step) * 2 + core, h)

    loads = []

    def load(src, dst):
        copy = pltpu.make_async_copy(src, dst, local_sem.at[len(loads)])
        copy.start()
        loads.append(copy)
        return copy

    own_weights = [load(out_ref, w_out.at[chip, own_side, :])] + [
        load(in_ref.at[e], w_in.at[chip, :, at_block(core * per_device + e, width)])
        for e in range(per_device)
    ]
    for_rows = [
        load(x_ref, rows.at[own_block, :]),
        load(gain_ref, gains),
        load(wg_ref, w_g),
        load(wq_ref, w_an.at[:, pl.ds(0, width)]),
        load(wk_ref, w_an.at[:, pl.ds(width, width)]),
        load(wv_ref, w_v),
        load(value_pick_ref, two_picks.at[0]),
        load(output_pick_ref, two_picks.at[1]),
        load(angle_ref, angles),
    ]
    for_scores = [load(seg_ref, seg), load(wo_ref, w_o)]
    for_mask = load(pick_ref, picks)
    for_cot = load(cot_ref, cot.at[own_block, :])
    for_router = load(router_ref, w_r)

    barrier = pltpu.get_barrier_semaphore()
    friends = [along(s) for s in peers] + [partner] + [across(s) for s in range(1, chips)]
    for friend in friends:
        pl.semaphore_signal(barrier, inc=1, device_id=friend, device_id_type=MESH)
    pl.semaphore_wait(barrier, len(friends))

    right, left = (d, jnp.minimum(h + 1, n_head - 1)), (d, jnp.maximum(h - 1, 0))
    last = n_head - 1

    def pick(*by_place):
        value = jnp.int32(by_place[-1])
        for place in range(n_head - 2, -1, -1):
            value = jnp.where(h == place, by_place[place], value)
        return value

    arrival = (xor(h, 1), pick(2, 2, 1, 1), pick(3, 3, 0, 0))
    leaving = (pick(3, 3, 0, 0), pick(2, 0, 3, 1), pick(1, 2, 1, 2))

    def gather(kind, buffer):
        def go(side, step):
            sign = 1 - 2 * side
            block = jnp.clip(h - sign * step, 0, last)
            where = (d, jnp.clip(h + sign, 0, last))
            copies = []
            for half in range(2):
                here = buffer.at[at_block(2 * block + half, tokens // 2), :]
                number = (side * last + step) * 2 + half
                copies.append(
                    remote(here, here, z_send.at[kind, number], z_recv.at[kind, number], where)
                )
            return copies

        def begin(side):
            for copy in go(side, 0):
                copy.start()

        def start():
            pl.when(h < last)(lambda: begin(0))
            pl.when(h > 0)(lambda: begin(1))

        def arrive(side, step, there, onward):
            for half in range(2):

                @pl.when(there)
                def _():
                    go(side, step - 1)[half].wait_recv()
                    if onward:
                        go(side, step)[half].start()

        def stage(step, which="all"):
            nearer = jnp.where(2 * h < n_head, 0, 1)
            ways = []
            for side in (nearer, 1 - nearer):
                there = jnp.where(side == 0, h >= step, h + step <= last)
                ways.append((side, there, jnp.where(side == 0, h < last, h > 0)))
            for side, there, onward in ways:
                if step < last and which != "rest":
                    arrive(side, step, there & onward, True)
            for side, there, onward in ways:
                if which != "duty":
                    ends_here = there if step == last else there & jnp.logical_not(onward)
                    arrive(side, step, ends_here, False)

        def follow(step):
            pl.when((h < last) & (jnp.maximum(h, 1) == step))(lambda: begin(0))
            pl.when((h > 0) & (jnp.maximum(last - h, 1) == step))(lambda: begin(1))

        def end():
            for step in range(last):
                for side, sent in (
                    (0, (h >= step) & (h < last)),
                    (1, (h + step <= last) & (h > 0)),
                ):

                    @pl.when(sent)
                    def _():
                        for copy in go(side, step):
                            copy.wait_send()

        return start, stage, end, follow

    def chain_sum(kind, parts, slots):
        def go(number):
            block = leaving[number]
            rightward = block > h
            slot = jnp.where(rightward, block - 1, last + block)
            where = (d, jnp.clip(jnp.where(rightward, h + 1, h - 1), 0, last))
            middle_one = (rightward & (h > 0)) | (jnp.logical_not(rightward) & (h < last))
            pieces = []
            for half in range(2):
                at = at_block(2 * block + half, tokens // 2)
                rows_of = pl.ds(half * (tokens // 2), tokens // 2)
                copy = remote(
                    parts.at[at, :],
                    slots.at[slot, rows_of, :],
                    z_send.at[kind, 2 * number + half],
                    z_recv.at[kind, 2 * slot + half],
                    where,
                )
                pieces.append((copy, at, slot, rows_of))
            return pieces, middle_one

        def now(number):
            pieces, middle_one = go(number)

            @pl.when(jnp.logical_not(middle_one))
            def _():
                for copy, _, _, _ in pieces:
                    copy.start()

        def later(number):
            pieces, middle_one = go(number)

            @pl.when(middle_one)
            def _():
                for copy, at, slot, rows_of in pieces:
                    copy.wait_recv()
                    parts[at, :] = parts[at, :] + slots[slot, rows_of, :]
                    copy.start()

        def end(total):
            ends = ((jnp.maximum(h - 1, 0), h > 0), (last + jnp.minimum(h, last - 1), h < last))
            for slot, there in ends:

                @pl.when(there)
                def _():
                    for half in range(2):
                        rows_of = pl.ds(half * (tokens // 2), tokens // 2)
                        remote(
                            parts.at[at_block(2 * h, tokens // 2), :],
                            slots.at[slot, rows_of, :],
                            z_send.at[kind, 0],
                            z_recv.at[kind, 2 * slot + half],
                            right,
                        ).wait_recv()
                    total[...] += slots[slot].astype(f32)

            for number in range(last):
                for copy, _, _, _ in go(number)[0]:
                    copy.wait_send()

        return now, later, end

    def spread(kind, src, dst, steps=peers):
        copies = {}
        for step in steps:
            copies[step] = remote(
                src(step), dst(step), z_send.at[kind, step - 1], z_recv.at[kind, step - 1], along(step)
            )
            copies[step].start()
        return copies

    x_start, x_stage, x_end, _ = gather(0, rows)
    for_rows[0].wait()
    x_start()

    def slot(array, place, side, half=None):
        if array == 0:
            at = halves_out(side)[half] if half is not None else at_block(side, slab)
            return w_out.at[place, at, :]
        at = halves_in[half] if half is not None else pl.ds(0, features)
        return w_in.at[place, at, at_block(side, slab)]

    def weights(number, ref, where):
        copy = remote(ref, ref, w_send.at[number], w_recv.at[number], where)
        copy.start()
        return copy

    slabs, halves_on, to_core, diagonal = {}, {}, {}, {}
    for copy in own_weights:
        copy.wait()
    for array in range(2):
        for first in range(2):
            for bit in (1, 2):
                half = bit - 1 if first == 0 else 2 - bit
                number = ((bit - 1) * 2 + half) * 2 + array
                slabs[bit, half, array] = weights(
                    number, slot(array, chip, core, half), across(bit)
                )
        to_core[0, array] = weights(12 + array, slot(array, chip, core), partner)

    for_mask.wait()
    own_picks = jnp.concatenate(
        [picks[...].astype(f32), jnp.zeros((lanes - picks.shape[0], tokens), f32)], axis=0
    ).T.astype(jnp.int32)
    lane = lax.broadcasted_iota(jnp.int32, (tokens, lanes), 1)
    for plane in range(n_head):
        expert = (lane // per_device * n_head + plane) * per_device + lane % per_device
        expert = jnp.where(lane < n_dp * per_device, expert, -1)
        hit = own_picks[:, 0:1] == expert
        for c in range(1, picks.shape[0]):
            hit = hit | (own_picks[:, c : c + 1] == expert)
        my_mask[plane] = jnp.where(hit, 1.0, 0.0).astype(bf16)
    mask_copies = spread(1, lambda s: my_mask.at[xor(h, s)], lambda s: all_mask.at[own_block, :])
    all_mask[own_block, :] = my_mask[h]

    for copy in for_rows[1:]:
        copy.wait()
    attend_gain = gains[0:1, :]
    expert_gain = gains[1:2, :]
    one_hot = lambda count: jnp.where(
        lax.broadcasted_iota(jnp.int32, (count, width), 0)
        == lax.broadcasted_iota(jnp.int32, (count, width), 1),
        1.0,
        0.0,
    ).astype(bf16)
    w_an[:, pl.ds(2 * width, width)] = dot(w_g[...], one_hot(w_g.shape[0]), TN).astype(bf16)
    uses = two_picks.shape[1]
    head_picks[...] = jnp.concatenate(
        [
            two_picks[0].astype(f32),
            two_picks[1].astype(f32) + experts,
            jnp.zeros((lanes - 2 * uses, group), f32),
        ],
        axis=0,
    ).T.astype(jnp.int32)
    half_lanes = lax.broadcasted_iota(jnp.int32, (1, width), 1) < width // 2

    def turns(at):
        both = angles[at, :]
        turned_over = swap_halves(both)
        return (
            jnp.where(half_lanes, both, turned_over),
            jnp.where(half_lanes, -turned_over, both),
        )

    def project(block):
        at = at_block(block, tokens)
        own = rows[at, :]
        full = own.astype(f32)
        inverse = lax.rsqrt(jnp.mean(full * full, axis=-1, keepdims=True) + epsilon)
        unit = (full * inverse * attend_gain).astype(bf16)
        qkg = dot(unit, w_an[...])
        c, s = turns(at)
        one, two = qkg[:, :width], qkg[:, width : 2 * width]
        q[at, :] = (one * c + swap_halves(one) * s).astype(bf16)
        k[at, :] = (two * c + swap_halves(two) * s).astype(bf16)
        lane = lax.broadcasted_iota(jnp.int32, (tokens, width), 1)
        chosen = head_picks[at, :]
        hit = lane == chosen[:, 0:1]
        for c in range(1, 2 * uses):
            hit = hit | (lane == chosen[:, c : c + 1])
        gate = jnp.where(hit, jax.nn.sigmoid(qkg[:, 2 * width :]), 0.0)
        gates[at, :] = jnp.where(lane == width - 1, inverse, gate)
        values = dot(own, w_v[...])
        vx[at, :] = values.astype(bf16)
        value = gate[:, 0:1] * values[:, :width]
        for e in range(1, experts):
            value += gate[:, e : e + 1] * values[:, e * width : (e + 1) * width]
        v[at, :] = value.astype(bf16)

    project(h)
    _, cot_stage, cot_end, cot_follow = gather(2, cot)
    for_cot.wait()
    for step in (1, 2, 3):
        x_stage(step)
        cot_follow(step)
        project(arrival[step - 1])
    for copy in for_scores:
        copy.wait()
    seg_col = gate_grads
    seg_col[...] = jnp.broadcast_to(seg[...].astype(f32), (lanes, group)).T

    def attend(block):
        at = at_block(block, tokens)
        score = dot(q[at, :], k[...], NT) * scale
        row = block * tokens + lax.broadcasted_iota(jnp.int32, (tokens, group), 0)
        place = lax.broadcasted_iota(jnp.int32, (tokens, group), 1)
        allowed = (place <= row) & (seg_col[at, 0:1] == seg[...].astype(f32))
        score = jnp.where(allowed, score, negative)
        exponents = jnp.exp(score - jnp.max(score, axis=-1, keepdims=True))
        chance = exponents / jnp.sum(exponents, axis=-1, keepdims=True)
        probs[at, :] = chance.astype(bf16)
        attended = dot(chance.astype(bf16), v[...])
        att[at, :] = attended
        gate = gates[at, :]
        weighted = jnp.concatenate(
            [
                (gate[:, experts + e : experts + e + 1] * attended).astype(bf16)
                for e in range(experts)
            ],
            axis=-1,
        )
        return dot(weighted, w_o[...])

    to_mid = chain_sum(3, part, got)
    for number in range(last):
        block = leaving[number]
        part[at_block(block, tokens), :] = attend(block).astype(bf16)
        to_mid[0](number)
    middle[...] = rows[own_block, :].astype(f32) + attend(h)
    cot_stage(1, "duty")
    to_mid[1](0)
    for array in range(2):
        for half in range(2):
            slabs[1 + half, half, array].wait_recv()
            halves_on[half, array] = weights(
                8 + 2 * half + array,
                slot(array, xor(chip, 1 + half), core, half),
                across(2 - half),
            )

    to_mid[1](1)
    cot_stage(2, "duty")
    to_mid[1](2)
    for bit in (1, 2):
        slabs[bit, 2 - bit, 0].wait_recv()
        to_core[bit, 0] = weights(14 + (bit - 1) * 2, slot(0, xor(chip, bit), core), partner)
        slabs[bit, 2 - bit, 1].wait_recv()
        to_core[bit, 1] = weights(15 + (bit - 1) * 2, slot(1, xor(chip, bit), core), partner)
    for_router.wait()
    slot_of = lax.broadcasted_iota(jnp.int32, (w_r.shape[0], lanes), 1)
    name = lax.broadcasted_iota(jnp.int32, (w_r.shape[0], lanes), 0)
    expert = (slot_of // per_device * n_head + h) * per_device + slot_of % per_device
    expert = jnp.where(slot_of < n_dp * per_device, expert, -1)
    my_router[...] = dot(
        w_r[...], jnp.where(name == expert, 1.0, 0.0).astype(bf16), TN
    ).astype(bf16)

    to_mid[2](middle)
    mid = middle[...]
    inverse = lax.rsqrt(jnp.mean(mid * mid, axis=-1, keepdims=True) + epsilon)
    mrs[own_block, :] = (mid * inverse * expert_gain).astype(bf16)
    mr_start, mr_stage, mr_end, _ = gather(4, mrs)
    mr_start()

    def last_halves(array):
        for half in range(2):
            halves_on[half, array].wait_recv()
            diagonal[half, array] = weights(
                18 + 2 * half + array, slot(array, xor(chip, 3), core, half), partner
            )

    for step in (1, 2, 3):
        cot_stage(step, "rest")
    last_halves(0)
    for step in peers:
        mask_copies[step].wait()
    cot_end()
    x_end()

    def weights_here(array):
        for bit in range(3):
            to_core[bit, array].wait_recv()
        for half in range(2):
            diagonal[half, array].wait_recv()

    def weights_sent():
        for array in range(2):
            for bit in range(3):
                to_core[bit, array].wait_send()
            for half in range(2):
                diagonal[half, array].wait_send()
                halves_on[half, array].wait_send()
                for bit in (1, 2):
                    slabs[bit, half, array].wait_send()

    weights_here(0)

    def lift_chip(j):
        lift = dot(cot[...], w_out[j], NT)
        lifted[j, 0] = lift[:, :slab].astype(bf16)
        lifted[j, 1] = lift[:, slab:].astype(bf16)

    pl.loop(0, chips // 2)(lift_chip)
    mr_stage(1, "duty")
    last_halves(1)
    pl.loop(chips // 2, chips)(lift_chip)

    weights_here(1)

    def spread_lanes(j):
        lane = lax.broadcasted_iota(jnp.int32, (lanes, wide), 1) // width
        slot = lax.broadcasted_iota(jnp.int32, (lanes, wide), 0)
        return jnp.where(slot == lane + j * (wide // width), 1.0, 0.0).astype(bf16)

    def pair_of_blocks(number, between):
        at = at_block(number, pair)
        own = mrs[at, :]
        gates = jax.nn.sigmoid(dot(own, my_router[...]))
        live = gates * all_mask[at, :].astype(f32)
        narrow = live.astype(bf16)

        def chip_step(j, total):
            pick = spread_lanes(j)
            hidden = dot(own, w_in[j])
            gate = dot(narrow, pick).astype(bf16)
            lift = jnp.concatenate([lifted[j, 0, at, :], lifted[j, 1, at, :]], axis=-1)
            square = hidden * hidden
            inner = jnp.tanh(0.7978845608028654 * hidden * (1.0 + 0.044715 * square))
            half = 0.5 * (1.0 + inner)
            act = hidden * half
            slope = half + act * (1.0 - inner) * (
                0.7978845608028654 + (0.7978845608028654 * 3.0 * 0.044715) * square
            )
            act = act.astype(bf16)
            acts[j, at, :] = act * gate
            hids[j, at, :] = slope.astype(bf16) * (lift * gate)
            return total + dot(act * lift, pick, NT)

        total = lax.fori_loop(0, chips // 2, chip_step, jnp.zeros((pair, lanes), f32))
        between()
        total = lax.fori_loop(chips // 2, chips, chip_step, total)
        dz = (total * live * (1.0 - gates)).astype(bf16)
        dzs[at, :] = dz

        @pl.loop(0, features // column)
        def _(c):
            part_of = at_block(c, column)
            total = dot(dz, my_router[part_of, :], NT)
            for j in range(chips):
                total += dot(hids[j, at, :], w_in[j, part_of, :], NT)
            part[at, part_of] = total.astype(bf16)

    def outputs():
        @pl.loop(0, features // column)
        def _(c):
            part_of = at_block(c, column)
            total = dot(acts[0], w_out[0, :, part_of])
            for j in range(1, chips):
                total += dot(acts[j], w_out[j, :, part_of])
            outs[:, part_of] = total.astype(bf16)

    near = h // 2
    mr_stage(1, "rest")
    to_dmr = chain_sum(5, part, got)
    pair_of_blocks(near, lambda: mr_stage(2, "duty"))
    to_dmr[0](2)
    mr_stage(2, "rest")
    mr_stage(3)
    pair_of_blocks(1 - near, lambda: None)
    to_dmr[0](0)
    to_dmr[0](1)
    pl.semaphore_signal(ready, inc=1, device_id=partner, device_id_type=MESH)

    weights_sent()
    turned[...] = mrs[...].T

    def to_other_core(n, array):
        place = xor(chip, chips - 1 - n)
        if array == 0:
            return [
                remote(
                    w_out.at[place, other_side, :],
                    core_out.at[place],
                    c_send.at[2, n],
                    c_recv.at[2, n],
                    partner,
                )
            ]
        return [
            remote(
                w_in.at[place, halves_in[half], other_side],
                lifted.at[place, half],
                c_send.at[half, n],
                c_recv.at[half, n],
                partner,
            )
            for half in range(2)
        ]

    pl.semaphore_wait(ready, 1)
    hops = {}

    def hop(half, index, place, toward, array):
        copy = remote(
            slot(array, place, core, half),
            (hop_out, hop_in)[array].at[half, index],
            e_send.at[1 - array, 2 * half + index],
            e_recv.at[1 - array, 2 * half + index],
            across(toward),
        )
        copy.start()
        hops[half, index, array] = copy

    def both_cores(n, array):
        step = chips - 1 - n
        place = xor(chip, step)
        for copy in to_other_core(n, array):
            copy.wait()
        if array == 0:
            w_out[place, own_side, :] = w_out[place, own_side, :] + core_out[place]
        else:
            for half in range(2):
                here = (place, halves_in[half], own_side)
                w_in[here] = w_in[here] + lifted[place, half]
        if step == 3:
            hop(0, 1, place, 1, array)
            hop(1, 1, place, 2, array)
        elif step:
            hop(step - 1, 0, place, step, array)

    def expert_grads(array, place, at):
        for half in halves_in:
            if array == 0:
                w_out[place, at, half] = dot(acts[place, :, at], cot[:, half], TN).astype(bf16)
            else:
                w_in[place, half, at] = dot(turned[half, :], hids[place, :, at]).astype(bf16)

    def all_grads(array):
        for n in range(chips):
            place = xor(chip, chips - 1 - n)
            expert_grads(array, place, other_side)
            for copy in to_other_core(n, array):
                copy.start()
            if n:
                both_cores(n - 1, array)
            expert_grads(array, place, own_side)

    all_grads(1)
    outputs()
    both_cores(chips - 1, 1)
    to_dmr[1](0)
    all_grads(0)
    both_cores(chips - 1, 0)
    to_dmr[1](1)
    to_dmr[1](2)
    side = features // 2
    strip = side // chips
    col = lambda c, j: at_block(c * chips + j, strip)

    def section(number, first, count):
        at = pl.ds(first, count)
        state = {}

        def sem(n):
            return s_send.at[number, n], s_recv.at[number, n]

        def start():
            state["core"] = remote(
                sums.at[at, at_block(1 - core, side)], core_got.at[at, :], *sem(0), partner
            )
            state["core"].start()

        def mid():
            state["core"].wait()
            half = at_block(core, side)
            sums[at, half] = sums[at, half] + core_got[at, :]
            state["chips"] = []
            for s in range(1, chips):
                copy = remote(
                    sums.at[at, col(core, xor(chip, s))], chip_got.at[s - 1, at, :], *sem(s), across(s)
                )
                copy.start()
                state["chips"].append(copy)

        def add():
            for copy in state["chips"]:
                copy.wait()
            total = sums[at, col(core, chip)].astype(f32)
            for s in range(1, chips):
                total += chip_got[s - 1, at, :].astype(f32)
            piece[at, :] = total.astype(bf16)

        return start, mid, add

    def two_hop_section(number, first, count):
        at = pl.ds(first, count)
        half_at = [pl.ds(first + n * (count // 2), count // 2) for n in range(2)]
        begin, state = section(number, first, count)[0], {}

        def hop(half, index, place, toward, n):
            copy = remote(
                sums.at[half_at[half], col(core, place)],
                chip_got.at[index, half_at[half], :],
                t_send.at[number, n],
                t_recv.at[number, n],
                across(toward),
            )
            copy.start()
            return copy

        def mid():
            over = remote(
                sums.at[at, at_block(1 - core, side)],
                core_got.at[at, :],
                s_send.at[number, 0],
                s_recv.at[number, 0],
                partner,
            )
            over.wait()
            half = at_block(core, side)
            sums[at, half] = sums[at, half] + core_got[at, :]
            for half in range(2):
                toward = 1 + half
                state[half, 1] = hop(half, 1, xor(chip, 3), toward, 2 * half + 1)
                state[half, 0] = hop(half, 0, xor(chip, toward), toward, 2 * half)

        def second():
            for half in range(2):
                here = (half_at[half], col(core, xor(chip, 2 - half)))
                state[half, 1].wait()
                sums[here] = sums[here] + chip_got[1, half_at[half], :]
                state[half, 2] = hop(half, 2, xor(chip, 2 - half), 2 - half, 4 + half)

        def add():
            for half in range(2):
                state[half, 0].wait()
                state[half, 2].wait()
            total = sums[at, col(core, chip)].astype(f32)
            for index in (0, 2):
                total += chip_got[index, at, :].astype(f32)
            piece[at, :] = total.astype(bf16)

        return begin, mid, second, add

    def two_hop_to_plane(number, first, count):
        at = pl.ds(first, count)
        half_at = [pl.ds(first + n * (count // 2), count // 2) for n in range(2)]
        state = {}

        def send(src, rows_of, place, where, n):
            copy = remote(
                src,
                wide_ref.at[rows_of, col(core, place)],
                t_send.at[number, n],
                t_recv.at[number, n],
                where,
            )
            copy.start()
            return copy

        def start():
            for urgent in range(2):
                for bit in (1, 2):
                    half = bit - 1 if urgent == 0 else 2 - bit
                    state[bit, half] = send(
                        piece.at[half_at[half], :],
                        half_at[half],
                        chip,
                        across(bit),
                        6 + 2 * (bit - 1) + half,
                    )
            over = send(piece.at[at, :], at, chip, partner, 12)
            own = pltpu.make_async_copy(
                piece.at[at, :], wide_ref.at[at, col(core, chip)], t_send.at[number, 15]
            )
            own.start()
            state["wait"] = [over, own]

        def relay():
            for half in range(2):
                bit = 1 + half
                state[bit, half].wait_recv()
                place = xor(chip, bit)
                here = wide_ref.at[half_at[half], col(core, place)]
                state[3, half] = send(here, half_at[half], place, across(2 - half), 10 + half)

        def forward():
            for bit in (1, 2):
                state[bit, 2 - bit].wait_recv()
                place = xor(chip, bit)
                here = wide_ref.at[at, col(core, place)]
                state["wait"].append(send(here, at, place, partner, 12 + bit))

        def end():
            for half in range(2):
                state[3, half].wait_recv()
            place = xor(chip, 3)
            here = wide_ref.at[at, col(core, place)]
            state["wait"].append(send(here, at, place, partner, 16))

        def done():
            for copy in state["wait"]:
                copy.wait()
            for half in range(2):
                state[3, half].wait_send()
                for bit in (1, 2):
                    state[bit, half].wait_send()

        return start, relay, forward, end, done

    def to_plane(number, src, rows_to):
        state = {}

        def sem(n):
            return s_send.at[number, chips + n], s_recv.at[number, chips + n]

        def start():
            here = wide_ref.at[rows_to, col(core, chip)]
            state["share"] = [remote(src, here, *sem(s), across(s)) for s in range(1, chips)]
            over = remote(src, here, *sem(0), partner)
            own = pltpu.make_async_copy(src, here, s_send.at[number, 3 * chips - 1])
            state["wait"] = [over, own]
            for copy in state["share"] + state["wait"]:
                copy.start()

        def forward():
            for s in range(1, chips):
                state["share"][s - 1].wait()
                here = wide_ref.at[rows_to, col(core, xor(chip, s))]
                copy = remote(here, here, *sem(chips - 1 + s), partner)
                copy.start()
                state["wait"].append(copy)

        def end():
            for copy in state["wait"]:
                copy.wait()

        return start, forward, end

    mixed = w_o.shape[0]
    small = ceil_to(named + 1, 16)
    at_a = pl.ds(features, 16)
    at_o = pl.ds(features + 16, mixed)
    at_g = pl.ds(features + 16 + mixed, small)
    of_d = [two_hop_section(n, n * features // 2, features // 2) for n in range(2)]
    of_o = two_hop_section(2, features + 16, mixed)
    of_g = section(3, features + 16 + mixed, small)
    of_a = section(4, features, 16)
    out_d = [two_hop_to_plane(n, n * features // 2, features // 2) for n in range(2)]
    out_o = two_hop_to_plane(2, features + 16, mixed)
    out_g = to_plane(3, blocks, pl.ds(features + 16 + mixed, n_head * small))
    out_a = to_plane(4, piece.at[at_a, :], at_a)
    router_part = dot(dzs[...], mrs[...], TN)[:named]

    grad_x_ref[...] = part[own_block, :].astype(f32)
    to_dmr[2](grad_x_ref)
    incoming = grad_x_ref[...]
    mid = middle[...]
    inverse = lax.rsqrt(jnp.mean(mid * mid, axis=-1, keepdims=True) + epsilon)
    unit = mid * inverse
    scaled = incoming * expert_gain
    dmid = cot[own_block, :].astype(f32) + inverse * (
        scaled - unit * jnp.mean(scaled * unit, axis=-1, keepdims=True)
    )
    grad_x_ref[...] = dmid
    das[own_block, :] = dmid.astype(bf16)
    da_start, da_stage, da_end, _ = gather(6, das)
    da_start()
    sums[at_g, :] = jnp.concatenate(
        [
            router_part,
            jnp.sum(incoming * unit, axis=0, keepdims=True),
            jnp.zeros((small - named - 1, features), f32),
        ],
        axis=0,
    ).astype(bf16)
    of_g[0]()
    turned[...] = rows[...].T
    of_g[1]()
    lasts = {}

    def first_hop(half, index, place):
        for array in range(2):
            hops[half, index, array].wait()
        at_in = (place, halves_in[half], own_side)
        at_out = (place, halves_out(core)[half], slice(None))
        w_in[at_in] = w_in[at_in] + hop_in[half, index]
        w_out[at_out] = w_out[at_out] + hop_out[half, index]

    for half in range(2):
        toward = 2 - half
        place = xor(chip, toward)
        first_hop(half, 1, place)
        pl.semaphore_signal(free.at[half], inc=1, device_id=across(toward), device_id_type=MESH)
        pl.semaphore_wait(free.at[half], 1)
        lasts[half] = (
            remote(
                slot(1, place, core, half),
                hop_in.at[half, 1],
                e_send.at[0, 4 + half],
                e_recv.at[0, 4 + half],
                across(toward),
            ),
            remote(
                slot(0, place, core, half),
                hop_out.at[half, 1],
                e_send.at[1, 4 + half],
                e_recv.at[1, 4 + half],
                across(toward),
            ),
        )
        for copy in lasts[half]:
            copy.start()
    lane = lax.broadcasted_iota(jnp.int32, (tokens, width), 1)

    def through_output(block):
        at = at_block(block, tokens)
        all_five = dot(das[at, :], w_o[...], NT)
        attended = att[at, :]
        total = jnp.zeros((tokens, width), f32)
        gate = jnp.zeros((tokens, width), f32)
        for e in range(experts):
            one = all_five[:, e * width : (e + 1) * width]
            total += gates[at, experts + e : experts + e + 1] * one
            gate = jnp.where(
                lane == experts + e, jnp.sum(one * attended, axis=-1, keepdims=True), gate
            )
        datt[at, :] = total.astype(bf16)
        gate_grads[at, :] = gate

    through_output(h)
    to_out = chain_sum(7, outs, got_out)
    for step in (1, 2, 3):
        da_stage(step)
        if step == 1:
            for number in range(last):
                to_out[0](number)
        through_output(arrival[step - 1])

    for e in range(experts):
        one = (gates[:, experts + e : experts + e + 1] * att[...]).astype(bf16)
        sums[pl.ds(features + 16 + e * width, width), :] = dot(one, das[...], TN).astype(bf16)
    of_o[0]()

    @pl.loop(0, n_head)
    def _(block):
        at = at_block(block, tokens)
        chance = probs[at, :].astype(f32)
        dprob = dot(datt[at, :], v[...], NT)
        centre = jnp.sum(chance * dprob, axis=-1, keepdims=True)
        scores[at, :] = (chance * (dprob - centre)).astype(bf16)

    dq = dot(scores[...], k[...]) * scale
    dk = dot(scores[...], q[...], TN) * scale
    dv = dot(probs[...], datt[...], TN)
    of_o[1]()
    c, s = turns(slice(None))
    qkz[:, pl.ds(0, width)] = (dq * c - swap_halves(dq) * s).astype(bf16)
    qkz[:, pl.ds(width, width)] = (dk * c - swap_halves(dk) * s).astype(bf16)
    gate = gate_grads[...]
    lane = lax.broadcasted_iota(jnp.int32, (group, width), 1)
    for e in range(experts):
        vgrads[:, pl.ds(e * width, width)] = (gates[:, e : e + 1] * dv).astype(bf16)
        one = jnp.sum(vx[:, pl.ds(e * width, width)].astype(f32) * dv, axis=-1, keepdims=True)
        gate = jnp.where(lane == e, one, gate)
    qkz[:, pl.ds(2 * width, width)] = (gate * gates[...] * (1.0 - gates[...])).astype(bf16)

    scaled_qkz = (qkz[...].astype(f32) * gates[:, width - 1 : width]).astype(bf16)

    def matrix_rows(c):
        at = at_block(c, column)
        sums[at, pl.ds(0, 3 * width)] = dot(turned[at, :], scaled_qkz).astype(bf16)
        sums[at, pl.ds(3 * width, experts * width)] = dot(turned[at, :], vgrads[...]).astype(bf16)

    steps_each = features // column // 2
    for n in range(2):
        pl.loop(n * steps_each, (n + 1) * steps_each)(matrix_rows)
        of_d[n][0]()
    def into_rows(block):
        at = at_block(block, tokens)
        inverse = gates[at, width - 1 : width]
        unit = rows[at, :].astype(f32) * inverse
        through = dot(qkz[at, :], w_an[...], NT)
        scaled = through * attend_gain
        total = inverse * (
            scaled - unit * jnp.mean(scaled * unit, axis=-1, keepdims=True)
        ) + dot(vgrads[at, :], w_v[...], NT)
        return total, jnp.sum(through * unit, axis=0, keepdims=True)

    to_x = chain_sum(8, part, got)
    gain = jnp.zeros((1, features), f32)
    for number in range(last):
        total, one = into_rows(leaving[number])
        gain += one
        part[at_block(leaving[number], tokens), :] = total.astype(bf16)
        to_x[0](number)
        if number < 2:
            of_d[number][1]()
    total, one = into_rows(h)
    sums[at_a, :] = jnp.broadcast_to(gain + one, (16, features)).astype(bf16)
    of_a[0]()
    grad_x_ref[...] += total
    to_out[1](0)
    to_out[1](1)
    of_a[1]()
    of_o[2]()
    of_g[2]()
    small_block = at_block(h, small)
    blocks[small_block, :] = piece[at_g, :]
    g_copies = spread(9, lambda s: blocks.at[small_block, :], lambda s: blocks.at[small_block, :])
    to_x[1](0)
    to_out[1](2)
    of_o[3]()
    out_o[0]()
    of_d[0][2]()
    to_x[1](1)
    to_x[1](2)
    of_d[1][2]()
    out_o[1]()
    of_d[0][3]()
    out_d[0][0]()
    of_a[2]()
    gain_part[...] = piece[at_a, :]
    gain_copies = spread(10, lambda s: gain_part, lambda s: gain_got.at[s - 1])
    out_o[2]()
    of_d[1][3]()
    out_d[1][0]()
    for step in peers:
        g_copies[step].wait()
    out_g[0]()
    gain = gain_part[...].astype(f32)
    for step in peers:
        gain_copies[step].wait()
        gain += gain_got[step - 1].astype(f32)
    piece[at_a, :] = gain.astype(bf16)
    out_a[0]()
    out_d[0][1]()
    to_x[2](grad_x_ref)
    output_ref[...] = middle[...] + outs[own_block, :].astype(f32)
    to_out[2](output_ref)
    for half in range(2):
        first_hop(half, 0, chip)
        for copy in lasts[half]:
            copy.wait()
        at_in = (chip, halves_in[half], own_side)
        at_out = (chip, halves_out(core)[half], slice(None))
        w_in[at_in] = w_in[at_in] + hop_in[half, 1]
        w_out[at_out] = w_out[at_out] + hop_out[half, 1]
    stores = (
        pltpu.make_async_copy(w_in.at[chip, :, own_side], fin_in_ref, local_sem.at[0]),
        pltpu.make_async_copy(w_out.at[chip, own_side, :], fin_out_ref, local_sem.at[1]),
    )
    for store in stores:
        store.start()
    out_d[1][1]()
    out_o[3]()
    out_d[0][2]()
    out_g[1]()
    out_a[1]()
    out_d[1][2]()
    out_d[0][3]()
    out_d[1][3]()
    for one in (out_o, out_d[0], out_g, out_a, out_d[1]):
        one[-1]()
    for store in stores:
        store.wait()
    mr_end()
    da_end()


def layer_call(n_dp, n_head, args):
    x, picks, router, value_mat, expert_in = args[0], args[2], args[13], args[11], args[14]
    tokens, features = x.shape
    per_device, _, width = expert_in.shape
    held_experts = value_mat.shape[1]
    group = tokens * n_head
    chips = n_dp // 2
    slab = per_device * width
    lanes = 128
    peers = n_head - 1
    named = ceil_to(n_dp * per_device, 8)
    small = ceil_to(named + 1, 16)
    top = features + held_experts
    held = top + 16 + small
    strip = features // n_dp
    shape = jax.ShapeDtypeStruct
    vm, dma = pltpu.VMEM, pltpu.SemaphoreType.DMA
    outs = [
        (shape((tokens, features), f32), VM),
        (shape((tokens, features), f32), VM),
        (shape((top + 16 + n_head * small, features), bf16), ANY),
        (shape((features, slab), bf16), ANY),
        (shape((slab, features), bf16), ANY),
    ]
    scratch = dict(
        picks=vm(picks.shape, jnp.int32),
        two_picks=vm((2, *args[3].shape), jnp.int32),
        head_picks=vm((group, lanes), jnp.int32),
        w_g=vm(args[10].shape, bf16),
        w_r=vm(router.shape, bf16),
        seg=vm((1, group), jnp.int32),
        gains=vm(args[6].shape, f32),
        angles=vm((group, width), f32),
        w_an=vm((features, 3 * width), bf16),
        w_v=vm((features, held_experts), bf16),
        w_o=vm((held_experts, features), bf16),
        my_router=vm((features, lanes), bf16),
        w_in=vm((chips, features, 2 * slab), bf16),
        w_out=vm((chips, 2 * slab, features), bf16),
        rows=vm((group, features), bf16),
        cot=vm((group, features), bf16),
        mrs=vm((group, features), bf16),
        das=vm((group, features), bf16),
        turned=vm((features, group), bf16),
        my_mask=vm((n_head, tokens, lanes), bf16),
        all_mask=vm((group, lanes), bf16),
        gates=vm((group, width), f32),
        q=vm((group, width), bf16),
        k=vm((group, width), bf16),
        v=vm((group, width), bf16),
        vx=vm((group, held_experts), bf16),
        att=vm((group, width), f32),
        part=vm((group, features), bf16),
        got=vm((2 * peers, tokens, features), bf16),
        outs=vm((group, features), bf16),
        got_out=vm((2 * peers, tokens, features), bf16),
        lifted=vm((chips, 2, group, slab), bf16),
        core_out=vm((chips, slab, features), bf16),
        acts=vm((chips, group, 2 * slab), bf16),
        hids=vm((chips, group, 2 * slab), bf16),
        dzs=vm((group, lanes), bf16),
        datt=vm((group, width), bf16),
        gate_grads=vm((group, width), f32),
        probs=vm((group, group), bf16),
        scores=vm((group, group), bf16),
        qkz=vm((group, 3 * width), bf16),
        vgrads=vm((group, held_experts), bf16),
        gain_part=vm((16, strip), bf16),
        gain_got=vm((peers, 16, strip), bf16),
        sums=vm((held, features), bf16),
        core_got=vm((held, features // 2), bf16),
        chip_got=vm((chips - 1, held, strip), bf16),
        piece=vm((held, strip), bf16),
        blocks=vm((n_head * small, strip), bf16),
        hop_in=vm((2, 2, features // 2, slab), bf16),
        hop_out=vm((2, 2, slab // 2, features), bf16),
        local_sem=dma((16 + 1 + per_device,)),
        z_send=dma((11, 4 * peers)),
        z_recv=dma((11, 4 * peers)),
        w_send=dma((22,)),
        w_recv=dma((22,)),
        c_send=dma((3, chips)),
        c_recv=dma((3, chips)),
        e_send=dma((2, 6)),
        e_recv=dma((2, 6)),
        s_send=dma((5, 3 * chips)),
        s_recv=dma((5, 3 * chips)),
        t_send=dma((3, 17)),
        t_recv=dma((3, 17)),
        ready=pltpu.SemaphoreType.REGULAR,
        free=pltpu.SemaphoreType.REGULAR((2,)),
    )
    return pl.pallas_call(
        functools.partial(layer_kernel, n_dp, n_head),
        out_shape=[o[0] for o in outs],
        out_specs=[o[1] for o in outs],
        in_specs=[ANY] * 16,
        scratch_shapes=list(scratch.values()),
        compiler_params=pltpu.CompilerParams(
            collective_id=1, has_side_effects=True, vmem_limit_bytes=vmem_bytes
        ),
    )(*args)


def finish_kernel(
    n_dp,
    n_head,
    output_ref,
    grad_x_ref,
    wide_ref,
    in_ref,
    out_ref,
    gain_ref,
    final_ref,
    input_ref,
    attend_ref,
    query_ref,
    key_ref,
    value_ref,
    mix_ref,
    gate_ref,
    expert_ref,
    router_ref,
    grad_in_ref,
    grad_out_ref,
    wide,
    flat_in,
    flat_out,
    value,
    mix,
    grad_in,
    grad_out,
    output,
    grad_x,
    sem,
):
    features, slab = in_ref.shape
    per_device, _, width = grad_in_ref.shape
    experts_total, gates = router_ref.shape[0], gate_ref.shape[0]
    mixed = mix_ref.shape[0]
    top = features + 16 + mixed
    small = (wide_ref.shape[0] - top) // n_head
    named = n_dp * per_device

    def copy(src, dst, number):
        one = pltpu.make_async_copy(src, dst, sem.at[number])
        one.start()
        return one

    rest = pl.ds(top, wide_ref.shape[0] - top)
    loads = [
        copy(wide_ref.at[pl.ds(0, features), :], wide.at[pl.ds(0, features), :], 0),
        copy(wide_ref.at[pl.ds(features, top - features), :], wide.at[pl.ds(features, top - features), :], 1),
        copy(in_ref, flat_in, 2),
        copy(out_ref, flat_out, 3),
        copy(wide_ref.at[rest, :], wide.at[rest, :], 4),
    ]
    loads += [copy(output_ref, output, 11), copy(grad_x_ref, grad_x, 12)]
    stores = []
    for number, (held, result) in enumerate(((output, final_ref), (grad_x, input_ref))):
        loads[5 + number].wait()
        stores.append(copy(held, result, 5 + number))
    loads[0].wait()
    first = pl.ds(0, features)
    value[...] = wide[first, pl.ds(3 * width, value.shape[1])].astype(f32)
    stores.append(copy(value, value_ref, 7))
    gain = jnp.broadcast_to(gain_ref[0:1, :], (width, features)).T
    query_ref[...] = wide[first, pl.ds(0, width)].astype(f32) * gain
    key_ref[...] = wide[first, pl.ds(width, width)].astype(f32) * gain
    turned = (wide[first, pl.ds(2 * width, width)].astype(f32) * gain).T
    for e in range(gates):
        gate_ref[e] = turned[e : e + 1]
    loads[1].wait()
    mix[...] = wide[pl.ds(features + 16, mixed), :].astype(f32)
    stores.append(copy(mix, mix_ref, 8))
    loads[2].wait()
    for e in range(per_device):
        grad_in[e] = flat_in[:, pl.ds(e * width, width)].astype(f32)
    stores.append(copy(grad_in, grad_in_ref, 9))
    loads[3].wait()
    for e in range(per_device):
        grad_out[e] = flat_out[pl.ds(e * width, width), :].astype(f32)
    stores.append(copy(grad_out, grad_out_ref, 10))
    loads[4].wait()
    attend_ref[...] = wide[pl.ds(features, 16), :][0:1].astype(f32)
    planes = wide[pl.ds(top, n_head * small), :]
    place = lax.broadcasted_iota(jnp.int32, (n_head * small, experts_total), 0)
    name = lax.broadcasted_iota(jnp.int32, (n_head * small, experts_total), 1)
    slot, plane = place % small, place // small
    expert = (slot // per_device * n_head + plane) * per_device + slot % per_device
    chosen = (slot < named) & (expert == name)
    router_ref[...] = dot(jnp.where(chosen, 1.0, 0.0).astype(bf16), planes, TN)
    gain = jnp.zeros((1, features), f32)
    for z in range(n_head):
        row = z * small + ceil_to(named, 8)
        gain += planes[row : row + 1].astype(f32)
    expert_ref[...] = gain
    for store in stores:
        store.wait()


def finish_call(n_dp, n_head, shapes, args):
    shape = jax.ShapeDtypeStruct
    wide, flat_in, flat_out = args[2], args[3], args[4]
    value, mix, grad_in, grad_out = shapes[5], shapes[6], shapes[10], shapes[11]
    specs = [VM] * 12
    for number in (0, 1, 5, 6, 10, 11):
        specs[number] = ANY
    return pl.pallas_call(
        functools.partial(finish_kernel, n_dp, n_head),
        out_shape=[shape(s, f32) for s in shapes],
        out_specs=specs,
        in_specs=[ANY] * 5 + [VM],
        scratch_shapes=[
            pltpu.VMEM(wide.shape, bf16),
            pltpu.VMEM(flat_in.shape, bf16),
            pltpu.VMEM(flat_out.shape, bf16),
            pltpu.VMEM(value, f32),
            pltpu.VMEM(mix, f32),
            pltpu.VMEM(grad_in, f32),
            pltpu.VMEM(grad_out, f32),
            pltpu.VMEM(shapes[0], f32),
            pltpu.VMEM(shapes[1], f32),
            pltpu.SemaphoreType.DMA((13,)),
        ],
        compiler_params=pltpu.CompilerParams(vmem_limit_bytes=60 << 20),
    )(*args)


def kernel_body(
    n_dp,
    n_head,
    hidden_in,
    segments,
    value_pick,
    output_pick,
    expert_pick,
    attend_gain,
    query_weight,
    key_weight,
    value_weight,
    output_weight,
    head_router,
    expert_gain,
    router,
    expert_in,
    expert_out,
    cotangent,
):
    tokens, features = hidden_in.shape
    per_device, _, width = expert_in.shape
    experts = head_router.shape[2] // 2
    group = tokens * n_head
    angles = np.arange(group)[:, None] * theta ** (-2.0 * np.arange(width // 2) / width)[None, :]
    angles = np.concatenate([np.cos(angles), np.sin(angles)], axis=1).astype(np.float32)
    both = np.eye(2, dtype=np.float32)
    gains = attend_gain.astype(f32) * both[:, :1] + expert_gain.astype(f32) * both[:, 1:]
    results = layer_call(
        n_dp,
        n_head,
        (
            hidden_in,
            cotangent,
            expert_pick.T,
            value_pick.transpose(1, 2, 0)[0],
            output_pick.transpose(1, 2, 0)[0],
            segments[None, :],
            gains,
            angles,
            query_weight[0],
            key_weight[0],
            head_router.transpose(0, 2, 1)[0],
            value_weight[0],
            output_weight[0],
            router.T,
            expert_in,
            expert_out.reshape(per_device * width, features),
        ),
    )
    shapes = (
        (tokens, features),
        (tokens, features),
        (1, features),
        query_weight.shape[1:],
        key_weight.shape[1:],
        value_weight.shape[1:],
        output_weight.shape[1:],
        (2 * experts, 1, features),
        (1, features),
        (router.shape[1], features),
        expert_in.shape,
        expert_out.shape,
    )
    done = list(finish_call(n_dp, n_head, shapes, (*results, gains)))
    for number in (3, 4, 5, 6):
        done[number] = done[number][None]
    done[7] = done[7].transpose(1, 2, 0)
    done[9] = done[9].T
    done[2], done[8] = done[2][0], done[8][0]
    return tuple(done)


def solution(mesh):
    rows = P(everywhere, None)
    heads = P("head", None, None)
    experts = P(everywhere, None, None)
    picks = P("dp", "head", None)
    in_specs = (
        rows, P("dp"), picks, picks, rows, P(), heads, heads, heads, heads, heads,
        P(), P(), experts, experts, rows,
    )
    out_specs = (
        rows, rows, P(), heads, heads, heads, heads, heads, P(), P(), experts, experts,
    )
    n_dp, n_head = mesh.shape["dp"], mesh.shape["head"]

    def program(*args):
        held = 2 * n_dp * args[13].shape[0] * args[13].shape[1] * args[13].shape[2] * 2
        if n_head == 4 and held <= vmem_for_weights:
            return kernel_body(n_dp, n_head, *args)
        return body(*args)

    return jax.shard_map(program, mesh=mesh, in_specs=in_specs, out_specs=out_specs, check_vma=False)
```

```python
import functools

import jax
import jax.numpy as jnp
import numpy as np
from jax import lax
from jax.experimental import pallas as pl
from jax.experimental.pallas import tpu as pltpu
from jax.sharding import PartitionSpec as P

epsilon = 1e-06
theta = 10000.0
negative = -1e30
f32 = jnp.float32
bf16 = jnp.bfloat16
everywhere = ("dp", "head")
whole_rows = 4096
vmem_for_weights = 16 << 20
vmem_bytes = 62 << 20


def product(left, right, left_axis, right_axis):
    return lax.dot_general(
        left, right, (((left_axis,), (right_axis,)), ((), ())), preferred_element_type=f32
    )


def rms_scale(residual):
    return lax.rsqrt(jnp.mean(residual * residual, axis=-1, keepdims=True) + epsilon)


def rotary_tables(row_count, head_width):
    half_width = head_width // 2
    position = jnp.arange(row_count, dtype=f32)[:, None]
    exponent = jnp.arange(half_width, dtype=f32)[None, :]
    angles = position * jnp.power(theta, -2.0 * exponent / head_width)
    return (jnp.cos(angles), jnp.sin(angles))


def rotate(matrix, cosine, sine):
    half = matrix.shape[-1] // 2
    first, second = matrix[:, :half], matrix[:, half:]
    return jnp.concatenate([first * cosine - second * sine, second * cosine + first * sine], axis=-1)


def pick_mask(picks, expert_count):
    hits = picks[:, 0, :, None] == jnp.arange(expert_count, dtype=jnp.int32)[None, None, :]
    return jnp.any(hits, axis=1).astype(f32)


def norm_back(residual, inverse, gain, incoming):
    unit_rows = residual * inverse
    scaled = incoming * gain
    gain_grad = jnp.sum(incoming * unit_rows, axis=0)
    row_grad = inverse * (scaled - unit_rows * jnp.mean(scaled * unit_rows, axis=-1, keepdims=True))
    return (row_grad, gain_grad)


def gelu_pair(value):
    inner = jnp.tanh(0.7978845608028654 * (value + 0.044715 * value * value * value))
    slope = 0.5 * (1.0 + inner) + 0.5 * value * (1.0 - inner * inner) * 0.7978845608028654 * (
        1.0 + 3.0 * 0.044715 * value * value
    )
    return (0.5 * value * (1.0 + inner), slope)


def body(
    hidden_in,
    segments,
    value_pick,
    output_pick,
    expert_pick,
    attend_gain,
    query_weight,
    key_weight,
    value_weight,
    output_weight,
    head_router,
    expert_gain,
    router,
    expert_in,
    expert_out,
    cotangent,
):
    tokens, features = hidden_in.shape
    per_device, _, width = expert_in.shape
    head_experts = head_router.shape[2] // 2
    head_width = query_weight.shape[2]
    scale = head_width ** (-0.5)
    query_mat, key_mat, value_mat = query_weight[0], key_weight[0], value_weight[0]
    output_mat, gate_mat = output_weight[0], head_router[0]
    value_mask = pick_mask(value_pick, head_experts)
    output_mask = pick_mask(output_pick, head_experts)
    attend_scale = attend_gain.astype(f32)
    expert_scale = expert_gain.astype(f32)
    me = lax.axis_index("dp") * lax.axis_size("head") + lax.axis_index("head")

    rows = lax.all_gather(hidden_in, "head", axis=0, tiled=True)
    grouped = rows.astype(f32)
    group = grouped.shape[0]
    inverse = rms_scale(grouped)
    normed = (grouped * inverse * attend_scale).astype(bf16)
    cosine, sine = rotary_tables(group, head_width)
    queries = rotate(product(normed, query_mat, 1, 0), cosine, sine).astype(bf16)
    key_rows = rotate(product(normed, key_mat, 1, 0), cosine, sine).astype(bf16)
    squash = jax.nn.sigmoid(product(normed, gate_mat, 1, 0))
    value_gates = squash[:, :head_experts] * value_mask
    output_gates = squash[:, head_experts:] * output_mask
    expert_values = product(rows, value_mat, 1, 0).reshape(group, head_experts, head_width)
    values = jnp.sum(expert_values * value_gates[:, :, None], axis=1).astype(bf16)
    places = jnp.arange(group, dtype=jnp.int32)
    allowed = (places[None, :] <= places[:, None]) & (segments[:, None] == segments[None, :])
    scores = jnp.where(allowed, product(queries, key_rows, 1, 1) * scale, negative)
    exponents = jnp.exp(scores - jnp.max(scores, axis=-1, keepdims=True))
    probabilities = exponents / jnp.sum(exponents, axis=-1, keepdims=True)
    attended = product(probabilities.astype(bf16), values, 1, 0)
    weighted = (
        (output_gates[:, :, None] * attended[:, None, :]).reshape(group, -1).astype(bf16)
    )
    middle = hidden_in.astype(f32) + lax.psum_scatter(
        product(weighted, output_mat, 1, 0).astype(bf16), "head", scatter_dimension=0, tiled=True
    ).astype(f32)
    middle_inverse = rms_scale(middle)
    middle_normed = (middle * middle_inverse * expert_scale).astype(bf16)
    mine = me * per_device + jnp.arange(per_device, dtype=jnp.int32)
    my_router = lax.dynamic_slice_in_dim(router, me * per_device, per_device, axis=1)
    in_mat = expert_in.transpose(1, 0, 2).reshape(features, per_device * width)
    out_mat = expert_out.reshape(per_device * width, features)

    def turn(running, own):
        own_rows, own_cot, own_picks = own
        all_cot = lax.all_gather(own_cot, everywhere, axis=0, tiled=True)
        all_picks = lax.all_gather(own_picks, everywhere, axis=0, tiled=True)
        all_rows = lax.all_gather(own_rows, everywhere, axis=0, tiled=True)
        mask = jnp.any(all_picks[:, :, None] == mine[None, None, :], axis=1).astype(f32)
        gates = jax.nn.sigmoid(product(all_rows, my_router, 1, 0))
        live = gates * mask
        act, slope = gelu_pair(product(all_rows, in_mat, 1, 0).reshape(-1, per_device, width))
        lifted = product(all_cot, out_mat, 1, 1).reshape(-1, per_device, width)
        dense_grad = (jnp.sum(act * lifted, axis=-1) * live * (1.0 - gates)).astype(bf16)
        act_live = (act * live[:, :, None]).astype(bf16).reshape(-1, per_device * width)
        hidden_grad = (slope * lifted * live[:, :, None]).astype(bf16)
        hidden_grad = hidden_grad.reshape(-1, per_device * width)
        part_out = product(act_live, out_mat, 1, 0).astype(bf16)
        part_grad = (
            product(hidden_grad, in_mat, 1, 1) + product(dense_grad, my_router, 1, 1)
        ).astype(bf16)
        back = lax.psum_scatter(part_grad, everywhere, scatter_dimension=0, tiled=True)
        forth = lax.psum_scatter(part_out, everywhere, scatter_dimension=0, tiled=True)
        grads = (
            product(all_rows, hidden_grad, 0, 0),
            product(act_live, all_cot, 0, 0),
            product(dense_grad, all_rows, 0, 0),
        )
        if running is not None:
            grads = jax.tree.map(jnp.add, running, grads)
        return grads, (forth, back)

    turns = max(1, lax.axis_size("dp") * lax.axis_size("head") * tokens // whole_rows)
    owned = (middle_normed, cotangent, expert_pick)
    if turns == 1:
        grads, (summed, normed_grad) = turn(None, owned)
    else:
        owned = jax.tree.map(lambda a: a.reshape(turns, -1, a.shape[1]), owned)
        zeros = (
            jnp.zeros(in_mat.shape, f32),
            jnp.zeros(out_mat.shape, f32),
            jnp.zeros((per_device, features), f32),
        )
        grads, sums = lax.scan(turn, zeros, owned)
        summed, normed_grad = (a.reshape(tokens, features) for a in sums)
    grad_in = grads[0].reshape(features, per_device, width).transpose(1, 0, 2)
    grad_out = grads[1].reshape(per_device, width, features)
    grad_router = lax.all_gather(grads[2], everywhere, axis=0, tiled=True).T
    output = middle + summed.astype(f32)
    incoming = cotangent.astype(f32)
    row_grad, grad_gain_expert = norm_back(
        middle, middle_inverse, expert_scale, normed_grad.astype(f32)
    )
    middle_grad = incoming + row_grad
    group_grads = lax.all_gather(middle_grad.astype(bf16), "head", axis=0, tiled=True)
    weighted_grad = product(group_grads, output_mat, 1, 1).reshape(group, head_experts, head_width)
    output_grad = product(weighted, group_grads, 0, 0)
    output_gate_grad = jnp.sum(weighted_grad * attended[:, None, :], axis=-1)
    attended_grad = jnp.sum(weighted_grad * output_gates[:, :, None], axis=1).astype(bf16)
    prob_grad = product(attended_grad, values, 1, 1)
    centre = jnp.sum(probabilities * prob_grad, axis=-1, keepdims=True)
    score_grad = (probabilities * (prob_grad - centre)).astype(bf16)
    query_grad = product(score_grad, key_rows, 1, 0) * scale
    key_grad = product(score_grad, queries, 0, 0) * scale
    values_grad = product(probabilities.astype(bf16), attended_grad, 0, 0)
    expert_grad = (value_gates[:, :, None] * values_grad[:, None, :]).reshape(group, -1).astype(bf16)
    value_gate_grad = jnp.sum(expert_values * values_grad[:, None, :], axis=-1)
    query_grad = rotate(query_grad, cosine, -sine).astype(bf16)
    key_grad = rotate(key_grad, cosine, -sine).astype(bf16)
    logit_grad = (
        jnp.concatenate([value_gate_grad * value_mask, output_gate_grad * output_mask], axis=1)
        * squash
        * (1.0 - squash)
    ).astype(bf16)
    head_grads = (
        product(normed, query_grad, 0, 0),
        product(normed, key_grad, 0, 0),
        product(rows, expert_grad, 0, 0),
        output_grad,
        product(normed, logit_grad, 0, 0),
    )
    head_grads = tuple(grad.astype(bf16) for grad in head_grads)
    head_grads = tuple(grad.astype(f32)[None] for grad in lax.psum(head_grads, "dp"))
    back = (
        product(query_grad, query_mat, 1, 1)
        + product(key_grad, key_mat, 1, 1)
        + product(logit_grad, gate_mat, 1, 1)
    )
    row_back, grad_attend = norm_back(grouped, inverse, attend_scale, back)
    partial = (row_back + product(expert_grad, value_mat, 1, 1)).astype(bf16)
    input_grad = middle_grad + lax.psum_scatter(
        partial, "head", scatter_dimension=0, tiled=True
    ).astype(f32)
    grad_attend, grad_gain_expert = lax.psum((grad_attend, grad_gain_expert), everywhere)
    return (
        output,
        input_grad,
        grad_attend,
        *head_grads,
        grad_gain_expert,
        grad_router,
        grad_in,
        grad_out,
    )


MESH = pl.DeviceIdType.MESH
VM = pl.BlockSpec(memory_space=pltpu.VMEM)
ANY = pl.BlockSpec(memory_space=pl.ANY)
NN = (((1,), (0,)), ((), ()))
NT = (((1,), (1,)), ((), ()))
TN = (((0,), (0,)), ((), ()))


def dot(left, right, dims=NN):
    return lax.dot_general(left, right, dims, preferred_element_type=f32)


def at_block(block, count):
    return pl.ds(pl.multiple_of(block * count, count), count)


def remote(src, dst, send, recv, where):
    return pltpu.make_async_remote_copy(
        src_ref=src, dst_ref=dst, send_sem=send, recv_sem=recv, device_id=where, device_id_type=MESH
    )


def swap_halves(value):
    half = value.shape[-1] // 2
    return jnp.concatenate([value[:, half:], value[:, :half]], axis=-1)


def ceil_to(number, step):
    return -(-number // step) * step


def layer_kernel(
    n_dp,
    n_head,
    x_ref,
    cot_ref,
    pick_ref,
    value_pick_ref,
    output_pick_ref,
    seg_ref,
    gain_ref,
    angle_ref,
    wq_ref,
    wk_ref,
    wg_ref,
    wv_ref,
    wo_ref,
    router_ref,
    in_ref,
    out_ref,
    output_ref,
    grad_x_ref,
    wide_ref,
    fin_in_ref,
    fin_out_ref,
    picks,
    two_picks,
    head_picks,
    w_g,
    w_r,
    seg,
    gains,
    angles,
    w_an,
    w_v,
    w_o,
    my_router,
    w_in,
    w_out,
    rows,
    cot,
    mrs,
    das,
    turned,
    my_mask,
    all_mask,
    gates,
    q,
    k,
    v,
    vx,
    att,
    part,
    got,
    outs,
    got_out,
    lifted,
    core_out,
    acts,
    hids,
    dzs,
    datt,
    gate_grads,
    probs,
    scores,
    qkz,
    vgrads,
    gain_part,
    gain_got,
    sums,
    core_got,
    chip_got,
    piece,
    blocks,
    hop_in,
    hop_out,
    local_sem,
    z_send,
    z_recv,
    w_send,
    w_recv,
    c_send,
    c_recv,
    e_send,
    e_recv,
    s_send,
    s_recv,
    t_send,
    t_recv,
    ready,
    free,
):
    middle = output_ref
    xor = jnp.bitwise_xor
    d, h = lax.axis_index("dp"), lax.axis_index("head")
    chip, core = d // 2, d % 2
    chips = n_dp // 2
    tokens, features = x_ref.shape
    per_device, _, width = in_ref.shape
    slab = per_device * width
    wide = 2 * slab
    experts = wv_ref.shape[1] // width
    named = ceil_to(n_dp * per_device, 8)
    group = tokens * n_head
    pair = 2 * tokens
    column = 256
    lanes = 128
    scale = width ** (-0.5)
    peers = (2, 3, 1)
    partner = (chip * 2 + 1 - core, h)
    own_block = at_block(h, tokens)
    own_side, other_side = at_block(core, slab), at_block(1 - core, slab)
    halves_in = (pl.ds(0, features // 2), pl.ds(features // 2, features // 2))
    halves_out = lambda side: (
        at_block(2 * side, slab // 2),
        at_block(2 * side + 1, slab // 2),
    )

    def along(step):
        return (d, xor(h, step))

    def across(step):
        return (xor(chip, step) * 2 + core, h)

    loads = []

    def load(src, dst):
        copy = pltpu.make_async_copy(src, dst, local_sem.at[len(loads)])
        copy.start()
        loads.append(copy)
        return copy

    own_weights = [load(out_ref, w_out.at[chip, own_side, :])] + [
        load(in_ref.at[e], w_in.at[chip, :, at_block(core * per_device + e, width)])
        for e in range(per_device)
    ]
    for_rows = [
        load(x_ref, rows.at[own_block, :]),
        load(gain_ref, gains),
        load(wg_ref, w_g),
        load(wq_ref, w_an.at[:, pl.ds(0, width)]),
        load(wk_ref, w_an.at[:, pl.ds(width, width)]),
        load(wv_ref, w_v),
        load(value_pick_ref, two_picks.at[0]),
        load(output_pick_ref, two_picks.at[1]),
        load(angle_ref, angles),
    ]
    for_scores = [load(seg_ref, seg), load(wo_ref, w_o)]
    for_mask = load(pick_ref, picks)
    for_cot = load(cot_ref, cot.at[own_block, :])
    for_router = load(router_ref, w_r)

    barrier = pltpu.get_barrier_semaphore()
    friends = [along(s) for s in peers] + [partner] + [across(s) for s in range(1, chips)]
    for friend in friends:
        pl.semaphore_signal(barrier, inc=1, device_id=friend, device_id_type=MESH)
    pl.semaphore_wait(barrier, len(friends))

    right, left = (d, jnp.minimum(h + 1, n_head - 1)), (d, jnp.maximum(h - 1, 0))
    last = n_head - 1

    def pick(*by_place):
        value = jnp.int32(by_place[-1])
        for place in range(n_head - 2, -1, -1):
            value = jnp.where(h == place, by_place[place], value)
        return value

    arrival = (xor(h, 1), pick(2, 2, 1, 1), pick(3, 3, 0, 0))
    leaving = (pick(3, 3, 0, 0), pick(2, 0, 3, 1), pick(1, 2, 1, 2))

    def gather(kind, buffer):
        def go(side, step):
            sign = 1 - 2 * side
            block = jnp.clip(h - sign * step, 0, last)
            where = (d, jnp.clip(h + sign, 0, last))
            copies = []
            for half in range(2):
                here = buffer.at[at_block(2 * block + half, tokens // 2), :]
                number = (side * last + step) * 2 + half
                copies.append(
                    remote(here, here, z_send.at[kind, number], z_recv.at[kind, number], where)
                )
            return copies

        def begin(side):
            for copy in go(side, 0):
                copy.start()

        def start():
            pl.when(h < last)(lambda: begin(0))
            pl.when(h > 0)(lambda: begin(1))

        def arrive(side, step, there, onward):
            for half in range(2):

                @pl.when(there)
                def _():
                    go(side, step - 1)[half].wait_recv()
                    if onward:
                        go(side, step)[half].start()

        def stage(step, which="all"):
            nearer = jnp.where(2 * h < n_head, 0, 1)
            ways = []
            for side in (nearer, 1 - nearer):
                there = jnp.where(side == 0, h >= step, h + step <= last)
                ways.append((side, there, jnp.where(side == 0, h < last, h > 0)))
            for side, there, onward in ways:
                if step < last and which != "rest":
                    arrive(side, step, there & onward, True)
            for side, there, onward in ways:
                if which != "duty":
                    ends_here = there if step == last else there & jnp.logical_not(onward)
                    arrive(side, step, ends_here, False)

        def follow(step):
            pl.when((h < last) & (jnp.maximum(h, 1) == step))(lambda: begin(0))
            pl.when((h > 0) & (jnp.maximum(last - h, 1) == step))(lambda: begin(1))

        def end():
            for step in range(last):
                for side, sent in (
                    (0, (h >= step) & (h < last)),
                    (1, (h + step <= last) & (h > 0)),
                ):

                    @pl.when(sent)
                    def _():
                        for copy in go(side, step):
                            copy.wait_send()

        return start, stage, end, follow

    def chain_sum(kind, parts, slots):
        def go(number):
            block = leaving[number]
            rightward = block > h
            slot = jnp.where(rightward, block - 1, last + block)
            where = (d, jnp.clip(jnp.where(rightward, h + 1, h - 1), 0, last))
            middle_one = (rightward & (h > 0)) | (jnp.logical_not(rightward) & (h < last))
            pieces = []
            for half in range(2):
                at = at_block(2 * block + half, tokens // 2)
                rows_of = pl.ds(half * (tokens // 2), tokens // 2)
                copy = remote(
                    parts.at[at, :],
                    slots.at[slot, rows_of, :],
                    z_send.at[kind, 2 * number + half],
                    z_recv.at[kind, 2 * slot + half],
                    where,
                )
                pieces.append((copy, at, slot, rows_of))
            return pieces, middle_one

        def now(number):
            pieces, middle_one = go(number)

            @pl.when(jnp.logical_not(middle_one))
            def _():
                for copy, _, _, _ in pieces:
                    copy.start()

        def later(number):
            pieces, middle_one = go(number)

            @pl.when(middle_one)
            def _():
                for copy, at, slot, rows_of in pieces:
                    copy.wait_recv()
                    parts[at, :] = parts[at, :] + slots[slot, rows_of, :]
                    copy.start()

        def end(total):
            ends = ((jnp.maximum(h - 1, 0), h > 0), (last + jnp.minimum(h, last - 1), h < last))
            for slot, there in ends:

                @pl.when(there)
                def _():
                    for half in range(2):
                        rows_of = pl.ds(half * (tokens // 2), tokens // 2)
                        remote(
                            parts.at[at_block(2 * h, tokens // 2), :],
                            slots.at[slot, rows_of, :],
                            z_send.at[kind, 0],
                            z_recv.at[kind, 2 * slot + half],
                            right,
                        ).wait_recv()
                    total[...] += slots[slot].astype(f32)

            for number in range(last):
                for copy, _, _, _ in go(number)[0]:
                    copy.wait_send()

        return now, later, end

    def spread(kind, src, dst, steps=peers):
        copies = {}
        for step in steps:
            copies[step] = remote(
                src(step), dst(step), z_send.at[kind, step - 1], z_recv.at[kind, step - 1], along(step)
            )
            copies[step].start()
        return copies

    x_start, x_stage, x_end, _ = gather(0, rows)
    for_rows[0].wait()
    x_start()

    def slot(array, place, side, half=None):
        if array == 0:
            at = halves_out(side)[half] if half is not None else at_block(side, slab)
            return w_out.at[place, at, :]
        at = halves_in[half] if half is not None else pl.ds(0, features)
        return w_in.at[place, at, at_block(side, slab)]

    def weights(number, ref, where):
        copy = remote(ref, ref, w_send.at[number], w_recv.at[number], where)
        copy.start()
        return copy

    slabs, halves_on, to_core, diagonal = {}, {}, {}, {}
    for copy in own_weights:
        copy.wait()
    for array in range(2):
        for first in range(2):
            for bit in (1, 2):
                half = bit - 1 if first == 0 else 2 - bit
                number = ((bit - 1) * 2 + half) * 2 + array
                slabs[bit, half, array] = weights(
                    number, slot(array, chip, core, half), across(bit)
                )
        to_core[0, array] = weights(12 + array, slot(array, chip, core), partner)

    for_mask.wait()
    own_picks = jnp.concatenate(
        [picks[...].astype(f32), jnp.zeros((lanes - picks.shape[0], tokens), f32)], axis=0
    ).T.astype(jnp.int32)
    lane = lax.broadcasted_iota(jnp.int32, (tokens, lanes), 1)
    for plane in range(n_head):
        expert = (lane // per_device * n_head + plane) * per_device + lane % per_device
        expert = jnp.where(lane < n_dp * per_device, expert, -1)
        hit = own_picks[:, 0:1] == expert
        for c in range(1, picks.shape[0]):
            hit = hit | (own_picks[:, c : c + 1] == expert)
        my_mask[plane] = jnp.where(hit, 1.0, 0.0).astype(bf16)
    mask_copies = spread(1, lambda s: my_mask.at[xor(h, s)], lambda s: all_mask.at[own_block, :])
    all_mask[own_block, :] = my_mask[h]

    for copy in for_rows[1:]:
        copy.wait()
    attend_gain = gains[0:1, :]
    expert_gain = gains[1:2, :]
    one_hot = lambda count: jnp.where(
        lax.broadcasted_iota(jnp.int32, (count, width), 0)
        == lax.broadcasted_iota(jnp.int32, (count, width), 1),
        1.0,
        0.0,
    ).astype(bf16)
    w_an[:, pl.ds(2 * width, width)] = dot(w_g[...], one_hot(w_g.shape[0]), TN).astype(bf16)
    uses = two_picks.shape[1]
    head_picks[...] = jnp.concatenate(
        [
            two_picks[0].astype(f32),
            two_picks[1].astype(f32) + experts,
            jnp.zeros((lanes - 2 * uses, group), f32),
        ],
        axis=0,
    ).T.astype(jnp.int32)
    half_lanes = lax.broadcasted_iota(jnp.int32, (1, width), 1) < width // 2

    def turns(at):
        both = angles[at, :]
        turned_over = swap_halves(both)
        return (
            jnp.where(half_lanes, both, turned_over),
            jnp.where(half_lanes, -turned_over, both),
        )

    def project(block):
        at = at_block(block, tokens)
        own = rows[at, :]
        full = own.astype(f32)
        inverse = lax.rsqrt(jnp.mean(full * full, axis=-1, keepdims=True) + epsilon)
        unit = (full * inverse * attend_gain).astype(bf16)
        qkg = dot(unit, w_an[...])
        c, s = turns(at)
        one, two = qkg[:, :width], qkg[:, width : 2 * width]
        q[at, :] = (one * c + swap_halves(one) * s).astype(bf16)
        k[at, :] = (two * c + swap_halves(two) * s).astype(bf16)
        lane = lax.broadcasted_iota(jnp.int32, (tokens, width), 1)
        chosen = head_picks[at, :]
        hit = lane == chosen[:, 0:1]
        for c in range(1, 2 * uses):
            hit = hit | (lane == chosen[:, c : c + 1])
        gate = jnp.where(hit, jax.nn.sigmoid(qkg[:, 2 * width :]), 0.0)
        gates[at, :] = jnp.where(lane == width - 1, inverse, gate)
        values = dot(own, w_v[...])
        vx[at, :] = values.astype(bf16)
        value = gate[:, 0:1] * values[:, :width]
        for e in range(1, experts):
            value += gate[:, e : e + 1] * values[:, e * width : (e + 1) * width]
        v[at, :] = value.astype(bf16)

    project(h)
    _, cot_stage, cot_end, cot_follow = gather(2, cot)
    for_cot.wait()
    for step in (1, 2, 3):
        x_stage(step)
        cot_follow(step)
        project(arrival[step - 1])
    for copy in for_scores:
        copy.wait()
    seg_col = gate_grads
    seg_col[...] = jnp.broadcast_to(seg[...].astype(f32), (lanes, group)).T

    def attend(block):
        at = at_block(block, tokens)
        score = dot(q[at, :], k[...], NT) * scale
        row = block * tokens + lax.broadcasted_iota(jnp.int32, (tokens, group), 0)
        place = lax.broadcasted_iota(jnp.int32, (tokens, group), 1)
        allowed = (place <= row) & (seg_col[at, 0:1] == seg[...].astype(f32))
        score = jnp.where(allowed, score, negative)
        exponents = jnp.exp(score - jnp.max(score, axis=-1, keepdims=True))
        chance = exponents / jnp.sum(exponents, axis=-1, keepdims=True)
        probs[at, :] = chance.astype(bf16)
        attended = dot(chance.astype(bf16), v[...])
        att[at, :] = attended
        gate = gates[at, :]
        weighted = jnp.concatenate(
            [
                (gate[:, experts + e : experts + e + 1] * attended).astype(bf16)
                for e in range(experts)
            ],
            axis=-1,
        )
        return dot(weighted, w_o[...])

    to_mid = chain_sum(3, part, got)
    for number in range(last):
        block = leaving[number]
        part[at_block(block, tokens), :] = attend(block).astype(bf16)
        to_mid[0](number)
    middle[...] = rows[own_block, :].astype(f32) + attend(h)
    cot_stage(1, "duty")
    to_mid[1](0)
    for array in range(2):
        for half in range(2):
            slabs[1 + half, half, array].wait_recv()
            halves_on[half, array] = weights(
                8 + 2 * half + array,
                slot(array, xor(chip, 1 + half), core, half),
                across(2 - half),
            )

    to_mid[1](1)
    cot_stage(2, "duty")
    to_mid[1](2)
    for bit in (1, 2):
        slabs[bit, 2 - bit, 0].wait_recv()
        to_core[bit, 0] = weights(14 + (bit - 1) * 2, slot(0, xor(chip, bit), core), partner)
        slabs[bit, 2 - bit, 1].wait_recv()
        to_core[bit, 1] = weights(15 + (bit - 1) * 2, slot(1, xor(chip, bit), core), partner)
    for_router.wait()
    slot_of = lax.broadcasted_iota(jnp.int32, (w_r.shape[0], lanes), 1)
    name = lax.broadcasted_iota(jnp.int32, (w_r.shape[0], lanes), 0)
    expert = (slot_of // per_device * n_head + h) * per_device + slot_of % per_device
    expert = jnp.where(slot_of < n_dp * per_device, expert, -1)
    my_router[...] = dot(
        w_r[...], jnp.where(name == expert, 1.0, 0.0).astype(bf16), TN
    ).astype(bf16)

    to_mid[2](middle)
    mid = middle[...]
    inverse = lax.rsqrt(jnp.mean(mid * mid, axis=-1, keepdims=True) + epsilon)
    mrs[own_block, :] = (mid * inverse * expert_gain).astype(bf16)
    mr_start, mr_stage, mr_end, _ = gather(4, mrs)
    mr_start()

    def last_halves(array):
        for half in range(2):
            halves_on[half, array].wait_recv()
            diagonal[half, array] = weights(
                18 + 2 * half + array, slot(array, xor(chip, 3), core, half), partner
            )

    for step in (1, 2, 3):
        cot_stage(step, "rest")
    last_halves(0)
    for step in peers:
        mask_copies[step].wait()
    cot_end()
    x_end()

    def weights_here(array):
        for bit in range(3):
            to_core[bit, array].wait_recv()
        for half in range(2):
            diagonal[half, array].wait_recv()

    def weights_sent():
        for array in range(2):
            for bit in range(3):
                to_core[bit, array].wait_send()
            for half in range(2):
                diagonal[half, array].wait_send()
                halves_on[half, array].wait_send()
                for bit in (1, 2):
                    slabs[bit, half, array].wait_send()

    weights_here(0)

    def lift_chip(j):
        lift = dot(cot[...], w_out[j], NT)
        lifted[j, 0] = lift[:, :slab].astype(bf16)
        lifted[j, 1] = lift[:, slab:].astype(bf16)

    pl.loop(0, chips // 2)(lift_chip)
    mr_stage(1, "duty")
    last_halves(1)
    pl.loop(chips // 2, chips)(lift_chip)

    weights_here(1)

    def spread_lanes(j):
        lane = lax.broadcasted_iota(jnp.int32, (lanes, wide), 1) // width
        slot = lax.broadcasted_iota(jnp.int32, (lanes, wide), 0)
        return jnp.where(slot == lane + j * (wide // width), 1.0, 0.0).astype(bf16)

    def pair_of_blocks(number, between):
        at = at_block(number, pair)
        own = mrs[at, :]
        gates = jax.nn.sigmoid(dot(own, my_router[...]))
        live = gates * all_mask[at, :].astype(f32)
        narrow = live.astype(bf16)

        def chip_step(j, total):
            pick = spread_lanes(j)
            hidden = dot(own, w_in[j])
            gate = dot(narrow, pick).astype(bf16)
            lift = jnp.concatenate([lifted[j, 0, at, :], lifted[j, 1, at, :]], axis=-1)
            square = hidden * hidden
            inner = jnp.tanh(0.7978845608028654 * hidden * (1.0 + 0.044715 * square))
            half = 0.5 * (1.0 + inner)
            act = hidden * half
            slope = half + act * (1.0 - inner) * (
                0.7978845608028654 + (0.7978845608028654 * 3.0 * 0.044715) * square
            )
            act = act.astype(bf16)
            acts[j, at, :] = act * gate
            hids[j, at, :] = slope.astype(bf16) * (lift * gate)
            return total + dot(act * lift, pick, NT)

        total = lax.fori_loop(0, chips // 2, chip_step, jnp.zeros((pair, lanes), f32))
        between()
        total = lax.fori_loop(chips // 2, chips, chip_step, total)
        dz = (total * live * (1.0 - gates)).astype(bf16)
        dzs[at, :] = dz

        @pl.loop(0, features // column)
        def _(c):
            part_of = at_block(c, column)
            total = dot(dz, my_router[part_of, :], NT)
            for j in range(chips):
                total += dot(hids[j, at, :], w_in[j, part_of, :], NT)
            part[at, part_of] = total.astype(bf16)

    def outputs():
        @pl.loop(0, features // column)
        def _(c):
            part_of = at_block(c, column)
            total = dot(acts[0], w_out[0, :, part_of])
            for j in range(1, chips):
                total += dot(acts[j], w_out[j, :, part_of])
            outs[:, part_of] = total.astype(bf16)

    near = h // 2
    mr_stage(1, "rest")
    to_dmr = chain_sum(5, part, got)
    pair_of_blocks(near, lambda: mr_stage(2, "duty"))
    to_dmr[0](2)
    mr_stage(2, "rest")
    mr_stage(3)
    pair_of_blocks(1 - near, lambda: None)
    to_dmr[0](0)
    to_dmr[0](1)
    pl.semaphore_signal(ready, inc=1, device_id=partner, device_id_type=MESH)

    weights_sent()
    turned[...] = mrs[...].T

    def to_other_core(n, array):
        place = xor(chip, chips - 1 - n)
        if array == 0:
            return [
                remote(
                    w_out.at[place, other_side, :],
                    core_out.at[place],
                    c_send.at[2, n],
                    c_recv.at[2, n],
                    partner,
                )
            ]
        return [
            remote(
                w_in.at[place, halves_in[half], other_side],
                lifted.at[place, half],
                c_send.at[half, n],
                c_recv.at[half, n],
                partner,
            )
            for half in range(2)
        ]

    pl.semaphore_wait(ready, 1)
    hops = {}

    def hop(half, index, place, toward, array):
        copy = remote(
            slot(array, place, core, half),
            (hop_out, hop_in)[array].at[half, index],
            e_send.at[1 - array, 2 * half + index],
            e_recv.at[1 - array, 2 * half + index],
            across(toward),
        )
        copy.start()
        hops[half, index, array] = copy

    def both_cores(n, array):
        step = chips - 1 - n
        place = xor(chip, step)
        for copy in to_other_core(n, array):
            copy.wait()
        if array == 0:
            w_out[place, own_side, :] = w_out[place, own_side, :] + core_out[place]
        else:
            for half in range(2):
                here = (place, halves_in[half], own_side)
                w_in[here] = w_in[here] + lifted[place, half]
        if step == 3:
            hop(0, 1, place, 1, array)
            hop(1, 1, place, 2, array)
        elif step:
            hop(step - 1, 0, place, step, array)

    def expert_grads(array, place, at):
        for half in halves_in:
            if array == 0:
                w_out[place, at, half] = dot(acts[place, :, at], cot[:, half], TN).astype(bf16)
            else:
                w_in[place, half, at] = dot(turned[half, :], hids[place, :, at]).astype(bf16)

    def all_grads(array):
        for n in range(chips):
            place = xor(chip, chips - 1 - n)
            expert_grads(array, place, other_side)
            for copy in to_other_core(n, array):
                copy.start()
            if n:
                both_cores(n - 1, array)
            expert_grads(array, place, own_side)

    all_grads(1)
    outputs()
    both_cores(chips - 1, 1)
    to_dmr[1](0)
    all_grads(0)
    both_cores(chips - 1, 0)
    to_dmr[1](1)
    to_dmr[1](2)
    side = features // 2
    strip = side // chips
    col = lambda c, j: at_block(c * chips + j, strip)

    def section(number, first, count):
        at = pl.ds(first, count)
        state = {}

        def sem(n):
            return s_send.at[number, n], s_recv.at[number, n]

        def start():
            state["core"] = remote(
                sums.at[at, at_block(1 - core, side)], core_got.at[at, :], *sem(0), partner
            )
            state["core"].start()

        def mid():
            state["core"].wait()
            half = at_block(core, side)
            sums[at, half] = sums[at, half] + core_got[at, :]
            state["chips"] = []
            for s in range(1, chips):
                copy = remote(
                    sums.at[at, col(core, xor(chip, s))], chip_got.at[s - 1, at, :], *sem(s), across(s)
                )
                copy.start()
                state["chips"].append(copy)

        def add():
            for copy in state["chips"]:
                copy.wait()
            total = sums[at, col(core, chip)].astype(f32)
            for s in range(1, chips):
                total += chip_got[s - 1, at, :].astype(f32)
            piece[at, :] = total.astype(bf16)

        return start, mid, add

    def two_hop_section(number, first, count):
        at = pl.ds(first, count)
        half_at = [pl.ds(first + n * (count // 2), count // 2) for n in range(2)]
        begin, state = section(number, first, count)[0], {}

        def hop(half, index, place, toward, n):
            copy = remote(
                sums.at[half_at[half], col(core, place)],
                chip_got.at[index, half_at[half], :],
                t_send.at[number, n],
                t_recv.at[number, n],
                across(toward),
            )
            copy.start()
            return copy

        def mid():
            over = remote(
                sums.at[at, at_block(1 - core, side)],
                core_got.at[at, :],
                s_send.at[number, 0],
                s_recv.at[number, 0],
                partner,
            )
            over.wait()
            half = at_block(core, side)
            sums[at, half] = sums[at, half] + core_got[at, :]
            for half in range(2):
                toward = 1 + half
                state[half, 1] = hop(half, 1, xor(chip, 3), toward, 2 * half + 1)
                state[half, 0] = hop(half, 0, xor(chip, toward), toward, 2 * half)

        def second():
            for half in range(2):
                here = (half_at[half], col(core, xor(chip, 2 - half)))
                state[half, 1].wait()
                sums[here] = sums[here] + chip_got[1, half_at[half], :]
                state[half, 2] = hop(half, 2, xor(chip, 2 - half), 2 - half, 4 + half)

        def add():
            for half in range(2):
                state[half, 0].wait()
                state[half, 2].wait()
            total = sums[at, col(core, chip)].astype(f32)
            for index in (0, 2):
                total += chip_got[index, at, :].astype(f32)
            piece[at, :] = total.astype(bf16)

        return begin, mid, second, add

    def two_hop_to_plane(number, first, count):
        at = pl.ds(first, count)
        half_at = [pl.ds(first + n * (count // 2), count // 2) for n in range(2)]
        state = {}

        def send(src, rows_of, place, where, n):
            copy = remote(
                src,
                wide_ref.at[rows_of, col(core, place)],
                t_send.at[number, n],
                t_recv.at[number, n],
                where,
            )
            copy.start()
            return copy

        def start():
            for urgent in range(2):
                for bit in (1, 2):
                    half = bit - 1 if urgent == 0 else 2 - bit
                    state[bit, half] = send(
                        piece.at[half_at[half], :],
                        half_at[half],
                        chip,
                        across(bit),
                        6 + 2 * (bit - 1) + half,
                    )
            over = send(piece.at[at, :], at, chip, partner, 12)
            own = pltpu.make_async_copy(
                piece.at[at, :], wide_ref.at[at, col(core, chip)], t_send.at[number, 15]
            )
            own.start()
            state["wait"] = [over, own]

        def relay():
            for half in range(2):
                bit = 1 + half
                state[bit, half].wait_recv()
                place = xor(chip, bit)
                here = wide_ref.at[half_at[half], col(core, place)]
                state[3, half] = send(here, half_at[half], place, across(2 - half), 10 + half)

        def forward():
            for bit in (1, 2):
                state[bit, 2 - bit].wait_recv()
                place = xor(chip, bit)
                here = wide_ref.at[at, col(core, place)]
                state["wait"].append(send(here, at, place, partner, 12 + bit))

        def end():
            for half in range(2):
                state[3, half].wait_recv()
            place = xor(chip, 3)
            here = wide_ref.at[at, col(core, place)]
            state["wait"].append(send(here, at, place, partner, 16))

        def done():
            for copy in state["wait"]:
                copy.wait()
            for half in range(2):
                state[3, half].wait_send()
                for bit in (1, 2):
                    state[bit, half].wait_send()

        return start, relay, forward, end, done

    def to_plane(number, src, rows_to):
        state = {}

        def sem(n):
            return s_send.at[number, chips + n], s_recv.at[number, chips + n]

        def start():
            here = wide_ref.at[rows_to, col(core, chip)]
            state["share"] = [remote(src, here, *sem(s), across(s)) for s in range(1, chips)]
            over = remote(src, here, *sem(0), partner)
            own = pltpu.make_async_copy(src, here, s_send.at[number, 3 * chips - 1])
            state["wait"] = [over, own]
            for copy in state["share"] + state["wait"]:
                copy.start()

        def forward():
            for s in range(1, chips):
                state["share"][s - 1].wait()
                here = wide_ref.at[rows_to, col(core, xor(chip, s))]
                copy = remote(here, here, *sem(chips - 1 + s), partner)
                copy.start()
                state["wait"].append(copy)

        def end():
            for copy in state["wait"]:
                copy.wait()

        return start, forward, end

    mixed = w_o.shape[0]
    small = ceil_to(named + 1, 16)
    at_a = pl.ds(features, 16)
    at_o = pl.ds(features + 16, mixed)
    at_g = pl.ds(features + 16 + mixed, small)
    of_d = [two_hop_section(n, n * features // 2, features // 2) for n in range(2)]
    of_o = two_hop_section(2, features + 16, mixed)
    of_g = section(3, features + 16 + mixed, small)
    of_a = section(4, features, 16)
    out_d = [two_hop_to_plane(n, n * features // 2, features // 2) for n in range(2)]
    out_o = two_hop_to_plane(2, features + 16, mixed)
    out_g = to_plane(3, blocks, pl.ds(features + 16 + mixed, n_head * small))
    out_a = to_plane(4, piece.at[at_a, :], at_a)
    router_part = dot(dzs[...], mrs[...], TN)[:named]

    grad_x_ref[...] = part[own_block, :].astype(f32)
    to_dmr[2](grad_x_ref)
    incoming = grad_x_ref[...]
    mid = middle[...]
    inverse = lax.rsqrt(jnp.mean(mid * mid, axis=-1, keepdims=True) + epsilon)
    unit = mid * inverse
    scaled = incoming * expert_gain
    dmid = cot[own_block, :].astype(f32) + inverse * (
        scaled - unit * jnp.mean(scaled * unit, axis=-1, keepdims=True)
    )
    grad_x_ref[...] = dmid
    das[own_block, :] = dmid.astype(bf16)
    da_start, da_stage, da_end, _ = gather(6, das)
    da_start()
    sums[at_g, :] = jnp.concatenate(
        [
            router_part,
            jnp.sum(incoming * unit, axis=0, keepdims=True),
            jnp.zeros((small - named - 1, features), f32),
        ],
        axis=0,
    ).astype(bf16)
    of_g[0]()
    turned[...] = rows[...].T
    of_g[1]()
    lasts = {}

    def first_hop(half, index, place):
        for array in range(2):
            hops[half, index, array].wait()
        at_in = (place, halves_in[half], own_side)
        at_out = (place, halves_out(core)[half], slice(None))
        w_in[at_in] = w_in[at_in] + hop_in[half, index]
        w_out[at_out] = w_out[at_out] + hop_out[half, index]

    for half in range(2):
        toward = 2 - half
        place = xor(chip, toward)
        first_hop(half, 1, place)
        pl.semaphore_signal(free.at[half], inc=1, device_id=across(toward), device_id_type=MESH)
        pl.semaphore_wait(free.at[half], 1)
        lasts[half] = (
            remote(
                slot(1, place, core, half),
                hop_in.at[half, 1],
                e_send.at[0, 4 + half],
                e_recv.at[0, 4 + half],
                across(toward),
            ),
            remote(
                slot(0, place, core, half),
                hop_out.at[half, 1],
                e_send.at[1, 4 + half],
                e_recv.at[1, 4 + half],
                across(toward),
            ),
        )
        for copy in lasts[half]:
            copy.start()
    lane = lax.broadcasted_iota(jnp.int32, (tokens, width), 1)

    def through_output(block):
        at = at_block(block, tokens)
        all_five = dot(das[at, :], w_o[...], NT)
        attended = att[at, :]
        total = jnp.zeros((tokens, width), f32)
        gate = jnp.zeros((tokens, width), f32)
        for e in range(experts):
            one = all_five[:, e * width : (e + 1) * width]
            total += gates[at, experts + e : experts + e + 1] * one
            gate = jnp.where(
                lane == experts + e, jnp.sum(one * attended, axis=-1, keepdims=True), gate
            )
        datt[at, :] = total.astype(bf16)
        gate_grads[at, :] = gate

    through_output(h)
    to_out = chain_sum(7, outs, got_out)
    for step in (1, 2, 3):
        da_stage(step)
        if step == 1:
            for number in range(last):
                to_out[0](number)
        through_output(arrival[step - 1])

    for e in range(experts):
        one = (gates[:, experts + e : experts + e + 1] * att[...]).astype(bf16)
        sums[pl.ds(features + 16 + e * width, width), :] = dot(one, das[...], TN).astype(bf16)
    of_o[0]()

    @pl.loop(0, n_head)
    def _(block):
        at = at_block(block, tokens)
        chance = probs[at, :].astype(f32)
        dprob = dot(datt[at, :], v[...], NT)
        centre = jnp.sum(chance * dprob, axis=-1, keepdims=True)
        scores[at, :] = (chance * (dprob - centre)).astype(bf16)

    dq = dot(scores[...], k[...]) * scale
    dk = dot(scores[...], q[...], TN) * scale
    dv = dot(probs[...], datt[...], TN)
    of_o[1]()
    c, s = turns(slice(None))
    qkz[:, pl.ds(0, width)] = (dq * c - swap_halves(dq) * s).astype(bf16)
    qkz[:, pl.ds(width, width)] = (dk * c - swap_halves(dk) * s).astype(bf16)
    gate = gate_grads[...]
    lane = lax.broadcasted_iota(jnp.int32, (group, width), 1)
    for e in range(experts):
        vgrads[:, pl.ds(e * width, width)] = (gates[:, e : e + 1] * dv).astype(bf16)
        one = jnp.sum(vx[:, pl.ds(e * width, width)].astype(f32) * dv, axis=-1, keepdims=True)
        gate = jnp.where(lane == e, one, gate)
    qkz[:, pl.ds(2 * width, width)] = (gate * gates[...] * (1.0 - gates[...])).astype(bf16)

    scaled_qkz = (qkz[...].astype(f32) * gates[:, width - 1 : width]).astype(bf16)

    def matrix_rows(c):
        at = at_block(c, column)
        sums[at, pl.ds(0, 3 * width)] = dot(turned[at, :], scaled_qkz).astype(bf16)
        sums[at, pl.ds(3 * width, experts * width)] = dot(turned[at, :], vgrads[...]).astype(bf16)

    steps_each = features // column // 2
    for n in range(2):
        pl.loop(n * steps_each, (n + 1) * steps_each)(matrix_rows)
        of_d[n][0]()
    def into_rows(block):
        at = at_block(block, tokens)
        inverse = gates[at, width - 1 : width]
        unit = rows[at, :].astype(f32) * inverse
        through = dot(qkz[at, :], w_an[...], NT)
        scaled = through * attend_gain
        total = inverse * (
            scaled - unit * jnp.mean(scaled * unit, axis=-1, keepdims=True)
        ) + dot(vgrads[at, :], w_v[...], NT)
        return total, jnp.sum(through * unit, axis=0, keepdims=True)

    to_x = chain_sum(8, part, got)
    gain = jnp.zeros((1, features), f32)
    for number in range(last):
        total, one = into_rows(leaving[number])
        gain += one
        part[at_block(leaving[number], tokens), :] = total.astype(bf16)
        to_x[0](number)
        if number < 2:
            of_d[number][1]()
    total, one = into_rows(h)
    sums[at_a, :] = jnp.broadcast_to(gain + one, (16, features)).astype(bf16)
    of_a[0]()
    grad_x_ref[...] += total
    to_out[1](0)
    to_out[1](1)
    of_a[1]()
    of_o[2]()
    to_x[1](0)
    of_d[0][2]()
    of_d[1][2]()
    of_g[2]()
    small_block = at_block(h, small)
    blocks[small_block, :] = piece[at_g, :]
    g_copies = spread(9, lambda s: blocks.at[small_block, :], lambda s: blocks.at[small_block, :])
    to_x[1](1)
    of_o[3]()
    out_o[0]()
    to_x[1](2)
    of_d[0][3]()
    out_d[0][0]()
    of_d[1][3]()
    out_d[1][0]()
    of_a[2]()
    gain_part[...] = piece[at_a, :]
    gain_copies = spread(10, lambda s: gain_part, lambda s: gain_got.at[s - 1])
    to_out[1](2)
    out_o[1]()
    for step in peers:
        g_copies[step].wait()
    out_g[0]()
    out_d[0][1]()
    gain = gain_part[...].astype(f32)
    for step in peers:
        gain_copies[step].wait()
        gain += gain_got[step - 1].astype(f32)
    piece[at_a, :] = gain.astype(bf16)
    out_a[0]()
    out_d[1][1]()
    out_o[2]()
    to_x[2](grad_x_ref)
    output_ref[...] = middle[...] + outs[own_block, :].astype(f32)
    to_out[2](output_ref)
    for half in range(2):
        first_hop(half, 0, chip)
        for copy in lasts[half]:
            copy.wait()
        at_in = (chip, halves_in[half], own_side)
        at_out = (chip, halves_out(core)[half], slice(None))
        w_in[at_in] = w_in[at_in] + hop_in[half, 1]
        w_out[at_out] = w_out[at_out] + hop_out[half, 1]
    stores = (
        pltpu.make_async_copy(w_in.at[chip, :, own_side], fin_in_ref, local_sem.at[0]),
        pltpu.make_async_copy(w_out.at[chip, own_side, :], fin_out_ref, local_sem.at[1]),
    )
    for store in stores:
        store.start()
    out_o[3]()
    out_d[0][2]()
    out_g[1]()
    out_a[1]()
    out_d[1][2]()
    out_d[0][3]()
    out_d[1][3]()
    for one in (out_o, out_d[0], out_g, out_a, out_d[1]):
        one[-1]()
    for store in stores:
        store.wait()
    mr_end()
    da_end()


def layer_call(n_dp, n_head, args):
    x, picks, router, value_mat, expert_in = args[0], args[2], args[13], args[11], args[14]
    tokens, features = x.shape
    per_device, _, width = expert_in.shape
    held_experts = value_mat.shape[1]
    group = tokens * n_head
    chips = n_dp // 2
    slab = per_device * width
    lanes = 128
    peers = n_head - 1
    named = ceil_to(n_dp * per_device, 8)
    small = ceil_to(named + 1, 16)
    top = features + held_experts
    held = top + 16 + small
    strip = features // n_dp
    shape = jax.ShapeDtypeStruct
    vm, dma = pltpu.VMEM, pltpu.SemaphoreType.DMA
    outs = [
        (shape((tokens, features), f32), VM),
        (shape((tokens, features), f32), VM),
        (shape((top + 16 + n_head * small, features), bf16), ANY),
        (shape((features, slab), bf16), ANY),
        (shape((slab, features), bf16), ANY),
    ]
    scratch = dict(
        picks=vm(picks.shape, jnp.int32),
        two_picks=vm((2, *args[3].shape), jnp.int32),
        head_picks=vm((group, lanes), jnp.int32),
        w_g=vm(args[10].shape, bf16),
        w_r=vm(router.shape, bf16),
        seg=vm((1, group), jnp.int32),
        gains=vm(args[6].shape, f32),
        angles=vm((group, width), f32),
        w_an=vm((features, 3 * width), bf16),
        w_v=vm((features, held_experts), bf16),
        w_o=vm((held_experts, features), bf16),
        my_router=vm((features, lanes), bf16),
        w_in=vm((chips, features, 2 * slab), bf16),
        w_out=vm((chips, 2 * slab, features), bf16),
        rows=vm((group, features), bf16),
        cot=vm((group, features), bf16),
        mrs=vm((group, features), bf16),
        das=vm((group, features), bf16),
        turned=vm((features, group), bf16),
        my_mask=vm((n_head, tokens, lanes), bf16),
        all_mask=vm((group, lanes), bf16),
        gates=vm((group, width), f32),
        q=vm((group, width), bf16),
        k=vm((group, width), bf16),
        v=vm((group, width), bf16),
        vx=vm((group, held_experts), bf16),
        att=vm((group, width), f32),
        part=vm((group, features), bf16),
        got=vm((2 * peers, tokens, features), bf16),
        outs=vm((group, features), bf16),
        got_out=vm((2 * peers, tokens, features), bf16),
        lifted=vm((chips, 2, group, slab), bf16),
        core_out=vm((chips, slab, features), bf16),
        acts=vm((chips, group, 2 * slab), bf16),
        hids=vm((chips, group, 2 * slab), bf16),
        dzs=vm((group, lanes), bf16),
        datt=vm((group, width), bf16),
        gate_grads=vm((group, width), f32),
        probs=vm((group, group), bf16),
        scores=vm((group, group), bf16),
        qkz=vm((group, 3 * width), bf16),
        vgrads=vm((group, held_experts), bf16),
        gain_part=vm((16, strip), bf16),
        gain_got=vm((peers, 16, strip), bf16),
        sums=vm((held, features), bf16),
        core_got=vm((held, features // 2), bf16),
        chip_got=vm((chips - 1, held, strip), bf16),
        piece=vm((held, strip), bf16),
        blocks=vm((n_head * small, strip), bf16),
        hop_in=vm((2, 2, features // 2, slab), bf16),
        hop_out=vm((2, 2, slab // 2, features), bf16),
        local_sem=dma((16 + 1 + per_device,)),
        z_send=dma((11, 4 * peers)),
        z_recv=dma((11, 4 * peers)),
        w_send=dma((22,)),
        w_recv=dma((22,)),
        c_send=dma((3, chips)),
        c_recv=dma((3, chips)),
        e_send=dma((2, 6)),
        e_recv=dma((2, 6)),
        s_send=dma((5, 3 * chips)),
        s_recv=dma((5, 3 * chips)),
        t_send=dma((3, 17)),
        t_recv=dma((3, 17)),
        ready=pltpu.SemaphoreType.REGULAR,
        free=pltpu.SemaphoreType.REGULAR((2,)),
    )
    return pl.pallas_call(
        functools.partial(layer_kernel, n_dp, n_head),
        out_shape=[o[0] for o in outs],
        out_specs=[o[1] for o in outs],
        in_specs=[ANY] * 16,
        scratch_shapes=list(scratch.values()),
        compiler_params=pltpu.CompilerParams(
            collective_id=1, has_side_effects=True, vmem_limit_bytes=vmem_bytes
        ),
    )(*args)


def finish_kernel(
    n_dp,
    n_head,
    output_ref,
    grad_x_ref,
    wide_ref,
    in_ref,
    out_ref,
    gain_ref,
    final_ref,
    input_ref,
    attend_ref,
    query_ref,
    key_ref,
    value_ref,
    mix_ref,
    gate_ref,
    expert_ref,
    router_ref,
    grad_in_ref,
    grad_out_ref,
    wide,
    flat_in,
    flat_out,
    value,
    mix,
    grad_in,
    grad_out,
    output,
    grad_x,
    query,
    key,
    sem,
):
    features, slab = in_ref.shape
    per_device, _, width = grad_in_ref.shape
    experts_total, gates = router_ref.shape[0], gate_ref.shape[0]
    mixed = mix_ref.shape[0]
    top = features + 16 + mixed
    small = (wide_ref.shape[0] - top) // n_head
    named = n_dp * per_device

    numbers = iter(range(sem.shape[0]))

    def copy(src, dst):
        one = pltpu.make_async_copy(src, dst, sem.at[next(numbers)])
        one.start()
        return one

    bands = 4
    band = features // bands
    load = lambda first, count: copy(
        wide_ref.at[pl.ds(first, count), :], wide.at[pl.ds(first, count), :]
    )
    plain = [(copy(output_ref, output), output, final_ref), (copy(grad_x_ref, grad_x), grad_x, input_ref)]
    for_out, for_in = copy(out_ref, flat_out), copy(in_ref, flat_in)
    for_bands = [load(n * band, band) for n in range(bands)]
    for_mix = [load(features + 16 + n * mixed // 2, mixed // 2) for n in range(2)]
    others = [load(features, 16), load(top, n_head * small)]
    stores = []
    gain = jnp.broadcast_to(gain_ref[0:1, :], (width, features)).T
    for loaded, held, result in plain:
        loaded.wait()
        stores.append(copy(held, result))
    for_out.wait()
    for e in range(per_device):
        grad_out[e] = flat_out[pl.ds(e * width, width), :].astype(f32)
        stores.append(copy(grad_out.at[e], grad_out_ref.at[e]))
    for_in.wait()
    for e in range(per_device):
        grad_in[e] = flat_in[:, pl.ds(e * width, width)].astype(f32)
        stores.append(copy(grad_in.at[e], grad_in_ref.at[e]))
    for n in range(bands):
        for_bands[n].wait()
        at = pl.ds(n * band, band)
        scale = gain[n * band : (n + 1) * band]
        value[at, :] = wide[at, pl.ds(3 * width, value.shape[1])].astype(f32)
        stores.append(copy(value.at[at, :], value_ref.at[at, :]))
        query[at, :] = wide[at, pl.ds(0, width)].astype(f32) * scale
        stores.append(copy(query.at[at, :], query_ref.at[at, :]))
        key[at, :] = wide[at, pl.ds(width, width)].astype(f32) * scale
        stores.append(copy(key.at[at, :], key_ref.at[at, :]))
    for n in range(2):
        for_mix[n].wait()
        at = pl.ds(n * mixed // 2, mixed // 2)
        mix[at, :] = wide[pl.ds(features + 16 + n * mixed // 2, mixed // 2), :].astype(f32)
        stores.append(copy(mix.at[at, :], mix_ref.at[at, :]))
    turned = (wide[pl.ds(0, features), pl.ds(2 * width, width)].astype(f32) * gain).T
    for e in range(gates):
        gate_ref[e] = turned[e : e + 1]
    for loaded in others:
        loaded.wait()
    attend_ref[...] = wide[pl.ds(features, 16), :][0:1].astype(f32)
    planes = wide[pl.ds(top, n_head * small), :]
    place = lax.broadcasted_iota(jnp.int32, (n_head * small, experts_total), 0)
    name = lax.broadcasted_iota(jnp.int32, (n_head * small, experts_total), 1)
    slot, plane = place % small, place // small
    expert = (slot // per_device * n_head + plane) * per_device + slot % per_device
    chosen = (slot < named) & (expert == name)
    router_ref[...] = dot(jnp.where(chosen, 1.0, 0.0).astype(bf16), planes, TN)
    gain = jnp.zeros((1, features), f32)
    for z in range(n_head):
        row = z * small + ceil_to(named, 8)
        gain += planes[row : row + 1].astype(f32)
    expert_ref[...] = gain
    for store in stores:
        store.wait()


def finish_call(n_dp, n_head, shapes, args):
    shape = jax.ShapeDtypeStruct
    wide, flat_in, flat_out = args[2], args[3], args[4]
    value, mix, grad_in, grad_out = shapes[5], shapes[6], shapes[10], shapes[11]
    specs = [VM] * 12
    for number in (0, 1, 3, 4, 5, 6, 10, 11):
        specs[number] = ANY
    return pl.pallas_call(
        functools.partial(finish_kernel, n_dp, n_head),
        out_shape=[shape(s, f32) for s in shapes],
        out_specs=specs,
        in_specs=[ANY] * 5 + [VM],
        scratch_shapes=[
            pltpu.VMEM(wide.shape, bf16),
            pltpu.VMEM(flat_in.shape, bf16),
            pltpu.VMEM(flat_out.shape, bf16),
            pltpu.VMEM(value, f32),
            pltpu.VMEM(mix, f32),
            pltpu.VMEM(grad_in, f32),
            pltpu.VMEM(grad_out, f32),
            pltpu.VMEM(shapes[0], f32),
            pltpu.VMEM(shapes[1], f32),
            pltpu.VMEM(shapes[3], f32),
            pltpu.VMEM(shapes[4], f32),
            pltpu.SemaphoreType.DMA((40,)),
        ],
        compiler_params=pltpu.CompilerParams(vmem_limit_bytes=60 << 20),
    )(*args)


def kernel_body(
    n_dp,
    n_head,
    hidden_in,
    segments,
    value_pick,
    output_pick,
    expert_pick,
    attend_gain,
    query_weight,
    key_weight,
    value_weight,
    output_weight,
    head_router,
    expert_gain,
    router,
    expert_in,
    expert_out,
    cotangent,
):
    tokens, features = hidden_in.shape
    per_device, _, width = expert_in.shape
    experts = head_router.shape[2] // 2
    group = tokens * n_head
    angles = np.arange(group)[:, None] * theta ** (-2.0 * np.arange(width // 2) / width)[None, :]
    angles = np.concatenate([np.cos(angles), np.sin(angles)], axis=1).astype(np.float32)
    first = np.arange(2)[:, None] == 0
    gains = jnp.where(first, attend_gain[None, :], expert_gain[None, :]).astype(f32)
    results = layer_call(
        n_dp,
        n_head,
        (
            hidden_in,
            cotangent,
            expert_pick.T,
            value_pick.transpose(1, 2, 0)[0],
            output_pick.transpose(1, 2, 0)[0],
            segments[None, :],
            gains,
            angles,
            query_weight[0],
            key_weight[0],
            head_router.transpose(0, 2, 1)[0],
            value_weight[0],
            output_weight[0],
            router.T,
            expert_in,
            expert_out.reshape(per_device * width, features),
        ),
    )
    shapes = (
        (tokens, features),
        (tokens, features),
        (1, features),
        query_weight.shape[1:],
        key_weight.shape[1:],
        value_weight.shape[1:],
        output_weight.shape[1:],
        (2 * experts, 1, features),
        (1, features),
        (router.shape[1], features),
        expert_in.shape,
        expert_out.shape,
    )
    done = list(finish_call(n_dp, n_head, shapes, (*results, gains)))
    for number in (3, 4, 5, 6):
        done[number] = done[number][None]
    done[7] = done[7].transpose(1, 2, 0)
    done[9] = done[9].T
    done[2], done[8] = done[2][0], done[8][0]
    return tuple(done)


def solution(mesh):
    rows = P(everywhere, None)
    heads = P("head", None, None)
    experts = P(everywhere, None, None)
    picks = P("dp", "head", None)
    in_specs = (
        rows, P("dp"), picks, picks, rows, P(), heads, heads, heads, heads, heads,
        P(), P(), experts, experts, rows,
    )
    out_specs = (
        rows, rows, P(), heads, heads, heads, heads, heads, P(), P(), experts, experts,
    )
    n_dp, n_head = mesh.shape["dp"], mesh.shape["head"]

    def program(*args):
        held = 2 * n_dp * args[13].shape[0] * args[13].shape[1] * args[13].shape[2] * 2
        if n_head == 4 and held <= vmem_for_weights:
            return kernel_body(n_dp, n_head, *args)
        return body(*args)

    return jax.shard_map(program, mesh=mesh, in_specs=in_specs, out_specs=out_specs, check_vma=False)
```

```python
import functools

import jax
import jax.numpy as jnp
import numpy as np
from jax import lax
from jax.experimental import pallas as pl
from jax.experimental.pallas import tpu as pltpu
from jax.sharding import PartitionSpec as P

epsilon = 1e-06
theta = 10000.0
negative = -1e30
f32 = jnp.float32
bf16 = jnp.bfloat16
everywhere = ("dp", "head")
whole_rows = 4096
vmem_for_weights = 16 << 20
vmem_bytes = 63 << 20


def product(left, right, left_axis, right_axis):
    return lax.dot_general(
        left, right, (((left_axis,), (right_axis,)), ((), ())), preferred_element_type=f32
    )


def rms_scale(residual):
    return lax.rsqrt(jnp.mean(residual * residual, axis=-1, keepdims=True) + epsilon)


def rotary_tables(row_count, head_width):
    half_width = head_width // 2
    position = jnp.arange(row_count, dtype=f32)[:, None]
    exponent = jnp.arange(half_width, dtype=f32)[None, :]
    angles = position * jnp.power(theta, -2.0 * exponent / head_width)
    return (jnp.cos(angles), jnp.sin(angles))


def rotate(matrix, cosine, sine):
    half = matrix.shape[-1] // 2
    first, second = matrix[:, :half], matrix[:, half:]
    return jnp.concatenate([first * cosine - second * sine, second * cosine + first * sine], axis=-1)


def pick_mask(picks, expert_count):
    hits = picks[:, 0, :, None] == jnp.arange(expert_count, dtype=jnp.int32)[None, None, :]
    return jnp.any(hits, axis=1).astype(f32)


def norm_back(residual, inverse, gain, incoming):
    unit_rows = residual * inverse
    scaled = incoming * gain
    gain_grad = jnp.sum(incoming * unit_rows, axis=0)
    row_grad = inverse * (scaled - unit_rows * jnp.mean(scaled * unit_rows, axis=-1, keepdims=True))
    return (row_grad, gain_grad)


def gelu_pair(value):
    inner = jnp.tanh(0.7978845608028654 * (value + 0.044715 * value * value * value))
    slope = 0.5 * (1.0 + inner) + 0.5 * value * (1.0 - inner * inner) * 0.7978845608028654 * (
        1.0 + 3.0 * 0.044715 * value * value
    )
    return (0.5 * value * (1.0 + inner), slope)


def body(
    hidden_in,
    segments,
    value_pick,
    output_pick,
    expert_pick,
    attend_gain,
    query_weight,
    key_weight,
    value_weight,
    output_weight,
    head_router,
    expert_gain,
    router,
    expert_in,
    expert_out,
    cotangent,
):
    tokens, features = hidden_in.shape
    per_device, _, width = expert_in.shape
    head_experts = head_router.shape[2] // 2
    head_width = query_weight.shape[2]
    scale = head_width ** (-0.5)
    query_mat, key_mat, value_mat = query_weight[0], key_weight[0], value_weight[0]
    output_mat, gate_mat = output_weight[0], head_router[0]
    value_mask = pick_mask(value_pick, head_experts)
    output_mask = pick_mask(output_pick, head_experts)
    attend_scale = attend_gain.astype(f32)
    expert_scale = expert_gain.astype(f32)
    me = lax.axis_index("dp") * lax.axis_size("head") + lax.axis_index("head")

    rows = lax.all_gather(hidden_in, "head", axis=0, tiled=True)
    grouped = rows.astype(f32)
    group = grouped.shape[0]
    inverse = rms_scale(grouped)
    normed = (grouped * inverse * attend_scale).astype(bf16)
    cosine, sine = rotary_tables(group, head_width)
    queries = rotate(product(normed, query_mat, 1, 0), cosine, sine).astype(bf16)
    key_rows = rotate(product(normed, key_mat, 1, 0), cosine, sine).astype(bf16)
    squash = jax.nn.sigmoid(product(normed, gate_mat, 1, 0))
    value_gates = squash[:, :head_experts] * value_mask
    output_gates = squash[:, head_experts:] * output_mask
    expert_values = product(rows, value_mat, 1, 0).reshape(group, head_experts, head_width)
    values = jnp.sum(expert_values * value_gates[:, :, None], axis=1).astype(bf16)
    places = jnp.arange(group, dtype=jnp.int32)
    allowed = (places[None, :] <= places[:, None]) & (segments[:, None] == segments[None, :])
    scores = jnp.where(allowed, product(queries, key_rows, 1, 1) * scale, negative)
    exponents = jnp.exp(scores - jnp.max(scores, axis=-1, keepdims=True))
    probabilities = exponents / jnp.sum(exponents, axis=-1, keepdims=True)
    attended = product(probabilities.astype(bf16), values, 1, 0)
    weighted = (
        (output_gates[:, :, None] * attended[:, None, :]).reshape(group, -1).astype(bf16)
    )
    middle = hidden_in.astype(f32) + lax.psum_scatter(
        product(weighted, output_mat, 1, 0).astype(bf16), "head", scatter_dimension=0, tiled=True
    ).astype(f32)
    middle_inverse = rms_scale(middle)
    middle_normed = (middle * middle_inverse * expert_scale).astype(bf16)
    mine = me * per_device + jnp.arange(per_device, dtype=jnp.int32)
    my_router = lax.dynamic_slice_in_dim(router, me * per_device, per_device, axis=1)
    in_mat = expert_in.transpose(1, 0, 2).reshape(features, per_device * width)
    out_mat = expert_out.reshape(per_device * width, features)

    def turn(running, own):
        own_rows, own_cot, own_picks = own
        all_cot = lax.all_gather(own_cot, everywhere, axis=0, tiled=True)
        all_picks = lax.all_gather(own_picks, everywhere, axis=0, tiled=True)
        all_rows = lax.all_gather(own_rows, everywhere, axis=0, tiled=True)
        mask = jnp.any(all_picks[:, :, None] == mine[None, None, :], axis=1).astype(f32)
        gates = jax.nn.sigmoid(product(all_rows, my_router, 1, 0))
        live = gates * mask
        act, slope = gelu_pair(product(all_rows, in_mat, 1, 0).reshape(-1, per_device, width))
        lifted = product(all_cot, out_mat, 1, 1).reshape(-1, per_device, width)
        dense_grad = (jnp.sum(act * lifted, axis=-1) * live * (1.0 - gates)).astype(bf16)
        act_live = (act * live[:, :, None]).astype(bf16).reshape(-1, per_device * width)
        hidden_grad = (slope * lifted * live[:, :, None]).astype(bf16)
        hidden_grad = hidden_grad.reshape(-1, per_device * width)
        part_out = product(act_live, out_mat, 1, 0).astype(bf16)
        part_grad = (
            product(hidden_grad, in_mat, 1, 1) + product(dense_grad, my_router, 1, 1)
        ).astype(bf16)
        back = lax.psum_scatter(part_grad, everywhere, scatter_dimension=0, tiled=True)
        forth = lax.psum_scatter(part_out, everywhere, scatter_dimension=0, tiled=True)
        grads = (
            product(all_rows, hidden_grad, 0, 0),
            product(act_live, all_cot, 0, 0),
            product(dense_grad, all_rows, 0, 0),
        )
        if running is not None:
            grads = jax.tree.map(jnp.add, running, grads)
        return grads, (forth, back)

    turns = max(1, lax.axis_size("dp") * lax.axis_size("head") * tokens // whole_rows)
    owned = (middle_normed, cotangent, expert_pick)
    if turns == 1:
        grads, (summed, normed_grad) = turn(None, owned)
    else:
        owned = jax.tree.map(lambda a: a.reshape(turns, -1, a.shape[1]), owned)
        zeros = (
            jnp.zeros(in_mat.shape, f32),
            jnp.zeros(out_mat.shape, f32),
            jnp.zeros((per_device, features), f32),
        )
        grads, sums = lax.scan(turn, zeros, owned)
        summed, normed_grad = (a.reshape(tokens, features) for a in sums)
    grad_in = grads[0].reshape(features, per_device, width).transpose(1, 0, 2)
    grad_out = grads[1].reshape(per_device, width, features)
    grad_router = lax.all_gather(grads[2], everywhere, axis=0, tiled=True).T
    output = middle + summed.astype(f32)
    incoming = cotangent.astype(f32)
    row_grad, grad_gain_expert = norm_back(
        middle, middle_inverse, expert_scale, normed_grad.astype(f32)
    )
    middle_grad = incoming + row_grad
    group_grads = lax.all_gather(middle_grad.astype(bf16), "head", axis=0, tiled=True)
    weighted_grad = product(group_grads, output_mat, 1, 1).reshape(group, head_experts, head_width)
    output_grad = product(weighted, group_grads, 0, 0)
    output_gate_grad = jnp.sum(weighted_grad * attended[:, None, :], axis=-1)
    attended_grad = jnp.sum(weighted_grad * output_gates[:, :, None], axis=1).astype(bf16)
    prob_grad = product(attended_grad, values, 1, 1)
    centre = jnp.sum(probabilities * prob_grad, axis=-1, keepdims=True)
    score_grad = (probabilities * (prob_grad - centre)).astype(bf16)
    query_grad = product(score_grad, key_rows, 1, 0) * scale
    key_grad = product(score_grad, queries, 0, 0) * scale
    values_grad = product(probabilities.astype(bf16), attended_grad, 0, 0)
    expert_grad = (value_gates[:, :, None] * values_grad[:, None, :]).reshape(group, -1).astype(bf16)
    value_gate_grad = jnp.sum(expert_values * values_grad[:, None, :], axis=-1)
    query_grad = rotate(query_grad, cosine, -sine).astype(bf16)
    key_grad = rotate(key_grad, cosine, -sine).astype(bf16)
    logit_grad = (
        jnp.concatenate([value_gate_grad * value_mask, output_gate_grad * output_mask], axis=1)
        * squash
        * (1.0 - squash)
    ).astype(bf16)
    head_grads = (
        product(normed, query_grad, 0, 0),
        product(normed, key_grad, 0, 0),
        product(rows, expert_grad, 0, 0),
        output_grad,
        product(normed, logit_grad, 0, 0),
    )
    head_grads = tuple(grad.astype(bf16) for grad in head_grads)
    head_grads = tuple(grad.astype(f32)[None] for grad in lax.psum(head_grads, "dp"))
    back = (
        product(query_grad, query_mat, 1, 1)
        + product(key_grad, key_mat, 1, 1)
        + product(logit_grad, gate_mat, 1, 1)
    )
    row_back, grad_attend = norm_back(grouped, inverse, attend_scale, back)
    partial = (row_back + product(expert_grad, value_mat, 1, 1)).astype(bf16)
    input_grad = middle_grad + lax.psum_scatter(
        partial, "head", scatter_dimension=0, tiled=True
    ).astype(f32)
    grad_attend, grad_gain_expert = lax.psum((grad_attend, grad_gain_expert), everywhere)
    return (
        output,
        input_grad,
        grad_attend,
        *head_grads,
        grad_gain_expert,
        grad_router,
        grad_in,
        grad_out,
    )


MESH = pl.DeviceIdType.MESH
VM = pl.BlockSpec(memory_space=pltpu.VMEM)
ANY = pl.BlockSpec(memory_space=pl.ANY)
NN = (((1,), (0,)), ((), ()))
NT = (((1,), (1,)), ((), ()))
TN = (((0,), (0,)), ((), ()))


def dot(left, right, dims=NN):
    return lax.dot_general(left, right, dims, preferred_element_type=f32)


def at_block(block, count):
    return pl.ds(pl.multiple_of(block * count, count), count)


def remote(src, dst, send, recv, where):
    return pltpu.make_async_remote_copy(
        src_ref=src, dst_ref=dst, send_sem=send, recv_sem=recv, device_id=where, device_id_type=MESH
    )


def swap_halves(value):
    half = value.shape[-1] // 2
    return jnp.concatenate([value[:, half:], value[:, :half]], axis=-1)


def ceil_to(number, step):
    return -(-number // step) * step


def one_row(stack):
    full = stack.astype(f32)
    return jnp.concatenate([full[n : n + 1] for n in range(full.shape[0])], axis=1)


def layer_kernel(
    n_dp,
    n_head,
    x_ref,
    cot_ref,
    pick_ref,
    value_pick_ref,
    output_pick_ref,
    seg_ref,
    gain_ref,
    expert_gain_ref,
    angle_ref,
    wq_ref,
    wk_ref,
    wg_ref,
    wv_ref,
    wo_ref,
    router_ref,
    in_ref,
    out_ref,
    final_ref,
    final_x_ref,
    wide_ref,
    fin_in_ref,
    fin_out_ref,
    output_ref,
    grad_x_ref,
    picks,
    two_picks,
    w_r,
    seg,
    angles,
    w_an,
    w_v,
    w_o,
    my_router,
    w_in,
    w_out,
    rows,
    cot,
    mrs,
    das,
    turned,
    my_mask,
    all_mask,
    gates,
    q,
    k,
    v,
    vx,
    att,
    part,
    got,
    outs,
    got_out,
    lifted,
    core_out,
    acts,
    hids,
    dzs,
    datt,
    gate_grads,
    probs,
    qkz,
    vgrads,
    gain_part,
    gain_got,
    sums,
    core_got,
    chip_got,
    piece,
    blocks,
    hop_in,
    hop_out,
    local_sem,
    z_send,
    z_recv,
    w_send,
    w_recv,
    c_send,
    c_recv,
    e_send,
    e_recv,
    s_send,
    s_recv,
    t_send,
    t_recv,
    ready,
    free,
):
    middle = output_ref
    xor = jnp.bitwise_xor
    d, h = lax.axis_index("dp"), lax.axis_index("head")
    chip, core = d // 2, d % 2
    chips = n_dp // 2
    tokens, features = x_ref.shape
    per_device, _, width = in_ref.shape
    slab = per_device * width
    wide = 2 * slab
    experts = wv_ref.shape[1] // width
    named = ceil_to(n_dp * per_device, 8)
    group = tokens * n_head
    pair = 2 * tokens
    column = 256
    lanes = 128
    scale = width ** (-0.5)
    peers = (2, 3, 1)
    partner = (chip * 2 + 1 - core, h)
    own_block = at_block(h, tokens)
    own_side, other_side = at_block(core, slab), at_block(1 - core, slab)
    halves_in = (pl.ds(0, features // 2), pl.ds(features // 2, features // 2))
    halves_out = lambda side: (
        at_block(2 * side, slab // 2),
        at_block(2 * side + 1, slab // 2),
    )

    def along(step):
        return (d, xor(h, step))

    def across(step):
        return (xor(chip, step) * 2 + core, h)

    loads = []

    def load(src, dst):
        copy = pltpu.make_async_copy(src, dst, local_sem.at[len(loads)])
        copy.start()
        loads.append(copy)
        return copy

    own_weights = [load(out_ref, w_out.at[chip, own_side, :])] + [
        load(in_ref.at[e], w_in.at[chip, :, at_block(core * per_device + e, width)])
        for e in range(per_device)
    ]
    for_rows = [
        load(x_ref, rows.at[own_block, :]),
        load(wq_ref, w_an.at[:, pl.ds(0, width)]),
        load(wk_ref, w_an.at[:, pl.ds(width, width)]),
        load(wv_ref, w_v),
        load(value_pick_ref, two_picks.at[0]),
        load(output_pick_ref, two_picks.at[1]),
        load(angle_ref, angles),
    ]
    for_scores = [load(seg_ref, seg), load(wo_ref, w_o)]
    for_mask = load(pick_ref, picks)
    for_cot = load(cot_ref, cot.at[own_block, :])
    for_router = load(router_ref, w_r)

    barrier = pltpu.get_barrier_semaphore()
    friends = [along(s) for s in peers] + [partner] + [across(s) for s in range(1, chips)]
    for friend in friends:
        pl.semaphore_signal(barrier, inc=1, device_id=friend, device_id_type=MESH)
    pl.semaphore_wait(barrier, len(friends))

    right, left = (d, jnp.minimum(h + 1, n_head - 1)), (d, jnp.maximum(h - 1, 0))
    last = n_head - 1

    def pick(*by_place):
        value = jnp.int32(by_place[-1])
        for place in range(n_head - 2, -1, -1):
            value = jnp.where(h == place, by_place[place], value)
        return value

    arrival = (xor(h, 1), pick(2, 2, 1, 1), pick(3, 3, 0, 0))
    leaving = (pick(3, 3, 0, 0), pick(2, 0, 3, 1), pick(1, 2, 1, 2))

    def gather(kind, buffer):
        def go(side, step):
            sign = 1 - 2 * side
            block = jnp.clip(h - sign * step, 0, last)
            where = (d, jnp.clip(h + sign, 0, last))
            copies = []
            for half in range(2):
                here = buffer.at[at_block(2 * block + half, tokens // 2), :]
                number = (side * last + step) * 2 + half
                copies.append(
                    remote(here, here, z_send.at[kind, number], z_recv.at[kind, number], where)
                )
            return copies

        def begin(side):
            for copy in go(side, 0):
                copy.start()

        def start():
            pl.when(h < last)(lambda: begin(0))
            pl.when(h > 0)(lambda: begin(1))

        def arrive(side, step, there, onward):
            for half in range(2):

                @pl.when(there)
                def _():
                    go(side, step - 1)[half].wait_recv()
                    if onward:
                        go(side, step)[half].start()

        def stage(step, which="all"):
            nearer = jnp.where(2 * h < n_head, 0, 1)
            ways = []
            for side in (nearer, 1 - nearer):
                there = jnp.where(side == 0, h >= step, h + step <= last)
                ways.append((side, there, jnp.where(side == 0, h < last, h > 0)))
            for number, (side, there, onward) in enumerate(ways):
                if step < last and which in ("all", "duty", ("near", "far")[number]):
                    arrive(side, step, there & onward, True)
            for side, there, onward in ways:
                if which in ("all", "rest"):
                    ends_here = there if step == last else there & jnp.logical_not(onward)
                    arrive(side, step, ends_here, False)

        def follow(step):
            pl.when((h < last) & (jnp.maximum(h, 1) == step))(lambda: begin(0))
            pl.when((h > 0) & (jnp.maximum(last - h, 1) == step))(lambda: begin(1))

        def end():
            for step in range(last):
                for side, sent in (
                    (0, (h >= step) & (h < last)),
                    (1, (h + step <= last) & (h > 0)),
                ):

                    @pl.when(sent)
                    def _():
                        for copy in go(side, step):
                            copy.wait_send()

        return start, stage, end, follow

    def chain_sum(kind, parts, slots, leaving=leaving):
        def go(number):
            block = leaving[number]
            rightward = block > h
            slot = jnp.where(rightward, block - 1, last + block)
            where = (d, jnp.clip(jnp.where(rightward, h + 1, h - 1), 0, last))
            middle_one = (rightward & (h > 0)) | (jnp.logical_not(rightward) & (h < last))
            pieces = []
            for half in range(2):
                at = at_block(2 * block + half, tokens // 2)
                rows_of = pl.ds(half * (tokens // 2), tokens // 2)
                copy = remote(
                    parts.at[at, :],
                    slots.at[slot, rows_of, :],
                    z_send.at[kind, 2 * number + half],
                    z_recv.at[kind, 2 * slot + half],
                    where,
                )
                pieces.append((copy, at, slot, rows_of))
            return pieces, middle_one

        def now(number):
            pieces, middle_one = go(number)

            @pl.when(jnp.logical_not(middle_one))
            def _():
                for copy, _, _, _ in pieces:
                    copy.start()

        def later(number):
            pieces, middle_one = go(number)

            @pl.when(middle_one)
            def _():
                for copy, at, slot, rows_of in pieces:
                    copy.wait_recv()
                    parts[at, :] = parts[at, :] + slots[slot, rows_of, :]
                    copy.start()

        def end(total):
            ends = ((jnp.maximum(h - 1, 0), h > 0), (last + jnp.minimum(h, last - 1), h < last))
            for slot, there in ends:

                @pl.when(there)
                def _():
                    for half in range(2):
                        rows_of = pl.ds(half * (tokens // 2), tokens // 2)
                        remote(
                            parts.at[at_block(2 * h, tokens // 2), :],
                            slots.at[slot, rows_of, :],
                            z_send.at[kind, 0],
                            z_recv.at[kind, 2 * slot + half],
                            right,
                        ).wait_recv()
                    total[...] += slots[slot].astype(f32)

            for number in range(last):
                for copy, _, _, _ in go(number)[0]:
                    copy.wait_send()

        return now, later, end

    def spread(kind, src, dst, steps=peers):
        copies = {}
        for step in steps:
            copies[step] = remote(
                src(step), dst(step), z_send.at[kind, step - 1], z_recv.at[kind, step - 1], along(step)
            )
            copies[step].start()
        return copies

    x_start, x_stage, x_end, _ = gather(0, rows)
    for_rows[0].wait()
    x_start()

    def slot(array, place, side, half=None):
        if array == 0:
            at = halves_out(side)[half] if half is not None else at_block(side, slab)
            return w_out.at[place, at, :]
        at = halves_in[half] if half is not None else pl.ds(0, features)
        return w_in.at[place, at, at_block(side, slab)]

    def weights(number, ref, where):
        copy = remote(ref, ref, w_send.at[number], w_recv.at[number], where)
        copy.start()
        return copy

    slabs, halves_on, to_core, diagonal = {}, {}, {}, {}
    for copy in own_weights:
        copy.wait()
    for array in range(2):
        for first in range(2):
            for bit in (1, 2):
                half = bit - 1 if first == 0 else 2 - bit
                number = ((bit - 1) * 2 + half) * 2 + array
                slabs[bit, half, array] = weights(
                    number, slot(array, chip, core, half), across(bit)
                )
        to_core[0, array] = weights(12 + array, slot(array, chip, core), partner)

    for_mask.wait()
    own_picks = jnp.concatenate(
        [picks[...].astype(f32), jnp.zeros((lanes - picks.shape[0], tokens), f32)], axis=0
    ).T.astype(jnp.int32)
    lane = lax.broadcasted_iota(jnp.int32, (tokens, lanes), 1)
    for plane in range(n_head):
        expert = (lane // per_device * n_head + plane) * per_device + lane % per_device
        expert = jnp.where(lane < n_dp * per_device, expert, -1)
        hit = own_picks[:, 0:1] == expert
        for c in range(1, picks.shape[0]):
            hit = hit | (own_picks[:, c : c + 1] == expert)
        my_mask[plane] = jnp.where(hit, 1.0, 0.0).astype(bf16)
    mask_copies = spread(1, lambda s: my_mask.at[xor(h, s)], lambda s: all_mask.at[own_block, :])
    all_mask[own_block, :] = my_mask[h]

    for copy in for_rows[1:]:
        copy.wait()
    attend_gain, expert_gain = one_row(gain_ref[...]), one_row(expert_gain_ref[...])
    one_hot = lambda count: jnp.where(
        lax.broadcasted_iota(jnp.int32, (count, width), 0)
        == lax.broadcasted_iota(jnp.int32, (count, width), 1),
        1.0,
        0.0,
    ).astype(bf16)
    w_an[:, pl.ds(2 * width, width)] = dot(wg_ref[...], one_hot(wg_ref.shape[0]), TN).astype(bf16)
    uses = two_picks.shape[1]
    vgrads[:, pl.ds(0, lanes)] = jnp.concatenate(
        [
            two_picks[0].astype(f32),
            two_picks[1].astype(f32) + experts,
            jnp.zeros((lanes - 2 * uses, group), f32),
        ],
        axis=0,
    ).T.astype(bf16)
    half_lanes = lax.broadcasted_iota(jnp.int32, (1, width), 1) < width // 2

    def turns(at):
        both = angles[at, :]
        turned_over = swap_halves(both)
        return (
            jnp.where(half_lanes, both, turned_over),
            jnp.where(half_lanes, -turned_over, both),
        )

    def project(block):
        at = at_block(block, tokens)
        own = rows[at, :]
        full = own.astype(f32)
        inverse = lax.rsqrt(jnp.mean(full * full, axis=-1, keepdims=True) + epsilon)
        unit = (full * inverse * attend_gain).astype(bf16)
        qkg = dot(unit, w_an[...])
        c, s = turns(at)
        one, two = qkg[:, :width], qkg[:, width : 2 * width]
        q[at, :] = (one * c + swap_halves(one) * s).astype(bf16)
        k[at, :] = (two * c + swap_halves(two) * s).astype(bf16)
        lane = lax.broadcasted_iota(jnp.int32, (tokens, width), 1)
        chosen = vgrads[at, pl.ds(0, lanes)].astype(f32).astype(jnp.int32)
        hit = lane == chosen[:, 0:1]
        for c in range(1, 2 * uses):
            hit = hit | (lane == chosen[:, c : c + 1])
        gate = jnp.where(hit, jax.nn.sigmoid(qkg[:, 2 * width :]), 0.0)
        gates[at, :] = jnp.where(lane == width - 1, inverse, gate)
        values = dot(own, w_v[...])
        vx[at, :] = values.astype(bf16)
        value = gate[:, 0:1] * values[:, :width]
        for e in range(1, experts):
            value += gate[:, e : e + 1] * values[:, e * width : (e + 1) * width]
        v[at, :] = value.astype(bf16)

    for copy in for_scores:
        copy.wait()
    seg_col = gate_grads
    seg_col[...] = jnp.broadcast_to(seg[...].astype(f32), (lanes, group)).T

    def attend(block):
        at = at_block(block, tokens)
        score = dot(q[at, :], k[...], NT) * scale
        row = block * tokens + lax.broadcasted_iota(jnp.int32, (tokens, group), 0)
        place = lax.broadcasted_iota(jnp.int32, (tokens, group), 1)
        allowed = (place <= row) & (seg_col[at, 0:1] == seg[...].astype(f32))
        score = jnp.where(allowed, score, negative)
        exponents = jnp.exp(score - jnp.max(score, axis=-1, keepdims=True))
        chance = exponents / jnp.sum(exponents, axis=-1, keepdims=True)
        probs[at, :] = chance.astype(bf16)
        attended = dot(chance.astype(bf16), v[...])
        att[at, :] = attended
        gate = gates[at, :]
        weighted = jnp.concatenate(
            [
                (gate[:, experts + e : experts + e + 1] * attended).astype(bf16)
                for e in range(experts)
            ],
            axis=-1,
        )
        return dot(weighted, w_o[...])

    to_mid = chain_sum(3, part, got, (pick(1, 3, 0, 0), pick(2, 0, 3, 1), pick(3, 2, 1, 2)))

    def send_mid(number):
        block = pick(number + 1, *((3, 0, 0), (0, 3, 1), (2, 1, 2))[number])
        part[at_block(block, tokens), :] = attend(block).astype(bf16)
        to_mid[0](number)

    k[...] = jnp.zeros_like(k)
    v[...] = jnp.zeros_like(v)
    project(h)
    _, cot_stage, cot_end, cot_follow = gather(2, cot)
    for_cot.wait()
    for step in (1, 2, 3):
        x_stage(step)
        cot_follow(step)
        project(arrival[step - 1])
        pl.when(h == 0)(lambda: send_mid(step - 1))

    @pl.when(h > 0)
    def _():
        for number in range(last):
            send_mid(number)

    middle[...] = rows[own_block, :].astype(f32) + attend(h)
    cot_stage(1, "duty")
    to_mid[1](0)
    for array in range(2):
        for half in range(2):
            slabs[1 + half, half, array].wait_recv()
            halves_on[half, array] = weights(
                8 + 2 * half + array,
                slot(array, xor(chip, 1 + half), core, half),
                across(2 - half),
            )

    to_mid[1](1)
    cot_stage(2, "duty")
    to_mid[1](2)
    for bit in (1, 2):
        slabs[bit, 2 - bit, 0].wait_recv()
        to_core[bit, 0] = weights(14 + (bit - 1) * 2, slot(0, xor(chip, bit), core), partner)
        slabs[bit, 2 - bit, 1].wait_recv()
        to_core[bit, 1] = weights(15 + (bit - 1) * 2, slot(1, xor(chip, bit), core), partner)
    for_router.wait()
    slot_of = lax.broadcasted_iota(jnp.int32, (w_r.shape[0], lanes), 1)
    name = lax.broadcasted_iota(jnp.int32, (w_r.shape[0], lanes), 0)
    expert = (slot_of // per_device * n_head + h) * per_device + slot_of % per_device
    expert = jnp.where(slot_of < n_dp * per_device, expert, -1)
    my_router[...] = dot(
        w_r[...], jnp.where(name == expert, 1.0, 0.0).astype(bf16), TN
    ).astype(bf16)

    to_mid[2](middle)
    mid = middle[...]
    inverse = lax.rsqrt(jnp.mean(mid * mid, axis=-1, keepdims=True) + epsilon)
    mrs[own_block, :] = (mid * inverse * expert_gain).astype(bf16)
    mr_start, mr_stage, mr_end, _ = gather(4, mrs)
    mr_start()

    def last_halves(array):
        for half in range(2):
            halves_on[half, array].wait_recv()
            diagonal[half, array] = weights(
                18 + 2 * half + array, slot(array, xor(chip, 3), core, half), partner
            )

    for step in (1, 2, 3):
        cot_stage(step, "rest")
    last_halves(0)
    for step in peers:
        mask_copies[step].wait()
    cot_end()
    x_end()

    def near_weights(array):
        for bit in range(3):
            to_core[bit, array].wait_recv()

    def far_weights(array):
        for half in range(2):
            diagonal[half, array].wait_recv()

    def weights_sent():
        for array in range(2):
            for bit in range(3):
                to_core[bit, array].wait_send()
            for half in range(2):
                diagonal[half, array].wait_send()
                halves_on[half, array].wait_send()
                for bit in (1, 2):
                    slabs[bit, half, array].wait_send()

    near_weights(0)

    def lift_chip(n):
        j = xor(chip, n)
        lift = dot(cot[...], w_out[j], NT)
        lifted[j, 0] = lift[:, :slab].astype(bf16)
        lifted[j, 1] = lift[:, slab:].astype(bf16)

    pl.loop(0, chips // 2)(lift_chip)
    mr_stage(1, "near")
    pl.loop(chips // 2, chips - 1)(lift_chip)
    far_weights(0)
    lift_chip(chips - 1)
    mr_stage(1, "far")
    mr_stage(1, "rest")
    near_weights(1)

    def spread_lanes(j):
        lane = lax.broadcasted_iota(jnp.int32, (lanes, wide), 1) // width
        slot = lax.broadcasted_iota(jnp.int32, (lanes, wide), 0)
        return jnp.where(slot == lane + j * (wide // width), 1.0, 0.0).astype(bf16)

    def pair_of_blocks(number, between, before_last):
        at = at_block(number, pair)
        own = mrs[at, :]
        gates = jax.nn.sigmoid(dot(own, my_router[...]))
        live = gates * all_mask[at, :].astype(f32)
        narrow = live.astype(bf16)

        def chip_step(n, total):
            j = xor(chip, n)
            pick = spread_lanes(j)
            hidden = dot(own, w_in[j])
            gate = dot(narrow, pick).astype(bf16)
            lift = jnp.concatenate([lifted[j, 0, at, :], lifted[j, 1, at, :]], axis=-1)
            square = hidden * hidden
            inner = jnp.tanh(0.7978845608028654 * hidden * (1.0 + 0.044715 * square))
            half = 0.5 * (1.0 + inner)
            act = hidden * half
            slope = half + act * (1.0 - inner) * (
                0.7978845608028654 + (0.7978845608028654 * 3.0 * 0.044715) * square
            )
            act = act.astype(bf16)
            acts[j, at, :] = act * gate
            hids[j, at, :] = slope.astype(bf16) * (lift * gate)
            return total + dot(act * lift, pick, NT)

        total = lax.fori_loop(0, chips // 2, chip_step, jnp.zeros((pair, lanes), f32))
        between()
        total = lax.fori_loop(chips // 2, chips - 1, chip_step, total)
        before_last()
        total = chip_step(chips - 1, total)
        dz = (total * live * (1.0 - gates)).astype(bf16)
        dzs[at, :] = dz

        @pl.loop(0, features // column)
        def _(c):
            part_of = at_block(c, column)
            total = dot(dz, my_router[part_of, :], NT)
            for j in range(chips):
                total += dot(hids[j, at, :], w_in[j, part_of, :], NT)
            part[at, part_of] = total.astype(bf16)

    def outputs():
        @pl.loop(0, features // column)
        def _(c):
            part_of = at_block(c, column)
            total = dot(acts[0], w_out[0, :, part_of])
            for j in range(1, chips):
                total += dot(acts[j], w_out[j, :, part_of])
            outs[:, part_of] = total.astype(bf16)

    near = h // 2
    to_dmr = chain_sum(5, part, got)

    def halfway():
        last_halves(1)
        mr_stage(2, "duty")

    pair_of_blocks(near, halfway, lambda: far_weights(1))
    to_dmr[0](2)
    mr_stage(2, "rest")
    mr_stage(3)
    pair_of_blocks(1 - near, lambda: None, lambda: None)
    to_dmr[0](0)
    to_dmr[0](1)
    pl.semaphore_signal(ready, inc=1, device_id=partner, device_id_type=MESH)

    weights_sent()
    turned[...] = mrs[...].T

    def to_other_core(n, array):
        place = xor(chip, chips - 1 - n)
        if array == 0:
            return [
                remote(
                    w_out.at[place, other_side, :],
                    core_out.at[place],
                    c_send.at[2, n],
                    c_recv.at[2, n],
                    partner,
                )
            ]
        return [
            remote(
                w_in.at[place, halves_in[half], other_side],
                lifted.at[place, half],
                c_send.at[half, n],
                c_recv.at[half, n],
                partner,
            )
            for half in range(2)
        ]

    pl.semaphore_wait(ready, 1)
    hops = {}

    def hop(half, index, place, toward, array):
        copy = remote(
            slot(array, place, core, half),
            (hop_out, hop_in)[array].at[half, index],
            e_send.at[1 - array, 2 * half + index],
            e_recv.at[1 - array, 2 * half + index],
            across(toward),
        )
        copy.start()
        hops[half, index, array] = copy

    def both_cores(n, array):
        step = chips - 1 - n
        place = xor(chip, step)
        for copy in to_other_core(n, array):
            copy.wait()
        if array == 0:
            w_out[place, own_side, :] = w_out[place, own_side, :] + core_out[place]
        else:
            for half in range(2):
                here = (place, halves_in[half], own_side)
                w_in[here] = w_in[here] + lifted[place, half]
        if step == 3:
            hop(0, 1, place, 1, array)
            hop(1, 1, place, 2, array)
        elif step:
            hop(step - 1, 0, place, step, array)

    def expert_grads(array, place, at):
        if array == 0:
            for half in halves_in:
                w_out[place, at, half] = dot(acts[place, :, at], cot[:, half], TN).astype(bf16)
        else:
            for n in range(features // column):
                band = pl.ds(n * column, column)
                w_in[place, band, at] = dot(turned[band, :], hids[place, :, at]).astype(bf16)

    def all_grads(array):
        for n in range(chips):
            place = xor(chip, chips - 1 - n)
            expert_grads(array, place, other_side if array == 0 else slice(None))
            for copy in to_other_core(n, array):
                copy.start()
            if n:
                both_cores(n - 1, array)
            if array == 0:
                expert_grads(array, place, own_side)

    all_grads(1)
    outputs()
    both_cores(chips - 1, 1)
    to_dmr[1](0)
    all_grads(0)
    both_cores(chips - 1, 0)
    to_dmr[1](1)
    to_dmr[1](2)
    side = features // 2
    strip = side // chips
    col = lambda c, j: at_block(c * chips + j, strip)

    def section(number, first, count):
        at = pl.ds(first, count)
        state = {}

        def sem(n):
            return s_send.at[number, n], s_recv.at[number, n]

        def start():
            state["core"] = remote(
                sums.at[at, at_block(1 - core, side)], core_got.at[at, :], *sem(0), partner
            )
            state["core"].start()

        def mid():
            state["core"].wait()
            half = at_block(core, side)
            sums[at, half] = sums[at, half] + core_got[at, :]
            state["chips"] = []
            for s in range(1, chips):
                copy = remote(
                    sums.at[at, col(core, xor(chip, s))], chip_got.at[s - 1, at, :], *sem(s), across(s)
                )
                copy.start()
                state["chips"].append(copy)

        def add():
            for copy in state["chips"]:
                copy.wait()
            total = sums[at, col(core, chip)].astype(f32)
            for s in range(1, chips):
                total += chip_got[s - 1, at, :].astype(f32)
            piece[at, :] = total.astype(bf16)

        return start, mid, add

    def two_hop_section(number, first, count):
        at = pl.ds(first, count)
        half_at = [pl.ds(first + n * (count // 2), count // 2) for n in range(2)]
        begin, state = section(number, first, count)[0], {}

        def hop(half, index, place, toward, n):
            copy = remote(
                sums.at[half_at[half], col(core, place)],
                chip_got.at[index, half_at[half], :],
                t_send.at[number, n],
                t_recv.at[number, n],
                across(toward),
            )
            copy.start()
            return copy

        def mid():
            over = remote(
                sums.at[at, at_block(1 - core, side)],
                core_got.at[at, :],
                s_send.at[number, 0],
                s_recv.at[number, 0],
                partner,
            )
            over.wait()
            half = at_block(core, side)
            sums[at, half] = sums[at, half] + core_got[at, :]
            for half in range(2):
                toward = 1 + half
                state[half, 1] = hop(half, 1, xor(chip, 3), toward, 2 * half + 1)
                state[half, 0] = hop(half, 0, xor(chip, toward), toward, 2 * half)

        def second():
            for half in range(2):
                here = (half_at[half], col(core, xor(chip, 2 - half)))
                state[half, 1].wait()
                sums[here] = sums[here] + chip_got[1, half_at[half], :]
                state[half, 2] = hop(half, 2, xor(chip, 2 - half), 2 - half, 4 + half)

        def add():
            for half in range(2):
                state[half, 0].wait()
                state[half, 2].wait()
            total = sums[at, col(core, chip)].astype(f32)
            for index in (0, 2):
                total += chip_got[index, at, :].astype(f32)
            piece[at, :] = total.astype(bf16)

        return begin, mid, second, add

    def two_hop_to_plane(number, first, count):
        at = pl.ds(first, count)
        half_at = [pl.ds(first + n * (count // 2), count // 2) for n in range(2)]
        state = {}

        def send(src, rows_of, place, where, n):
            copy = remote(
                src,
                wide_ref.at[rows_of, col(core, place)],
                t_send.at[number, n],
                t_recv.at[number, n],
                where,
            )
            copy.start()
            return copy

        def start():
            for urgent in range(2):
                for bit in (1, 2):
                    half = bit - 1 if urgent == 0 else 2 - bit
                    state[bit, half] = send(
                        piece.at[half_at[half], :],
                        half_at[half],
                        chip,
                        across(bit),
                        6 + 2 * (bit - 1) + half,
                    )
            over = send(piece.at[at, :], at, chip, partner, 12)
            own = pltpu.make_async_copy(
                piece.at[at, :], wide_ref.at[at, col(core, chip)], t_send.at[number, 15]
            )
            own.start()
            state["wait"] = [over, own]

        def relay():
            for half in range(2):
                bit = 1 + half
                state[bit, half].wait_recv()
                place = xor(chip, bit)
                here = wide_ref.at[half_at[half], col(core, place)]
                state[3, half] = send(here, half_at[half], place, across(2 - half), 10 + half)

        def forward():
            for bit in (1, 2):
                state[bit, 2 - bit].wait_recv()
                place = xor(chip, bit)
                here = wide_ref.at[at, col(core, place)]
                state["wait"].append(send(here, at, place, partner, 12 + bit))

        def end():
            for half in range(2):
                state[3, half].wait_recv()
            place = xor(chip, 3)
            here = wide_ref.at[at, col(core, place)]
            state["wait"].append(send(here, at, place, partner, 16))

        def done():
            for copy in state["wait"]:
                copy.wait()
            for half in range(2):
                state[3, half].wait_send()
                for bit in (1, 2):
                    state[bit, half].wait_send()

        return start, relay, forward, end, done

    def to_plane(number, src, rows_to):
        state = {}

        def sem(n):
            return s_send.at[number, chips + n], s_recv.at[number, chips + n]

        def start():
            here = wide_ref.at[rows_to, col(core, chip)]
            state["share"] = [remote(src, here, *sem(s), across(s)) for s in range(1, chips)]
            over = remote(src, here, *sem(0), partner)
            own = pltpu.make_async_copy(src, here, s_send.at[number, 3 * chips - 1])
            state["wait"] = [over, own]
            for copy in state["share"] + state["wait"]:
                copy.start()

        def forward():
            for s in range(1, chips):
                state["share"][s - 1].wait()
                here = wide_ref.at[rows_to, col(core, xor(chip, s))]
                copy = remote(here, here, *sem(chips - 1 + s), partner)
                copy.start()
                state["wait"].append(copy)

        def end():
            for copy in state["wait"]:
                copy.wait()

        return start, forward, end

    mixed = w_o.shape[0]
    small = ceil_to(named + 1, 16)
    at_a = pl.ds(features, 16)
    at_o = pl.ds(features + 16, mixed)
    at_g = pl.ds(features + 16 + mixed, small)
    of_d = [two_hop_section(n, n * features // 2, features // 2) for n in range(2)]
    of_o = two_hop_section(2, features + 16, mixed)
    of_g = section(3, features + 16 + mixed, small)
    of_a = section(4, features, 16)
    out_d = [two_hop_to_plane(n, n * features // 2, features // 2) for n in range(2)]
    out_o = two_hop_to_plane(2, features + 16, mixed)
    out_g = to_plane(3, blocks, pl.ds(features + 16 + mixed, n_head * small))
    out_a = to_plane(4, piece.at[at_a, :], at_a)
    router_part = dot(dzs[...], mrs[...], TN)[:named]

    grad_x_ref[...] = part[own_block, :].astype(f32)
    to_dmr[2](grad_x_ref)
    incoming = grad_x_ref[...]
    mid = middle[...]
    inverse = lax.rsqrt(jnp.mean(mid * mid, axis=-1, keepdims=True) + epsilon)
    unit = mid * inverse
    scaled = incoming * expert_gain
    dmid = cot[own_block, :].astype(f32) + inverse * (
        scaled - unit * jnp.mean(scaled * unit, axis=-1, keepdims=True)
    )
    grad_x_ref[...] = dmid
    das[own_block, :] = dmid.astype(bf16)
    da_start, da_stage, da_end, _ = gather(6, das)
    da_start()
    sums[at_g, :] = jnp.concatenate(
        [
            router_part,
            jnp.sum(incoming * unit, axis=0, keepdims=True),
            jnp.zeros((small - named - 1, features), f32),
        ],
        axis=0,
    ).astype(bf16)
    of_g[0]()
    turned[...] = rows[...].T
    of_g[1]()
    lasts = {}

    def first_hop(half, index, place):
        for array in range(2):
            hops[half, index, array].wait()
        at_in = (place, halves_in[half], own_side)
        at_out = (place, halves_out(core)[half], slice(None))
        w_in[at_in] = w_in[at_in] + hop_in[half, index]
        w_out[at_out] = w_out[at_out] + hop_out[half, index]

    for half in range(2):
        toward = 2 - half
        place = xor(chip, toward)
        first_hop(half, 1, place)
        pl.semaphore_signal(free.at[half], inc=1, device_id=across(toward), device_id_type=MESH)
        pl.semaphore_wait(free.at[half], 1)
        lasts[half] = (
            remote(
                slot(1, place, core, half),
                hop_in.at[half, 1],
                e_send.at[0, 4 + half],
                e_recv.at[0, 4 + half],
                across(toward),
            ),
            remote(
                slot(0, place, core, half),
                hop_out.at[half, 1],
                e_send.at[1, 4 + half],
                e_recv.at[1, 4 + half],
                across(toward),
            ),
        )
        for copy in lasts[half]:
            copy.start()
    lane = lax.broadcasted_iota(jnp.int32, (tokens, width), 1)

    def through_output(block):
        at = at_block(block, tokens)
        all_five = dot(das[at, :], w_o[...], NT)
        attended = att[at, :]
        total = jnp.zeros((tokens, width), f32)
        gate = jnp.zeros((tokens, width), f32)
        for e in range(experts):
            one = all_five[:, e * width : (e + 1) * width]
            total += gates[at, experts + e : experts + e + 1] * one
            gate = jnp.where(
                lane == experts + e, jnp.sum(one * attended, axis=-1, keepdims=True), gate
            )
        datt[at, :] = total.astype(bf16)
        gate_grads[at, :] = gate

    through_output(h)
    to_out = chain_sum(7, outs, got_out)
    for step in (1, 2, 3):
        da_stage(step)
        if step == 1:
            for number in range(last):
                to_out[0](number)
        through_output(arrival[step - 1])

    for e in range(experts):
        one = (gates[:, experts + e : experts + e + 1] * att[...]).astype(bf16)
        sums[pl.ds(features + 16 + e * width, width), :] = dot(one, das[...], TN).astype(bf16)
    of_o[0]()

    @pl.loop(0, n_head)
    def _(block):
        at = at_block(block, tokens)
        chance = probs[at, :].astype(f32)
        dprob = dot(datt[at, :], v[...], NT)
        centre = jnp.sum(chance * dprob, axis=-1, keepdims=True)
        vgrads[at, pl.ds(0, group)] = (chance * (dprob - centre)).astype(bf16)

    dq = dot(vgrads[:, pl.ds(0, group)], k[...]) * scale
    dk = dot(vgrads[:, pl.ds(0, group)], q[...], TN) * scale
    dv = dot(probs[...], datt[...], TN)
    of_o[1]()
    c, s = turns(slice(None))
    qkz[:, pl.ds(0, width)] = (dq * c - swap_halves(dq) * s).astype(bf16)
    qkz[:, pl.ds(width, width)] = (dk * c - swap_halves(dk) * s).astype(bf16)
    gate = gate_grads[...]
    lane = lax.broadcasted_iota(jnp.int32, (group, width), 1)
    for e in range(experts):
        vgrads[:, pl.ds(e * width, width)] = (gates[:, e : e + 1] * dv).astype(bf16)
        one = jnp.sum(vx[:, pl.ds(e * width, width)].astype(f32) * dv, axis=-1, keepdims=True)
        gate = jnp.where(lane == e, one, gate)
    qkz[:, pl.ds(2 * width, width)] = (gate * gates[...] * (1.0 - gates[...])).astype(bf16)

    scaled_qkz = (qkz[...].astype(f32) * gates[:, width - 1 : width]).astype(bf16)

    def matrix_rows(c):
        at = at_block(c, column)
        sums[at, pl.ds(0, 3 * width)] = dot(turned[at, :], scaled_qkz).astype(bf16)
        sums[at, pl.ds(3 * width, experts * width)] = dot(turned[at, :], vgrads[...]).astype(bf16)

    steps_each = features // column // 2
    for n in range(2):
        pl.loop(n * steps_each, (n + 1) * steps_each)(matrix_rows)
        of_d[n][0]()
    def into_rows(block):
        at = at_block(block, tokens)
        inverse = gates[at, width - 1 : width]
        unit = rows[at, :].astype(f32) * inverse
        through = dot(qkz[at, :], w_an[...], NT)
        scaled = through * attend_gain
        total = inverse * (
            scaled - unit * jnp.mean(scaled * unit, axis=-1, keepdims=True)
        ) + dot(vgrads[at, :], w_v[...], NT)
        return total, jnp.sum(through * unit, axis=0, keepdims=True)

    to_x = chain_sum(8, part, got)
    gain = jnp.zeros((1, features), f32)
    for number in range(last):
        total, one = into_rows(leaving[number])
        gain += one
        part[at_block(leaving[number], tokens), :] = total.astype(bf16)
        to_x[0](number)
        if number < 2:
            of_d[number][1]()
    total, one = into_rows(h)
    sums[at_a, :] = jnp.broadcast_to(gain + one, (16, features)).astype(bf16)
    of_a[0]()
    grad_x_ref[...] += total
    to_out[1](0)
    to_out[1](1)
    of_a[1]()
    of_o[2]()
    to_x[1](0)
    of_d[0][2]()
    of_d[1][2]()
    of_g[2]()
    small_block = at_block(h, small)
    blocks[small_block, :] = piece[at_g, :]
    g_copies = spread(9, lambda s: blocks.at[small_block, :], lambda s: blocks.at[small_block, :])
    to_x[1](1)
    of_o[3]()
    out_o[0]()
    to_x[1](2)
    of_d[0][3]()
    out_d[0][0]()
    of_d[1][3]()
    out_d[1][0]()
    of_a[2]()
    gain_part[...] = piece[at_a, :]
    gain_copies = spread(10, lambda s: gain_part, lambda s: gain_got.at[s - 1])
    to_out[1](2)
    out_o[1]()
    for step in peers:
        g_copies[step].wait()
    out_g[0]()
    out_d[0][1]()
    gain = gain_part[...].astype(f32)
    for step in peers:
        gain_copies[step].wait()
        gain += gain_got[step - 1].astype(f32)
    piece[at_a, :] = gain.astype(bf16)
    out_a[0]()
    out_d[1][1]()
    out_o[2]()
    to_x[2](grad_x_ref)
    rows_out = [pltpu.make_async_copy(grad_x_ref, final_x_ref, local_sem.at[2])]
    rows_out[0].start()
    output_ref[...] = middle[...] + outs[own_block, :].astype(f32)
    to_out[2](output_ref)
    rows_out.append(pltpu.make_async_copy(output_ref, final_ref, local_sem.at[3]))
    rows_out[1].start()
    for half in range(2):
        first_hop(half, 0, chip)
        for copy in lasts[half]:
            copy.wait()
        at_in = (chip, halves_in[half], own_side)
        at_out = (chip, halves_out(core)[half], slice(None))
        w_in[at_in] = w_in[at_in] + hop_in[half, 1]
        w_out[at_out] = w_out[at_out] + hop_out[half, 1]
    stores = (
        pltpu.make_async_copy(w_in.at[chip, :, own_side], fin_in_ref, local_sem.at[0]),
        pltpu.make_async_copy(w_out.at[chip, own_side, :], fin_out_ref, local_sem.at[1]),
    )
    for store in stores:
        store.start()
    out_o[3]()
    out_d[0][2]()
    out_g[1]()
    out_a[1]()
    out_d[1][2]()
    out_d[0][3]()
    out_d[1][3]()
    for one in (out_o, out_d[0], out_g, out_a, out_d[1]):
        one[-1]()
    for store in (*stores, *rows_out):
        store.wait()
    mr_end()
    da_end()


def layer_call(n_dp, n_head, args):
    x, picks, router, value_mat, expert_in = args[0], args[2], args[14], args[12], args[15]
    tokens, features = x.shape
    per_device, _, width = expert_in.shape
    held_experts = value_mat.shape[1]
    group = tokens * n_head
    chips = n_dp // 2
    slab = per_device * width
    lanes = 128
    peers = n_head - 1
    named = ceil_to(n_dp * per_device, 8)
    small = ceil_to(named + 1, 16)
    top = features + held_experts
    held = top + 16 + small
    strip = features // n_dp
    shape = jax.ShapeDtypeStruct
    vm, dma = pltpu.VMEM, pltpu.SemaphoreType.DMA
    outs = [
        (shape((tokens, features), f32), ANY),
        (shape((tokens, features), f32), ANY),
        (shape((top + 16 + n_head * small, features), bf16), ANY),
        (shape((features, slab), bf16), ANY),
        (shape((slab, features), bf16), ANY),
    ]
    scratch = dict(
        output_rows=vm((tokens, features), f32),
        grad_rows=vm((tokens, features), f32),
        picks=vm(picks.shape, jnp.int32),
        two_picks=vm((2, *args[3].shape), jnp.int32),
        w_r=vm(router.shape, bf16),
        seg=vm((1, group), jnp.int32),
        angles=vm((group, width), f32),
        w_an=vm((features, 3 * width), bf16),
        w_v=vm((features, held_experts), bf16),
        w_o=vm((held_experts, features), bf16),
        my_router=vm((features, lanes), bf16),
        w_in=vm((chips, features, 2 * slab), bf16),
        w_out=vm((chips, 2 * slab, features), bf16),
        rows=vm((group, features), bf16),
        cot=vm((group, features), bf16),
        mrs=vm((group, features), bf16),
        das=vm((group, features), bf16),
        turned=vm((features, group), bf16),
        my_mask=vm((n_head, tokens, lanes), bf16),
        all_mask=vm((group, lanes), bf16),
        gates=vm((group, width), f32),
        q=vm((group, width), bf16),
        k=vm((group, width), bf16),
        v=vm((group, width), bf16),
        vx=vm((group, held_experts), bf16),
        att=vm((group, width), f32),
        part=vm((group, features), bf16),
        got=vm((2 * peers, tokens, features), bf16),
        outs=vm((group, features), bf16),
        got_out=vm((2 * peers, tokens, features), bf16),
        lifted=vm((chips, 2, group, slab), bf16),
        core_out=vm((chips, slab, features), bf16),
        acts=vm((chips, group, 2 * slab), bf16),
        hids=vm((chips, group, 2 * slab), bf16),
        dzs=vm((group, lanes), bf16),
        datt=vm((group, width), bf16),
        gate_grads=vm((group, width), f32),
        probs=vm((group, group), bf16),
        qkz=vm((group, 3 * width), bf16),
        vgrads=vm((group, held_experts), bf16),
        gain_part=vm((16, strip), bf16),
        gain_got=vm((peers, 16, strip), bf16),
        sums=vm((held, features), bf16),
        core_got=vm((held, features // 2), bf16),
        chip_got=vm((chips - 1, held, strip), bf16),
        piece=vm((held, strip), bf16),
        blocks=vm((n_head * small, strip), bf16),
        hop_in=vm((2, 2, features // 2, slab), bf16),
        hop_out=vm((2, 2, slab // 2, features), bf16),
        local_sem=dma((17 + 1 + per_device,)),
        z_send=dma((11, 4 * peers)),
        z_recv=dma((11, 4 * peers)),
        w_send=dma((22,)),
        w_recv=dma((22,)),
        c_send=dma((3, chips)),
        c_recv=dma((3, chips)),
        e_send=dma((2, 6)),
        e_recv=dma((2, 6)),
        s_send=dma((5, 3 * chips)),
        s_recv=dma((5, 3 * chips)),
        t_send=dma((3, 17)),
        t_recv=dma((3, 17)),
        ready=pltpu.SemaphoreType.REGULAR,
        free=pltpu.SemaphoreType.REGULAR((2,)),
    )
    return pl.pallas_call(
        functools.partial(layer_kernel, n_dp, n_head),
        out_shape=[o[0] for o in outs],
        out_specs=[o[1] for o in outs],
        in_specs=[VM if number in (6, 7, 11) else ANY for number in range(17)],
        scratch_shapes=list(scratch.values()),
        compiler_params=pltpu.CompilerParams(
            collective_id=1, has_side_effects=True, vmem_limit_bytes=vmem_bytes
        ),
    )(*args)


def finish_kernel(
    n_dp,
    n_head,
    output_ref,
    grad_x_ref,
    wide_ref,
    in_ref,
    out_ref,
    gain_ref,
    final_ref,
    input_ref,
    attend_ref,
    query_ref,
    key_ref,
    value_ref,
    mix_ref,
    gate_ref,
    expert_ref,
    router_ref,
    grad_in_ref,
    grad_out_ref,
    wide,
    flat_in,
    flat_out,
    value,
    mix,
    grad_in,
    grad_out,
    output,
    grad_x,
    query,
    key,
    sem,
):
    features, slab = in_ref.shape
    per_device, _, width = grad_in_ref.shape
    experts_total, gates = router_ref.shape[0], gate_ref.shape[0]
    mixed = mix_ref.shape[0]
    top = features + 16 + mixed
    small = (wide_ref.shape[0] - top) // n_head
    named = n_dp * per_device

    numbers = iter(range(sem.shape[0]))

    def copy(src, dst):
        one = pltpu.make_async_copy(src, dst, sem.at[next(numbers)])
        one.start()
        return one

    bands = 4
    band = features // bands
    load = lambda first, count: copy(
        wide_ref.at[pl.ds(first, count), :], wide.at[pl.ds(first, count), :]
    )
    plain = [(copy(output_ref, output), output, final_ref), (copy(grad_x_ref, grad_x), grad_x, input_ref)]
    for_out, for_in = copy(out_ref, flat_out), copy(in_ref, flat_in)
    for_bands = [load(n * band, band) for n in range(bands)]
    for_mix = [load(features + 16 + n * mixed // 2, mixed // 2) for n in range(2)]
    others = [load(features, 16), load(top, n_head * small)]
    stores = []
    gain = jnp.broadcast_to(one_row(gain_ref[...]), (width, features)).T
    for loaded, held, result in plain:
        loaded.wait()
        stores.append(copy(held, result))
    for_out.wait()
    for e in range(per_device):
        grad_out[e] = flat_out[pl.ds(e * width, width), :].astype(f32)
        stores.append(copy(grad_out.at[e], grad_out_ref.at[e]))
    for_in.wait()
    for e in range(per_device):
        grad_in[e] = flat_in[:, pl.ds(e * width, width)].astype(f32)
        stores.append(copy(grad_in.at[e], grad_in_ref.at[e]))
    for n in range(bands):
        for_bands[n].wait()
        at = pl.ds(n * band, band)
        scale = gain[n * band : (n + 1) * band]
        value[at, :] = wide[at, pl.ds(3 * width, value.shape[1])].astype(f32)
        stores.append(copy(value.at[at, :], value_ref.at[at, :]))
        query[at, :] = wide[at, pl.ds(0, width)].astype(f32) * scale
        stores.append(copy(query.at[at, :], query_ref.at[at, :]))
        key[at, :] = wide[at, pl.ds(width, width)].astype(f32) * scale
        stores.append(copy(key.at[at, :], key_ref.at[at, :]))
    for n in range(2):
        for_mix[n].wait()
        at = pl.ds(n * mixed // 2, mixed // 2)
        mix[at, :] = wide[pl.ds(features + 16 + n * mixed // 2, mixed // 2), :].astype(f32)
        stores.append(copy(mix.at[at, :], mix_ref.at[at, :]))
    turned = (wide[pl.ds(0, features), pl.ds(2 * width, width)].astype(f32) * gain).T
    for e in range(gates):
        gate_ref[e] = turned[e : e + 1]
    for loaded in others:
        loaded.wait()
    attend_ref[...] = wide[pl.ds(features, 16), :][0:1].astype(f32)
    planes = wide[pl.ds(top, n_head * small), :]
    place = lax.broadcasted_iota(jnp.int32, (n_head * small, experts_total), 0)
    name = lax.broadcasted_iota(jnp.int32, (n_head * small, experts_total), 1)
    slot, plane = place % small, place // small
    expert = (slot // per_device * n_head + plane) * per_device + slot % per_device
    chosen = (slot < named) & (expert == name)
    router_ref[...] = dot(jnp.where(chosen, 1.0, 0.0).astype(bf16), planes, TN)
    gain = jnp.zeros((1, features), f32)
    for z in range(n_head):
        row = z * small + ceil_to(named, 8)
        gain += planes[row : row + 1].astype(f32)
    expert_ref[...] = gain
    for store in stores:
        store.wait()


def finish_call(n_dp, n_head, shapes, args):
    shape = jax.ShapeDtypeStruct
    wide, flat_in, flat_out = args[2], args[3], args[4]
    value, mix, grad_in, grad_out = shapes[5], shapes[6], shapes[10], shapes[11]
    specs = [VM] * 12
    for number in (0, 1, 3, 4, 5, 6, 10, 11):
        specs[number] = ANY
    return pl.pallas_call(
        functools.partial(finish_kernel, n_dp, n_head),
        out_shape=[shape(s, f32) for s in shapes],
        out_specs=specs,
        in_specs=[ANY] * 5 + [VM],
        scratch_shapes=[
            pltpu.VMEM(wide.shape, bf16),
            pltpu.VMEM(flat_in.shape, bf16),
            pltpu.VMEM(flat_out.shape, bf16),
            pltpu.VMEM(value, f32),
            pltpu.VMEM(mix, f32),
            pltpu.VMEM(grad_in, f32),
            pltpu.VMEM(grad_out, f32),
            pltpu.VMEM(shapes[0], f32),
            pltpu.VMEM(shapes[1], f32),
            pltpu.VMEM(shapes[3], f32),
            pltpu.VMEM(shapes[4], f32),
            pltpu.SemaphoreType.DMA((40,)),
        ],
        compiler_params=pltpu.CompilerParams(vmem_limit_bytes=60 << 20),
    )(*args)


def kernel_body(
    n_dp,
    n_head,
    hidden_in,
    segments,
    value_pick,
    output_pick,
    expert_pick,
    attend_gain,
    query_weight,
    key_weight,
    value_weight,
    output_weight,
    head_router,
    expert_gain,
    router,
    expert_in,
    expert_out,
    cotangent,
):
    tokens, features = hidden_in.shape
    per_device, _, width = expert_in.shape
    experts = head_router.shape[2] // 2
    group = tokens * n_head
    angles = np.arange(group)[:, None] * theta ** (-2.0 * np.arange(width // 2) / width)[None, :]
    angles = np.concatenate([np.cos(angles), np.sin(angles)], axis=1).astype(np.float32)
    stacked = lambda gain: gain.reshape(-1, 128)
    results = layer_call(
        n_dp,
        n_head,
        (
            hidden_in,
            cotangent,
            expert_pick.T,
            value_pick.transpose(1, 2, 0)[0],
            output_pick.transpose(1, 2, 0)[0],
            segments[None, :],
            stacked(attend_gain),
            stacked(expert_gain),
            angles,
            query_weight[0],
            key_weight[0],
            head_router.transpose(0, 2, 1)[0],
            value_weight[0],
            output_weight[0],
            router.T,
            expert_in,
            expert_out.reshape(per_device * width, features),
        ),
    )
    shapes = (
        (tokens, features),
        (tokens, features),
        (1, features),
        query_weight.shape[1:],
        key_weight.shape[1:],
        value_weight.shape[1:],
        output_weight.shape[1:],
        (2 * experts, 1, features),
        (1, features),
        (router.shape[1], features),
        expert_in.shape,
        expert_out.shape,
    )
    done = list(finish_call(n_dp, n_head, shapes, (*results, stacked(attend_gain))))
    for number in (3, 4, 5, 6):
        done[number] = done[number][None]
    done[7] = done[7].transpose(1, 2, 0)
    done[9] = done[9].T
    done[2], done[8] = done[2][0], done[8][0]
    return tuple(done)


def solution(mesh):
    rows = P(everywhere, None)
    heads = P("head", None, None)
    experts = P(everywhere, None, None)
    picks = P("dp", "head", None)
    in_specs = (
        rows, P("dp"), picks, picks, rows, P(), heads, heads, heads, heads, heads,
        P(), P(), experts, experts, rows,
    )
    out_specs = (
        rows, rows, P(), heads, heads, heads, heads, heads, P(), P(), experts, experts,
    )
    n_dp, n_head = mesh.shape["dp"], mesh.shape["head"]

    def program(*args):
        held = 2 * n_dp * args[13].shape[0] * args[13].shape[1] * args[13].shape[2] * 2
        if n_head == 4 and held <= vmem_for_weights:
            return kernel_body(n_dp, n_head, *args)
        return body(*args)

    return jax.shard_map(program, mesh=mesh, in_specs=in_specs, out_specs=out_specs, check_vma=False)
```

```python
import functools

import jax
import jax.numpy as jnp
import numpy as np
from jax import lax
from jax.experimental import pallas as pl
from jax.experimental.pallas import tpu as pltpu
from jax.sharding import PartitionSpec as P

epsilon = 1e-06
theta = 10000.0
negative = -1e30
f32 = jnp.float32
bf16 = jnp.bfloat16
everywhere = ("dp", "head")
whole_rows = 4096
vmem_for_weights = 16 << 20
vmem_bytes = 63 << 20


def product(left, right, left_axis, right_axis):
    return lax.dot_general(
        left, right, (((left_axis,), (right_axis,)), ((), ())), preferred_element_type=f32
    )


def rms_scale(residual):
    return lax.rsqrt(jnp.mean(residual * residual, axis=-1, keepdims=True) + epsilon)


def rotary_tables(row_count, head_width):
    half_width = head_width // 2
    position = jnp.arange(row_count, dtype=f32)[:, None]
    exponent = jnp.arange(half_width, dtype=f32)[None, :]
    angles = position * jnp.power(theta, -2.0 * exponent / head_width)
    return (jnp.cos(angles), jnp.sin(angles))


def rotate(matrix, cosine, sine):
    half = matrix.shape[-1] // 2
    first, second = matrix[:, :half], matrix[:, half:]
    return jnp.concatenate([first * cosine - second * sine, second * cosine + first * sine], axis=-1)


def pick_mask(picks, expert_count):
    hits = picks[:, 0, :, None] == jnp.arange(expert_count, dtype=jnp.int32)[None, None, :]
    return jnp.any(hits, axis=1).astype(f32)


def norm_back(residual, inverse, gain, incoming):
    unit_rows = residual * inverse
    scaled = incoming * gain
    gain_grad = jnp.sum(incoming * unit_rows, axis=0)
    row_grad = inverse * (scaled - unit_rows * jnp.mean(scaled * unit_rows, axis=-1, keepdims=True))
    return (row_grad, gain_grad)


def gelu_pair(value):
    inner = jnp.tanh(0.7978845608028654 * (value + 0.044715 * value * value * value))
    slope = 0.5 * (1.0 + inner) + 0.5 * value * (1.0 - inner * inner) * 0.7978845608028654 * (
        1.0 + 3.0 * 0.044715 * value * value
    )
    return (0.5 * value * (1.0 + inner), slope)


def body(
    hidden_in,
    segments,
    value_pick,
    output_pick,
    expert_pick,
    attend_gain,
    query_weight,
    key_weight,
    value_weight,
    output_weight,
    head_router,
    expert_gain,
    router,
    expert_in,
    expert_out,
    cotangent,
):
    tokens, features = hidden_in.shape
    per_device, _, width = expert_in.shape
    head_experts = head_router.shape[2] // 2
    head_width = query_weight.shape[2]
    scale = head_width ** (-0.5)
    query_mat, key_mat, value_mat = query_weight[0], key_weight[0], value_weight[0]
    output_mat, gate_mat = output_weight[0], head_router[0]
    value_mask = pick_mask(value_pick, head_experts)
    output_mask = pick_mask(output_pick, head_experts)
    attend_scale = attend_gain.astype(f32)
    expert_scale = expert_gain.astype(f32)
    me = lax.axis_index("dp") * lax.axis_size("head") + lax.axis_index("head")

    rows = lax.all_gather(hidden_in, "head", axis=0, tiled=True)
    grouped = rows.astype(f32)
    group = grouped.shape[0]
    inverse = rms_scale(grouped)
    normed = (grouped * inverse * attend_scale).astype(bf16)
    cosine, sine = rotary_tables(group, head_width)
    queries = rotate(product(normed, query_mat, 1, 0), cosine, sine).astype(bf16)
    key_rows = rotate(product(normed, key_mat, 1, 0), cosine, sine).astype(bf16)
    squash = jax.nn.sigmoid(product(normed, gate_mat, 1, 0))
    value_gates = squash[:, :head_experts] * value_mask
    output_gates = squash[:, head_experts:] * output_mask
    expert_values = product(rows, value_mat, 1, 0).reshape(group, head_experts, head_width)
    values = jnp.sum(expert_values * value_gates[:, :, None], axis=1).astype(bf16)
    places = jnp.arange(group, dtype=jnp.int32)
    allowed = (places[None, :] <= places[:, None]) & (segments[:, None] == segments[None, :])
    scores = jnp.where(allowed, product(queries, key_rows, 1, 1) * scale, negative)
    exponents = jnp.exp(scores - jnp.max(scores, axis=-1, keepdims=True))
    probabilities = exponents / jnp.sum(exponents, axis=-1, keepdims=True)
    attended = product(probabilities.astype(bf16), values, 1, 0)
    weighted = (
        (output_gates[:, :, None] * attended[:, None, :]).reshape(group, -1).astype(bf16)
    )
    middle = hidden_in.astype(f32) + lax.psum_scatter(
        product(weighted, output_mat, 1, 0).astype(bf16), "head", scatter_dimension=0, tiled=True
    ).astype(f32)
    middle_inverse = rms_scale(middle)
    middle_normed = (middle * middle_inverse * expert_scale).astype(bf16)
    mine = me * per_device + jnp.arange(per_device, dtype=jnp.int32)
    my_router = lax.dynamic_slice_in_dim(router, me * per_device, per_device, axis=1)
    in_mat = expert_in.transpose(1, 0, 2).reshape(features, per_device * width)
    out_mat = expert_out.reshape(per_device * width, features)

    def turn(running, own):
        own_rows, own_cot, own_picks = own
        all_cot = lax.all_gather(own_cot, everywhere, axis=0, tiled=True)
        all_picks = lax.all_gather(own_picks, everywhere, axis=0, tiled=True)
        all_rows = lax.all_gather(own_rows, everywhere, axis=0, tiled=True)
        mask = jnp.any(all_picks[:, :, None] == mine[None, None, :], axis=1).astype(f32)
        gates = jax.nn.sigmoid(product(all_rows, my_router, 1, 0))
        live = gates * mask
        act, slope = gelu_pair(product(all_rows, in_mat, 1, 0).reshape(-1, per_device, width))
        lifted = product(all_cot, out_mat, 1, 1).reshape(-1, per_device, width)
        dense_grad = (jnp.sum(act * lifted, axis=-1) * live * (1.0 - gates)).astype(bf16)
        act_live = (act * live[:, :, None]).astype(bf16).reshape(-1, per_device * width)
        hidden_grad = (slope * lifted * live[:, :, None]).astype(bf16)
        hidden_grad = hidden_grad.reshape(-1, per_device * width)
        part_out = product(act_live, out_mat, 1, 0).astype(bf16)
        part_grad = (
            product(hidden_grad, in_mat, 1, 1) + product(dense_grad, my_router, 1, 1)
        ).astype(bf16)
        back = lax.psum_scatter(part_grad, everywhere, scatter_dimension=0, tiled=True)
        forth = lax.psum_scatter(part_out, everywhere, scatter_dimension=0, tiled=True)
        grads = (
            product(all_rows, hidden_grad, 0, 0),
            product(act_live, all_cot, 0, 0),
            product(dense_grad, all_rows, 0, 0),
        )
        if running is not None:
            grads = jax.tree.map(jnp.add, running, grads)
        return grads, (forth, back)

    turns = max(1, lax.axis_size("dp") * lax.axis_size("head") * tokens // whole_rows)
    owned = (middle_normed, cotangent, expert_pick)
    if turns == 1:
        grads, (summed, normed_grad) = turn(None, owned)
    else:
        owned = jax.tree.map(lambda a: a.reshape(turns, -1, a.shape[1]), owned)
        zeros = (
            jnp.zeros(in_mat.shape, f32),
            jnp.zeros(out_mat.shape, f32),
            jnp.zeros((per_device, features), f32),
        )
        grads, sums = lax.scan(turn, zeros, owned)
        summed, normed_grad = (a.reshape(tokens, features) for a in sums)
    grad_in = grads[0].reshape(features, per_device, width).transpose(1, 0, 2)
    grad_out = grads[1].reshape(per_device, width, features)
    grad_router = lax.all_gather(grads[2], everywhere, axis=0, tiled=True).T
    output = middle + summed.astype(f32)
    incoming = cotangent.astype(f32)
    row_grad, grad_gain_expert = norm_back(
        middle, middle_inverse, expert_scale, normed_grad.astype(f32)
    )
    middle_grad = incoming + row_grad
    group_grads = lax.all_gather(middle_grad.astype(bf16), "head", axis=0, tiled=True)
    weighted_grad = product(group_grads, output_mat, 1, 1).reshape(group, head_experts, head_width)
    output_grad = product(weighted, group_grads, 0, 0)
    output_gate_grad = jnp.sum(weighted_grad * attended[:, None, :], axis=-1)
    attended_grad = jnp.sum(weighted_grad * output_gates[:, :, None], axis=1).astype(bf16)
    prob_grad = product(attended_grad, values, 1, 1)
    centre = jnp.sum(probabilities * prob_grad, axis=-1, keepdims=True)
    score_grad = (probabilities * (prob_grad - centre)).astype(bf16)
    query_grad = product(score_grad, key_rows, 1, 0) * scale
    key_grad = product(score_grad, queries, 0, 0) * scale
    values_grad = product(probabilities.astype(bf16), attended_grad, 0, 0)
    expert_grad = (value_gates[:, :, None] * values_grad[:, None, :]).reshape(group, -1).astype(bf16)
    value_gate_grad = jnp.sum(expert_values * values_grad[:, None, :], axis=-1)
    query_grad = rotate(query_grad, cosine, -sine).astype(bf16)
    key_grad = rotate(key_grad, cosine, -sine).astype(bf16)
    logit_grad = (
        jnp.concatenate([value_gate_grad * value_mask, output_gate_grad * output_mask], axis=1)
        * squash
        * (1.0 - squash)
    ).astype(bf16)
    head_grads = (
        product(normed, query_grad, 0, 0),
        product(normed, key_grad, 0, 0),
        product(rows, expert_grad, 0, 0),
        output_grad,
        product(normed, logit_grad, 0, 0),
    )
    head_grads = tuple(grad.astype(bf16) for grad in head_grads)
    head_grads = tuple(grad.astype(f32)[None] for grad in lax.psum(head_grads, "dp"))
    back = (
        product(query_grad, query_mat, 1, 1)
        + product(key_grad, key_mat, 1, 1)
        + product(logit_grad, gate_mat, 1, 1)
    )
    row_back, grad_attend = norm_back(grouped, inverse, attend_scale, back)
    partial = (row_back + product(expert_grad, value_mat, 1, 1)).astype(bf16)
    input_grad = middle_grad + lax.psum_scatter(
        partial, "head", scatter_dimension=0, tiled=True
    ).astype(f32)
    grad_attend, grad_gain_expert = lax.psum((grad_attend, grad_gain_expert), everywhere)
    return (
        output,
        input_grad,
        grad_attend,
        *head_grads,
        grad_gain_expert,
        grad_router,
        grad_in,
        grad_out,
    )


MESH = pl.DeviceIdType.MESH
VM = pl.BlockSpec(memory_space=pltpu.VMEM)
ANY = pl.BlockSpec(memory_space=pl.ANY)
NN = (((1,), (0,)), ((), ()))
NT = (((1,), (1,)), ((), ()))
TN = (((0,), (0,)), ((), ()))


def dot(left, right, dims=NN):
    return lax.dot_general(left, right, dims, preferred_element_type=f32)


def at_block(block, count):
    return pl.ds(pl.multiple_of(block * count, count), count)


def remote(src, dst, send, recv, where):
    return pltpu.make_async_remote_copy(
        src_ref=src, dst_ref=dst, send_sem=send, recv_sem=recv, device_id=where, device_id_type=MESH
    )


def swap_halves(value):
    half = value.shape[-1] // 2
    return jnp.concatenate([value[:, half:], value[:, :half]], axis=-1)


def ceil_to(number, step):
    return -(-number // step) * step


def one_row(stack):
    full = stack.astype(f32)
    return jnp.concatenate([full[n : n + 1] for n in range(full.shape[0])], axis=1)


def layer_kernel(
    n_dp,
    n_head,
    x_ref,
    cot_ref,
    pick_ref,
    value_pick_ref,
    output_pick_ref,
    seg_ref,
    gain_ref,
    expert_gain_ref,
    angle_ref,
    wq_ref,
    wk_ref,
    wg_ref,
    wv_ref,
    wo_ref,
    router_ref,
    in_ref,
    out_ref,
    final_ref,
    final_x_ref,
    wide_ref,
    fin_in_ref,
    fin_out_ref,
    output_ref,
    grad_x_ref,
    picks,
    two_picks,
    w_r,
    seg,
    angles,
    w_an,
    w_v,
    w_o,
    my_router,
    w_in,
    w_out,
    rows,
    cot,
    mrs,
    das,
    turned,
    my_mask,
    all_mask,
    gates,
    q,
    k,
    v,
    vx,
    att,
    part,
    got,
    outs,
    got_out,
    lifted,
    core_out,
    acts,
    hids,
    dzs,
    datt,
    gate_grads,
    probs,
    qkz,
    vgrads,
    gain_part,
    gain_got,
    sums,
    core_got,
    chip_got,
    piece,
    blocks,
    hop_in,
    hop_out,
    local_sem,
    z_send,
    z_recv,
    w_send,
    w_recv,
    c_send,
    c_recv,
    e_send,
    e_recv,
    s_send,
    s_recv,
    t_send,
    t_recv,
    ready,
    free,
):
    middle = output_ref
    xor = jnp.bitwise_xor
    d, h = lax.axis_index("dp"), lax.axis_index("head")
    chip, core = d // 2, d % 2
    chips = n_dp // 2
    tokens, features = x_ref.shape
    per_device, _, width = in_ref.shape
    slab = per_device * width
    wide = 2 * slab
    experts = wv_ref.shape[1] // width
    named = ceil_to(n_dp * per_device, 8)
    group = tokens * n_head
    pair = 2 * tokens
    column = 256
    lanes = 128
    scale = width ** (-0.5)
    peers = (2, 3, 1)
    partner = (chip * 2 + 1 - core, h)
    own_block = at_block(h, tokens)
    own_side, other_side = at_block(core, slab), at_block(1 - core, slab)
    halves_in = (pl.ds(0, features // 2), pl.ds(features // 2, features // 2))
    halves_out = lambda side: (
        at_block(2 * side, slab // 2),
        at_block(2 * side + 1, slab // 2),
    )

    def along(step):
        return (d, xor(h, step))

    def across(step):
        return (xor(chip, step) * 2 + core, h)

    loads = []

    def load(src, dst):
        copy = pltpu.make_async_copy(src, dst, local_sem.at[len(loads)])
        copy.start()
        loads.append(copy)
        return copy

    own_weights = [load(out_ref, w_out.at[chip, own_side, :])] + [
        load(in_ref.at[e], w_in.at[chip, :, at_block(core * per_device + e, width)])
        for e in range(per_device)
    ]
    for_rows = [
        load(x_ref, rows.at[own_block, :]),
        load(wq_ref, w_an.at[:, pl.ds(0, width)]),
        load(wk_ref, w_an.at[:, pl.ds(width, width)]),
        load(wv_ref, w_v),
        load(value_pick_ref, two_picks.at[0]),
        load(output_pick_ref, two_picks.at[1]),
        load(angle_ref, angles),
    ]
    for_scores = [load(seg_ref, seg), load(wo_ref, w_o)]
    for_mask = load(pick_ref, picks)
    for_cot = load(cot_ref, cot.at[own_block, :])
    for_router = load(router_ref, w_r)

    barrier = pltpu.get_barrier_semaphore()
    friends = [along(s) for s in peers] + [partner] + [across(s) for s in range(1, chips)]
    for friend in friends:
        pl.semaphore_signal(barrier, inc=1, device_id=friend, device_id_type=MESH)
    pl.semaphore_wait(barrier, len(friends))

    right, left = (d, jnp.minimum(h + 1, n_head - 1)), (d, jnp.maximum(h - 1, 0))
    last = n_head - 1

    def pick(*by_place):
        value = jnp.int32(by_place[-1])
        for place in range(n_head - 2, -1, -1):
            value = jnp.where(h == place, by_place[place], value)
        return value

    arrival = (xor(h, 1), pick(2, 2, 1, 1), pick(3, 3, 0, 0))
    leaving = (pick(3, 3, 0, 0), pick(2, 0, 3, 1), pick(1, 2, 1, 2))

    def gather(kind, buffer):
        def go(side, step):
            sign = 1 - 2 * side
            block = jnp.clip(h - sign * step, 0, last)
            where = (d, jnp.clip(h + sign, 0, last))
            copies = []
            for half in range(2):
                here = buffer.at[at_block(2 * block + half, tokens // 2), :]
                number = (side * last + step) * 2 + half
                copies.append(
                    remote(here, here, z_send.at[kind, number], z_recv.at[kind, number], where)
                )
            return copies

        def begin(side):
            for copy in go(side, 0):
                copy.start()

        def start():
            pl.when(h < last)(lambda: begin(0))
            pl.when(h > 0)(lambda: begin(1))

        def arrive(side, step, there, onward):
            for half in range(2):

                @pl.when(there)
                def _():
                    go(side, step - 1)[half].wait_recv()
                    if onward:
                        go(side, step)[half].start()

        def stage(step, which="all"):
            nearer = jnp.where(2 * h < n_head, 0, 1)
            ways = []
            for side in (nearer, 1 - nearer):
                there = jnp.where(side == 0, h >= step, h + step <= last)
                ways.append((side, there, jnp.where(side == 0, h < last, h > 0)))
            for number, (side, there, onward) in enumerate(ways):
                if step < last and which in ("all", "duty", ("near", "far")[number]):
                    arrive(side, step, there & onward, True)
            for side, there, onward in ways:
                if which in ("all", "rest"):
                    ends_here = there if step == last else there & jnp.logical_not(onward)
                    arrive(side, step, ends_here, False)

        def follow(step):
            pl.when((h < last) & (jnp.maximum(h, 1) == step))(lambda: begin(0))
            pl.when((h > 0) & (jnp.maximum(last - h, 1) == step))(lambda: begin(1))

        def end():
            for step in range(last):
                for side, sent in (
                    (0, (h >= step) & (h < last)),
                    (1, (h + step <= last) & (h > 0)),
                ):

                    @pl.when(sent)
                    def _():
                        for copy in go(side, step):
                            copy.wait_send()

        return start, stage, end, follow

    def chain_sum(kind, parts, slots, leaving=leaving):
        def go(number):
            block = leaving[number]
            rightward = block > h
            slot = jnp.where(rightward, block - 1, last + block)
            where = (d, jnp.clip(jnp.where(rightward, h + 1, h - 1), 0, last))
            middle_one = (rightward & (h > 0)) | (jnp.logical_not(rightward) & (h < last))
            pieces = []
            for half in range(2):
                at = at_block(2 * block + half, tokens // 2)
                rows_of = pl.ds(half * (tokens // 2), tokens // 2)
                copy = remote(
                    parts.at[at, :],
                    slots.at[slot, rows_of, :],
                    z_send.at[kind, 2 * number + half],
                    z_recv.at[kind, 2 * slot + half],
                    where,
                )
                pieces.append((copy, at, slot, rows_of))
            return pieces, middle_one

        def now(number):
            pieces, middle_one = go(number)

            @pl.when(jnp.logical_not(middle_one))
            def _():
                for copy, _, _, _ in pieces:
                    copy.start()

        def later(number):
            pieces, middle_one = go(number)

            @pl.when(middle_one)
            def _():
                for copy, at, slot, rows_of in pieces:
                    copy.wait_recv()
                    parts[at, :] = parts[at, :] + slots[slot, rows_of, :]
                    copy.start()

        def end(total):
            ends = ((jnp.maximum(h - 1, 0), h > 0), (last + jnp.minimum(h, last - 1), h < last))
            for slot, there in ends:

                @pl.when(there)
                def _():
                    for half in range(2):
                        rows_of = pl.ds(half * (tokens // 2), tokens // 2)
                        remote(
                            parts.at[at_block(2 * h, tokens // 2), :],
                            slots.at[slot, rows_of, :],
                            z_send.at[kind, 0],
                            z_recv.at[kind, 2 * slot + half],
                            right,
                        ).wait_recv()
                    total[...] += slots[slot].astype(f32)

            for number in range(last):
                for copy, _, _, _ in go(number)[0]:
                    copy.wait_send()

        return now, later, end

    def spread(kind, src, dst, steps=peers):
        copies = {}
        for step in steps:
            copies[step] = remote(
                src(step), dst(step), z_send.at[kind, step - 1], z_recv.at[kind, step - 1], along(step)
            )
            copies[step].start()
        return copies

    x_start, x_stage, x_end, _ = gather(0, rows)
    for_rows[0].wait()
    x_start()

    def slot(array, place, side, half=None):
        if array == 0:
            at = halves_out(side)[half] if half is not None else at_block(side, slab)
            return w_out.at[place, at, :]
        at = halves_in[half] if half is not None else pl.ds(0, features)
        return w_in.at[place, at, at_block(side, slab)]

    def weights(number, ref, where):
        copy = remote(ref, ref, w_send.at[number], w_recv.at[number], where)
        copy.start()
        return copy

    slabs, halves_on, to_core, diagonal = {}, {}, {}, {}
    for copy in own_weights:
        copy.wait()
    for array in range(2):
        for first in range(2):
            for bit in (1, 2):
                half = bit - 1 if first == 0 else 2 - bit
                number = ((bit - 1) * 2 + half) * 2 + array
                slabs[bit, half, array] = weights(
                    number, slot(array, chip, core, half), across(bit)
                )
        to_core[0, array] = weights(12 + array, slot(array, chip, core), partner)

    for_mask.wait()
    own_picks = jnp.concatenate(
        [picks[...].astype(f32), jnp.zeros((lanes - picks.shape[0], tokens), f32)], axis=0
    ).T.astype(jnp.int32)
    lane = lax.broadcasted_iota(jnp.int32, (tokens, lanes), 1)
    for plane in range(n_head):
        expert = (lane // per_device * n_head + plane) * per_device + lane % per_device
        expert = jnp.where(lane < n_dp * per_device, expert, -1)
        hit = own_picks[:, 0:1] == expert
        for c in range(1, picks.shape[0]):
            hit = hit | (own_picks[:, c : c + 1] == expert)
        my_mask[plane] = jnp.where(hit, 1.0, 0.0).astype(bf16)
    mask_copies = spread(1, lambda s: my_mask.at[xor(h, s)], lambda s: all_mask.at[own_block, :])
    all_mask[own_block, :] = my_mask[h]

    for copy in for_rows[1:]:
        copy.wait()
    attend_gain, expert_gain = one_row(gain_ref[...]), one_row(expert_gain_ref[...])
    one_hot = lambda count: jnp.where(
        lax.broadcasted_iota(jnp.int32, (count, width), 0)
        == lax.broadcasted_iota(jnp.int32, (count, width), 1),
        1.0,
        0.0,
    ).astype(bf16)
    w_an[:, pl.ds(2 * width, width)] = dot(wg_ref[...], one_hot(wg_ref.shape[0]), TN).astype(bf16)
    uses = two_picks.shape[1]
    vgrads[:, pl.ds(0, lanes)] = jnp.concatenate(
        [
            two_picks[0].astype(f32),
            two_picks[1].astype(f32) + experts,
            jnp.zeros((lanes - 2 * uses, group), f32),
        ],
        axis=0,
    ).T.astype(bf16)
    half_lanes = lax.broadcasted_iota(jnp.int32, (1, width), 1) < width // 2

    def turns(at):
        both = angles[at, :]
        turned_over = swap_halves(both)
        return (
            jnp.where(half_lanes, both, turned_over),
            jnp.where(half_lanes, -turned_over, both),
        )

    def project(block):
        at = at_block(block, tokens)
        own = rows[at, :]
        full = own.astype(f32)
        inverse = lax.rsqrt(jnp.mean(full * full, axis=-1, keepdims=True) + epsilon)
        unit = (full * inverse * attend_gain).astype(bf16)
        qkg = dot(unit, w_an[...])
        c, s = turns(at)
        one, two = qkg[:, :width], qkg[:, width : 2 * width]
        q[at, :] = (one * c + swap_halves(one) * s).astype(bf16)
        k[at, :] = (two * c + swap_halves(two) * s).astype(bf16)
        lane = lax.broadcasted_iota(jnp.int32, (tokens, width), 1)
        chosen = vgrads[at, pl.ds(0, lanes)].astype(f32).astype(jnp.int32)
        hit = lane == chosen[:, 0:1]
        for c in range(1, 2 * uses):
            hit = hit | (lane == chosen[:, c : c + 1])
        gate = jnp.where(hit, jax.nn.sigmoid(qkg[:, 2 * width :]), 0.0)
        gates[at, :] = jnp.where(lane == width - 1, inverse, gate)
        values = dot(own, w_v[...])
        vx[at, :] = values.astype(bf16)
        value = gate[:, 0:1] * values[:, :width]
        for e in range(1, experts):
            value += gate[:, e : e + 1] * values[:, e * width : (e + 1) * width]
        v[at, :] = value.astype(bf16)

    for copy in for_scores:
        copy.wait()
    seg_col = gate_grads
    seg_col[...] = jnp.broadcast_to(seg[...].astype(f32), (lanes, group)).T

    def attend(block):
        at = at_block(block, tokens)
        score = dot(q[at, :], k[...], NT) * scale
        row = block * tokens + lax.broadcasted_iota(jnp.int32, (tokens, group), 0)
        place = lax.broadcasted_iota(jnp.int32, (tokens, group), 1)
        allowed = (place <= row) & (seg_col[at, 0:1] == seg[...].astype(f32))
        score = jnp.where(allowed, score, negative)
        exponents = jnp.exp(score - jnp.max(score, axis=-1, keepdims=True))
        chance = exponents / jnp.sum(exponents, axis=-1, keepdims=True)
        probs[at, :] = chance.astype(bf16)
        attended = dot(chance.astype(bf16), v[...])
        att[at, :] = attended
        gate = gates[at, :]
        weighted = jnp.concatenate(
            [
                (gate[:, experts + e : experts + e + 1] * attended).astype(bf16)
                for e in range(experts)
            ],
            axis=-1,
        )
        return dot(weighted, w_o[...])

    to_mid = chain_sum(3, part, got, (pick(1, 3, 0, 0), pick(2, 0, 3, 1), pick(3, 2, 1, 2)))

    def send_mid(number):
        block = pick(number + 1, *((3, 0, 0), (0, 3, 1), (2, 1, 2))[number])
        part[at_block(block, tokens), :] = attend(block).astype(bf16)
        to_mid[0](number)

    k[...] = jnp.zeros_like(k)
    v[...] = jnp.zeros_like(v)
    project(h)
    _, cot_stage, cot_end, cot_follow = gather(2, cot)
    for_cot.wait()
    for step in (1, 2, 3):
        x_stage(step)
        cot_follow(step)
        project(arrival[step - 1])
        pl.when(h == 0)(lambda: send_mid(step - 1))

    @pl.when(h > 0)
    def _():
        for number in range(last):
            send_mid(number)

    middle[...] = rows[own_block, :].astype(f32) + attend(h)
    cot_stage(1, "duty")
    to_mid[1](0)
    for array in range(2):
        for half in range(2):
            slabs[1 + half, half, array].wait_recv()
            halves_on[half, array] = weights(
                8 + 2 * half + array,
                slot(array, xor(chip, 1 + half), core, half),
                across(2 - half),
            )

    to_mid[1](1)
    cot_stage(2, "duty")
    to_mid[1](2)
    for bit in (1, 2):
        slabs[bit, 2 - bit, 0].wait_recv()
        to_core[bit, 0] = weights(14 + (bit - 1) * 2, slot(0, xor(chip, bit), core), partner)
        slabs[bit, 2 - bit, 1].wait_recv()
        to_core[bit, 1] = weights(15 + (bit - 1) * 2, slot(1, xor(chip, bit), core), partner)
    for_router.wait()
    slot_of = lax.broadcasted_iota(jnp.int32, (w_r.shape[0], lanes), 1)
    name = lax.broadcasted_iota(jnp.int32, (w_r.shape[0], lanes), 0)
    expert = (slot_of // per_device * n_head + h) * per_device + slot_of % per_device
    expert = jnp.where(slot_of < n_dp * per_device, expert, -1)
    my_router[...] = dot(
        w_r[...], jnp.where(name == expert, 1.0, 0.0).astype(bf16), TN
    ).astype(bf16)

    to_mid[2](middle)
    mid = middle[...]
    inverse = lax.rsqrt(jnp.mean(mid * mid, axis=-1, keepdims=True) + epsilon)
    mrs[own_block, :] = (mid * inverse * expert_gain).astype(bf16)
    mr_start, mr_stage, mr_end, _ = gather(4, mrs)
    mr_start()

    def last_halves(array):
        for half in range(2):
            halves_on[half, array].wait_recv()
            diagonal[half, array] = weights(
                18 + 2 * half + array, slot(array, xor(chip, 3), core, half), partner
            )

    for step in (1, 2, 3):
        cot_stage(step, "rest")
    last_halves(0)
    for step in peers:
        mask_copies[step].wait()
    cot_end()
    x_end()

    def near_weights(array):
        for bit in range(3):
            to_core[bit, array].wait_recv()

    def far_weights(array):
        for half in range(2):
            diagonal[half, array].wait_recv()

    def weights_sent():
        for array in range(2):
            for bit in range(3):
                to_core[bit, array].wait_send()
            for half in range(2):
                diagonal[half, array].wait_send()
                halves_on[half, array].wait_send()
                for bit in (1, 2):
                    slabs[bit, half, array].wait_send()

    near_weights(0)

    def lift_chip(n):
        j = xor(chip, n)
        lift = dot(cot[...], w_out[j], NT)
        lifted[j, 0] = lift[:, :slab].astype(bf16)
        lifted[j, 1] = lift[:, slab:].astype(bf16)

    pl.loop(0, chips // 2)(lift_chip)
    mr_stage(1, "near")
    pl.loop(chips // 2, chips - 1)(lift_chip)
    far_weights(0)
    lift_chip(chips - 1)
    mr_stage(1, "far")
    mr_stage(1, "rest")
    near_weights(1)

    def spread_lanes(j):
        lane = lax.broadcasted_iota(jnp.int32, (lanes, wide), 1) // width
        slot = lax.broadcasted_iota(jnp.int32, (lanes, wide), 0)
        return jnp.where(slot == lane + j * (wide // width), 1.0, 0.0).astype(bf16)

    def pair_of_blocks(number, between, before_last):
        at = at_block(number, pair)
        own = mrs[at, :]
        gates = jax.nn.sigmoid(dot(own, my_router[...]))
        live = gates * all_mask[at, :].astype(f32)
        narrow = live.astype(bf16)

        def chip_step(n, total):
            j = xor(chip, n)
            pick = spread_lanes(j)
            hidden = dot(own, w_in[j])
            gate = dot(narrow, pick).astype(bf16)
            lift = jnp.concatenate([lifted[j, 0, at, :], lifted[j, 1, at, :]], axis=-1)
            square = hidden * hidden
            inner = jnp.tanh(0.7978845608028654 * hidden * (1.0 + 0.044715 * square))
            half = 0.5 * (1.0 + inner)
            act = hidden * half
            slope = half + act * (1.0 - inner) * (
                0.7978845608028654 + (0.7978845608028654 * 3.0 * 0.044715) * square
            )
            act = act.astype(bf16)
            acts[j, at, :] = act * gate
            hids[j, at, :] = slope.astype(bf16) * (lift * gate)
            return total + dot(act * lift, pick, NT)

        total = lax.fori_loop(0, chips // 2, chip_step, jnp.zeros((pair, lanes), f32))
        between()
        total = lax.fori_loop(chips // 2, chips - 1, chip_step, total)
        before_last()
        total = chip_step(chips - 1, total)
        dz = (total * live * (1.0 - gates)).astype(bf16)
        dzs[at, :] = dz

        @pl.loop(0, features // column)
        def _(c):
            part_of = at_block(c, column)
            total = dot(dz, my_router[part_of, :], NT)
            for j in range(chips):
                total += dot(hids[j, at, :], w_in[j, part_of, :], NT)
            part[at, part_of] = total.astype(bf16)

    def outputs():
        @pl.loop(0, features // column)
        def _(c):
            part_of = at_block(c, column)
            total = dot(acts[0], w_out[0, :, part_of])
            for j in range(1, chips):
                total += dot(acts[j], w_out[j, :, part_of])
            outs[:, part_of] = total.astype(bf16)

    near = h // 2
    to_dmr = chain_sum(5, part, got)

    def halfway():
        last_halves(1)
        mr_stage(2, "duty")

    pair_of_blocks(near, halfway, lambda: far_weights(1))
    to_dmr[0](2)
    mr_stage(2, "rest")
    mr_stage(3)
    pair_of_blocks(1 - near, lambda: None, lambda: None)
    to_dmr[0](0)
    to_dmr[0](1)
    pl.semaphore_signal(ready, inc=1, device_id=partner, device_id_type=MESH)

    weights_sent()
    turned[...] = mrs[...].T

    def to_other_core(n, array):
        place = xor(chip, chips - 1 - n)
        if array == 0:
            return [
                remote(
                    w_out.at[place, other_side, :],
                    core_out.at[place],
                    c_send.at[2, n],
                    c_recv.at[2, n],
                    partner,
                )
            ]
        return [
            remote(
                w_in.at[place, halves_in[half], other_side],
                lifted.at[place, half],
                c_send.at[half, n],
                c_recv.at[half, n],
                partner,
            )
            for half in range(2)
        ]

    pl.semaphore_wait(ready, 1)
    hops = {}

    def hop(half, index, place, toward, array):
        copy = remote(
            slot(array, place, core, half),
            (hop_out, hop_in)[array].at[half, index],
            e_send.at[1 - array, 2 * half + index],
            e_recv.at[1 - array, 2 * half + index],
            across(toward),
        )
        copy.start()
        hops[half, index, array] = copy

    def both_cores(n, array):
        step = chips - 1 - n
        place = xor(chip, step)
        for copy in to_other_core(n, array):
            copy.wait()
        if array == 0:
            w_out[place, own_side, :] = w_out[place, own_side, :] + core_out[place]
        else:
            for half in range(2):
                here = (place, halves_in[half], own_side)
                w_in[here] = w_in[here] + lifted[place, half]
        if step == 3:
            hop(0, 1, place, 1, array)
            hop(1, 1, place, 2, array)
        elif step:
            hop(step - 1, 0, place, step, array)

    def expert_grads(array, place, at):
        if array == 0:
            for half in halves_in:
                w_out[place, at, half] = dot(acts[place, :, at], cot[:, half], TN).astype(bf16)
        else:
            for n in range(features // column):
                band = pl.ds(n * column, column)
                w_in[place, band, at] = dot(turned[band, :], hids[place, :, at]).astype(bf16)

    def all_grads(array):
        for n in range(chips):
            place = xor(chip, chips - 1 - n)
            expert_grads(array, place, other_side if array == 0 else slice(None))
            for copy in to_other_core(n, array):
                copy.start()
            if n:
                both_cores(n - 1, array)
            if array == 0:
                expert_grads(array, place, own_side)

    all_grads(1)
    outputs()
    both_cores(chips - 1, 1)
    to_dmr[1](0)
    all_grads(0)
    both_cores(chips - 1, 0)
    to_dmr[1](1)
    to_dmr[1](2)
    side = features // 2
    strip = side // chips
    col = lambda c, j: at_block(c * chips + j, strip)

    def section(number, first, count):
        at = pl.ds(first, count)
        state = {}

        def sem(n):
            return s_send.at[number, n], s_recv.at[number, n]

        def start():
            state["core"] = remote(
                sums.at[at, at_block(1 - core, side)], core_got.at[at, :], *sem(0), partner
            )
            state["core"].start()

        def mid():
            state["core"].wait()
            half = at_block(core, side)
            sums[at, half] = sums[at, half] + core_got[at, :]
            state["chips"] = []
            for s in range(1, chips):
                copy = remote(
                    sums.at[at, col(core, xor(chip, s))], chip_got.at[s - 1, at, :], *sem(s), across(s)
                )
                copy.start()
                state["chips"].append(copy)

        def add():
            for copy in state["chips"]:
                copy.wait()
            total = sums[at, col(core, chip)].astype(f32)
            for s in range(1, chips):
                total += chip_got[s - 1, at, :].astype(f32)
            piece[at, :] = total.astype(bf16)

        return start, mid, add

    def two_hop_section(number, first, count):
        at = pl.ds(first, count)
        half_at = [pl.ds(first + n * (count // 2), count // 2) for n in range(2)]
        begin, state = section(number, first, count)[0], {}

        def hop(half, index, place, toward, n):
            copy = remote(
                sums.at[half_at[half], col(core, place)],
                chip_got.at[index, half_at[half], :],
                t_send.at[number, n],
                t_recv.at[number, n],
                across(toward),
            )
            copy.start()
            return copy

        def mid():
            over = remote(
                sums.at[at, at_block(1 - core, side)],
                core_got.at[at, :],
                s_send.at[number, 0],
                s_recv.at[number, 0],
                partner,
            )
            over.wait()
            half = at_block(core, side)
            sums[at, half] = sums[at, half] + core_got[at, :]
            for half in range(2):
                toward = 1 + half
                state[half, 1] = hop(half, 1, xor(chip, 3), toward, 2 * half + 1)
                state[half, 0] = hop(half, 0, xor(chip, toward), toward, 2 * half)

        def second():
            for half in range(2):
                here = (half_at[half], col(core, xor(chip, 2 - half)))
                state[half, 1].wait()
                sums[here] = sums[here] + chip_got[1, half_at[half], :]
                state[half, 2] = hop(half, 2, xor(chip, 2 - half), 2 - half, 4 + half)

        def add():
            for half in range(2):
                state[half, 0].wait()
                state[half, 2].wait()
            total = sums[at, col(core, chip)].astype(f32)
            for index in (0, 2):
                total += chip_got[index, at, :].astype(f32)
            piece[at, :] = total.astype(bf16)

        return begin, mid, second, add

    def two_hop_to_plane(number, first, count):
        at = pl.ds(first, count)
        half_at = [pl.ds(first + n * (count // 2), count // 2) for n in range(2)]
        state = {}

        def send(src, rows_of, place, where, n):
            copy = remote(
                src,
                wide_ref.at[rows_of, col(core, place)],
                t_send.at[number, n],
                t_recv.at[number, n],
                where,
            )
            copy.start()
            return copy

        def start():
            for urgent in range(2):
                for bit in (1, 2):
                    half = bit - 1 if urgent == 0 else 2 - bit
                    state[bit, half] = send(
                        piece.at[half_at[half], :],
                        half_at[half],
                        chip,
                        across(bit),
                        6 + 2 * (bit - 1) + half,
                    )
            over = send(piece.at[at, :], at, chip, partner, 12)
            own = pltpu.make_async_copy(
                piece.at[at, :], wide_ref.at[at, col(core, chip)], t_send.at[number, 15]
            )
            own.start()
            state["wait"] = [over, own]

        def relay():
            for half in range(2):
                bit = 1 + half
                state[bit, half].wait_recv()
                place = xor(chip, bit)
                here = wide_ref.at[half_at[half], col(core, place)]
                state[3, half] = send(here, half_at[half], place, across(2 - half), 10 + half)

        def forward():
            for bit in (1, 2):
                state[bit, 2 - bit].wait_recv()
                place = xor(chip, bit)
                here = wide_ref.at[at, col(core, place)]
                state["wait"].append(send(here, at, place, partner, 12 + bit))

        def end():
            for half in range(2):
                state[3, half].wait_recv()
            place = xor(chip, 3)
            here = wide_ref.at[at, col(core, place)]
            state["wait"].append(send(here, at, place, partner, 16))

        def done():
            for copy in state["wait"]:
                copy.wait()
            for half in range(2):
                state[3, half].wait_send()
                for bit in (1, 2):
                    state[bit, half].wait_send()

        return start, relay, forward, end, done

    def to_plane(number, src, rows_to):
        state = {}

        def sem(n):
            return s_send.at[number, chips + n], s_recv.at[number, chips + n]

        def start():
            here = wide_ref.at[rows_to, col(core, chip)]
            state["share"] = [remote(src, here, *sem(s), across(s)) for s in range(1, chips)]
            over = remote(src, here, *sem(0), partner)
            own = pltpu.make_async_copy(src, here, s_send.at[number, 3 * chips - 1])
            state["wait"] = [over, own]
            for copy in state["share"] + state["wait"]:
                copy.start()

        def forward():
            for s in range(1, chips):
                state["share"][s - 1].wait()
                here = wide_ref.at[rows_to, col(core, xor(chip, s))]
                copy = remote(here, here, *sem(chips - 1 + s), partner)
                copy.start()
                state["wait"].append(copy)

        def end():
            for copy in state["wait"]:
                copy.wait()

        return start, forward, end

    mixed = w_o.shape[0]
    small = ceil_to(named + 1, 16)
    at_a = pl.ds(features, 16)
    at_o = pl.ds(features + 16, mixed)
    at_g = pl.ds(features + 16 + mixed, small)
    of_d = [two_hop_section(n, n * features // 2, features // 2) for n in range(2)]
    of_o = two_hop_section(2, features + 16, mixed)
    of_g = section(3, features + 16 + mixed, small)
    of_a = section(4, features, 16)
    out_d = [two_hop_to_plane(n, n * features // 2, features // 2) for n in range(2)]
    out_o = two_hop_to_plane(2, features + 16, mixed)
    out_g = to_plane(3, blocks, pl.ds(features + 16 + mixed, n_head * small))
    out_a = to_plane(4, piece.at[at_a, :], at_a)
    router_part = dot(dzs[...], mrs[...], TN)[:named]

    grad_x_ref[...] = part[own_block, :].astype(f32)
    to_dmr[2](grad_x_ref)
    incoming = grad_x_ref[...]
    mid = middle[...]
    inverse = lax.rsqrt(jnp.mean(mid * mid, axis=-1, keepdims=True) + epsilon)
    unit = mid * inverse
    scaled = incoming * expert_gain
    dmid = cot[own_block, :].astype(f32) + inverse * (
        scaled - unit * jnp.mean(scaled * unit, axis=-1, keepdims=True)
    )
    grad_x_ref[...] = dmid
    das[own_block, :] = dmid.astype(bf16)
    da_start, da_stage, da_end, _ = gather(6, das)
    da_start()
    sums[at_g, :] = jnp.concatenate(
        [
            router_part,
            jnp.sum(incoming * unit, axis=0, keepdims=True),
            jnp.zeros((small - named - 1, features), f32),
        ],
        axis=0,
    ).astype(bf16)
    of_g[0]()
    turned[...] = rows[...].T
    of_g[1]()
    lasts = {}

    def first_hop(half, index, place):
        for array in range(2):
            hops[half, index, array].wait()
        at_in = (place, halves_in[half], own_side)
        at_out = (place, halves_out(core)[half], slice(None))
        w_in[at_in] = w_in[at_in] + hop_in[half, index]
        w_out[at_out] = w_out[at_out] + hop_out[half, index]

    for half in range(2):
        toward = 2 - half
        place = xor(chip, toward)
        first_hop(half, 1, place)
        pl.semaphore_signal(free.at[half], inc=1, device_id=across(toward), device_id_type=MESH)
        pl.semaphore_wait(free.at[half], 1)
        lasts[half] = (
            remote(
                slot(1, place, core, half),
                hop_in.at[half, 1],
                e_send.at[0, 4 + half],
                e_recv.at[0, 4 + half],
                across(toward),
            ),
            remote(
                slot(0, place, core, half),
                hop_out.at[half, 1],
                e_send.at[1, 4 + half],
                e_recv.at[1, 4 + half],
                across(toward),
            ),
        )
        for copy in lasts[half]:
            copy.start()
    lane = lax.broadcasted_iota(jnp.int32, (tokens, width), 1)

    def through_output(block):
        at = at_block(block, tokens)
        all_five = dot(das[at, :], w_o[...], NT)
        attended = att[at, :]
        total = jnp.zeros((tokens, width), f32)
        gate = jnp.zeros((tokens, width), f32)
        for e in range(experts):
            one = all_five[:, e * width : (e + 1) * width]
            total += gates[at, experts + e : experts + e + 1] * one
            gate = jnp.where(
                lane == experts + e, jnp.sum(one * attended, axis=-1, keepdims=True), gate
            )
        datt[at, :] = total.astype(bf16)
        gate_grads[at, :] = gate

    through_output(h)
    to_out = chain_sum(7, outs, got_out)
    for step in (1, 2, 3):
        da_stage(step)
        if step == 1:
            for number in range(last):
                to_out[0](number)
        through_output(arrival[step - 1])

    for e in range(experts):
        one = (gates[:, experts + e : experts + e + 1] * att[...]).astype(bf16)
        sums[pl.ds(features + 16 + e * width, width), :] = dot(one, das[...], TN).astype(bf16)
    of_o[0]()

    @pl.loop(0, n_head)
    def _(block):
        at = at_block(block, tokens)
        chance = probs[at, :].astype(f32)
        dprob = dot(datt[at, :], v[...], NT)
        centre = jnp.sum(chance * dprob, axis=-1, keepdims=True)
        vgrads[at, pl.ds(0, group)] = (chance * (dprob - centre)).astype(bf16)

    dq = dot(vgrads[:, pl.ds(0, group)], k[...]) * scale
    dk = dot(vgrads[:, pl.ds(0, group)], q[...], TN) * scale
    dv = dot(probs[...], datt[...], TN)
    of_o[1]()
    c, s = turns(slice(None))
    qkz[:, pl.ds(0, width)] = (dq * c - swap_halves(dq) * s).astype(bf16)
    qkz[:, pl.ds(width, width)] = (dk * c - swap_halves(dk) * s).astype(bf16)
    gate = gate_grads[...]
    lane = lax.broadcasted_iota(jnp.int32, (group, width), 1)
    for e in range(experts):
        vgrads[:, pl.ds(e * width, width)] = (gates[:, e : e + 1] * dv).astype(bf16)
        one = jnp.sum(vx[:, pl.ds(e * width, width)].astype(f32) * dv, axis=-1, keepdims=True)
        gate = jnp.where(lane == e, one, gate)
    qkz[:, pl.ds(2 * width, width)] = (gate * gates[...] * (1.0 - gates[...])).astype(bf16)

    scaled_qkz = (qkz[...].astype(f32) * gates[:, width - 1 : width]).astype(bf16)

    def matrix_rows(c):
        at = at_block(c, column)
        sums[at, pl.ds(0, 3 * width)] = dot(turned[at, :], scaled_qkz).astype(bf16)
        sums[at, pl.ds(3 * width, experts * width)] = dot(turned[at, :], vgrads[...]).astype(bf16)

    steps_each = features // column // 2
    for n in range(2):
        pl.loop(n * steps_each, (n + 1) * steps_each)(matrix_rows)
        of_d[n][0]()
    def into_rows(block):
        at = at_block(block, tokens)
        inverse = gates[at, width - 1 : width]
        unit = rows[at, :].astype(f32) * inverse
        through = dot(qkz[at, :], w_an[...], NT)
        scaled = through * attend_gain
        total = inverse * (
            scaled - unit * jnp.mean(scaled * unit, axis=-1, keepdims=True)
        ) + dot(vgrads[at, :], w_v[...], NT)
        return total, jnp.sum(through * unit, axis=0, keepdims=True)

    to_x = chain_sum(8, part, got)
    gain = jnp.zeros((1, features), f32)
    for number in range(last):
        total, one = into_rows(leaving[number])
        gain += one
        part[at_block(leaving[number], tokens), :] = total.astype(bf16)
        to_x[0](number)
        if number < 2:
            of_d[number][1]()
    total, one = into_rows(h)
    sums[at_a, :] = jnp.broadcast_to(gain + one, (16, features)).astype(bf16)
    of_a[0]()
    grad_x_ref[...] += total
    to_out[1](0)
    to_out[1](1)
    of_a[1]()
    of_o[2]()
    to_x[1](0)
    of_d[0][2]()
    of_d[1][2]()
    of_g[2]()
    small_block = at_block(h, small)
    blocks[small_block, :] = piece[at_g, :]
    g_copies = spread(9, lambda s: blocks.at[small_block, :], lambda s: blocks.at[small_block, :])
    to_x[1](1)
    of_o[3]()
    out_o[0]()
    to_x[1](2)
    of_d[0][3]()
    out_d[0][0]()
    of_d[1][3]()
    out_d[1][0]()
    of_a[2]()
    gain_part[...] = piece[at_a, :]
    gain_copies = spread(10, lambda s: gain_part, lambda s: gain_got.at[s - 1])
    to_out[1](2)
    out_o[1]()
    for step in peers:
        g_copies[step].wait()
    out_g[0]()
    out_d[0][1]()
    gain = gain_part[...].astype(f32)
    for step in peers:
        gain_copies[step].wait()
        gain += gain_got[step - 1].astype(f32)
    piece[at_a, :] = gain.astype(bf16)
    out_a[0]()
    out_d[1][1]()
    out_o[2]()
    to_x[2](grad_x_ref)
    rows_out = [pltpu.make_async_copy(grad_x_ref, final_x_ref, local_sem.at[2])]
    rows_out[0].start()
    output_ref[...] = middle[...] + outs[own_block, :].astype(f32)
    to_out[2](output_ref)
    rows_out.append(pltpu.make_async_copy(output_ref, final_ref, local_sem.at[3]))
    rows_out[1].start()
    for half in range(2):
        first_hop(half, 0, chip)
        for copy in lasts[half]:
            copy.wait()
        at_in = (chip, halves_in[half], own_side)
        at_out = (chip, halves_out(core)[half], slice(None))
        w_in[at_in] = w_in[at_in] + hop_in[half, 1]
        w_out[at_out] = w_out[at_out] + hop_out[half, 1]
    stores = (
        pltpu.make_async_copy(w_in.at[chip, :, own_side], fin_in_ref, local_sem.at[0]),
        pltpu.make_async_copy(w_out.at[chip, own_side, :], fin_out_ref, local_sem.at[1]),
    )
    for store in stores:
        store.start()
    out_o[3]()
    out_d[0][2]()
    out_g[1]()
    out_a[1]()
    out_d[1][2]()
    out_d[0][3]()
    out_d[1][3]()
    for one in (out_o, out_d[0], out_g, out_a, out_d[1]):
        one[-1]()
    for store in (*stores, *rows_out):
        store.wait()
    mr_end()
    da_end()


def layer_call(n_dp, n_head, args):
    x, picks, router, value_mat, expert_in = args[0], args[2], args[14], args[12], args[15]
    tokens, features = x.shape
    per_device, _, width = expert_in.shape
    held_experts = value_mat.shape[1]
    group = tokens * n_head
    chips = n_dp // 2
    slab = per_device * width
    lanes = 128
    peers = n_head - 1
    named = ceil_to(n_dp * per_device, 8)
    small = ceil_to(named + 1, 16)
    top = features + held_experts
    held = top + 16 + small
    strip = features // n_dp
    shape = jax.ShapeDtypeStruct
    vm, dma = pltpu.VMEM, pltpu.SemaphoreType.DMA
    outs = [
        (shape((tokens, features), f32), ANY),
        (shape((tokens, features), f32), ANY),
        (shape((top + 16 + n_head * small, features), bf16), ANY),
        (shape((features, slab), bf16), ANY),
        (shape((slab, features), bf16), ANY),
    ]
    scratch = dict(
        output_rows=vm((tokens, features), f32),
        grad_rows=vm((tokens, features), f32),
        picks=vm(picks.shape, jnp.int32),
        two_picks=vm((2, *args[3].shape), jnp.int32),
        w_r=vm(router.shape, bf16),
        seg=vm((1, group), jnp.int32),
        angles=vm((group, width), f32),
        w_an=vm((features, 3 * width), bf16),
        w_v=vm((features, held_experts), bf16),
        w_o=vm((held_experts, features), bf16),
        my_router=vm((features, lanes), bf16),
        w_in=vm((chips, features, 2 * slab), bf16),
        w_out=vm((chips, 2 * slab, features), bf16),
        rows=vm((group, features), bf16),
        cot=vm((group, features), bf16),
        mrs=vm((group, features), bf16),
        das=vm((group, features), bf16),
        turned=vm((features, group), bf16),
        my_mask=vm((n_head, tokens, lanes), bf16),
        all_mask=vm((group, lanes), bf16),
        gates=vm((group, width), f32),
        q=vm((group, width), bf16),
        k=vm((group, width), bf16),
        v=vm((group, width), bf16),
        vx=vm((group, held_experts), bf16),
        att=vm((group, width), f32),
        part=vm((group, features), bf16),
        got=vm((2 * peers, tokens, features), bf16),
        outs=vm((group, features), bf16),
        got_out=vm((2 * peers, tokens, features), bf16),
        lifted=vm((chips, 2, group, slab), bf16),
        core_out=vm((chips, slab, features), bf16),
        acts=vm((chips, group, 2 * slab), bf16),
        hids=vm((chips, group, 2 * slab), bf16),
        dzs=vm((group, lanes), bf16),
        datt=vm((group, width), bf16),
        gate_grads=vm((group, width), f32),
        probs=vm((group, group), bf16),
        qkz=vm((group, 3 * width), bf16),
        vgrads=vm((group, held_experts), bf16),
        gain_part=vm((16, strip), bf16),
        gain_got=vm((peers, 16, strip), bf16),
        sums=vm((held, features), bf16),
        core_got=vm((held, features // 2), bf16),
        chip_got=vm((chips - 1, held, strip), bf16),
        piece=vm((held, strip), bf16),
        blocks=vm((n_head * small, strip), bf16),
        hop_in=vm((2, 2, features // 2, slab), bf16),
        hop_out=vm((2, 2, slab // 2, features), bf16),
        local_sem=dma((17 + 1 + per_device,)),
        z_send=dma((11, 4 * peers)),
        z_recv=dma((11, 4 * peers)),
        w_send=dma((22,)),
        w_recv=dma((22,)),
        c_send=dma((3, chips)),
        c_recv=dma((3, chips)),
        e_send=dma((2, 6)),
        e_recv=dma((2, 6)),
        s_send=dma((5, 3 * chips)),
        s_recv=dma((5, 3 * chips)),
        t_send=dma((3, 17)),
        t_recv=dma((3, 17)),
        ready=pltpu.SemaphoreType.REGULAR,
        free=pltpu.SemaphoreType.REGULAR((2,)),
    )
    return pl.pallas_call(
        functools.partial(layer_kernel, n_dp, n_head),
        out_shape=[o[0] for o in outs],
        out_specs=[o[1] for o in outs],
        in_specs=[VM if number in (6, 7, 11) else ANY for number in range(17)],
        scratch_shapes=list(scratch.values()),
        compiler_params=pltpu.CompilerParams(
            collective_id=1, has_side_effects=True, vmem_limit_bytes=vmem_bytes
        ),
    )(*args)


def finish_kernel(
    n_dp,
    n_head,
    output_ref,
    grad_x_ref,
    wide_ref,
    in_ref,
    out_ref,
    gain_ref,
    final_ref,
    input_ref,
    attend_ref,
    query_ref,
    key_ref,
    value_ref,
    mix_ref,
    gate_ref,
    expert_ref,
    router_ref,
    grad_in_ref,
    grad_out_ref,
    wide,
    flat_in,
    flat_out,
    value,
    mix,
    grad_in,
    grad_out,
    output,
    grad_x,
    query,
    key,
    sem,
):
    features, slab = in_ref.shape
    per_device, _, width = grad_in_ref.shape
    experts_total, gates = router_ref.shape[0], gate_ref.shape[0]
    mixed = mix_ref.shape[0]
    top = features + 16 + mixed
    small = (wide_ref.shape[0] - top) // n_head
    named = n_dp * per_device

    numbers = iter(range(sem.shape[0]))

    def copy(src, dst):
        one = pltpu.make_async_copy(src, dst, sem.at[next(numbers)])
        one.start()
        return one

    bands = 4
    band = features // bands
    load = lambda first, count: copy(
        wide_ref.at[pl.ds(first, count), :], wide.at[pl.ds(first, count), :]
    )
    plain = [(copy(output_ref, output), output, final_ref), (copy(grad_x_ref, grad_x), grad_x, input_ref)]
    for_out, for_in = copy(out_ref, flat_out), copy(in_ref, flat_in)
    for_bands = [load(n * band, band) for n in range(bands)]
    for_mix = [load(features + 16 + n * mixed // 2, mixed // 2) for n in range(2)]
    others = [load(features, 16), load(top, n_head * small)]
    stores = []
    gain = jnp.broadcast_to(one_row(gain_ref[...]), (width, features)).T
    for loaded, held, result in plain:
        loaded.wait()
        stores.append(copy(held, result))
    for_out.wait()
    for e in range(per_device):
        grad_out[e] = flat_out[pl.ds(e * width, width), :].astype(f32)
        stores.append(copy(grad_out.at[e], grad_out_ref.at[e]))
    for_in.wait()
    for e in range(per_device):
        grad_in[e] = flat_in[:, pl.ds(e * width, width)].astype(f32)
        stores.append(copy(grad_in.at[e], grad_in_ref.at[e]))
    for n in range(bands):
        for_bands[n].wait()
        at = pl.ds(n * band, band)
        scale = gain[n * band : (n + 1) * band]
        value[at, :] = wide[at, pl.ds(3 * width, value.shape[1])].astype(f32)
        stores.append(copy(value.at[at, :], value_ref.at[at, :]))
        query[at, :] = wide[at, pl.ds(0, width)].astype(f32) * scale
        stores.append(copy(query.at[at, :], query_ref.at[at, :]))
        key[at, :] = wide[at, pl.ds(width, width)].astype(f32) * scale
        stores.append(copy(key.at[at, :], key_ref.at[at, :]))
    for n in range(2):
        for_mix[n].wait()
        at = pl.ds(n * mixed // 2, mixed // 2)
        mix[at, :] = wide[pl.ds(features + 16 + n * mixed // 2, mixed // 2), :].astype(f32)
        stores.append(copy(mix.at[at, :], mix_ref.at[at, :]))
    turned = (wide[pl.ds(0, features), pl.ds(2 * width, width)].astype(f32) * gain).T
    for e in range(gates):
        gate_ref[e] = turned[e : e + 1]
    for loaded in others:
        loaded.wait()
    attend_ref[...] = wide[pl.ds(features, 16), :][0:1].astype(f32)
    planes = wide[pl.ds(top, n_head * small), :]
    place = lax.broadcasted_iota(jnp.int32, (n_head * small, experts_total), 0)
    name = lax.broadcasted_iota(jnp.int32, (n_head * small, experts_total), 1)
    slot, plane = place % small, place // small
    expert = (slot // per_device * n_head + plane) * per_device + slot % per_device
    chosen = (slot < named) & (expert == name)
    router_ref[...] = dot(jnp.where(chosen, 1.0, 0.0).astype(bf16), planes, TN)
    gain = jnp.zeros((1, features), f32)
    for z in range(n_head):
        row = z * small + ceil_to(named, 8)
        gain += planes[row : row + 1].astype(f32)
    expert_ref[...] = gain
    for store in stores:
        store.wait()


def finish_call(n_dp, n_head, shapes, args):
    shape = jax.ShapeDtypeStruct
    wide, flat_in, flat_out = args[2], args[3], args[4]
    value, mix, grad_in, grad_out = shapes[5], shapes[6], shapes[10], shapes[11]
    specs = [VM] * 12
    for number in (0, 1, 3, 4, 5, 6, 10, 11):
        specs[number] = ANY
    return pl.pallas_call(
        functools.partial(finish_kernel, n_dp, n_head),
        out_shape=[shape(s, f32) for s in shapes],
        out_specs=specs,
        in_specs=[ANY] * 5 + [VM],
        scratch_shapes=[
            pltpu.VMEM(wide.shape, bf16),
            pltpu.VMEM(flat_in.shape, bf16),
            pltpu.VMEM(flat_out.shape, bf16),
            pltpu.VMEM(value, f32),
            pltpu.VMEM(mix, f32),
            pltpu.VMEM(grad_in, f32),
            pltpu.VMEM(grad_out, f32),
            pltpu.VMEM(shapes[0], f32),
            pltpu.VMEM(shapes[1], f32),
            pltpu.VMEM(shapes[3], f32),
            pltpu.VMEM(shapes[4], f32),
            pltpu.SemaphoreType.DMA((40,)),
        ],
        compiler_params=pltpu.CompilerParams(vmem_limit_bytes=60 << 20),
    )(*args)


def kernel_body(
    n_dp,
    n_head,
    hidden_in,
    segments,
    value_pick,
    output_pick,
    expert_pick,
    attend_gain,
    query_weight,
    key_weight,
    value_weight,
    output_weight,
    head_router,
    expert_gain,
    router,
    expert_in,
    expert_out,
    cotangent,
):
    tokens, features = hidden_in.shape
    per_device, _, width = expert_in.shape
    experts = head_router.shape[2] // 2
    group = tokens * n_head
    angles = np.arange(group)[:, None] * theta ** (-2.0 * np.arange(width // 2) / width)[None, :]
    angles = np.concatenate([np.cos(angles), np.sin(angles)], axis=1).astype(np.float32)
    stacked = lambda gain: gain.reshape(-1, 128).astype(f32)
    results = layer_call(
        n_dp,
        n_head,
        (
            hidden_in,
            cotangent,
            expert_pick.T,
            value_pick.transpose(1, 2, 0)[0],
            output_pick.transpose(1, 2, 0)[0],
            segments[None, :],
            stacked(attend_gain),
            stacked(expert_gain),
            angles,
            query_weight[0],
            key_weight[0],
            head_router.transpose(0, 2, 1)[0],
            value_weight[0],
            output_weight[0],
            router.T,
            expert_in,
            expert_out.reshape(per_device * width, features),
        ),
    )
    shapes = (
        (tokens, features),
        (tokens, features),
        (1, features),
        query_weight.shape[1:],
        key_weight.shape[1:],
        value_weight.shape[1:],
        output_weight.shape[1:],
        (2 * experts, 1, features),
        (1, features),
        (router.shape[1], features),
        expert_in.shape,
        expert_out.shape,
    )
    done = list(finish_call(n_dp, n_head, shapes, (*results, stacked(attend_gain))))
    for number in (3, 4, 5, 6):
        done[number] = done[number][None]
    done[7] = done[7].transpose(1, 2, 0)
    done[9] = done[9].T
    done[2], done[8] = done[2][0], done[8][0]
    return tuple(done)


def solution(mesh):
    rows = P(everywhere, None)
    heads = P("head", None, None)
    experts = P(everywhere, None, None)
    picks = P("dp", "head", None)
    in_specs = (
        rows, P("dp"), picks, picks, rows, P(), heads, heads, heads, heads, heads,
        P(), P(), experts, experts, rows,
    )
    out_specs = (
        rows, rows, P(), heads, heads, heads, heads, heads, P(), P(), experts, experts,
    )
    n_dp, n_head = mesh.shape["dp"], mesh.shape["head"]

    def program(*args):
        held = 2 * n_dp * args[13].shape[0] * args[13].shape[1] * args[13].shape[2] * 2
        if n_head == 4 and held <= vmem_for_weights:
            return kernel_body(n_dp, n_head, *args)
        return body(*args)

    return jax.shard_map(program, mesh=mesh, in_specs=in_specs, out_specs=out_specs, check_vma=False)
```

```python
import functools

import jax
import jax.numpy as jnp
import numpy as np
from jax import lax
from jax.experimental import pallas as pl
from jax.experimental.pallas import tpu as pltpu
from jax.sharding import PartitionSpec as P

epsilon = 1e-06
theta = 10000.0
negative = -1e30
f32 = jnp.float32
bf16 = jnp.bfloat16
everywhere = ("dp", "head")
whole_rows = 4096
vmem_for_weights = 16 << 20
vmem_bytes = 62 << 20


def product(left, right, left_axis, right_axis):
    return lax.dot_general(
        left, right, (((left_axis,), (right_axis,)), ((), ())), preferred_element_type=f32
    )


def rms_scale(residual):
    return lax.rsqrt(jnp.mean(residual * residual, axis=-1, keepdims=True) + epsilon)


def rotary_tables(row_count, head_width):
    half_width = head_width // 2
    position = jnp.arange(row_count, dtype=f32)[:, None]
    exponent = jnp.arange(half_width, dtype=f32)[None, :]
    angles = position * jnp.power(theta, -2.0 * exponent / head_width)
    return (jnp.cos(angles), jnp.sin(angles))


def rotate(matrix, cosine, sine):
    half = matrix.shape[-1] // 2
    first, second = matrix[:, :half], matrix[:, half:]
    return jnp.concatenate([first * cosine - second * sine, second * cosine + first * sine], axis=-1)


def pick_mask(picks, expert_count):
    hits = picks[:, 0, :, None] == jnp.arange(expert_count, dtype=jnp.int32)[None, None, :]
    return jnp.any(hits, axis=1).astype(f32)


def norm_back(residual, inverse, gain, incoming):
    unit_rows = residual * inverse
    scaled = incoming * gain
    gain_grad = jnp.sum(incoming * unit_rows, axis=0)
    row_grad = inverse * (scaled - unit_rows * jnp.mean(scaled * unit_rows, axis=-1, keepdims=True))
    return (row_grad, gain_grad)


def gelu_pair(value):
    inner = jnp.tanh(0.7978845608028654 * (value + 0.044715 * value * value * value))
    slope = 0.5 * (1.0 + inner) + 0.5 * value * (1.0 - inner * inner) * 0.7978845608028654 * (
        1.0 + 3.0 * 0.044715 * value * value
    )
    return (0.5 * value * (1.0 + inner), slope)


def body(
    hidden_in,
    segments,
    value_pick,
    output_pick,
    expert_pick,
    attend_gain,
    query_weight,
    key_weight,
    value_weight,
    output_weight,
    head_router,
    expert_gain,
    router,
    expert_in,
    expert_out,
    cotangent,
):
    tokens, features = hidden_in.shape
    per_device, _, width = expert_in.shape
    head_experts = head_router.shape[2] // 2
    head_width = query_weight.shape[2]
    scale = head_width ** (-0.5)
    query_mat, key_mat, value_mat = query_weight[0], key_weight[0], value_weight[0]
    output_mat, gate_mat = output_weight[0], head_router[0]
    value_mask = pick_mask(value_pick, head_experts)
    output_mask = pick_mask(output_pick, head_experts)
    attend_scale = attend_gain.astype(f32)
    expert_scale = expert_gain.astype(f32)
    me = lax.axis_index("dp") * lax.axis_size("head") + lax.axis_index("head")

    rows = lax.all_gather(hidden_in, "head", axis=0, tiled=True)
    grouped = rows.astype(f32)
    group = grouped.shape[0]
    inverse = rms_scale(grouped)
    normed = (grouped * inverse * attend_scale).astype(bf16)
    cosine, sine = rotary_tables(group, head_width)
    queries = rotate(product(normed, query_mat, 1, 0), cosine, sine).astype(bf16)
    key_rows = rotate(product(normed, key_mat, 1, 0), cosine, sine).astype(bf16)
    squash = jax.nn.sigmoid(product(normed, gate_mat, 1, 0))
    value_gates = squash[:, :head_experts] * value_mask
    output_gates = squash[:, head_experts:] * output_mask
    expert_values = product(rows, value_mat, 1, 0).reshape(group, head_experts, head_width)
    values = jnp.sum(expert_values * value_gates[:, :, None], axis=1).astype(bf16)
    places = jnp.arange(group, dtype=jnp.int32)
    allowed = (places[None, :] <= places[:, None]) & (segments[:, None] == segments[None, :])
    scores = jnp.where(allowed, product(queries, key_rows, 1, 1) * scale, negative)
    exponents = jnp.exp(scores - jnp.max(scores, axis=-1, keepdims=True))
    probabilities = exponents / jnp.sum(exponents, axis=-1, keepdims=True)
    attended = product(probabilities.astype(bf16), values, 1, 0)
    weighted = (
        (output_gates[:, :, None] * attended[:, None, :]).reshape(group, -1).astype(bf16)
    )
    middle = hidden_in.astype(f32) + lax.psum_scatter(
        product(weighted, output_mat, 1, 0).astype(bf16), "head", scatter_dimension=0, tiled=True
    ).astype(f32)
    middle_inverse = rms_scale(middle)
    middle_normed = (middle * middle_inverse * expert_scale).astype(bf16)
    mine = me * per_device + jnp.arange(per_device, dtype=jnp.int32)
    my_router = lax.dynamic_slice_in_dim(router, me * per_device, per_device, axis=1)
    in_mat = expert_in.transpose(1, 0, 2).reshape(features, per_device * width)
    out_mat = expert_out.reshape(per_device * width, features)

    def turn(running, own):
        own_rows, own_cot, own_picks = own
        all_cot = lax.all_gather(own_cot, everywhere, axis=0, tiled=True)
        all_picks = lax.all_gather(own_picks, everywhere, axis=0, tiled=True)
        all_rows = lax.all_gather(own_rows, everywhere, axis=0, tiled=True)
        mask = jnp.any(all_picks[:, :, None] == mine[None, None, :], axis=1).astype(f32)
        gates = jax.nn.sigmoid(product(all_rows, my_router, 1, 0))
        live = gates * mask
        act, slope = gelu_pair(product(all_rows, in_mat, 1, 0).reshape(-1, per_device, width))
        lifted = product(all_cot, out_mat, 1, 1).reshape(-1, per_device, width)
        dense_grad = (jnp.sum(act * lifted, axis=-1) * live * (1.0 - gates)).astype(bf16)
        act_live = (act * live[:, :, None]).astype(bf16).reshape(-1, per_device * width)
        hidden_grad = (slope * lifted * live[:, :, None]).astype(bf16)
        hidden_grad = hidden_grad.reshape(-1, per_device * width)
        part_out = product(act_live, out_mat, 1, 0).astype(bf16)
        part_grad = (
            product(hidden_grad, in_mat, 1, 1) + product(dense_grad, my_router, 1, 1)
        ).astype(bf16)
        back = lax.psum_scatter(part_grad, everywhere, scatter_dimension=0, tiled=True)
        forth = lax.psum_scatter(part_out, everywhere, scatter_dimension=0, tiled=True)
        grads = (
            product(all_rows, hidden_grad, 0, 0),
            product(act_live, all_cot, 0, 0),
            product(dense_grad, all_rows, 0, 0),
        )
        if running is not None:
            grads = jax.tree.map(jnp.add, running, grads)
        return grads, (forth, back)

    turns = max(1, lax.axis_size("dp") * lax.axis_size("head") * tokens // whole_rows)
    owned = (middle_normed, cotangent, expert_pick)
    if turns == 1:
        grads, (summed, normed_grad) = turn(None, owned)
    else:
        owned = jax.tree.map(lambda a: a.reshape(turns, -1, a.shape[1]), owned)
        zeros = (
            jnp.zeros(in_mat.shape, f32),
            jnp.zeros(out_mat.shape, f32),
            jnp.zeros((per_device, features), f32),
        )
        grads, sums = lax.scan(turn, zeros, owned)
        summed, normed_grad = (a.reshape(tokens, features) for a in sums)
    grad_in = grads[0].reshape(features, per_device, width).transpose(1, 0, 2)
    grad_out = grads[1].reshape(per_device, width, features)
    grad_router = lax.all_gather(grads[2], everywhere, axis=0, tiled=True).T
    output = middle + summed.astype(f32)
    incoming = cotangent.astype(f32)
    row_grad, grad_gain_expert = norm_back(
        middle, middle_inverse, expert_scale, normed_grad.astype(f32)
    )
    middle_grad = incoming + row_grad
    group_grads = lax.all_gather(middle_grad.astype(bf16), "head", axis=0, tiled=True)
    weighted_grad = product(group_grads, output_mat, 1, 1).reshape(group, head_experts, head_width)
    output_grad = product(weighted, group_grads, 0, 0)
    output_gate_grad = jnp.sum(weighted_grad * attended[:, None, :], axis=-1)
    attended_grad = jnp.sum(weighted_grad * output_gates[:, :, None], axis=1).astype(bf16)
    prob_grad = product(attended_grad, values, 1, 1)
    centre = jnp.sum(probabilities * prob_grad, axis=-1, keepdims=True)
    score_grad = (probabilities * (prob_grad - centre)).astype(bf16)
    query_grad = product(score_grad, key_rows, 1, 0) * scale
    key_grad = product(score_grad, queries, 0, 0) * scale
    values_grad = product(probabilities.astype(bf16), attended_grad, 0, 0)
    expert_grad = (value_gates[:, :, None] * values_grad[:, None, :]).reshape(group, -1).astype(bf16)
    value_gate_grad = jnp.sum(expert_values * values_grad[:, None, :], axis=-1)
    query_grad = rotate(query_grad, cosine, -sine).astype(bf16)
    key_grad = rotate(key_grad, cosine, -sine).astype(bf16)
    logit_grad = (
        jnp.concatenate([value_gate_grad * value_mask, output_gate_grad * output_mask], axis=1)
        * squash
        * (1.0 - squash)
    ).astype(bf16)
    head_grads = (
        product(normed, query_grad, 0, 0),
        product(normed, key_grad, 0, 0),
        product(rows, expert_grad, 0, 0),
        output_grad,
        product(normed, logit_grad, 0, 0),
    )
    head_grads = tuple(grad.astype(bf16) for grad in head_grads)
    head_grads = tuple(grad.astype(f32)[None] for grad in lax.psum(head_grads, "dp"))
    back = (
        product(query_grad, query_mat, 1, 1)
        + product(key_grad, key_mat, 1, 1)
        + product(logit_grad, gate_mat, 1, 1)
    )
    row_back, grad_attend = norm_back(grouped, inverse, attend_scale, back)
    partial = (row_back + product(expert_grad, value_mat, 1, 1)).astype(bf16)
    input_grad = middle_grad + lax.psum_scatter(
        partial, "head", scatter_dimension=0, tiled=True
    ).astype(f32)
    grad_attend, grad_gain_expert = lax.psum((grad_attend, grad_gain_expert), everywhere)
    return (
        output,
        input_grad,
        grad_attend,
        *head_grads,
        grad_gain_expert,
        grad_router,
        grad_in,
        grad_out,
    )


MESH = pl.DeviceIdType.MESH
VM = pl.BlockSpec(memory_space=pltpu.VMEM)
ANY = pl.BlockSpec(memory_space=pl.ANY)
NN = (((1,), (0,)), ((), ()))
NT = (((1,), (1,)), ((), ()))
TN = (((0,), (0,)), ((), ()))


def dot(left, right, dims=NN):
    return lax.dot_general(left, right, dims, preferred_element_type=f32)


def at_block(block, count):
    return pl.ds(pl.multiple_of(block * count, count), count)


def remote(src, dst, send, recv, where):
    return pltpu.make_async_remote_copy(
        src_ref=src, dst_ref=dst, send_sem=send, recv_sem=recv, device_id=where, device_id_type=MESH
    )


def swap_halves(value):
    half = value.shape[-1] // 2
    return jnp.concatenate([value[:, half:], value[:, :half]], axis=-1)


def ceil_to(number, step):
    return -(-number // step) * step


def layer_kernel(
    n_dp,
    n_head,
    x_ref,
    cot_ref,
    pick_ref,
    value_pick_ref,
    output_pick_ref,
    seg_ref,
    gain_ref,
    angle_ref,
    wq_ref,
    wk_ref,
    wg_ref,
    wv_ref,
    wo_ref,
    router_ref,
    in_ref,
    out_ref,
    output_ref,
    grad_x_ref,
    wide_ref,
    fin_in_ref,
    fin_out_ref,
    picks,
    two_picks,
    head_picks,
    w_r,
    seg,
    gains,
    angles,
    w_an,
    w_v,
    w_o,
    my_router,
    w_in,
    w_out,
    rows,
    cot,
    mrs,
    das,
    turned,
    my_mask,
    all_mask,
    gates,
    q,
    k,
    v,
    vx,
    att,
    part,
    got,
    outs,
    got_out,
    lifted,
    core_out,
    acts,
    hids,
    dzs,
    datt,
    gate_grads,
    probs,
    scores,
    qkz,
    vgrads,
    gain_part,
    gain_got,
    sums,
    core_got,
    chip_got,
    piece,
    blocks,
    hop_in,
    hop_out,
    local_sem,
    z_send,
    z_recv,
    w_send,
    w_recv,
    c_send,
    c_recv,
    e_send,
    e_recv,
    s_send,
    s_recv,
    t_send,
    t_recv,
    ready,
    free,
):
    middle = output_ref
    xor = jnp.bitwise_xor
    d, h = lax.axis_index("dp"), lax.axis_index("head")
    chip, core = d // 2, d % 2
    chips = n_dp // 2
    tokens, features = x_ref.shape
    per_device, _, width = in_ref.shape
    slab = per_device * width
    wide = 2 * slab
    experts = wv_ref.shape[1] // width
    named = ceil_to(n_dp * per_device, 8)
    group = tokens * n_head
    pair = 2 * tokens
    column = 256
    lanes = 128
    scale = width ** (-0.5)
    peers = (2, 3, 1)
    partner = (chip * 2 + 1 - core, h)
    own_block = at_block(h, tokens)
    own_side, other_side = at_block(core, slab), at_block(1 - core, slab)
    halves_in = (pl.ds(0, features // 2), pl.ds(features // 2, features // 2))
    halves_out = lambda side: (
        at_block(2 * side, slab // 2),
        at_block(2 * side + 1, slab // 2),
    )

    def along(step):
        return (d, xor(h, step))

    def across(step):
        return (xor(chip, step) * 2 + core, h)

    loads = []

    def load(src, dst):
        copy = pltpu.make_async_copy(src, dst, local_sem.at[len(loads)])
        copy.start()
        loads.append(copy)
        return copy

    own_weights = [load(out_ref, w_out.at[chip, own_side, :])] + [
        load(in_ref.at[e], w_in.at[chip, :, at_block(core * per_device + e, width)])
        for e in range(per_device)
    ]
    for_rows = [
        load(x_ref, rows.at[own_block, :]),
        load(gain_ref, gains),
        load(wq_ref, w_an.at[:, pl.ds(0, width)]),
        load(wk_ref, w_an.at[:, pl.ds(width, width)]),
        load(wv_ref, w_v),
        load(value_pick_ref, two_picks.at[0]),
        load(output_pick_ref, two_picks.at[1]),
        load(angle_ref, angles),
    ]
    for_scores = [load(seg_ref, seg), load(wo_ref, w_o)]
    for_mask = load(pick_ref, picks)
    for_cot = load(cot_ref, cot.at[own_block, :])
    for_router = load(router_ref, w_r)

    barrier = pltpu.get_barrier_semaphore()
    friends = [along(s) for s in peers] + [partner] + [across(s) for s in range(1, chips)]
    for friend in friends:
        pl.semaphore_signal(barrier, inc=1, device_id=friend, device_id_type=MESH)
    pl.semaphore_wait(barrier, len(friends))

    right, left = (d, jnp.minimum(h + 1, n_head - 1)), (d, jnp.maximum(h - 1, 0))
    last = n_head - 1

    def pick(*by_place):
        value = jnp.int32(by_place[-1])
        for place in range(n_head - 2, -1, -1):
            value = jnp.where(h == place, by_place[place], value)
        return value

    arrival = (xor(h, 1), pick(2, 2, 1, 1), pick(3, 3, 0, 0))
    leaving = (pick(3, 3, 0, 0), pick(2, 0, 3, 1), pick(1, 2, 1, 2))

    def gather(kind, buffer):
        def go(side, step):
            sign = 1 - 2 * side
            block = jnp.clip(h - sign * step, 0, last)
            where = (d, jnp.clip(h + sign, 0, last))
            copies = []
            for half in range(2):
                here = buffer.at[at_block(2 * block + half, tokens // 2), :]
                number = (side * last + step) * 2 + half
                copies.append(
                    remote(here, here, z_send.at[kind, number], z_recv.at[kind, number], where)
                )
            return copies

        def begin(side):
            for copy in go(side, 0):
                copy.start()

        def start():
            pl.when(h < last)(lambda: begin(0))
            pl.when(h > 0)(lambda: begin(1))

        def arrive(side, step, there, onward):
            for half in range(2):

                @pl.when(there)
                def _():
                    go(side, step - 1)[half].wait_recv()
                    if onward:
                        go(side, step)[half].start()

        def stage(step, which="all"):
            nearer = jnp.where(2 * h < n_head, 0, 1)
            ways = []
            for side in (nearer, 1 - nearer):
                there = jnp.where(side == 0, h >= step, h + step <= last)
                ways.append((side, there, jnp.where(side == 0, h < last, h > 0)))
            for side, there, onward in ways:
                if step < last and which != "rest":
                    arrive(side, step, there & onward, True)
            for side, there, onward in ways:
                if which != "duty":
                    ends_here = there if step == last else there & jnp.logical_not(onward)
                    arrive(side, step, ends_here, False)

        def follow(step):
            pl.when((h < last) & (jnp.maximum(h, 1) == step))(lambda: begin(0))
            pl.when((h > 0) & (jnp.maximum(last - h, 1) == step))(lambda: begin(1))

        def end():
            for step in range(last):
                for side, sent in (
                    (0, (h >= step) & (h < last)),
                    (1, (h + step <= last) & (h > 0)),
                ):

                    @pl.when(sent)
                    def _():
                        for copy in go(side, step):
                            copy.wait_send()

        return start, stage, end, follow

    def chain_sum(kind, parts, slots):
        def go(number):
            block = leaving[number]
            rightward = block > h
            slot = jnp.where(rightward, block - 1, last + block)
            where = (d, jnp.clip(jnp.where(rightward, h + 1, h - 1), 0, last))
            middle_one = (rightward & (h > 0)) | (jnp.logical_not(rightward) & (h < last))
            pieces = []
            for half in range(2):
                at = at_block(2 * block + half, tokens // 2)
                rows_of = pl.ds(half * (tokens // 2), tokens // 2)
                copy = remote(
                    parts.at[at, :],
                    slots.at[slot, rows_of, :],
                    z_send.at[kind, 2 * number + half],
                    z_recv.at[kind, 2 * slot + half],
                    where,
                )
                pieces.append((copy, at, slot, rows_of))
            return pieces, middle_one

        def now(number):
            pieces, middle_one = go(number)

            @pl.when(jnp.logical_not(middle_one))
            def _():
                for copy, _, _, _ in pieces:
                    copy.start()

        def later(number):
            pieces, middle_one = go(number)

            @pl.when(middle_one)
            def _():
                for copy, at, slot, rows_of in pieces:
                    copy.wait_recv()
                    parts[at, :] = parts[at, :] + slots[slot, rows_of, :]
                    copy.start()

        def end(total):
            ends = ((jnp.maximum(h - 1, 0), h > 0), (last + jnp.minimum(h, last - 1), h < last))
            for slot, there in ends:

                @pl.when(there)
                def _():
                    for half in range(2):
                        rows_of = pl.ds(half * (tokens // 2), tokens // 2)
                        remote(
                            parts.at[at_block(2 * h, tokens // 2), :],
                            slots.at[slot, rows_of, :],
                            z_send.at[kind, 0],
                            z_recv.at[kind, 2 * slot + half],
                            right,
                        ).wait_recv()
                    total[...] += slots[slot].astype(f32)

            for number in range(last):
                for copy, _, _, _ in go(number)[0]:
                    copy.wait_send()

        return now, later, end

    def spread(kind, src, dst, steps=peers):
        copies = {}
        for step in steps:
            copies[step] = remote(
                src(step), dst(step), z_send.at[kind, step - 1], z_recv.at[kind, step - 1], along(step)
            )
            copies[step].start()
        return copies

    x_start, x_stage, x_end, _ = gather(0, rows)
    for_rows[0].wait()
    x_start()

    def slot(array, place, side, half=None):
        if array == 0:
            at = halves_out(side)[half] if half is not None else at_block(side, slab)
            return w_out.at[place, at, :]
        at = halves_in[half] if half is not None else pl.ds(0, features)
        return w_in.at[place, at, at_block(side, slab)]

    def weights(number, ref, where):
        copy = remote(ref, ref, w_send.at[number], w_recv.at[number], where)
        copy.start()
        return copy

    slabs, halves_on, to_core, diagonal = {}, {}, {}, {}
    for copy in own_weights:
        copy.wait()
    for array in range(2):
        for first in range(2):
            for bit in (1, 2):
                half = bit - 1 if first == 0 else 2 - bit
                number = ((bit - 1) * 2 + half) * 2 + array
                slabs[bit, half, array] = weights(
                    number, slot(array, chip, core, half), across(bit)
                )
        to_core[0, array] = weights(12 + array, slot(array, chip, core), partner)

    for_mask.wait()
    own_picks = jnp.concatenate(
        [picks[...].astype(f32), jnp.zeros((lanes - picks.shape[0], tokens), f32)], axis=0
    ).T.astype(jnp.int32)
    lane = lax.broadcasted_iota(jnp.int32, (tokens, lanes), 1)
    for plane in range(n_head):
        expert = (lane // per_device * n_head + plane) * per_device + lane % per_device
        expert = jnp.where(lane < n_dp * per_device, expert, -1)
        hit = own_picks[:, 0:1] == expert
        for c in range(1, picks.shape[0]):
            hit = hit | (own_picks[:, c : c + 1] == expert)
        my_mask[plane] = jnp.where(hit, 1.0, 0.0).astype(bf16)
    mask_copies = spread(1, lambda s: my_mask.at[xor(h, s)], lambda s: all_mask.at[own_block, :])
    all_mask[own_block, :] = my_mask[h]

    for copy in for_rows[1:]:
        copy.wait()
    attend_gain = gains[0:1, :]
    expert_gain = gains[1:2, :]
    one_hot = lambda count: jnp.where(
        lax.broadcasted_iota(jnp.int32, (count, width), 0)
        == lax.broadcasted_iota(jnp.int32, (count, width), 1),
        1.0,
        0.0,
    ).astype(bf16)
    w_an[:, pl.ds(2 * width, width)] = dot(wg_ref[...], one_hot(wg_ref.shape[0]), TN).astype(bf16)
    uses = two_picks.shape[1]
    head_picks[...] = jnp.concatenate(
        [
            two_picks[0].astype(f32),
            two_picks[1].astype(f32) + experts,
            jnp.zeros((lanes - 2 * uses, group), f32),
        ],
        axis=0,
    ).T.astype(jnp.int32)
    half_lanes = lax.broadcasted_iota(jnp.int32, (1, width), 1) < width // 2

    def turns(at):
        both = angles[at, :]
        turned_over = swap_halves(both)
        return (
            jnp.where(half_lanes, both, turned_over),
            jnp.where(half_lanes, -turned_over, both),
        )

    def project(block):
        at = at_block(block, tokens)
        own = rows[at, :]
        full = own.astype(f32)
        inverse = lax.rsqrt(jnp.mean(full * full, axis=-1, keepdims=True) + epsilon)
        unit = (full * inverse * attend_gain).astype(bf16)
        qkg = dot(unit, w_an[...])
        c, s = turns(at)
        one, two = qkg[:, :width], qkg[:, width : 2 * width]
        q[at, :] = (one * c + swap_halves(one) * s).astype(bf16)
        k[at, :] = (two * c + swap_halves(two) * s).astype(bf16)
        lane = lax.broadcasted_iota(jnp.int32, (tokens, width), 1)
        chosen = head_picks[at, :]
        hit = lane == chosen[:, 0:1]
        for c in range(1, 2 * uses):
            hit = hit | (lane == chosen[:, c : c + 1])
        gate = jnp.where(hit, jax.nn.sigmoid(qkg[:, 2 * width :]), 0.0)
        gates[at, :] = jnp.where(lane == width - 1, inverse, gate)
        values = dot(own, w_v[...])
        vx[at, :] = values.astype(bf16)
        value = gate[:, 0:1] * values[:, :width]
        for e in range(1, experts):
            value += gate[:, e : e + 1] * values[:, e * width : (e + 1) * width]
        v[at, :] = value.astype(bf16)

    project(h)
    _, cot_stage, cot_end, cot_follow = gather(2, cot)
    for_cot.wait()
    for step in (1, 2, 3):
        x_stage(step)
        cot_follow(step)
        project(arrival[step - 1])
    for copy in for_scores:
        copy.wait()
    seg_col = gate_grads
    seg_col[...] = jnp.broadcast_to(seg[...].astype(f32), (lanes, group)).T

    def attend(block):
        at = at_block(block, tokens)
        score = dot(q[at, :], k[...], NT) * scale
        row = block * tokens + lax.broadcasted_iota(jnp.int32, (tokens, group), 0)
        place = lax.broadcasted_iota(jnp.int32, (tokens, group), 1)
        allowed = (place <= row) & (seg_col[at, 0:1] == seg[...].astype(f32))
        score = jnp.where(allowed, score, negative)
        exponents = jnp.exp(score - jnp.max(score, axis=-1, keepdims=True))
        chance = exponents / jnp.sum(exponents, axis=-1, keepdims=True)
        probs[at, :] = chance.astype(bf16)
        attended = dot(chance.astype(bf16), v[...])
        att[at, :] = attended
        gate = gates[at, :]
        weighted = jnp.concatenate(
            [
                (gate[:, experts + e : experts + e + 1] * attended).astype(bf16)
                for e in range(experts)
            ],
            axis=-1,
        )
        return dot(weighted, w_o[...])

    to_mid = chain_sum(3, part, got)
    for number in range(last):
        block = leaving[number]
        part[at_block(block, tokens), :] = attend(block).astype(bf16)
        to_mid[0](number)
    middle[...] = rows[own_block, :].astype(f32) + attend(h)
    cot_stage(1, "duty")
    to_mid[1](0)
    for array in range(2):
        for half in range(2):
            slabs[1 + half, half, array].wait_recv()
            halves_on[half, array] = weights(
                8 + 2 * half + array,
                slot(array, xor(chip, 1 + half), core, half),
                across(2 - half),
            )

    to_mid[1](1)
    cot_stage(2, "duty")
    to_mid[1](2)
    for bit in (1, 2):
        slabs[bit, 2 - bit, 0].wait_recv()
        to_core[bit, 0] = weights(14 + (bit - 1) * 2, slot(0, xor(chip, bit), core), partner)
        slabs[bit, 2 - bit, 1].wait_recv()
        to_core[bit, 1] = weights(15 + (bit - 1) * 2, slot(1, xor(chip, bit), core), partner)
    for_router.wait()
    slot_of = lax.broadcasted_iota(jnp.int32, (w_r.shape[0], lanes), 1)
    name = lax.broadcasted_iota(jnp.int32, (w_r.shape[0], lanes), 0)
    expert = (slot_of // per_device * n_head + h) * per_device + slot_of % per_device
    expert = jnp.where(slot_of < n_dp * per_device, expert, -1)
    my_router[...] = dot(
        w_r[...], jnp.where(name == expert, 1.0, 0.0).astype(bf16), TN
    ).astype(bf16)

    to_mid[2](middle)
    mid = middle[...]
    inverse = lax.rsqrt(jnp.mean(mid * mid, axis=-1, keepdims=True) + epsilon)
    mrs[own_block, :] = (mid * inverse * expert_gain).astype(bf16)
    mr_start, mr_stage, mr_end, _ = gather(4, mrs)
    mr_start()

    def last_halves(array):
        for half in range(2):
            halves_on[half, array].wait_recv()
            diagonal[half, array] = weights(
                18 + 2 * half + array, slot(array, xor(chip, 3), core, half), partner
            )

    for step in (1, 2, 3):
        cot_stage(step, "rest")
    last_halves(0)
    for step in peers:
        mask_copies[step].wait()
    cot_end()
    x_end()

    def weights_here(array):
        for bit in range(3):
            to_core[bit, array].wait_recv()
        for half in range(2):
            diagonal[half, array].wait_recv()

    def weights_sent():
        for array in range(2):
            for bit in range(3):
                to_core[bit, array].wait_send()
            for half in range(2):
                diagonal[half, array].wait_send()
                halves_on[half, array].wait_send()
                for bit in (1, 2):
                    slabs[bit, half, array].wait_send()

    weights_here(0)

    def lift_chip(j):
        lift = dot(cot[...], w_out[j], NT)
        lifted[j, 0] = lift[:, :slab].astype(bf16)
        lifted[j, 1] = lift[:, slab:].astype(bf16)

    pl.loop(0, chips // 2)(lift_chip)
    mr_stage(1, "duty")
    last_halves(1)
    pl.loop(chips // 2, chips)(lift_chip)

    weights_here(1)

    def spread_lanes(j):
        lane = lax.broadcasted_iota(jnp.int32, (lanes, wide), 1) // width
        slot = lax.broadcasted_iota(jnp.int32, (lanes, wide), 0)
        return jnp.where(slot == lane + j * (wide // width), 1.0, 0.0).astype(bf16)

    def pair_of_blocks(number, between):
        at = at_block(number, pair)
        own = mrs[at, :]
        gates = jax.nn.sigmoid(dot(own, my_router[...]))
        live = gates * all_mask[at, :].astype(f32)
        narrow = live.astype(bf16)

        def chip_step(j, total):
            pick = spread_lanes(j)
            hidden = dot(own, w_in[j])
            gate = dot(narrow, pick).astype(bf16)
            lift = jnp.concatenate([lifted[j, 0, at, :], lifted[j, 1, at, :]], axis=-1)
            square = hidden * hidden
            inner = jnp.tanh(0.7978845608028654 * hidden * (1.0 + 0.044715 * square))
            half = 0.5 * (1.0 + inner)
            act = hidden * half
            slope = half + act * (1.0 - inner) * (
                0.7978845608028654 + (0.7978845608028654 * 3.0 * 0.044715) * square
            )
            act = act.astype(bf16)
            acts[j, at, :] = act * gate
            hids[j, at, :] = slope.astype(bf16) * (lift * gate)
            return total + dot(act * lift, pick, NT)

        total = lax.fori_loop(0, chips // 2, chip_step, jnp.zeros((pair, lanes), f32))
        between()
        total = lax.fori_loop(chips // 2, chips, chip_step, total)
        dz = (total * live * (1.0 - gates)).astype(bf16)
        dzs[at, :] = dz

        @pl.loop(0, features // column)
        def _(c):
            part_of = at_block(c, column)
            total = dot(dz, my_router[part_of, :], NT)
            for j in range(chips):
                total += dot(hids[j, at, :], w_in[j, part_of, :], NT)
            part[at, part_of] = total.astype(bf16)

    def outputs():
        @pl.loop(0, features // column)
        def _(c):
            part_of = at_block(c, column)
            total = dot(acts[0], w_out[0, :, part_of])
            for j in range(1, chips):
                total += dot(acts[j], w_out[j, :, part_of])
            outs[:, part_of] = total.astype(bf16)

    near = h // 2
    mr_stage(1, "rest")
    to_dmr = chain_sum(5, part, got)
    pair_of_blocks(near, lambda: mr_stage(2, "duty"))
    to_dmr[0](2)
    mr_stage(2, "rest")
    mr_stage(3)
    pair_of_blocks(1 - near, lambda: None)
    to_dmr[0](0)
    to_dmr[0](1)
    pl.semaphore_signal(ready, inc=1, device_id=partner, device_id_type=MESH)

    weights_sent()
    turned[...] = mrs[...].T

    def to_other_core(n, array):
        place = xor(chip, chips - 1 - n)
        if array == 0:
            return [
                remote(
                    w_out.at[place, other_side, :],
                    core_out.at[place],
                    c_send.at[2, n],
                    c_recv.at[2, n],
                    partner,
                )
            ]
        return [
            remote(
                w_in.at[place, halves_in[half], other_side],
                lifted.at[place, half],
                c_send.at[half, n],
                c_recv.at[half, n],
                partner,
            )
            for half in range(2)
        ]

    pl.semaphore_wait(ready, 1)
    hops = {}

    def hop(half, index, place, toward, array):
        copy = remote(
            slot(array, place, core, half),
            (hop_out, hop_in)[array].at[half, index],
            e_send.at[1 - array, 2 * half + index],
            e_recv.at[1 - array, 2 * half + index],
            across(toward),
        )
        copy.start()
        hops[half, index, array] = copy

    def both_cores(n, array):
        step = chips - 1 - n
        place = xor(chip, step)
        for copy in to_other_core(n, array):
            copy.wait()
        if array == 0:
            w_out[place, own_side, :] = w_out[place, own_side, :] + core_out[place]
        else:
            for half in range(2):
                here = (place, halves_in[half], own_side)
                w_in[here] = w_in[here] + lifted[place, half]
        if step == 3:
            hop(0, 1, place, 1, array)
            hop(1, 1, place, 2, array)
        elif step:
            hop(step - 1, 0, place, step, array)

    def expert_grads(array, place, at):
        if array == 0:
            for half in halves_in:
                w_out[place, at, half] = dot(acts[place, :, at], cot[:, half], TN).astype(bf16)
        else:
            for n in range(features // column):
                band = pl.ds(n * column, column)
                w_in[place, band, at] = dot(turned[band, :], hids[place, :, at]).astype(bf16)

    def all_grads(array):
        for n in range(chips):
            place = xor(chip, chips - 1 - n)
            expert_grads(array, place, other_side if array == 0 else slice(None))
            for copy in to_other_core(n, array):
                copy.start()
            if n:
                both_cores(n - 1, array)
            if array == 0:
                expert_grads(array, place, own_side)

    all_grads(1)
    outputs()
    both_cores(chips - 1, 1)
    to_dmr[1](0)
    all_grads(0)
    both_cores(chips - 1, 0)
    to_dmr[1](1)
    to_dmr[1](2)
    side = features // 2
    strip = side // chips
    col = lambda c, j: at_block(c * chips + j, strip)

    def section(number, first, count):
        at = pl.ds(first, count)
        state = {}

        def sem(n):
            return s_send.at[number, n], s_recv.at[number, n]

        def start():
            state["core"] = remote(
                sums.at[at, at_block(1 - core, side)], core_got.at[at, :], *sem(0), partner
            )
            state["core"].start()

        def mid():
            state["core"].wait()
            half = at_block(core, side)
            sums[at, half] = sums[at, half] + core_got[at, :]
            state["chips"] = []
            for s in range(1, chips):
                copy = remote(
                    sums.at[at, col(core, xor(chip, s))], chip_got.at[s - 1, at, :], *sem(s), across(s)
                )
                copy.start()
                state["chips"].append(copy)

        def add():
            for copy in state["chips"]:
                copy.wait()
            total = sums[at, col(core, chip)].astype(f32)
            for s in range(1, chips):
                total += chip_got[s - 1, at, :].astype(f32)
            piece[at, :] = total.astype(bf16)

        return start, mid, add

    def two_hop_section(number, first, count):
        at = pl.ds(first, count)
        half_at = [pl.ds(first + n * (count // 2), count // 2) for n in range(2)]
        begin, state = section(number, first, count)[0], {}

        def hop(half, index, place, toward, n):
            copy = remote(
                sums.at[half_at[half], col(core, place)],
                chip_got.at[index, half_at[half], :],
                t_send.at[number, n],
                t_recv.at[number, n],
                across(toward),
            )
            copy.start()
            return copy

        def mid():
            over = remote(
                sums.at[at, at_block(1 - core, side)],
                core_got.at[at, :],
                s_send.at[number, 0],
                s_recv.at[number, 0],
                partner,
            )
            over.wait()
            half = at_block(core, side)
            sums[at, half] = sums[at, half] + core_got[at, :]
            for half in range(2):
                toward = 1 + half
                state[half, 1] = hop(half, 1, xor(chip, 3), toward, 2 * half + 1)
                state[half, 0] = hop(half, 0, xor(chip, toward), toward, 2 * half)

        def second():
            for half in range(2):
                here = (half_at[half], col(core, xor(chip, 2 - half)))
                state[half, 1].wait()
                sums[here] = sums[here] + chip_got[1, half_at[half], :]
                state[half, 2] = hop(half, 2, xor(chip, 2 - half), 2 - half, 4 + half)

        def add():
            for half in range(2):
                state[half, 0].wait()
                state[half, 2].wait()
            total = sums[at, col(core, chip)].astype(f32)
            for index in (0, 2):
                total += chip_got[index, at, :].astype(f32)
            piece[at, :] = total.astype(bf16)

        return begin, mid, second, add

    def two_hop_to_plane(number, first, count):
        at = pl.ds(first, count)
        half_at = [pl.ds(first + n * (count // 2), count // 2) for n in range(2)]
        state = {}

        def send(src, rows_of, place, where, n):
            copy = remote(
                src,
                wide_ref.at[rows_of, col(core, place)],
                t_send.at[number, n],
                t_recv.at[number, n],
                where,
            )
            copy.start()
            return copy

        def start():
            for urgent in range(2):
                for bit in (1, 2):
                    half = bit - 1 if urgent == 0 else 2 - bit
                    state[bit, half] = send(
                        piece.at[half_at[half], :],
                        half_at[half],
                        chip,
                        across(bit),
                        6 + 2 * (bit - 1) + half,
                    )
            over = send(piece.at[at, :], at, chip, partner, 12)
            own = pltpu.make_async_copy(
                piece.at[at, :], wide_ref.at[at, col(core, chip)], t_send.at[number, 15]
            )
            own.start()
            state["wait"] = [over, own]

        def relay():
            for half in range(2):
                bit = 1 + half
                state[bit, half].wait_recv()
                place = xor(chip, bit)
                here = wide_ref.at[half_at[half], col(core, place)]
                state[3, half] = send(here, half_at[half], place, across(2 - half), 10 + half)

        def forward():
            for bit in (1, 2):
                state[bit, 2 - bit].wait_recv()
                place = xor(chip, bit)
                here = wide_ref.at[at, col(core, place)]
                state["wait"].append(send(here, at, place, partner, 12 + bit))

        def end():
            for half in range(2):
                state[3, half].wait_recv()
            place = xor(chip, 3)
            here = wide_ref.at[at, col(core, place)]
            state["wait"].append(send(here, at, place, partner, 16))

        def done():
            for copy in state["wait"]:
                copy.wait()
            for half in range(2):
                state[3, half].wait_send()
                for bit in (1, 2):
                    state[bit, half].wait_send()

        return start, relay, forward, end, done

    def to_plane(number, src, rows_to):
        state = {}

        def sem(n):
            return s_send.at[number, chips + n], s_recv.at[number, chips + n]

        def start():
            here = wide_ref.at[rows_to, col(core, chip)]
            state["share"] = [remote(src, here, *sem(s), across(s)) for s in range(1, chips)]
            over = remote(src, here, *sem(0), partner)
            own = pltpu.make_async_copy(src, here, s_send.at[number, 3 * chips - 1])
            state["wait"] = [over, own]
            for copy in state["share"] + state["wait"]:
                copy.start()

        def forward():
            for s in range(1, chips):
                state["share"][s - 1].wait()
                here = wide_ref.at[rows_to, col(core, xor(chip, s))]
                copy = remote(here, here, *sem(chips - 1 + s), partner)
                copy.start()
                state["wait"].append(copy)

        def end():
            for copy in state["wait"]:
                copy.wait()

        return start, forward, end

    mixed = w_o.shape[0]
    small = ceil_to(named + 1, 16)
    at_a = pl.ds(features, 16)
    at_o = pl.ds(features + 16, mixed)
    at_g = pl.ds(features + 16 + mixed, small)
    of_d = [two_hop_section(n, n * features // 2, features // 2) for n in range(2)]
    of_o = two_hop_section(2, features + 16, mixed)
    of_g = section(3, features + 16 + mixed, small)
    of_a = section(4, features, 16)
    out_d = [two_hop_to_plane(n, n * features // 2, features // 2) for n in range(2)]
    out_o = two_hop_to_plane(2, features + 16, mixed)
    out_g = to_plane(3, blocks, pl.ds(features + 16 + mixed, n_head * small))
    out_a = to_plane(4, piece.at[at_a, :], at_a)
    router_part = dot(dzs[...], mrs[...], TN)[:named]

    grad_x_ref[...] = part[own_block, :].astype(f32)
    to_dmr[2](grad_x_ref)
    incoming = grad_x_ref[...]
    mid = middle[...]
    inverse = lax.rsqrt(jnp.mean(mid * mid, axis=-1, keepdims=True) + epsilon)
    unit = mid * inverse
    scaled = incoming * expert_gain
    dmid = cot[own_block, :].astype(f32) + inverse * (
        scaled - unit * jnp.mean(scaled * unit, axis=-1, keepdims=True)
    )
    grad_x_ref[...] = dmid
    das[own_block, :] = dmid.astype(bf16)
    da_start, da_stage, da_end, _ = gather(6, das)
    da_start()
    sums[at_g, :] = jnp.concatenate(
        [
            router_part,
            jnp.sum(incoming * unit, axis=0, keepdims=True),
            jnp.zeros((small - named - 1, features), f32),
        ],
        axis=0,
    ).astype(bf16)
    of_g[0]()
    turned[...] = rows[...].T
    of_g[1]()
    lasts = {}

    def first_hop(half, index, place):
        for array in range(2):
            hops[half, index, array].wait()
        at_in = (place, halves_in[half], own_side)
        at_out = (place, halves_out(core)[half], slice(None))
        w_in[at_in] = w_in[at_in] + hop_in[half, index]
        w_out[at_out] = w_out[at_out] + hop_out[half, index]

    for half in range(2):
        toward = 2 - half
        place = xor(chip, toward)
        first_hop(half, 1, place)
        pl.semaphore_signal(free.at[half], inc=1, device_id=across(toward), device_id_type=MESH)
        pl.semaphore_wait(free.at[half], 1)
        lasts[half] = (
            remote(
                slot(1, place, core, half),
                hop_in.at[half, 1],
                e_send.at[0, 4 + half],
                e_recv.at[0, 4 + half],
                across(toward),
            ),
            remote(
                slot(0, place, core, half),
                hop_out.at[half, 1],
                e_send.at[1, 4 + half],
                e_recv.at[1, 4 + half],
                across(toward),
            ),
        )
        for copy in lasts[half]:
            copy.start()
    lane = lax.broadcasted_iota(jnp.int32, (tokens, width), 1)

    def through_output(block):
        at = at_block(block, tokens)
        all_five = dot(das[at, :], w_o[...], NT)
        attended = att[at, :]
        total = jnp.zeros((tokens, width), f32)
        gate = jnp.zeros((tokens, width), f32)
        for e in range(experts):
            one = all_five[:, e * width : (e + 1) * width]
            total += gates[at, experts + e : experts + e + 1] * one
            gate = jnp.where(
                lane == experts + e, jnp.sum(one * attended, axis=-1, keepdims=True), gate
            )
        datt[at, :] = total.astype(bf16)
        gate_grads[at, :] = gate

    through_output(h)
    to_out = chain_sum(7, outs, got_out)
    for step in (1, 2, 3):
        da_stage(step)
        if step == 1:
            for number in range(last):
                to_out[0](number)
        through_output(arrival[step - 1])

    for e in range(experts):
        one = (gates[:, experts + e : experts + e + 1] * att[...]).astype(bf16)
        sums[pl.ds(features + 16 + e * width, width), :] = dot(one, das[...], TN).astype(bf16)
    of_o[0]()

    @pl.loop(0, n_head)
    def _(block):
        at = at_block(block, tokens)
        chance = probs[at, :].astype(f32)
        dprob = dot(datt[at, :], v[...], NT)
        centre = jnp.sum(chance * dprob, axis=-1, keepdims=True)
        scores[at, :] = (chance * (dprob - centre)).astype(bf16)

    dq = dot(scores[...], k[...]) * scale
    dk = dot(scores[...], q[...], TN) * scale
    dv = dot(probs[...], datt[...], TN)
    of_o[1]()
    c, s = turns(slice(None))
    qkz[:, pl.ds(0, width)] = (dq * c - swap_halves(dq) * s).astype(bf16)
    qkz[:, pl.ds(width, width)] = (dk * c - swap_halves(dk) * s).astype(bf16)
    gate = gate_grads[...]
    lane = lax.broadcasted_iota(jnp.int32, (group, width), 1)
    for e in range(experts):
        vgrads[:, pl.ds(e * width, width)] = (gates[:, e : e + 1] * dv).astype(bf16)
        one = jnp.sum(vx[:, pl.ds(e * width, width)].astype(f32) * dv, axis=-1, keepdims=True)
        gate = jnp.where(lane == e, one, gate)
    qkz[:, pl.ds(2 * width, width)] = (gate * gates[...] * (1.0 - gates[...])).astype(bf16)

    scaled_qkz = (qkz[...].astype(f32) * gates[:, width - 1 : width]).astype(bf16)

    def matrix_rows(c):
        at = at_block(c, column)
        sums[at, pl.ds(0, 3 * width)] = dot(turned[at, :], scaled_qkz).astype(bf16)
        sums[at, pl.ds(3 * width, experts * width)] = dot(turned[at, :], vgrads[...]).astype(bf16)

    steps_each = features // column // 2
    for n in range(2):
        pl.loop(n * steps_each, (n + 1) * steps_each)(matrix_rows)
        of_d[n][0]()
    def into_rows(block):
        at = at_block(block, tokens)
        inverse = gates[at, width - 1 : width]
        unit = rows[at, :].astype(f32) * inverse
        through = dot(qkz[at, :], w_an[...], NT)
        scaled = through * attend_gain
        total = inverse * (
            scaled - unit * jnp.mean(scaled * unit, axis=-1, keepdims=True)
        ) + dot(vgrads[at, :], w_v[...], NT)
        return total, jnp.sum(through * unit, axis=0, keepdims=True)

    to_x = chain_sum(8, part, got)
    gain = jnp.zeros((1, features), f32)
    for number in range(last):
        total, one = into_rows(leaving[number])
        gain += one
        part[at_block(leaving[number], tokens), :] = total.astype(bf16)
        to_x[0](number)
        if number < 2:
            of_d[number][1]()
    total, one = into_rows(h)
    sums[at_a, :] = jnp.broadcast_to(gain + one, (16, features)).astype(bf16)
    of_a[0]()
    grad_x_ref[...] += total
    to_out[1](0)
    to_out[1](1)
    of_a[1]()
    of_o[2]()
    to_x[1](0)
    of_d[0][2]()
    of_d[1][2]()
    of_g[2]()
    small_block = at_block(h, small)
    blocks[small_block, :] = piece[at_g, :]
    g_copies = spread(9, lambda s: blocks.at[small_block, :], lambda s: blocks.at[small_block, :])
    to_x[1](1)
    of_o[3]()
    out_o[0]()
    to_x[1](2)
    of_d[0][3]()
    out_d[0][0]()
    of_d[1][3]()
    out_d[1][0]()
    of_a[2]()
    gain_part[...] = piece[at_a, :]
    gain_copies = spread(10, lambda s: gain_part, lambda s: gain_got.at[s - 1])
    to_out[1](2)
    out_o[1]()
    for step in peers:
        g_copies[step].wait()
    out_g[0]()
    out_d[0][1]()
    gain = gain_part[...].astype(f32)
    for step in peers:
        gain_copies[step].wait()
        gain += gain_got[step - 1].astype(f32)
    piece[at_a, :] = gain.astype(bf16)
    out_a[0]()
    out_d[1][1]()
    out_o[2]()
    to_x[2](grad_x_ref)
    output_ref[...] = middle[...] + outs[own_block, :].astype(f32)
    to_out[2](output_ref)
    for half in range(2):
        first_hop(half, 0, chip)
        for copy in lasts[half]:
            copy.wait()
        at_in = (chip, halves_in[half], own_side)
        at_out = (chip, halves_out(core)[half], slice(None))
        w_in[at_in] = w_in[at_in] + hop_in[half, 1]
        w_out[at_out] = w_out[at_out] + hop_out[half, 1]
    stores = (
        pltpu.make_async_copy(w_in.at[chip, :, own_side], fin_in_ref, local_sem.at[0]),
        pltpu.make_async_copy(w_out.at[chip, own_side, :], fin_out_ref, local_sem.at[1]),
    )
    for store in stores:
        store.start()
    out_o[3]()
    out_d[0][2]()
    out_g[1]()
    out_a[1]()
    out_d[1][2]()
    out_d[0][3]()
    out_d[1][3]()
    for one in (out_o, out_d[0], out_g, out_a, out_d[1]):
        one[-1]()
    for store in stores:
        store.wait()
    mr_end()
    da_end()


def layer_call(n_dp, n_head, args):
    x, picks, router, value_mat, expert_in = args[0], args[2], args[13], args[11], args[14]
    tokens, features = x.shape
    per_device, _, width = expert_in.shape
    held_experts = value_mat.shape[1]
    group = tokens * n_head
    chips = n_dp // 2
    slab = per_device * width
    lanes = 128
    peers = n_head - 1
    named = ceil_to(n_dp * per_device, 8)
    small = ceil_to(named + 1, 16)
    top = features + held_experts
    held = top + 16 + small
    strip = features // n_dp
    shape = jax.ShapeDtypeStruct
    vm, dma = pltpu.VMEM, pltpu.SemaphoreType.DMA
    outs = [
        (shape((tokens, features), f32), VM),
        (shape((tokens, features), f32), VM),
        (shape((top + 16 + n_head * small, features), bf16), ANY),
        (shape((features, slab), bf16), ANY),
        (shape((slab, features), bf16), ANY),
    ]
    scratch = dict(
        picks=vm(picks.shape, jnp.int32),
        two_picks=vm((2, *args[3].shape), jnp.int32),
        head_picks=vm((group, lanes), jnp.int32),
        w_r=vm(router.shape, bf16),
        seg=vm((1, group), jnp.int32),
        gains=vm(args[6].shape, f32),
        angles=vm((group, width), f32),
        w_an=vm((features, 3 * width), bf16),
        w_v=vm((features, held_experts), bf16),
        w_o=vm((held_experts, features), bf16),
        my_router=vm((features, lanes), bf16),
        w_in=vm((chips, features, 2 * slab), bf16),
        w_out=vm((chips, 2 * slab, features), bf16),
        rows=vm((group, features), bf16),
        cot=vm((group, features), bf16),
        mrs=vm((group, features), bf16),
        das=vm((group, features), bf16),
        turned=vm((features, group), bf16),
        my_mask=vm((n_head, tokens, lanes), bf16),
        all_mask=vm((group, lanes), bf16),
        gates=vm((group, width), f32),
        q=vm((group, width), bf16),
        k=vm((group, width), bf16),
        v=vm((group, width), bf16),
        vx=vm((group, held_experts), bf16),
        att=vm((group, width), f32),
        part=vm((group, features), bf16),
        got=vm((2 * peers, tokens, features), bf16),
        outs=vm((group, features), bf16),
        got_out=vm((2 * peers, tokens, features), bf16),
        lifted=vm((chips, 2, group, slab), bf16),
        core_out=vm((chips, slab, features), bf16),
        acts=vm((chips, group, 2 * slab), bf16),
        hids=vm((chips, group, 2 * slab), bf16),
        dzs=vm((group, lanes), bf16),
        datt=vm((group, width), bf16),
        gate_grads=vm((group, width), f32),
        probs=vm((group, group), bf16),
        scores=vm((group, group), bf16),
        qkz=vm((group, 3 * width), bf16),
        vgrads=vm((group, held_experts), bf16),
        gain_part=vm((16, strip), bf16),
        gain_got=vm((peers, 16, strip), bf16),
        sums=vm((held, features), bf16),
        core_got=vm((held, features // 2), bf16),
        chip_got=vm((chips - 1, held, strip), bf16),
        piece=vm((held, strip), bf16),
        blocks=vm((n_head * small, strip), bf16),
        hop_in=vm((2, 2, features // 2, slab), bf16),
        hop_out=vm((2, 2, slab // 2, features), bf16),
        local_sem=dma((16 + 1 + per_device,)),
        z_send=dma((11, 4 * peers)),
        z_recv=dma((11, 4 * peers)),
        w_send=dma((22,)),
        w_recv=dma((22,)),
        c_send=dma((3, chips)),
        c_recv=dma((3, chips)),
        e_send=dma((2, 6)),
        e_recv=dma((2, 6)),
        s_send=dma((5, 3 * chips)),
        s_recv=dma((5, 3 * chips)),
        t_send=dma((3, 17)),
        t_recv=dma((3, 17)),
        ready=pltpu.SemaphoreType.REGULAR,
        free=pltpu.SemaphoreType.REGULAR((2,)),
    )
    return pl.pallas_call(
        functools.partial(layer_kernel, n_dp, n_head),
        out_shape=[o[0] for o in outs],
        out_specs=[o[1] for o in outs],
        in_specs=[VM if number == 10 else ANY for number in range(16)],
        scratch_shapes=list(scratch.values()),
        compiler_params=pltpu.CompilerParams(
            collective_id=1, has_side_effects=True, vmem_limit_bytes=vmem_bytes
        ),
    )(*args)


def finish_kernel(
    n_dp,
    n_head,
    output_ref,
    grad_x_ref,
    wide_ref,
    in_ref,
    out_ref,
    gain_ref,
    final_ref,
    input_ref,
    attend_ref,
    query_ref,
    key_ref,
    value_ref,
    mix_ref,
    gate_ref,
    expert_ref,
    router_ref,
    grad_in_ref,
    grad_out_ref,
    wide,
    flat_in,
    flat_out,
    value,
    mix,
    grad_in,
    grad_out,
    output,
    grad_x,
    query,
    key,
    sem,
):
    features, slab = in_ref.shape
    per_device, _, width = grad_in_ref.shape
    experts_total, gates = router_ref.shape[0], gate_ref.shape[0]
    mixed = mix_ref.shape[0]
    top = features + 16 + mixed
    small = (wide_ref.shape[0] - top) // n_head
    named = n_dp * per_device

    numbers = iter(range(sem.shape[0]))

    def copy(src, dst):
        one = pltpu.make_async_copy(src, dst, sem.at[next(numbers)])
        one.start()
        return one

    bands = 4
    band = features // bands
    load = lambda first, count: copy(
        wide_ref.at[pl.ds(first, count), :], wide.at[pl.ds(first, count), :]
    )
    plain = [(copy(output_ref, output), output, final_ref), (copy(grad_x_ref, grad_x), grad_x, input_ref)]
    for_out, for_in = copy(out_ref, flat_out), copy(in_ref, flat_in)
    for_bands = [load(n * band, band) for n in range(bands)]
    for_mix = [load(features + 16 + n * mixed // 2, mixed // 2) for n in range(2)]
    others = [load(features, 16), load(top, n_head * small)]
    stores = []
    gain = jnp.broadcast_to(gain_ref[0:1, :], (width, features)).T
    for loaded, held, result in plain:
        loaded.wait()
        stores.append(copy(held, result))
    for_out.wait()
    for e in range(per_device):
        grad_out[e] = flat_out[pl.ds(e * width, width), :].astype(f32)
        stores.append(copy(grad_out.at[e], grad_out_ref.at[e]))
    for_in.wait()
    for e in range(per_device):
        grad_in[e] = flat_in[:, pl.ds(e * width, width)].astype(f32)
        stores.append(copy(grad_in.at[e], grad_in_ref.at[e]))
    for n in range(bands):
        for_bands[n].wait()
        at = pl.ds(n * band, band)
        scale = gain[n * band : (n + 1) * band]
        value[at, :] = wide[at, pl.ds(3 * width, value.shape[1])].astype(f32)
        stores.append(copy(value.at[at, :], value_ref.at[at, :]))
        query[at, :] = wide[at, pl.ds(0, width)].astype(f32) * scale
        stores.append(copy(query.at[at, :], query_ref.at[at, :]))
        key[at, :] = wide[at, pl.ds(width, width)].astype(f32) * scale
        stores.append(copy(key.at[at, :], key_ref.at[at, :]))
    for n in range(2):
        for_mix[n].wait()
        at = pl.ds(n * mixed // 2, mixed // 2)
        mix[at, :] = wide[pl.ds(features + 16 + n * mixed // 2, mixed // 2), :].astype(f32)
        stores.append(copy(mix.at[at, :], mix_ref.at[at, :]))
    turned = (wide[pl.ds(0, features), pl.ds(2 * width, width)].astype(f32) * gain).T
    for e in range(gates):
        gate_ref[e] = turned[e : e + 1]
    for loaded in others:
        loaded.wait()
    attend_ref[...] = wide[pl.ds(features, 16), :][0:1].astype(f32)
    planes = wide[pl.ds(top, n_head * small), :]
    place = lax.broadcasted_iota(jnp.int32, (n_head * small, experts_total), 0)
    name = lax.broadcasted_iota(jnp.int32, (n_head * small, experts_total), 1)
    slot, plane = place % small, place // small
    expert = (slot // per_device * n_head + plane) * per_device + slot % per_device
    chosen = (slot < named) & (expert == name)
    router_ref[...] = dot(jnp.where(chosen, 1.0, 0.0).astype(bf16), planes, TN)
    gain = jnp.zeros((1, features), f32)
    for z in range(n_head):
        row = z * small + ceil_to(named, 8)
        gain += planes[row : row + 1].astype(f32)
    expert_ref[...] = gain
    for store in stores:
        store.wait()


def finish_call(n_dp, n_head, shapes, args):
    shape = jax.ShapeDtypeStruct
    wide, flat_in, flat_out = args[2], args[3], args[4]
    value, mix, grad_in, grad_out = shapes[5], shapes[6], shapes[10], shapes[11]
    specs = [VM] * 12
    for number in (0, 1, 3, 4, 5, 6, 10, 11):
        specs[number] = ANY
    return pl.pallas_call(
        functools.partial(finish_kernel, n_dp, n_head),
        out_shape=[shape(s, f32) for s in shapes],
        out_specs=specs,
        in_specs=[ANY] * 5 + [VM],
        scratch_shapes=[
            pltpu.VMEM(wide.shape, bf16),
            pltpu.VMEM(flat_in.shape, bf16),
            pltpu.VMEM(flat_out.shape, bf16),
            pltpu.VMEM(value, f32),
            pltpu.VMEM(mix, f32),
            pltpu.VMEM(grad_in, f32),
            pltpu.VMEM(grad_out, f32),
            pltpu.VMEM(shapes[0], f32),
            pltpu.VMEM(shapes[1], f32),
            pltpu.VMEM(shapes[3], f32),
            pltpu.VMEM(shapes[4], f32),
            pltpu.SemaphoreType.DMA((40,)),
        ],
        compiler_params=pltpu.CompilerParams(vmem_limit_bytes=60 << 20),
    )(*args)


def kernel_body(
    n_dp,
    n_head,
    hidden_in,
    segments,
    value_pick,
    output_pick,
    expert_pick,
    attend_gain,
    query_weight,
    key_weight,
    value_weight,
    output_weight,
    head_router,
    expert_gain,
    router,
    expert_in,
    expert_out,
    cotangent,
):
    tokens, features = hidden_in.shape
    per_device, _, width = expert_in.shape
    experts = head_router.shape[2] // 2
    group = tokens * n_head
    angles = np.arange(group)[:, None] * theta ** (-2.0 * np.arange(width // 2) / width)[None, :]
    angles = np.concatenate([np.cos(angles), np.sin(angles)], axis=1).astype(np.float32)
    first = np.arange(2)[:, None] == 0
    gains = jnp.where(first, attend_gain[None, :], expert_gain[None, :]).astype(f32)
    results = layer_call(
        n_dp,
        n_head,
        (
            hidden_in,
            cotangent,
            expert_pick.T,
            value_pick.transpose(1, 2, 0)[0],
            output_pick.transpose(1, 2, 0)[0],
            segments[None, :],
            gains,
            angles,
            query_weight[0],
            key_weight[0],
            head_router.transpose(0, 2, 1)[0],
            value_weight[0],
            output_weight[0],
            router.T,
            expert_in,
            expert_out.reshape(per_device * width, features),
        ),
    )
    shapes = (
        (tokens, features),
        (tokens, features),
        (1, features),
        query_weight.shape[1:],
        key_weight.shape[1:],
        value_weight.shape[1:],
        output_weight.shape[1:],
        (2 * experts, 1, features),
        (1, features),
        (router.shape[1], features),
        expert_in.shape,
        expert_out.shape,
    )
    done = list(finish_call(n_dp, n_head, shapes, (*results, gains)))
    for number in (3, 4, 5, 6):
        done[number] = done[number][None]
    done[7] = done[7].transpose(1, 2, 0)
    done[9] = done[9].T
    done[2], done[8] = done[2][0], done[8][0]
    return tuple(done)


def solution(mesh):
    rows = P(everywhere, None)
    heads = P("head", None, None)
    experts = P(everywhere, None, None)
    picks = P("dp", "head", None)
    in_specs = (
        rows, P("dp"), picks, picks, rows, P(), heads, heads, heads, heads, heads,
        P(), P(), experts, experts, rows,
    )
    out_specs = (
        rows, rows, P(), heads, heads, heads, heads, heads, P(), P(), experts, experts,
    )
    n_dp, n_head = mesh.shape["dp"], mesh.shape["head"]

    def program(*args):
        held = 2 * n_dp * args[13].shape[0] * args[13].shape[1] * args[13].shape[2] * 2
        if n_head == 4 and held <= vmem_for_weights:
            return kernel_body(n_dp, n_head, *args)
        return body(*args)

    return jax.shard_map(program, mesh=mesh, in_specs=in_specs, out_specs=out_specs, check_vma=False)
```
